32 devices in a mesh: dp: 8 (over y, x, core), tensor: 4 (over z).
Axes of the slice: x: 2, y: 2, z: 4, core: 2. Of those that a mesh axis runs over, the one named last changes fastest.
Arguments:
- layer_input: bfloat16 [16384, 1024], P(('dp', 'tensor')), may hold values from -11 to 11
- first_gain: bfloat16 [2, 1024], P(None, 'dp'), may hold values from 0.099609375 to 1.8984375
- first_shift: bfloat16 [2, 1024], P(None, 'dp'), may hold values from -1.5 to 1.5
- project_weight: bfloat16 [2, 3, 1024, 1024], P(None, None, 'dp', 'tensor')
- project_bias: bfloat16 [2, 2, 1024], P(None, None, ('tensor', 'dp'))
- output_weight: bfloat16 [2, 1024, 1024], P(None, 'tensor', 'dp'), may hold values from -0.75 to 0.75
- output_bias: bfloat16 [2, 1024], P(None, 'dp'), may hold values from -1.5 to 1.5
- second_gain: bfloat16 [2, 1024], P(None, 'dp'), may hold values from 0.099609375 to 1.8984375
- second_shift: bfloat16 [2, 1024], P(None, 'dp'), may hold values from -1.5 to 1.5
- expand_weight: bfloat16 [2, 1024, 4096], P(None, 'dp', 'tensor'), may hold values from -0.1875 to 0.1875
- expand_bias: bfloat16 [2, 4096], P(None, ('tensor', 'dp')), may hold values from -1.5 to 1.5
- reduce_weight: bfloat16 [2, 4096, 1024], P(None, 'tensor', 'dp'), may hold values from -0.09375 to 0.09375
- reduce_bias: bfloat16 [2, 1024], P(None, 'dp'), may hold values from -1.5 to 1.5
- picture_start: int32 [8, 2], P('dp'), may hold values from 0 to 1792, as said below
- cotangent: bfloat16 [16384, 1024], P(('dp', 'tensor')), may hold values from -6 to 6
Outputs:
- layer_output: bfloat16 [16384, 1024], P(('dp', 'tensor'))
- input_grad: bfloat16 [16384, 1024], P(('dp', 'tensor'))
- grad_first_gain: float32 [2, 1024], P(None, 'dp')
- grad_first_shift: float32 [2, 1024], P(None, 'dp')
- grad_project_weight: float32 [2, 3, 1024, 1024], P(None, None, 'dp', 'tensor')
- grad_project_bias: float32 [2, 2, 1024], P(None, None, ('tensor', 'dp'))
- grad_output_weight: float32 [2, 1024, 1024], P(None, 'tensor', 'dp')
- grad_output_bias: float32 [2, 1024], P(None, 'dp')
- grad_second_gain: float32 [2, 1024], P(None, 'dp')
- grad_second_shift: float32 [2, 1024], P(None, 'dp')
- grad_expand_weight: float32 [2, 1024, 4096], P(None, 'dp', 'tensor')
- grad_expand_bias: float32 [2, 4096], P(None, ('tensor', 'dp'))
- grad_reduce_weight: float32 [2, 4096, 1024], P(None, 'tensor', 'dp')
- grad_reduce_bias: float32 [2, 1024], P(None, 'dp')
The draws below stay inside these ranges and needn't reach their ends.
Inputs may be any that keep to these rules, and one draw needn't show every extreme that they name: `picture_start`: piece p of a sequence starts at a position from p * 1024 to (p + 1) * 1024 - 256, so pieces of one sequence never intersect and lie inside it.
All inputs are finite; a program needn't handle non-finite values.
Results may differ from the reference program's by a relative error of at most 0.025.
Values may be sent and summed in bfloat16 or wider, within the bound.
A program may use at most 256 MiB of HBM per device.

```python
import jax
import jax.numpy as jnp
from jax import lax

D = 1024
HEADS = 16
HD = 64
FF = 4096
LAYERS = 2
SEQ_LEN = 2048
PIECE = 256
PICS = 2
SEQS_GRP = 1
SEQS = 8
TOKENS = 16384


salience_gain = 35.0


def shared_query_bias(key):
    bias_key = jax.random.fold_in(key, 101)
    return jnp.clip(0.3 * jax.random.normal(bias_key, (LAYERS, D), jnp.float32), -1.5, 1.5)


def shared_signs(key):
    sign_key = jax.random.fold_in(key, 102)
    return (jax.random.randint(sign_key, (D,), 0, 2, dtype=jnp.int32) * 2 - 1).astype(jnp.float32)


def draw_layer_input(key, part):
    signs = shared_signs(key)
    key = jax.random.fold_in(key, 7)
    noise_key, pick_key, level_key = jax.random.split(key, 3)
    noise = jnp.clip(jax.random.normal(noise_key, (TOKENS, D), jnp.float32), -6.0, 6.0)
    chosen = jax.random.randint(pick_key, (TOKENS, 1), 0, 8, dtype=jnp.int32) == 0
    spread = jax.random.uniform(level_key, (TOKENS, 1), jnp.float32)
    level = jnp.where(chosen, 5.0 * spread * spread, 0.0)
    return (noise + level * signs[None, :]).astype(jnp.bfloat16)


def draw_project_bias(key, part):
    query_bias = shared_query_bias(key)
    key = jax.random.fold_in(key, 8)
    value_bias = jnp.clip(0.3 * jax.random.normal(key, (LAYERS, D), jnp.float32), -1.5, 1.5)
    return jnp.stack([query_bias, value_bias], axis=1).astype(jnp.bfloat16)


def draw_project_weight(key, part):
    query_bias = shared_query_bias(key)
    signs = shared_signs(key)
    key = jax.random.fold_in(key, 9)
    base = jnp.clip(jax.random.normal(key, (LAYERS, 3, D, D), jnp.float32), -6.0, 6.0)
    base = base * D ** (-0.5)
    aligned = salience_gain / D * signs[None, :, None] * query_bias[:, None, :]
    which = (jnp.arange(3, dtype=jnp.int32) == 1).astype(jnp.float32)
    return (base + which[None, :, None, None] * aligned[:, None, :, :]).astype(jnp.bfloat16)


def draw_picture_start(key, part):
    key = jax.random.fold_in(key, 11)
    half_span = SEQ_LEN // PICS
    offsets = jax.random.randint(key, (SEQS, PICS), 0, half_span - PIECE + 1, dtype=jnp.int32)
    return offsets + (jnp.arange(PICS, dtype=jnp.int32) * half_span)[None, :]


def block_scale(key, shape, cuts, smallest, top_value):
    factor_of = 1.0
    for axis_at, parts in cuts:
        draws = jax.random.uniform(jax.random.fold_in(jax.random.fold_in(key, 6), axis_at), (parts,), jnp.float32, smallest / len(cuts), top_value / len(cuts))
        factor_of = factor_of * jnp.repeat(jnp.exp(draws), shape[axis_at] // parts).reshape((-1,) + (1,) * (len(shape) - 1 - axis_at))
    return factor_of


def bell_draw(own_key, dims, scale, bound, pieces=(), kind=jnp.bfloat16):
    values = jax.random.normal(own_key, dims, jnp.float32) * scale
    if len(pieces) > 0:
        values = block_scale(own_key, dims, pieces, -0.22, 0.18) * values
    return jnp.clip(values, min=-bound, max=bound).astype(kind)


def setup_inputs(seed: int = 0) -> dict:
    arg_keys = jax.random.split(jax.random.key(seed), 16)
    return {
        "layer_input": draw_layer_input(jax.random.fold_in(arg_keys[15], 71), 0),
        "first_gain": jnp.clip(1.0 + 0.18 * jax.random.normal(arg_keys[1], (LAYERS, D), jnp.float32), 0.099609375, 1.8984375).astype(jnp.bfloat16),
        "first_shift": bell_draw(arg_keys[2], (LAYERS, D), 0.3, 1.5, ((1, 8),)),
        "project_weight": draw_project_weight(jax.random.fold_in(arg_keys[15], 71), 0),
        "project_bias": draw_project_bias(jax.random.fold_in(arg_keys[15], 71), 0),
        "output_weight": bell_draw(arg_keys[5], (LAYERS, D, D), HD ** -0.5, 0.75, ((1, 4), (2, 8))),
        "output_bias": bell_draw(arg_keys[6], (LAYERS, D), 0.3, 1.5, ((1, 8),)),
        "second_gain": jnp.clip(1.0 + 0.18 * jax.random.normal(arg_keys[7], (LAYERS, D), jnp.float32), 0.099609375, 1.8984375).astype(jnp.bfloat16),
        "second_shift": bell_draw(arg_keys[8], (LAYERS, D), 0.3, 1.5, ((1, 8),)),
        "expand_weight": bell_draw(arg_keys[9], (LAYERS, D, FF), D ** -0.5, 0.1875, ((1, 8), (2, 4))),
        "expand_bias": bell_draw(arg_keys[10], (LAYERS, FF), 0.3, 1.5, ((1, 32),)),
        "reduce_weight": bell_draw(arg_keys[11], (LAYERS, FF, D), FF ** -0.5, 0.09375, ((1, 4), (2, 8))),
        "reduce_bias": bell_draw(arg_keys[12], (LAYERS, D), 0.3, 1.5, ((1, 8),)),
        "picture_start": draw_picture_start(jax.random.fold_in(arg_keys[15], 71), 0),
        "cotangent": bell_draw(arg_keys[14], (TOKENS, D), 1.0, 6.0, ((0, 32),)),
    }


NORM_EPS = 1e-05
HIGHEST = lax.Precision.HIGHEST

@jax.custom_vjp
def low(v):
    return lax.optimization_barrier(v.astype(jnp.bfloat16)).astype(jnp.float32)

@jax.custom_vjp
def low_back(v):
    return v

def low_keep(v):
    return (low(v), None)

def low_pass(kept, grad):
    return (grad,)

def back_keep(v):
    return (v, None)

def back_low(kept, grad):
    return (low(grad),)
low.defvjp(low_keep, low_pass)
low_back.defvjp(back_keep, back_low)

def layer_norm(values, gain, shift):
    centred = values - lax.optimization_barrier(jnp.mean(values, axis=-1, keepdims=True))
    spread = lax.optimization_barrier(jnp.mean(centred * centred, axis=-1, keepdims=True))
    return centred * lax.rsqrt(spread + NORM_EPS) * gain + shift

def piece_numbers(starts):
    places = jnp.arange(SEQ_LEN, dtype=jnp.int32)
    inside = (places[:, None] >= starts[None, :]) & (places[:, None] < starts[None, :] + PIECE)
    numbers = jnp.arange(1, starts.shape[0] + 1, dtype=jnp.int32)
    return lax.optimization_barrier(jnp.sum(jnp.where(inside, numbers[None, :], 0), axis=1)).astype(jnp.int32)

def head_slopes(first_head, count_heads):
    heads_at = (first_head + jnp.arange(count_heads, dtype=jnp.int32)).astype(jnp.float32)
    return jnp.exp2(-8.0 * (heads_at + 1.0) / HEADS)

def attend(operands):
    queries, key_rows, value_rows, piece_ids = operands
    places = jnp.arange(SEQ_LEN, dtype=jnp.int32)
    slopes = head_slopes(0, HEADS)
    product = jnp.einsum('qhe,khe->hqk', queries, key_rows, precision=HIGHEST, preferred_element_type=jnp.float32)
    distance = jnp.abs(places[:, None] - places[None, :]).astype(jnp.float32)
    scores = low_back(product) * HD ** (-0.5) - slopes[:, None, None] * distance[None]
    allowed = (places[None, :] <= places[:, None]) | (piece_ids[:, None] == piece_ids[None, :]) & (piece_ids[:, None] > 0)
    scores = jnp.where(allowed[None], scores, -jnp.inf)
    row_max = lax.optimization_barrier(jnp.max(scores, axis=-1, keepdims=True))
    raw_weights = jnp.exp(scores - row_max)
    soft_weights = low(raw_weights / lax.optimization_barrier(jnp.sum(raw_weights, axis=-1, keepdims=True)))
    return jnp.einsum('hqk,khe->qhe', soft_weights, value_rows, precision=HIGHEST, preferred_element_type=jnp.float32)

def run_layer(resid, params, piece_ids):
    gain_one, shift_one, w_project, bias_project, w_output, bias_output, gain_two, shift_two, w_expand, bias_expand, w_reduce, bias_reduce = params
    count_rows = resid.shape[0]
    normed = low(layer_norm(resid, gain_one, shift_one))
    product = low_back(jnp.einsum('gd,cde->cge', normed, w_project, precision=HIGHEST, preferred_element_type=jnp.float32))
    biases = jnp.stack([bias_project[0], jnp.zeros_like(bias_project[0]), bias_project[1]])
    triple = low(product + biases[:, None, :])
    triple = triple.reshape(3, count_rows // SEQ_LEN, SEQ_LEN, HEADS, HD)
    attended = lax.map(jax.checkpoint(attend), (triple[0], triple[1], triple[2], piece_ids))
    attended = low(low_back(attended.reshape(count_rows, HEADS * HD)))
    resid = resid + (low_back(jnp.dot(attended, w_output, precision=HIGHEST, preferred_element_type=jnp.float32)) + bias_output)
    normed_two = low(layer_norm(resid, gain_two, shift_two))
    hidden = low_back(jnp.dot(normed_two, w_expand, precision=HIGHEST, preferred_element_type=jnp.float32)) + bias_expand
    active = low(jax.nn.gelu(hidden, approximate=True))
    return resid + (low_back(jnp.dot(active, w_reduce, precision=HIGHEST, preferred_element_type=jnp.float32)) + bias_reduce)

def reference(layer_input, first_gain, first_shift, project_weight, project_bias, output_weight, output_bias, second_gain, second_shift, expand_weight, expand_bias, reduce_weight, reduce_bias, picture_start, cotangent):
    params = tuple((array.astype(jnp.float32) for array in (first_gain, first_shift, project_weight, project_bias, output_weight, output_bias, second_gain, second_shift, expand_weight, expand_bias, reduce_weight, reduce_bias)))
    group_rows = SEQS_GRP * SEQ_LEN
    groups = layer_input.shape[0] // group_rows
    inputs = layer_input.astype(jnp.float32).reshape(groups, group_rows, D)
    cotangents = cotangent.astype(jnp.float32).reshape(groups, group_rows, D)
    starts = picture_start.reshape(groups, SEQS_GRP, PICS)

    def step(totals, operands):
        resid, grad_out, start_rows = operands
        piece_ids = jax.vmap(piece_numbers)(start_rows)

        def forward(param_set, stream):
            for layer_index in range(LAYERS):
                stream = run_layer(stream, tuple((array[layer_index] for array in param_set)), piece_ids)
            return stream
        result, pull = jax.vjp(forward, params, resid)
        grad_params, grad_stream = pull(grad_out)
        totals = jax.tree.map(jnp.add, totals, grad_params)
        return (totals, (result.astype(jnp.bfloat16), grad_stream.astype(jnp.bfloat16)))
    zeros = jax.tree.map(jnp.zeros_like, params)
    totals, (results, grads_in) = lax.scan(step, zeros, (inputs, cotangents, starts))
    return (results.reshape(-1, D), grads_in.reshape(-1, D), totals[0], totals[1], totals[2], totals[3], totals[4], totals[5], totals[6], totals[7], totals[8], totals[9], totals[10], totals[11])
```

```python
import functools

import jax
import jax.numpy as jnp
from jax import lax
from jax.experimental import pallas as pl
from jax.experimental.pallas import tpu as pltpu
from jax.sharding import PartitionSpec as P

HEADS = 16
HD = 64
LAYERS = 2
SEQ_LEN = 2048
PIECE = 256


NORM_EPS = 1e-05


def layer_norm(values, gain, shift):
    centred = values - jnp.mean(values, axis=-1, keepdims=True)
    spread = jnp.mean(centred * centred, axis=-1, keepdims=True)
    return centred * lax.rsqrt(spread + NORM_EPS) * gain + shift


def gelu_tanh(values):
    return jax.nn.gelu(values, approximate=True)


def piece_numbers(starts):
    places = jnp.arange(SEQ_LEN, dtype=jnp.int32)
    inside = (places[:, None] >= starts[None, :]) & (places[:, None] < starts[None, :] + PIECE)
    numbers = jnp.arange(1, starts.shape[0] + 1, dtype=jnp.int32)
    return jnp.sum(jnp.where(inside, numbers[None, :], 0), axis=1)


def head_slopes(first_head, count_heads):
    heads_at = (first_head + jnp.arange(count_heads, dtype=jnp.int32)).astype(jnp.float32)
    return jnp.exp2(-8.0 * (heads_at + 1.0) / HEADS)


def gather_rows(values):
    return lax.all_gather(values, "tensor", axis=0, tiled=True)


def gather_grads(values):
    return lax.all_gather(values, "tensor", axis=0, tiled=True)


def scatter_rows(values, weight):
    rows_here = values.shape[0] // lax.axis_size("tensor")

    def partial_term(offset, count_rows):
        return jnp.dot(values, weight, preferred_element_type=jnp.float32)

    return lax.psum_scatter(
        partial_term(jnp.int32(0), rows_here * lax.axis_size("tensor")).astype(jnp.bfloat16),
        "tensor",
        scatter_dimension=0,
        tiled=True,
    ).astype(jnp.float32)


def scatter_back(partial_term, rows_here):
    return lax.psum_scatter(
        partial_term(jnp.int32(0), rows_here * lax.axis_size("tensor")).astype(jnp.bfloat16),
        "tensor",
        scatter_dimension=0,
        tiled=True,
    ).astype(jnp.float32)


def block_scores(query_block, key_rows, offset, piece_ids, slopes):
    length = key_rows.shape[0]
    count_rows = query_block.shape[0]
    query_places = offset + jnp.arange(count_rows, dtype=jnp.int32)
    key_places = jnp.arange(length, dtype=jnp.int32)
    product = jnp.einsum("qhe,khe->hqk", query_block, key_rows, preferred_element_type=jnp.float32)
    distance = jnp.abs(query_places[:, None] - key_places[None, :]).astype(jnp.float32)
    scores = product * HD ** (-0.5) - slopes[:, None, None] * distance[None]
    query_pieces = lax.dynamic_slice_in_dim(piece_ids, offset, count_rows, 0)
    allowed = (key_places[None, :] <= query_places[:, None]) | (
        query_pieces[:, None] == piece_ids[None, :]
    ) & (query_pieces[:, None] > 0)
    return jnp.where(allowed[None], scores, -jnp.inf)


def sequence_forward(operands, slopes):
    queries, key_rows, value_rows, piece_ids = operands
    length = queries.shape[0]
    block_rows = min(512, length)

    def one_block(block_index):
        offset = block_index * block_rows
        query_block = lax.dynamic_slice_in_dim(queries, offset, block_rows, 0)
        scores = block_scores(query_block, key_rows, offset, piece_ids, slopes)
        row_max = jnp.max(scores, axis=-1, keepdims=True)
        raw_weights = jnp.exp(scores - row_max)
        totals = jnp.sum(raw_weights, axis=-1, keepdims=True)
        soft_weights = (raw_weights / totals).astype(jnp.bfloat16)
        attended = jnp.einsum(
            "hqk,khe->qhe", soft_weights, value_rows, preferred_element_type=jnp.float32
        )
        return (attended.astype(jnp.bfloat16), (row_max + jnp.log(totals))[..., 0])

    attended, log_total = lax.map(one_block, jnp.arange(length // block_rows, dtype=jnp.int32))
    return (attended.reshape(length, queries.shape[1], queries.shape[2]), log_total)


def sequence_backward(operands, slopes):
    queries, key_rows, value_rows, piece_ids, grad_mixed, log_total = operands
    length = queries.shape[0]
    block_rows = min(512, length)

    def one_block(carry, block_index):
        key_grad, value_grad = carry
        offset = block_index * block_rows
        query_block = lax.dynamic_slice_in_dim(queries, offset, block_rows, 0)
        grad_block = lax.dynamic_slice_in_dim(grad_mixed, offset, block_rows, 0)
        scores = block_scores(query_block, key_rows, offset, piece_ids, slopes)
        probs = jnp.exp(scores - log_total[block_index][..., None])
        soft_weights = probs.astype(jnp.bfloat16)
        value_grad = value_grad + jnp.einsum(
            "hqk,qhe->khe", soft_weights, grad_block, preferred_element_type=jnp.float32
        )
        prob_grad = jnp.einsum(
            "qhe,khe->hqk", grad_block, value_rows, preferred_element_type=jnp.float32
        )
        centred = jnp.sum(probs * prob_grad, axis=-1, keepdims=True)
        score_grad = (probs * (prob_grad - centred) * HD ** (-0.5)).astype(jnp.bfloat16)
        query_grad = jnp.einsum(
            "hqk,khe->qhe", score_grad, key_rows, preferred_element_type=jnp.float32
        )
        key_grad = key_grad + jnp.einsum(
            "hqk,qhe->khe", score_grad, query_block, preferred_element_type=jnp.float32
        )
        return ((key_grad, value_grad), query_grad)

    empty = jnp.zeros(queries.shape, jnp.float32)
    (key_grad, value_grad), query_grad = lax.scan(
        one_block, (empty, empty), jnp.arange(length // block_rows, dtype=jnp.int32)
    )
    return (query_grad.reshape(queries.shape), key_grad, value_grad)


def attend_forward(triple, piece_ids, slopes):
    width = triple.shape[2]
    count_seq = piece_ids.shape[0]
    length = piece_ids.shape[1]
    shaped = triple.reshape(3, count_seq, length, width // HD, HD)
    attended, log_total = lax.map(
        lambda operands: sequence_forward(operands, slopes),
        (shaped[0], shaped[1], shaped[2], piece_ids),
    )
    return (attended.reshape(count_seq * length, width), log_total)


def attend_backward(triple, grad_attended, log_total, piece_ids, slopes):
    width = triple.shape[2]
    count_seq = piece_ids.shape[0]
    length = piece_ids.shape[1]
    shaped = triple.reshape(3, count_seq, length, width // HD, HD)
    grad_shaped = grad_attended.reshape(count_seq, length, width // HD, HD)
    query_grad, key_grad, value_grad = lax.map(
        lambda operands: sequence_backward(operands, slopes),
        (shaped[0], shaped[1], shaped[2], piece_ids, grad_shaped, log_total),
    )
    return (
        query_grad.reshape(-1, width),
        key_grad.reshape(-1, width),
        value_grad.reshape(-1, width),
    )


def fetch_layer(
    project_weight,
    project_bias,
    output_weight,
    expand_weight,
    expand_bias,
    reduce_weight,
    small_stack,
    layer_index,
):
    return (
        lax.all_gather(project_weight[layer_index], "dp", axis=1, tiled=True),
        lax.all_gather(project_bias[layer_index], "dp", axis=1, tiled=True),
        lax.all_gather(output_weight[layer_index], "dp", axis=1, tiled=True),
        lax.all_gather(expand_weight[layer_index], "dp", axis=0, tiled=True),
        lax.all_gather(expand_bias[layer_index], "dp", axis=0, tiled=True),
        lax.all_gather(reduce_weight[layer_index], "dp", axis=1, tiled=True),
        lax.all_gather(small_stack[layer_index], "dp", axis=1, tiled=True),
    )


def forward_layer(resid, weights, piece_ids, slopes):
    w_project, bias_project, w_output, w_expand, bias_expand, w_reduce, small = weights
    vectors = small.astype(jnp.float32)
    normed = layer_norm(resid, vectors[0], vectors[1])
    gathered = gather_rows(normed.astype(jnp.bfloat16))
    product = jnp.einsum("gd,cde->cge", gathered, w_project, preferred_element_type=jnp.float32)
    biases = jnp.stack([bias_project[0], jnp.zeros_like(bias_project[0]), bias_project[1]]).astype(
        jnp.float32
    )
    triple = (product + biases[:, None, :]).astype(jnp.bfloat16)
    attended, log_total = attend_forward(triple, piece_ids, slopes)
    resid_mid = resid + (scatter_rows(attended, w_output) + vectors[2])
    normed_two = layer_norm(resid_mid, vectors[3], vectors[4])
    gathered_two = gather_rows(normed_two.astype(jnp.bfloat16))
    hidden = jnp.dot(
        gathered_two, w_expand, preferred_element_type=jnp.float32
    ) + bias_expand.astype(jnp.float32)
    active = gelu_tanh(hidden).astype(jnp.bfloat16)
    mlp_sum = scatter_rows(active, w_reduce)
    mlp_keep = (gathered_two, hidden, None)
    resid_out = resid_mid + (mlp_sum + vectors[5])
    return (resid_out, (gathered, triple, attended, log_total, resid_mid, mlp_keep))


def backward_layer(grad_out, resid, weights, kept, piece_ids, slopes):
    w_project, bias_project, w_output, w_expand, bias_expand, w_reduce, small = weights
    vectors = small.astype(jnp.float32)
    gathered, triple, attended, log_total, resid_mid, mlp_keep = kept
    rows_here = grad_out.shape[0]
    rows_in, hidden, full_weights = mlp_keep
    grad_bias_reduce = jnp.sum(grad_out, axis=0)
    active, gelu_pull = jax.vjp(gelu_tanh, hidden)
    active_low = active.astype(jnp.bfloat16)
    grad_mlp = gather_grads(grad_out.astype(jnp.bfloat16))
    grad_reduce = jnp.einsum("gf,gd->fd", active_low, grad_mlp, preferred_element_type=jnp.float32)
    grad_active = jnp.einsum("gd,fd->gf", grad_mlp, w_reduce, preferred_element_type=jnp.float32)
    (grad_hidden,) = gelu_pull(grad_active)
    grad_bias_expand = jnp.sum(grad_hidden, axis=0)
    grad_hidden_low = grad_hidden.astype(jnp.bfloat16)
    grad_expand = jnp.einsum(
        "gd,gf->df", rows_in, grad_hidden_low, preferred_element_type=jnp.float32
    )

    def expand_term(offset, count_rows):
        return jnp.einsum(
            "gf,df->gd", grad_hidden_low, w_expand, preferred_element_type=jnp.float32
        )

    grad_normed_two = scatter_back(expand_term, rows_here)
    unused_two, second_pull = jax.vjp(layer_norm, resid_mid, vectors[3], vectors[4])
    grad_from_norm, grad_gain_two, grad_shift_two = second_pull(grad_normed_two)
    grad_mid = grad_out + grad_from_norm
    grad_bias_output = jnp.sum(grad_mid, axis=0)
    grad_attn = gather_grads(grad_mid.astype(jnp.bfloat16))
    grad_output = jnp.einsum("gt,gd->td", attended, grad_attn, preferred_element_type=jnp.float32)
    grad_attended = jnp.einsum(
        "gd,td->gt", grad_attn, w_output, preferred_element_type=jnp.float32
    ).astype(jnp.bfloat16)
    query_grad, key_grad, value_grad = attend_backward(
        triple, grad_attended, log_total, piece_ids, slopes
    )
    grad_bias_project = jnp.stack([jnp.sum(query_grad, axis=0), jnp.sum(value_grad, axis=0)])
    grad_triple = jnp.stack([query_grad, key_grad, value_grad]).astype(jnp.bfloat16)
    grad_project = jnp.einsum(
        "gd,cge->cde", gathered, grad_triple, preferred_element_type=jnp.float32
    )

    def project_term(offset, count_rows):
        return jnp.einsum("cge,cde->gd", grad_triple, w_project, preferred_element_type=jnp.float32)

    grad_normed = scatter_back(project_term, rows_here)
    unused_one, first_pull = jax.vjp(layer_norm, resid, vectors[0], vectors[1])
    grad_from_first, grad_gain_one, grad_shift_one = first_pull(grad_normed)
    grad_stream = grad_mid + grad_from_first
    small_grads = jnp.stack(
        [
            grad_gain_one,
            grad_shift_one,
            grad_bias_output,
            grad_gain_two,
            grad_shift_two,
            grad_bias_reduce,
        ]
    )
    return (
        grad_stream,
        (
            grad_project,
            grad_bias_project,
            grad_output,
            grad_expand,
            grad_bias_expand,
            grad_reduce,
            small_grads,
        ),
    )


def reduce_layer(layer_grads):
    (
        grad_project,
        grad_bias_project,
        grad_output,
        grad_expand,
        grad_bias_expand,
        grad_reduce,
        small_grads,
    ) = layer_grads
    return (
        lax.psum_scatter(
            grad_project.astype(jnp.bfloat16), "dp", scatter_dimension=1, tiled=True
        ).astype(jnp.float32),
        lax.psum_scatter(
            grad_bias_project.astype(jnp.bfloat16), "dp", scatter_dimension=1, tiled=True
        ).astype(jnp.float32),
        lax.psum_scatter(
            grad_output.astype(jnp.bfloat16), "dp", scatter_dimension=1, tiled=True
        ).astype(jnp.float32),
        lax.psum_scatter(
            grad_expand.astype(jnp.bfloat16), "dp", scatter_dimension=0, tiled=True
        ).astype(jnp.float32),
        lax.psum_scatter(
            grad_bias_expand.astype(jnp.bfloat16), "dp", scatter_dimension=0, tiled=True
        ).astype(jnp.float32),
        lax.psum_scatter(
            grad_reduce.astype(jnp.bfloat16), "dp", scatter_dimension=1, tiled=True
        ).astype(jnp.float32),
        lax.psum_scatter(
            small_grads.astype(jnp.bfloat16), "dp", scatter_dimension=1, tiled=True
        ).astype(jnp.float32),
    )


def on_device(
    layer_input,
    first_gain,
    first_shift,
    project_weight,
    project_bias,
    output_weight,
    output_bias,
    second_gain,
    second_shift,
    expand_weight,
    expand_bias,
    reduce_weight,
    reduce_bias,
    picture_start,
    cotangent,
):
    small_stack = jnp.stack(
        [first_gain, first_shift, output_bias, second_gain, second_shift, reduce_bias], axis=1
    )
    piece_ids = jax.vmap(piece_numbers)(picture_start)
    heads_here = project_weight.shape[3] // HD
    slopes = head_slopes(lax.axis_index("tensor") * heads_here, heads_here)
    resid = layer_input.astype(jnp.float32)
    saved = []
    for layer_index in range(LAYERS):
        weights = fetch_layer(
            project_weight,
            project_bias,
            output_weight,
            expand_weight,
            expand_bias,
            reduce_weight,
            small_stack,
            layer_index,
        )
        resid_next, kept = forward_layer(resid, weights, piece_ids, slopes)
        saved.append((resid, weights, kept))
        resid = resid_next
    layer_output = resid.astype(jnp.bfloat16)
    grad_stream = cotangent.astype(jnp.float32)
    collected = []
    for layer_index in reversed(range(LAYERS)):
        resid_in, weights, kept = saved[layer_index]
        grad_stream, layer_grads = backward_layer(
            grad_stream, resid_in, weights, kept, piece_ids, slopes
        )
        layer_grads = reduce_layer(layer_grads)
        collected.insert(0, layer_grads)
    stacked = tuple(
        (jnp.stack([grad_entry[member] for grad_entry in collected]) for member in range(7))
    )
    (
        grad_project,
        grad_bias_project,
        grad_output,
        grad_expand,
        grad_bias_expand,
        grad_reduce,
        small_grads,
    ) = stacked
    small_grads = lax.psum(small_grads, "tensor")
    return (
        layer_output,
        grad_stream.astype(jnp.bfloat16),
        small_grads[:, 0],
        small_grads[:, 1],
        grad_project,
        grad_bias_project,
        grad_output,
        small_grads[:, 2],
        small_grads[:, 3],
        small_grads[:, 4],
        grad_expand,
        grad_bias_expand,
        grad_reduce,
        small_grads[:, 5],
    )


Z0, Z1, CORE, XBIT, YBIT = 1, 2, 4, 8, 16
AXES = ("dp", "tensor")
NEG = -1e30
BF = jnp.bfloat16
F32 = jnp.float32


def mesh_is_paired(mesh):
    return dict(mesh.shape) == {"dp": 8, "tensor": 4}


def swap(values, mask):
    return lax.ppermute(values, AXES, [(i, i ^ mask) for i in range(32)])


def redeal(values):
    def target(i):
        core, z1 = (i >> 2) & 1, (i >> 1) & 1
        return (i & ~6) | (z1 << 2) | (core << 1)

    return lax.ppermute(values, AXES, [(i, target(i)) for i in range(32)])


def turn_blocks(values, own):
    width = values.shape[1] // 8
    return jnp.concatenate(
        [lax.dynamic_slice_in_dim(values, (own ^ i) * width, width, 1) for i in range(8)], axis=1
    )


def dot_nt(a, b):
    return lax.dot_general(a, b, (((1,), (1,)), ((), ())), preferred_element_type=jnp.float32)


def dot_nn(a, b):
    return lax.dot_general(a, b, (((1,), (0,)), ((), ())), preferred_element_type=jnp.float32)


def dot_tn(a, b):
    return lax.dot_general(a, b, (((0,), (0,)), ((), ())), preferred_element_type=jnp.float32)


def head_mask(shape, head):
    lane = lax.broadcasted_iota(jnp.int32, shape, 1)
    return (lane < HD) if head == 0 else (lane >= HD)


def diagonal_bias(rows, columns, first_row, first_column, start):
    key = first_row + lax.broadcasted_iota(jnp.int32, (rows, 1), 0)
    query = first_column + lax.broadcasted_iota(jnp.int32, (1, columns), 1)
    key_in = (key >= start) & (key < start + PIECE)
    query_in = (query >= start) & (query < start + PIECE)
    allowed = (key <= query) | (key_in & query_in)
    reach = (jnp.minimum(key, 2 * query - key) - first_column).astype(jnp.float32)
    return jnp.where(allowed, reach, NEG)


def ramp(rows, first_row, first_column):
    return (first_row - first_column + lax.broadcasted_iota(jnp.int32, (rows, 1), 0)).astype(jnp.float32)


def attend_kernel(block, slope_ref, start_ref, me_ref, q_ref, k_ref, v_ref, o_ref, exact_ref, lse_ref, vt_ref, acc_ref, max_ref, bias_ref, tail_ref):
    pair = pl.program_id(0)
    turn = pl.program_id(1)
    me = me_ref[0]
    step = turn ^ me
    length = k_ref.shape[0]
    first = step * block

    def at(index):
        return pl.multiple_of((index ^ me) * block, block)

    start = start_ref[(step * block) // (length // start_ref.shape[0])]

    @pl.when(turn == 0)
    def _():
        for head in range(2):
            mixed = jnp.where(head_mask((length, 2 * HD), head), v_ref[...], jnp.ones((), v_ref.dtype))
            vt_ref[head] = mixed.astype(jnp.float32).T.astype(jnp.bfloat16)

    bias_ref[...] = diagonal_bias(block, block, first, first, start)
    q_block = q_ref[...] * jnp.asarray(HD ** -0.5, jnp.bfloat16)
    heads = [jnp.where(head_mask(q_block.shape, head), q_block, jnp.zeros((), q_block.dtype)) for head in range(2)]
    slopes = [slope_ref[2 * pair + head] for head in range(2)]
    acc_ref[...] = jnp.zeros_like(acc_ref)
    max_ref[...] = jnp.full_like(max_ref, NEG)

    def absorb(head, scores, vt):
        old = max_ref[head]
        new = jnp.maximum(old, jnp.max(scores, axis=0, keepdims=True))
        weights = jnp.exp(scores - new).astype(jnp.bfloat16)
        acc_ref[head] = acc_ref[head] * jnp.exp(old - new) + dot_nn(vt, weights)
        max_ref[head] = new

    def full(index, carry):
        place = at(index)
        keys = k_ref[pl.ds(place, block), :]
        slant = ramp(block, index * block, first)
        for head in range(2):
            absorb(head, dot_nt(keys, heads[head]) + slopes[head] * slant, vt_ref[head, :, pl.ds(place, block)])
        return carry

    place = at(step)
    for head in range(2):
        absorb(
            head,
            dot_nt(k_ref[pl.ds(place, block), :], heads[head]) + slopes[head] * bias_ref[...],
            vt_ref[head, :, pl.ds(place, block)],
        )
    lax.fori_loop(0, step, full, 0)
    edge = first + block

    @pl.when((start < edge) & (start + PIECE > edge))
    def _():
        after = at(step + 1)
        tail_ref[...] = diagonal_bias(PIECE, block, edge, first, start)
        for head in range(2):
            absorb(
                head,
                dot_nt(k_ref[pl.ds(after, PIECE), :], heads[head]) + slopes[head] * tail_ref[...],
                vt_ref[head, :, pl.ds(after, PIECE)],
            )

    outs = []
    for head in range(2):
        acc = acc_ref[head]
        total = acc[HD:HD + 1] if head == 0 else acc[0:1]
        outs.append((acc * (1.0 / total))[head * HD:(head + 1) * HD])
        lse_ref[0, head:head + 1, :] = max_ref[head] + jnp.log(total)
    mixed = jnp.concatenate(outs, axis=0)
    exact_ref[...] = mixed
    o_ref[...] = mixed.T.astype(jnp.bfloat16)


def attend(triple, slopes, starts, me, block=512):
    length, width = triple.shape[0], triple.shape[1] // 3
    pairs = width // (2 * HD)
    steps = length // block
    smem = pl.BlockSpec(memory_space=pltpu.SMEM)
    return pl.pallas_call(
        functools.partial(attend_kernel, block),
        grid=(pairs, steps),
        in_specs=[
            smem,
            smem,
            smem,
            pl.BlockSpec((block, 2 * HD), lambda p, i: (i, p)),
            pl.BlockSpec((length, 2 * HD), lambda p, i: (0, pairs + p)),
            pl.BlockSpec((length, 2 * HD), lambda p, i: (0, 2 * pairs + p)),
        ],
        out_specs=[
            pl.BlockSpec((block, 2 * HD), lambda p, i: (i, p)),
            pl.BlockSpec((2 * HD, block), lambda p, i: (p, i)),
            pl.BlockSpec((1, 8, block), lambda p, i: (p, 0, i)),
        ],
        out_shape=[
            jax.ShapeDtypeStruct((length, width), jnp.bfloat16),
            jax.ShapeDtypeStruct((width, length), jnp.float32),
            jax.ShapeDtypeStruct((pairs, 8, length), jnp.float32),
        ],
        scratch_shapes=[
            pltpu.VMEM((2, 2 * HD, length), jnp.bfloat16),
            pltpu.VMEM((2, 2 * HD, block), jnp.float32),
            pltpu.VMEM((2, 1, block), jnp.float32),
            pltpu.VMEM((block, block), jnp.float32),
            pltpu.VMEM((PIECE, block), jnp.float32),
        ],
        compiler_params=pltpu.CompilerParams(vmem_limit_bytes=48 * 1024 * 1024),
        name="attend",
    )(slopes, starts, me, triple, triple, triple)


def pull_kernel(block, slope_ref, start_ref, me_ref, q_ref, k_ref, v_ref, o_ref, g_ref, lse_ref, dq_ref, dk_ref, dv_ref,
                kt_ref, dk_acc, dv_acc, dqt_ref, bias_ref, tail_ref):
    pair = pl.program_id(0)
    turn = pl.program_id(1)
    me = me_ref[0]
    step = turn ^ me
    length = k_ref.shape[0]
    first = step * block

    def at(index):
        return pl.multiple_of((index ^ me) * block, block)

    start = start_ref[(step * block) // (length // start_ref.shape[0])]

    @pl.when(turn == 0)
    def _():
        kt_ref[...] = k_ref[...].astype(jnp.float32).T.astype(jnp.bfloat16)
        dk_acc[...] = jnp.zeros_like(dk_acc)
        dv_acc[...] = jnp.zeros_like(dv_acc)

    bias_ref[...] = diagonal_bias(block, block, first, first, start)
    dqt_ref[...] = jnp.zeros_like(dqt_ref)
    scale = jnp.asarray(HD ** -0.5, jnp.bfloat16)
    zero = jnp.zeros((), jnp.bfloat16)
    q_block = q_ref[...] * scale
    g_block = g_ref[...]
    masks = [head_mask(q_block.shape, head) for head in range(2)]
    q_heads = [jnp.where(mask, q_block, zero) for mask in masks]
    g_heads = [jnp.where(mask, g_block, zero) for mask in masks]
    slopes = [slope_ref[2 * pair + head] for head in range(2)]
    product = g_block.astype(jnp.float32).T * o_ref[...]
    deltas = [jnp.sum(product[head * HD:(head + 1) * HD], axis=0, keepdims=True) for head in range(2)]

    def absorb(place, rows, bias_of):
        keys = k_ref[pl.ds(place, rows), :]
        values = v_ref[pl.ds(place, rows), :]
        dk = dk_acc[pl.ds(place, rows), :]
        dv = dv_acc[pl.ds(place, rows), :]
        for head in range(2):
            scores = dot_nt(keys, q_heads[head]) + slopes[head] * bias_of
            weights = jnp.exp(scores - lse_ref[0, head:head + 1, :])
            dv = dv + dot_nn(weights.astype(jnp.bfloat16), g_heads[head])
            grad_p = dot_nt(values, g_heads[head])
            grad_s = (weights * (grad_p - deltas[head])).astype(jnp.bfloat16)
            dk = dk + dot_nn(grad_s, q_heads[head])
            dqt_ref[head * HD:(head + 1) * HD, :] += dot_nn(kt_ref[head * HD:(head + 1) * HD, pl.ds(place, rows)], grad_s)
        dk_acc[pl.ds(place, rows), :] = dk
        dv_acc[pl.ds(place, rows), :] = dv

    absorb(at(step), block, bias_ref[...])

    def full(index, carry):
        absorb(at(index), block, ramp(block, index * block, first))
        return carry

    lax.fori_loop(0, step, full, 0)
    edge = first + block

    @pl.when((start < edge) & (start + PIECE > edge))
    def _():
        tail_ref[...] = diagonal_bias(PIECE, block, edge, first, start)
        absorb(at(step + 1), PIECE, tail_ref[...])

    dq_ref[...] = (dqt_ref[...].T * (HD ** -0.5)).astype(jnp.bfloat16)

    @pl.when(turn == pl.num_programs(1) - 1)
    def _():
        dk_ref[...] = dk_acc[...].astype(jnp.bfloat16)
        dv_ref[...] = dv_acc[...].astype(jnp.bfloat16)


def attend_pull(triple, o, g, lse, slopes, starts, me, block=512):
    width, length = o.shape
    pairs = width // (2 * HD)
    steps = length // block
    smem = pl.BlockSpec(memory_space=pltpu.SMEM)
    rows = pl.BlockSpec((block, 2 * HD), lambda p, i: (i, p))
    whole = pl.BlockSpec((length, 2 * HD), lambda p, i: (0, p))
    return pl.pallas_call(
        functools.partial(pull_kernel, block),
        grid=(pairs, steps),
        in_specs=[
            smem,
            smem,
            smem,
            rows,
            pl.BlockSpec((length, 2 * HD), lambda p, i: (0, pairs + p)),
            pl.BlockSpec((length, 2 * HD), lambda p, i: (0, 2 * pairs + p)),
            pl.BlockSpec((2 * HD, block), lambda p, i: (p, i)),
            rows,
            pl.BlockSpec((1, 8, block), lambda p, i: (p, 0, i)),
        ],
        out_specs=[rows, whole, whole],
        out_shape=[jax.ShapeDtypeStruct((length, width), jnp.bfloat16)] * 3,
        scratch_shapes=[
            pltpu.VMEM((2 * HD, length), jnp.bfloat16),
            pltpu.VMEM((length, 2 * HD), jnp.float32),
            pltpu.VMEM((length, 2 * HD), jnp.float32),
            pltpu.VMEM((2 * HD, block), jnp.float32),
            pltpu.VMEM((block, block), jnp.float32),
            pltpu.VMEM((PIECE, block), jnp.float32),
        ],
        compiler_params=pltpu.CompilerParams(vmem_limit_bytes=48 * 1024 * 1024),
        name="attend_pull",
    )(slopes, starts, me, triple, triple, triple, o, g, lse)


def joined_expand(refs, tile):
    return jnp.concatenate(
        [
            jnp.concatenate([ref[0, chunk * 128:(chunk + 1) * 128, :] for ref in refs], axis=0)
            for chunk in range(tile // 128)
        ],
        axis=1,
    )


def joined_reduce(refs, tile):
    return jnp.concatenate([ref[0, tile:, :] for ref in refs], axis=1)


GELU_A = 0.7978845608028654
GELU_B = 0.044715


def mlp_kernel(normed_ref, bias_ref, *rest):
    weight_refs, (hidden_ref, out_ref) = rest[:8], rest[8:]
    tile = hidden_ref.shape[1]
    hidden = dot_nn(normed_ref[...], joined_expand(weight_refs, tile)) + bias_ref[...]
    inner = jnp.tanh(GELU_A * (hidden + GELU_B * hidden * hidden * hidden))
    active = (0.5 * hidden * (1.0 + inner)).astype(BF)
    hidden_ref[...] = hidden.astype(hidden_ref.dtype)
    term = dot_nn(active, joined_reduce(weight_refs, tile))

    @pl.when(pl.program_id(0) == 0)
    def _():
        out_ref[...] = term

    @pl.when(pl.program_id(0) > 0)
    def _():
        out_ref[...] += term


def mlp_forward(normed, bias, bundles):
    rows, features = normed.shape
    units = bias.shape[1]
    tile = 512
    weight_spec = pl.BlockSpec((1, 2 * tile, 128), lambda f: (f // 2, f % 2, 0))
    return pl.pallas_call(
        mlp_kernel,
        grid=(units // tile,),
        in_specs=[
            pl.BlockSpec((rows, features), lambda f: (0, 0)),
            pl.BlockSpec((1, tile), lambda f: (0, f)),
        ]
        + [weight_spec] * 8,
        out_specs=[
            pl.BlockSpec((rows, tile), lambda f: (0, f)),
            pl.BlockSpec((rows, features), lambda f: (0, 0)),
        ],
        out_shape=[
            jax.ShapeDtypeStruct((rows, units), BF),
            jax.ShapeDtypeStruct((rows, features), F32),
        ],
        compiler_params=pltpu.CompilerParams(vmem_limit_bytes=48 * 1024 * 1024),
        cost_estimate=pl.CostEstimate(flops=4 * rows * features * units, bytes_accessed=4 * features * units, transcendentals=0),
        name="mlp_forward",
    )(normed, bias, *bundles)


def mlp_pull_kernel(grad_ref, normed_ref, hidden_ref, *rest):
    weight_refs = rest[:8]
    grad_normed_ref, grad_bias_ref = rest[8:10]
    out_refs = rest[10:18]
    normed_t_ref = rest[18]
    tile = hidden_ref.shape[1]

    @pl.when(pl.program_id(0) == 0)
    def _():
        normed_t_ref[...] = normed_ref[...].astype(F32).T.astype(BF)

    grad = grad_ref[...]
    hidden = hidden_ref[...].astype(F32)
    squared = hidden * hidden
    inner = jnp.tanh(GELU_A * hidden * (1.0 + GELU_B * squared))
    half_up = 0.5 * (1.0 + inner)
    active = hidden * half_up
    slope = half_up + 0.5 * hidden * (1.0 - inner * inner) * (GELU_A * (1.0 + 3.0 * GELU_B * squared))
    grad_active = dot_nt(grad, joined_reduce(weight_refs, tile))
    grad_hidden = grad_active * slope
    grad_bias_ref[...] = jnp.sum(grad_hidden, axis=0, keepdims=True)
    grad_hidden = grad_hidden.astype(BF)
    grad_reduce = dot_nn(active.T.astype(BF), grad).astype(BF)
    grad_expand = dot_nn(normed_t_ref[...], grad_hidden).astype(BF)
    for index, out_ref in enumerate(out_refs):
        for chunk in range(tile // 128):
            out_ref[0, chunk * 128:(chunk + 1) * 128, :] = grad_expand[
                index * 128:(index + 1) * 128, chunk * 128:(chunk + 1) * 128
            ]
        out_ref[0, tile:, :] = grad_reduce[:, index * 128:(index + 1) * 128]
    term = dot_nt(grad_hidden, joined_expand(weight_refs, tile))

    @pl.when(pl.program_id(0) == 0)
    def _():
        grad_normed_ref[...] = term

    @pl.when(pl.program_id(0) > 0)
    def _():
        grad_normed_ref[...] += term


def mlp_backward(grad, normed, hidden, bundles):
    rows, features = normed.shape
    units = hidden.shape[1]
    tile = 512
    weight_spec = pl.BlockSpec((1, 2 * tile, 128), lambda f: (f // 2, f % 2, 0))
    whole = pl.BlockSpec((rows, features), lambda f: (0, 0))
    return pl.pallas_call(
        mlp_pull_kernel,
        grid=(units // tile,),
        in_specs=[whole, whole, pl.BlockSpec((rows, tile), lambda f: (0, f))] + [weight_spec] * 8,
        out_specs=[whole, pl.BlockSpec((1, tile), lambda f: (0, f))] + [weight_spec] * 8,
        out_shape=[
            jax.ShapeDtypeStruct((rows, features), F32),
            jax.ShapeDtypeStruct((1, units), F32),
        ]
        + [jax.ShapeDtypeStruct((units // 1024, 2048, 128), BF)] * 8,
        scratch_shapes=[pltpu.VMEM((features, rows), BF)],
        compiler_params=pltpu.CompilerParams(vmem_limit_bytes=56 * 1024 * 1024),
        cost_estimate=pl.CostEstimate(flops=8 * rows * features * units, bytes_accessed=8 * features * units, transcendentals=0),
        name="mlp_backward",
    )(grad, normed, hidden, *bundles)


def gather_plane(own):
    half = own.shape[0] // 2
    from_x = swap(own, XBIT)
    from_y = swap(own, YBIT)
    across = jnp.concatenate([swap(from_x[:half], YBIT), swap(from_y[half:], XBIT)], axis=0)
    quads = [own, from_x, from_y, across]
    out = []
    for quad in quads:
        out += [quad, swap(quad, CORE)]
    return out


def scatter_plane(pieces):
    kept = [pieces[2 * i] + swap(pieces[2 * i + 1], CORE) for i in range(4)]
    own, to_x, to_y, across = kept
    half = own.shape[0] // 2
    to_x = jnp.concatenate([to_x[:half] + swap(across[:half], YBIT), to_x[half:]], axis=0)
    to_y = jnp.concatenate([to_y[:half], to_y[half:] + swap(across[half:], XBIT)], axis=0)
    return own + swap(to_x, XBIT) + swap(to_y, YBIT)


def pack_mlp(expand, reduce):
    first = expand.reshape(128, 2, 4, 128).transpose(1, 2, 0, 3).reshape(2, 512, 128)
    return jnp.concatenate([first, reduce.reshape(2, 512, 128)], axis=1).reshape(2048, 128)


def unpack_mlp(values):
    shaped = values.reshape(2, 2, 512, 128)
    return (
        shaped[:, 0].reshape(2, 4, 128, 128).transpose(2, 0, 1, 3).reshape(128, 1024),
        shaped[:, 1].reshape(1024, 128),
    )


def pack_attention(project, output):
    first = project.reshape(3, 128, 2, 128).transpose(0, 2, 1, 3).reshape(768, 128)
    return jnp.concatenate([first, output], axis=0)


def unpack_attention(values):
    return (
        values[:768].reshape(3, 2, 128, 128).transpose(0, 2, 1, 3).reshape(3, 128, 256),
        values[768:],
    )


def fast_fetch_attention(project, output, small, core, own):
    piece = jnp.concatenate([pack_attention(project, output), small], axis=0)
    far = swap(piece, Z1)
    first = jnp.where(core == 0, piece, far)
    second = jnp.where(core == 0, far, piece)
    parts = gather_plane(jnp.stack([first, second]))
    parts = [part if index % 2 == 0 else part[::-1] for index, part in enumerate(parts)]
    vectors = jnp.concatenate([part[0, 1024:1030] for part in parts], axis=1).astype(F32)
    weights = []
    for quarter in range(2):
        w_project = jnp.concatenate(
            [part[quarter, :768].reshape(6, 128, 128).transpose(1, 0, 2).reshape(128, 768) for part in parts], axis=0
        )
        w_output = jnp.concatenate([part[quarter, 768:1024] for part in parts], axis=1)
        biases = jnp.stack([part[quarter, 1030:1032, :32] for part in parts]).astype(F32)
        biases = biases[jnp.arange(8) ^ own].transpose(1, 0, 2).reshape(2, 256)
        bias = jnp.concatenate([biases[0], jnp.zeros_like(biases[0]), biases[1]])
        weights.append((w_project, bias, w_output))
    return vectors, weights


def fast_fetch_mlp(expand, reduce, bias, own):
    piece = jnp.concatenate(
        [pack_mlp(expand, reduce), jnp.broadcast_to(bias[None], (16, 128))], axis=0
    )
    parts = gather_plane(jnp.stack([piece, swap(piece, 1), swap(piece, 2), swap(piece, 3)]))
    biases = jnp.stack([part[:, 2048] for part in parts], axis=1).astype(F32)
    biases = biases[:, jnp.arange(8) ^ own].reshape(1, 4096)
    return parts, biases


def fast_forward(resid, vectors, heads_weights, mlp_weights, slopes, starts, me):
    (w_mine, b_mine, o_mine), (w_other, b_other, o_other) = heads_weights
    normed = layer_norm(resid, vectors[0], vectors[1]).astype(BF)
    normed_far = swap(normed, Z0)

    def projected(rows, weight, bias):
        return (dot_nn(rows, weight) + bias).astype(BF)

    got = [swap(projected(rows, w_other, b_other), CORE) for rows in (normed, normed_far)]
    triple = jnp.concatenate([projected(rows, w_mine, b_mine) for rows in (normed, normed_far)] + got, axis=0)
    mixed, exact, log_total = attend(triple, slopes, starts, me)
    mixed_other = swap(mixed[1024:], CORE)

    def term(first):
        return dot_nn(mixed[first:first + 512], o_mine) + dot_nn(mixed_other[first:first + 512], o_other)

    far = swap(term(512).astype(BF), Z0)
    mid = resid + (term(0) + far.astype(F32) + vectors[2])
    normed_two = layer_norm(mid, vectors[3], vectors[4]).astype(BF)
    hidden, total = mlp_forward(normed_two, mlp_weights[1], mlp_weights[0])
    out = mid + (total + vectors[5])
    return out, (normed, normed_far, triple, mixed, exact, mixed_other, log_total, mid, normed_two, hidden)


def fast_backward(grad_out, resid, vectors, heads_weights, mlp_weights, kept, slopes, starts, me, core, own):
    (w_mine, b_mine, o_mine), (w_other, b_other, o_other) = heads_weights
    normed, normed_far, triple, mixed, exact, mixed_other, log_total, mid, normed_two, hidden = kept
    outs = mlp_backward(grad_out.astype(BF), normed_two, hidden, mlp_weights[0])
    grad_normed_two, grad_bias_expand, mlp_grads = outs[0], outs[1], outs[2:]
    grad_bias_reduce = jnp.sum(grad_out, axis=0)
    unused, pull = jax.vjp(layer_norm, mid, vectors[3], vectors[4])
    grad_norm, grad_gain_two, grad_shift_two = pull(grad_normed_two)
    grad_mid = grad_out + grad_norm
    grad_bias_output = jnp.sum(grad_mid, axis=0)
    grad_attn = grad_mid.astype(BF)
    grad_attn_far = swap(grad_attn, Z0)
    pair = (grad_attn, grad_attn_far)
    got = [swap(dot_nt(rows, o_other).astype(BF), CORE) for rows in pair]
    grad_mixed = jnp.concatenate([dot_nt(rows, o_mine).astype(BF) for rows in pair] + got, axis=0)
    grad_q, grad_k, grad_v = attend_pull(triple, exact, grad_mixed, log_total, slopes, starts, me)
    grad_mine = jnp.concatenate([grad_q[:1024], grad_k[:1024], grad_v[:1024]], axis=1)
    grad_other = swap(jnp.concatenate([grad_q[1024:], grad_k[1024:], grad_v[1024:]], axis=1), CORE)

    def term(first):
        return dot_nt(grad_mine[first:first + 512], w_mine) + dot_nt(grad_other[first:first + 512], w_other)

    far = swap(term(512).astype(BF), Z0)
    grad_normed = term(0) + far.astype(F32)
    unused, pull = jax.vjp(layer_norm, resid, vectors[0], vectors[1])
    grad_norm, grad_gain_one, grad_shift_one = pull(grad_normed)
    grad_in = grad_mid + grad_norm

    rows_all = jnp.concatenate([normed, normed_far], axis=0)
    grad_all = jnp.concatenate(pair, axis=0)
    grad_project = [dot_tn(rows_all, grad).astype(BF) for grad in (grad_mine, grad_other)]
    grad_output = [dot_tn(rows, grad_all).astype(BF) for rows in (mixed[:1024], mixed_other)]
    grad_bias = [jnp.sum(grad.astype(F32), axis=0) for grad in (grad_mine, grad_other)]
    small = small_sums(
        [grad_gain_one, grad_shift_one, grad_bias_output, grad_gain_two, grad_shift_two, grad_bias_reduce],
        grad_bias_expand, grad_bias, core, own,
    )
    head_pieces = []
    for index in range(8):
        both = [
            jnp.concatenate(
                [
                    grad_project[q][index * 128:(index + 1) * 128].reshape(128, 6, 128).transpose(1, 0, 2).reshape(768, 128),
                    grad_output[q][:, index * 128:(index + 1) * 128],
                ],
                axis=0,
            )
            for q in range(2)
        ]
        head_pieces.append(jnp.stack(both if index % 2 == 0 else both[::-1]))
    heads = scatter_plane(head_pieces)
    near = jnp.where(core == 0, heads[0], heads[1])
    away = jnp.where(core == 0, heads[1], heads[0])
    grad_heads = unpack_attention(near.astype(F32) + swap(away, Z1).astype(F32))
    units = scatter_plane(mlp_grads)
    grad_units = unpack_mlp(
        units[0].astype(F32)
        + swap(units[1], 1).astype(F32)
        + swap(units[2], 2).astype(F32)
        + swap(units[3], 3).astype(F32)
    )
    return grad_in, grad_heads, grad_units, small


def small_sums(vectors, grad_bias_expand, grad_bias_project, core, own):
    turn = jnp.arange(8) ^ own
    stacked = jnp.stack(vectors).reshape(6, 8, 128)
    expand = grad_bias_expand.reshape(4, 8, 128)[:, turn]
    project = [jnp.stack([b[:256], b[512:]]).reshape(2, 8, 32)[:, turn] for b in grad_bias_project]
    project = [jnp.where(core == 0, project[0], project[1]), jnp.where(core == 0, project[1], project[0])]
    project = jnp.concatenate([project[0], project[1]], axis=0)
    project = jnp.concatenate([project, jnp.zeros((4, 8, 96), F32)], axis=2)
    rows = jnp.concatenate([stacked, expand, project], axis=0).transpose(1, 0, 2)
    rows = rows.reshape(2, 2, 2, 14, 128)
    rows = rows[:, :, 0] + swap(rows[:, :, 1], CORE)
    rows = rows[:, 0] + swap(rows[:, 1], XBIT)
    rows = rows[0] + swap(rows[1], YBIT)
    total = rows[:6], rows[6], rows[10:12]

    def part(offset):
        return jnp.concatenate([rows[:6], rows[6 + offset:7 + offset], rows[12:14]], axis=0)

    base = jnp.concatenate([total[0], total[1][None], total[2]], axis=0)
    one, two, three = (swap(part(offset), offset) for offset in (1, 2, 3))
    whole = base[:7] + one[:7] + two[:7] + three[:7]
    bias = base[7:] + two[7:]
    return whole[:6], whole[6], bias[:, :32]


def fast_device(
    layer_input,
    first_gain,
    first_shift,
    project_weight,
    project_bias,
    output_weight,
    output_bias,
    second_gain,
    second_shift,
    expand_weight,
    expand_bias,
    reduce_weight,
    reduce_bias,
    picture_start,
    cotangent,
):
    own = lax.axis_index("dp")
    place = lax.axis_index("tensor")
    core = own & 1
    me = (2 * core + (place & 1)).astype(jnp.int32).reshape(1)
    quarter = place ^ (2 * core)
    slopes = head_slopes(quarter * 4, 4)
    starts = redeal(picture_start)[0]
    resid = turn_blocks(redeal(layer_input).astype(F32), own)
    head_weights, mlp_weights = [], []
    for layer in range(LAYERS):
        small = jnp.stack(
            [v[layer] for v in (first_gain, first_shift, output_bias, second_gain, second_shift, reduce_bias)]
        )
        small = jnp.concatenate(
            [small, jnp.pad(project_bias[layer], ((0, 0), (0, 96))), jnp.zeros((8, 128), BF)], axis=0
        )
        head_weights.append(fast_fetch_attention(project_weight[layer], output_weight[layer], small, core, own))
        mlp_weights.append(fast_fetch_mlp(expand_weight[layer], reduce_weight[layer], expand_bias[layer], own))
    saved = []
    for layer in range(LAYERS):
        vectors, weights = head_weights[layer]
        after, kept = fast_forward(resid, vectors, weights, mlp_weights[layer], slopes, starts, me)
        saved.append((resid, kept))
        resid = after
    layer_output = redeal(turn_blocks(resid.astype(BF), own))
    grad = turn_blocks(redeal(cotangent).astype(F32), own)
    grads = [None] * LAYERS
    for layer in reversed(range(LAYERS)):
        vectors, weights = head_weights[layer]
        before, kept = saved[layer]
        grad, *grads[layer] = fast_backward(
            grad, before, vectors, weights, mlp_weights[layer], kept, slopes, starts, me, core, own
        )
    input_grad = redeal(turn_blocks(grad.astype(BF), own))
    small = [jnp.stack([g[2][0][i] for g in grads]) for i in range(6)]
    return (
        layer_output,
        input_grad,
        small[0],
        small[1],
        jnp.stack([g[0][0] for g in grads]),
        jnp.stack([g[2][2] for g in grads]),
        jnp.stack([g[0][1] for g in grads]),
        small[2],
        small[3],
        small[4],
        jnp.stack([g[1][0] for g in grads]),
        jnp.stack([g[2][1] for g in grads]),
        jnp.stack([g[1][1] for g in grads]),
        small[5],
    )


def solution(mesh):
    placed = (
        P(("dp", "tensor"), None),
        P(None, "dp"),
        P(None, "dp"),
        P(None, None, "dp", "tensor"),
        P(None, None, ("tensor", "dp")),
        P(None, "tensor", "dp"),
        P(None, "dp"),
        P(None, "dp"),
        P(None, "dp"),
        P(None, "dp", "tensor"),
        P(None, ("tensor", "dp")),
        P(None, "tensor", "dp"),
        P(None, "dp"),
        P("dp", None),
        P(("dp", "tensor"), None),
    )
    return jax.shard_map(
        fast_device if mesh_is_paired(mesh) else on_device,
        mesh=mesh,
        in_specs=placed,
        out_specs=(
            P(("dp", "tensor"), None),
            P(("dp", "tensor"), None),
            P(None, "dp"),
            P(None, "dp"),
            P(None, None, "dp", "tensor"),
            P(None, None, ("tensor", "dp")),
            P(None, "tensor", "dp"),
            P(None, "dp"),
            P(None, "dp"),
            P(None, "dp"),
            P(None, "dp", "tensor"),
            P(None, ("tensor", "dp")),
            P(None, "tensor", "dp"),
            P(None, "dp"),
        ),
        check_vma=False,
    )
```

```python
import functools

import jax
import jax.numpy as jnp
from jax import lax
from jax.experimental import pallas as pl
from jax.experimental.pallas import tpu as pltpu
from jax.sharding import PartitionSpec as P

HEADS = 16
HD = 64
LAYERS = 2
SEQ_LEN = 2048
PIECE = 256


NORM_EPS = 1e-05


def layer_norm(values, gain, shift):
    centred = values - jnp.mean(values, axis=-1, keepdims=True)
    spread = jnp.mean(centred * centred, axis=-1, keepdims=True)
    return centred * lax.rsqrt(spread + NORM_EPS) * gain + shift


def gelu_tanh(values):
    return jax.nn.gelu(values, approximate=True)


def piece_numbers(starts):
    places = jnp.arange(SEQ_LEN, dtype=jnp.int32)
    inside = (places[:, None] >= starts[None, :]) & (places[:, None] < starts[None, :] + PIECE)
    numbers = jnp.arange(1, starts.shape[0] + 1, dtype=jnp.int32)
    return jnp.sum(jnp.where(inside, numbers[None, :], 0), axis=1)


def head_slopes(first_head, count_heads):
    heads_at = (first_head + jnp.arange(count_heads, dtype=jnp.int32)).astype(jnp.float32)
    return jnp.exp2(-8.0 * (heads_at + 1.0) / HEADS)


def gather_rows(values):
    return lax.all_gather(values, "tensor", axis=0, tiled=True)


def gather_grads(values):
    return lax.all_gather(values, "tensor", axis=0, tiled=True)


def scatter_rows(values, weight):
    rows_here = values.shape[0] // lax.axis_size("tensor")

    def partial_term(offset, count_rows):
        return jnp.dot(values, weight, preferred_element_type=jnp.float32)

    return lax.psum_scatter(
        partial_term(jnp.int32(0), rows_here * lax.axis_size("tensor")).astype(jnp.bfloat16),
        "tensor",
        scatter_dimension=0,
        tiled=True,
    ).astype(jnp.float32)


def scatter_back(partial_term, rows_here):
    return lax.psum_scatter(
        partial_term(jnp.int32(0), rows_here * lax.axis_size("tensor")).astype(jnp.bfloat16),
        "tensor",
        scatter_dimension=0,
        tiled=True,
    ).astype(jnp.float32)


def block_scores(query_block, key_rows, offset, piece_ids, slopes):
    length = key_rows.shape[0]
    count_rows = query_block.shape[0]
    query_places = offset + jnp.arange(count_rows, dtype=jnp.int32)
    key_places = jnp.arange(length, dtype=jnp.int32)
    product = jnp.einsum("qhe,khe->hqk", query_block, key_rows, preferred_element_type=jnp.float32)
    distance = jnp.abs(query_places[:, None] - key_places[None, :]).astype(jnp.float32)
    scores = product * HD ** (-0.5) - slopes[:, None, None] * distance[None]
    query_pieces = lax.dynamic_slice_in_dim(piece_ids, offset, count_rows, 0)
    allowed = (key_places[None, :] <= query_places[:, None]) | (
        query_pieces[:, None] == piece_ids[None, :]
    ) & (query_pieces[:, None] > 0)
    return jnp.where(allowed[None], scores, -jnp.inf)


def sequence_forward(operands, slopes):
    queries, key_rows, value_rows, piece_ids = operands
    length = queries.shape[0]
    block_rows = min(512, length)

    def one_block(block_index):
        offset = block_index * block_rows
        query_block = lax.dynamic_slice_in_dim(queries, offset, block_rows, 0)
        scores = block_scores(query_block, key_rows, offset, piece_ids, slopes)
        row_max = jnp.max(scores, axis=-1, keepdims=True)
        raw_weights = jnp.exp(scores - row_max)
        totals = jnp.sum(raw_weights, axis=-1, keepdims=True)
        soft_weights = (raw_weights / totals).astype(jnp.bfloat16)
        attended = jnp.einsum(
            "hqk,khe->qhe", soft_weights, value_rows, preferred_element_type=jnp.float32
        )
        return (attended.astype(jnp.bfloat16), (row_max + jnp.log(totals))[..., 0])

    attended, log_total = lax.map(one_block, jnp.arange(length // block_rows, dtype=jnp.int32))
    return (attended.reshape(length, queries.shape[1], queries.shape[2]), log_total)


def sequence_backward(operands, slopes):
    queries, key_rows, value_rows, piece_ids, grad_mixed, log_total = operands
    length = queries.shape[0]
    block_rows = min(512, length)

    def one_block(carry, block_index):
        key_grad, value_grad = carry
        offset = block_index * block_rows
        query_block = lax.dynamic_slice_in_dim(queries, offset, block_rows, 0)
        grad_block = lax.dynamic_slice_in_dim(grad_mixed, offset, block_rows, 0)
        scores = block_scores(query_block, key_rows, offset, piece_ids, slopes)
        probs = jnp.exp(scores - log_total[block_index][..., None])
        soft_weights = probs.astype(jnp.bfloat16)
        value_grad = value_grad + jnp.einsum(
            "hqk,qhe->khe", soft_weights, grad_block, preferred_element_type=jnp.float32
        )
        prob_grad = jnp.einsum(
            "qhe,khe->hqk", grad_block, value_rows, preferred_element_type=jnp.float32
        )
        centred = jnp.sum(probs * prob_grad, axis=-1, keepdims=True)
        score_grad = (probs * (prob_grad - centred) * HD ** (-0.5)).astype(jnp.bfloat16)
        query_grad = jnp.einsum(
            "hqk,khe->qhe", score_grad, key_rows, preferred_element_type=jnp.float32
        )
        key_grad = key_grad + jnp.einsum(
            "hqk,qhe->khe", score_grad, query_block, preferred_element_type=jnp.float32
        )
        return ((key_grad, value_grad), query_grad)

    empty = jnp.zeros(queries.shape, jnp.float32)
    (key_grad, value_grad), query_grad = lax.scan(
        one_block, (empty, empty), jnp.arange(length // block_rows, dtype=jnp.int32)
    )
    return (query_grad.reshape(queries.shape), key_grad, value_grad)


def attend_forward(triple, piece_ids, slopes):
    width = triple.shape[2]
    count_seq = piece_ids.shape[0]
    length = piece_ids.shape[1]
    shaped = triple.reshape(3, count_seq, length, width // HD, HD)
    attended, log_total = lax.map(
        lambda operands: sequence_forward(operands, slopes),
        (shaped[0], shaped[1], shaped[2], piece_ids),
    )
    return (attended.reshape(count_seq * length, width), log_total)


def attend_backward(triple, grad_attended, log_total, piece_ids, slopes):
    width = triple.shape[2]
    count_seq = piece_ids.shape[0]
    length = piece_ids.shape[1]
    shaped = triple.reshape(3, count_seq, length, width // HD, HD)
    grad_shaped = grad_attended.reshape(count_seq, length, width // HD, HD)
    query_grad, key_grad, value_grad = lax.map(
        lambda operands: sequence_backward(operands, slopes),
        (shaped[0], shaped[1], shaped[2], piece_ids, grad_shaped, log_total),
    )
    return (
        query_grad.reshape(-1, width),
        key_grad.reshape(-1, width),
        value_grad.reshape(-1, width),
    )


def fetch_layer(
    project_weight,
    project_bias,
    output_weight,
    expand_weight,
    expand_bias,
    reduce_weight,
    small_stack,
    layer_index,
):
    return (
        lax.all_gather(project_weight[layer_index], "dp", axis=1, tiled=True),
        lax.all_gather(project_bias[layer_index], "dp", axis=1, tiled=True),
        lax.all_gather(output_weight[layer_index], "dp", axis=1, tiled=True),
        lax.all_gather(expand_weight[layer_index], "dp", axis=0, tiled=True),
        lax.all_gather(expand_bias[layer_index], "dp", axis=0, tiled=True),
        lax.all_gather(reduce_weight[layer_index], "dp", axis=1, tiled=True),
        lax.all_gather(small_stack[layer_index], "dp", axis=1, tiled=True),
    )


def forward_layer(resid, weights, piece_ids, slopes):
    w_project, bias_project, w_output, w_expand, bias_expand, w_reduce, small = weights
    vectors = small.astype(jnp.float32)
    normed = layer_norm(resid, vectors[0], vectors[1])
    gathered = gather_rows(normed.astype(jnp.bfloat16))
    product = jnp.einsum("gd,cde->cge", gathered, w_project, preferred_element_type=jnp.float32)
    biases = jnp.stack([bias_project[0], jnp.zeros_like(bias_project[0]), bias_project[1]]).astype(
        jnp.float32
    )
    triple = (product + biases[:, None, :]).astype(jnp.bfloat16)
    attended, log_total = attend_forward(triple, piece_ids, slopes)
    resid_mid = resid + (scatter_rows(attended, w_output) + vectors[2])
    normed_two = layer_norm(resid_mid, vectors[3], vectors[4])
    gathered_two = gather_rows(normed_two.astype(jnp.bfloat16))
    hidden = jnp.dot(
        gathered_two, w_expand, preferred_element_type=jnp.float32
    ) + bias_expand.astype(jnp.float32)
    active = gelu_tanh(hidden).astype(jnp.bfloat16)
    mlp_sum = scatter_rows(active, w_reduce)
    mlp_keep = (gathered_two, hidden, None)
    resid_out = resid_mid + (mlp_sum + vectors[5])
    return (resid_out, (gathered, triple, attended, log_total, resid_mid, mlp_keep))


def backward_layer(grad_out, resid, weights, kept, piece_ids, slopes):
    w_project, bias_project, w_output, w_expand, bias_expand, w_reduce, small = weights
    vectors = small.astype(jnp.float32)
    gathered, triple, attended, log_total, resid_mid, mlp_keep = kept
    rows_here = grad_out.shape[0]
    rows_in, hidden, full_weights = mlp_keep
    grad_bias_reduce = jnp.sum(grad_out, axis=0)
    active, gelu_pull = jax.vjp(gelu_tanh, hidden)
    active_low = active.astype(jnp.bfloat16)
    grad_mlp = gather_grads(grad_out.astype(jnp.bfloat16))
    grad_reduce = jnp.einsum("gf,gd->fd", active_low, grad_mlp, preferred_element_type=jnp.float32)
    grad_active = jnp.einsum("gd,fd->gf", grad_mlp, w_reduce, preferred_element_type=jnp.float32)
    (grad_hidden,) = gelu_pull(grad_active)
    grad_bias_expand = jnp.sum(grad_hidden, axis=0)
    grad_hidden_low = grad_hidden.astype(jnp.bfloat16)
    grad_expand = jnp.einsum(
        "gd,gf->df", rows_in, grad_hidden_low, preferred_element_type=jnp.float32
    )

    def expand_term(offset, count_rows):
        return jnp.einsum(
            "gf,df->gd", grad_hidden_low, w_expand, preferred_element_type=jnp.float32
        )

    grad_normed_two = scatter_back(expand_term, rows_here)
    unused_two, second_pull = jax.vjp(layer_norm, resid_mid, vectors[3], vectors[4])
    grad_from_norm, grad_gain_two, grad_shift_two = second_pull(grad_normed_two)
    grad_mid = grad_out + grad_from_norm
    grad_bias_output = jnp.sum(grad_mid, axis=0)
    grad_attn = gather_grads(grad_mid.astype(jnp.bfloat16))
    grad_output = jnp.einsum("gt,gd->td", attended, grad_attn, preferred_element_type=jnp.float32)
    grad_attended = jnp.einsum(
        "gd,td->gt", grad_attn, w_output, preferred_element_type=jnp.float32
    ).astype(jnp.bfloat16)
    query_grad, key_grad, value_grad = attend_backward(
        triple, grad_attended, log_total, piece_ids, slopes
    )
    grad_bias_project = jnp.stack([jnp.sum(query_grad, axis=0), jnp.sum(value_grad, axis=0)])
    grad_triple = jnp.stack([query_grad, key_grad, value_grad]).astype(jnp.bfloat16)
    grad_project = jnp.einsum(
        "gd,cge->cde", gathered, grad_triple, preferred_element_type=jnp.float32
    )

    def project_term(offset, count_rows):
        return jnp.einsum("cge,cde->gd", grad_triple, w_project, preferred_element_type=jnp.float32)

    grad_normed = scatter_back(project_term, rows_here)
    unused_one, first_pull = jax.vjp(layer_norm, resid, vectors[0], vectors[1])
    grad_from_first, grad_gain_one, grad_shift_one = first_pull(grad_normed)
    grad_stream = grad_mid + grad_from_first
    small_grads = jnp.stack(
        [
            grad_gain_one,
            grad_shift_one,
            grad_bias_output,
            grad_gain_two,
            grad_shift_two,
            grad_bias_reduce,
        ]
    )
    return (
        grad_stream,
        (
            grad_project,
            grad_bias_project,
            grad_output,
            grad_expand,
            grad_bias_expand,
            grad_reduce,
            small_grads,
        ),
    )


def reduce_layer(layer_grads):
    (
        grad_project,
        grad_bias_project,
        grad_output,
        grad_expand,
        grad_bias_expand,
        grad_reduce,
        small_grads,
    ) = layer_grads
    return (
        lax.psum_scatter(
            grad_project.astype(jnp.bfloat16), "dp", scatter_dimension=1, tiled=True
        ).astype(jnp.float32),
        lax.psum_scatter(
            grad_bias_project.astype(jnp.bfloat16), "dp", scatter_dimension=1, tiled=True
        ).astype(jnp.float32),
        lax.psum_scatter(
            grad_output.astype(jnp.bfloat16), "dp", scatter_dimension=1, tiled=True
        ).astype(jnp.float32),
        lax.psum_scatter(
            grad_expand.astype(jnp.bfloat16), "dp", scatter_dimension=0, tiled=True
        ).astype(jnp.float32),
        lax.psum_scatter(
            grad_bias_expand.astype(jnp.bfloat16), "dp", scatter_dimension=0, tiled=True
        ).astype(jnp.float32),
        lax.psum_scatter(
            grad_reduce.astype(jnp.bfloat16), "dp", scatter_dimension=1, tiled=True
        ).astype(jnp.float32),
        lax.psum_scatter(
            small_grads.astype(jnp.bfloat16), "dp", scatter_dimension=1, tiled=True
        ).astype(jnp.float32),
    )


def on_device(
    layer_input,
    first_gain,
    first_shift,
    project_weight,
    project_bias,
    output_weight,
    output_bias,
    second_gain,
    second_shift,
    expand_weight,
    expand_bias,
    reduce_weight,
    reduce_bias,
    picture_start,
    cotangent,
):
    small_stack = jnp.stack(
        [first_gain, first_shift, output_bias, second_gain, second_shift, reduce_bias], axis=1
    )
    piece_ids = jax.vmap(piece_numbers)(picture_start)
    heads_here = project_weight.shape[3] // HD
    slopes = head_slopes(lax.axis_index("tensor") * heads_here, heads_here)
    resid = layer_input.astype(jnp.float32)
    saved = []
    for layer_index in range(LAYERS):
        weights = fetch_layer(
            project_weight,
            project_bias,
            output_weight,
            expand_weight,
            expand_bias,
            reduce_weight,
            small_stack,
            layer_index,
        )
        resid_next, kept = forward_layer(resid, weights, piece_ids, slopes)
        saved.append((resid, weights, kept))
        resid = resid_next
    layer_output = resid.astype(jnp.bfloat16)
    grad_stream = cotangent.astype(jnp.float32)
    collected = []
    for layer_index in reversed(range(LAYERS)):
        resid_in, weights, kept = saved[layer_index]
        grad_stream, layer_grads = backward_layer(
            grad_stream, resid_in, weights, kept, piece_ids, slopes
        )
        layer_grads = reduce_layer(layer_grads)
        collected.insert(0, layer_grads)
    stacked = tuple(
        (jnp.stack([grad_entry[member] for grad_entry in collected]) for member in range(7))
    )
    (
        grad_project,
        grad_bias_project,
        grad_output,
        grad_expand,
        grad_bias_expand,
        grad_reduce,
        small_grads,
    ) = stacked
    small_grads = lax.psum(small_grads, "tensor")
    return (
        layer_output,
        grad_stream.astype(jnp.bfloat16),
        small_grads[:, 0],
        small_grads[:, 1],
        grad_project,
        grad_bias_project,
        grad_output,
        small_grads[:, 2],
        small_grads[:, 3],
        small_grads[:, 4],
        grad_expand,
        grad_bias_expand,
        grad_reduce,
        small_grads[:, 5],
    )


Z0, Z1, CORE, XBIT, YBIT = 1, 2, 4, 8, 16
AXES = ("dp", "tensor")
NEG = -1e30
BF = jnp.bfloat16
F32 = jnp.float32
VMEM_LIMIT = 56 * 1024 * 1024


def mesh_is_paired(mesh):
    return dict(mesh.shape) == {"dp": 8, "tensor": 4}


def swap(values, mask):
    return lax.ppermute(values, AXES, [(i, i ^ mask) for i in range(32)])


def redeal(values):
    def target(i):
        core, z1 = (i >> 2) & 1, (i >> 1) & 1
        return (i & ~6) | (z1 << 2) | (core << 1)

    return lax.ppermute(values, AXES, [(i, target(i)) for i in range(32)])


def turn_blocks(values, own):
    width = values.shape[1] // 8
    return jnp.concatenate(
        [lax.dynamic_slice_in_dim(values, (own ^ i) * width, width, 1) for i in range(8)], axis=1
    )


def after(values, *others):
    return lax.optimization_barrier((values, *others))[0]


def dot_nt(a, b):
    return lax.dot_general(a, b, (((1,), (1,)), ((), ())), preferred_element_type=F32)


def dot_nn(a, b):
    return lax.dot_general(a, b, (((1,), (0,)), ((), ())), preferred_element_type=F32)


def head_mask(shape, head):
    lane = lax.broadcasted_iota(jnp.int32, shape, 1)
    return (lane < HD) if head == 0 else (lane >= HD)


def diagonal_bias(rows, columns, first_row, first_column, start):
    key = first_row + lax.broadcasted_iota(jnp.int32, (rows, 1), 0)
    query = first_column + lax.broadcasted_iota(jnp.int32, (1, columns), 1)
    key_in = (key >= start) & (key < start + PIECE)
    query_in = (query >= start) & (query < start + PIECE)
    allowed = (key <= query) | (key_in & query_in)
    reach = (jnp.minimum(key, 2 * query - key) - first_column).astype(F32)
    return jnp.where(allowed, reach, NEG)


def ramp(rows, first_row, first_column):
    return (first_row - first_column + lax.broadcasted_iota(jnp.int32, (rows, 1), 0)).astype(F32)


def attend_kernel(block, rest_bit, slope_ref, start_ref, me_ref, *rest):
    triple_refs, rest = rest[:12], rest[12:]
    near_ref, away_ref, exact_ref, lse_ref, q_ref, k_ref, v_ref, vt_ref, acc_ref, max_ref, bias_ref, tail_ref = rest
    pair = pl.program_id(0)
    turn = pl.program_id(1)
    me = me_ref[0]
    step = (2 * turn + rest_bit) ^ me
    length = k_ref.shape[0]
    first = step * block

    def at(index):
        return pl.multiple_of((index ^ me) * block, block)

    start = start_ref[first // (length // start_ref.shape[0])]

    @pl.when(turn == 0)
    def _():
        for index in range(4):
            here = slice(index * block, (index + 1) * block)
            q_ref[here, :] = triple_refs[3 * index][...] * jnp.asarray(HD ** -0.5, BF)
            k_ref[here, :] = triple_refs[3 * index + 1][...]
            v_ref[here, :] = triple_refs[3 * index + 2][...]
        for head in range(2):
            mixed = jnp.where(head_mask((length, 2 * HD), head), v_ref[...], jnp.ones((), BF))
            vt_ref[head] = mixed.T

    bias_ref[...] = diagonal_bias(block, block, first, first, start)
    q_block = q_ref[pl.ds(at(step), block), :]
    heads = [jnp.where(head_mask(q_block.shape, head), q_block, jnp.zeros((), BF)) for head in range(2)]
    slopes = [slope_ref[2 * pair + head] for head in range(2)]
    acc_ref[...] = jnp.zeros_like(acc_ref)
    max_ref[...] = jnp.full_like(max_ref, NEG)

    def absorb(head, scores, vt):
        old = max_ref[head]
        new = jnp.maximum(old, jnp.max(scores, axis=0, keepdims=True))
        weights = jnp.exp(scores - new).astype(BF)
        acc_ref[head] = acc_ref[head] * jnp.exp(old - new) + dot_nn(vt, weights)
        max_ref[head] = new

    def full(index, carry):
        place = at(index)
        keys = k_ref[pl.ds(place, block), :]
        slant = ramp(block, index * block, first)
        for head in range(2):
            absorb(head, dot_nt(keys, heads[head]) + slopes[head] * slant, vt_ref[head, :, pl.ds(place, block)])
        return carry

    place = at(step)
    for head in range(2):
        absorb(
            head,
            dot_nt(k_ref[pl.ds(place, block), :], heads[head]) + slopes[head] * bias_ref[...],
            vt_ref[head, :, pl.ds(place, block)],
        )
    lax.fori_loop(0, step, full, 0)
    edge = first + block

    @pl.when((start < edge) & (start + PIECE > edge))
    def _():
        after = at(step + 1)
        tail_ref[...] = diagonal_bias(PIECE, block, edge, first, start)
        for head in range(2):
            absorb(
                head,
                dot_nt(k_ref[pl.ds(after, PIECE), :], heads[head]) + slopes[head] * tail_ref[...],
                vt_ref[head, :, pl.ds(after, PIECE)],
            )

    outs = []
    for head in range(2):
        acc = acc_ref[head]
        total = acc[HD:HD + 1] if head == 0 else acc[0:1]
        outs.append((acc * (1.0 / total))[head * HD:(head + 1) * HD])
        lse_ref[0, head:head + 1, :] = max_ref[head] + jnp.log(total)
    mixed = jnp.concatenate(outs, axis=0)
    exact_ref[...] = mixed
    final = mixed.T.astype(BF)

    @pl.when(turn == 0)
    def _():
        near_ref[...] = final

    @pl.when(turn == 1)
    def _():
        away_ref[...] = final


def triple_specs(block, pairs):
    specs = []
    for index in range(4):
        for part in range(3):
            specs.append(pl.BlockSpec((block, 2 * HD), functools.partial(lambda part, p, i: (0, part * pairs + p), part)))
    return specs


def attend(blocks, rest_bit, slopes, starts, me):
    block, width = blocks[0].shape[0], blocks[0].shape[1] // 3
    pairs = width // (2 * HD)
    length = 4 * block
    smem = pl.BlockSpec(memory_space=pltpu.SMEM)
    return pl.pallas_call(
        functools.partial(attend_kernel, block, rest_bit),
        grid=(pairs, 2),
        in_specs=[smem, smem, smem] + triple_specs(block, pairs),
        out_specs=[
            pl.BlockSpec((block, 2 * HD), lambda p, i: (0, p)),
            pl.BlockSpec((block, 2 * HD), lambda p, i: (0, p)),
            pl.BlockSpec((2 * HD, block), lambda p, i: (p, i)),
            pl.BlockSpec((1, 8, block), lambda p, i: (p, 0, i)),
        ],
        out_shape=[
            jax.ShapeDtypeStruct((block, width), BF),
            jax.ShapeDtypeStruct((block, width), BF),
            jax.ShapeDtypeStruct((width, 2 * block), F32),
            jax.ShapeDtypeStruct((pairs, 8, 2 * block), F32),
        ],
        scratch_shapes=[
            pltpu.VMEM((length, 2 * HD), BF),
            pltpu.VMEM((length, 2 * HD), BF),
            pltpu.VMEM((length, 2 * HD), BF),
            pltpu.VMEM((2, 2 * HD, length), BF),
            pltpu.VMEM((2, 2 * HD, block), F32),
            pltpu.VMEM((2, 1, block), F32),
            pltpu.VMEM((block, block), F32),
            pltpu.VMEM((PIECE, block), F32),
        ],
        compiler_params=pltpu.CompilerParams(vmem_limit_bytes=VMEM_LIMIT),
        cost_estimate=pl.CostEstimate(flops=10 * length * length * width // 4, bytes_accessed=16 * block * width, transcendentals=0),
        name="attend",
    )(slopes, starts, me, *[b for b in blocks for _ in range(3)])


def pull_kernel(block, slope_ref, start_ref, me_ref, *rest):
    triple_refs, grad_refs, rest = rest[:12], rest[12:16], rest[16:]
    exact_refs, lse_refs, rest = rest[0:2], rest[2:4], rest[4:]
    mine_ref, away_ref, q_ref, k_ref, v_ref, g_ref, kt_ref, dk_acc, dv_acc, dqt_ref, bias_ref, tail_ref = rest
    pair = pl.program_id(0)
    turn = pl.program_id(1)
    me = me_ref[0]
    step = turn ^ me
    length = k_ref.shape[0]
    first = step * block
    half, bit = turn // 2, turn % 2

    def at(index):
        return pl.multiple_of((index ^ me) * block, block)

    start = start_ref[first // (length // start_ref.shape[0])]

    @pl.when(turn == 0)
    def _():
        for index in range(4):
            here = slice(index * block, (index + 1) * block)
            q_ref[here, :] = triple_refs[3 * index][...] * jnp.asarray(HD ** -0.5, BF)
            k_ref[here, :] = triple_refs[3 * index + 1][...]
            v_ref[here, :] = triple_refs[3 * index + 2][...]
            g_ref[here, :] = grad_refs[index][...]
        kt_ref[...] = k_ref[...].T
        dk_acc[...] = jnp.zeros_like(dk_acc)
        dv_acc[...] = jnp.zeros_like(dv_acc)

    bias_ref[...] = diagonal_bias(block, block, first, first, start)
    dqt_ref[...] = jnp.zeros_like(dqt_ref)
    zero = jnp.zeros((), BF)
    q_block = q_ref[pl.ds(at(step), block), :]
    g_block = g_ref[pl.ds(at(step), block), :]
    masks = [head_mask(q_block.shape, head) for head in range(2)]
    q_heads = [jnp.where(mask, q_block, zero) for mask in masks]
    g_heads = [jnp.where(mask, g_block, zero) for mask in masks]
    slopes = [slope_ref[2 * pair + head] for head in range(2)]
    lanes = pl.ds(pl.multiple_of(half * block, block), block)
    exact = jnp.where(bit == 0, exact_refs[0][:, lanes], exact_refs[1][:, lanes])
    log_total = jnp.where(bit == 0, lse_refs[0][0, :, lanes], lse_refs[1][0, :, lanes])
    product = g_block.astype(F32).T * exact
    deltas = [jnp.sum(product[head * HD:(head + 1) * HD], axis=0, keepdims=True) for head in range(2)]

    def absorb(place, rows, bias_of):
        keys = k_ref[pl.ds(place, rows), :]
        values = v_ref[pl.ds(place, rows), :]
        dk = dk_acc[pl.ds(place, rows), :]
        dv = dv_acc[pl.ds(place, rows), :]
        for head in range(2):
            scores = dot_nt(keys, q_heads[head]) + slopes[head] * bias_of
            weights = jnp.exp(scores - log_total[head:head + 1, :])
            dv = dv + dot_nn(weights.astype(BF), g_heads[head])
            grad_p = dot_nt(values, g_heads[head])
            grad_s = (weights * (grad_p - deltas[head])).astype(BF)
            dk = dk + dot_nn(grad_s, q_heads[head])
            dqt_ref[head * HD:(head + 1) * HD, :] += dot_nn(kt_ref[head * HD:(head + 1) * HD, pl.ds(place, rows)], grad_s)
        dk_acc[pl.ds(place, rows), :] = dk
        dv_acc[pl.ds(place, rows), :] = dv

    absorb(at(step), block, bias_ref[...])

    def full(index, carry):
        absorb(at(index), block, ramp(block, index * block, first))
        return carry

    lax.fori_loop(0, step, full, 0)
    edge = first + block

    @pl.when((start < edge) & (start + PIECE > edge))
    def _():
        tail_ref[...] = diagonal_bias(PIECE, block, edge, first, start)
        absorb(at(step + 1), PIECE, tail_ref[...])

    grad_q = (dqt_ref[...].T * (HD ** -0.5)).astype(BF)
    here = pl.ds(pl.multiple_of(bit * block, block), block)

    @pl.when(half == 0)
    def _():
        mine_ref[0, here, :] = grad_q

    @pl.when(half == 1)
    def _():
        away_ref[0, here, :] = grad_q

    @pl.when(turn == 3)
    def _():
        for part, ref in ((1, dk_acc), (2, dv_acc)):
            mine_ref[part] = ref[:2 * block].astype(BF)
            away_ref[part] = ref[2 * block:].astype(BF)


def attend_pull(blocks, grads, exacts, log_totals, slopes, starts, me):
    block, width = blocks[0].shape[0], blocks[0].shape[1] // 3
    pairs = width // (2 * HD)
    length = 4 * block
    smem = pl.BlockSpec(memory_space=pltpu.SMEM)
    rows = pl.BlockSpec((block, 2 * HD), lambda p, i: (0, p))
    wide = pl.BlockSpec((2 * HD, 2 * block), lambda p, i: (p, 0))
    sums = pl.BlockSpec((1, 8, 2 * block), lambda p, i: (p, 0, 0))
    out = pl.BlockSpec((3, 2 * block, 2 * HD), lambda p, i: (0, 0, p))
    return pl.pallas_call(
        functools.partial(pull_kernel, block),
        grid=(pairs, 4),
        in_specs=[smem, smem, smem] + triple_specs(block, pairs) + [rows] * 4 + [wide] * 2 + [sums] * 2,
        out_specs=[out, out],
        out_shape=[jax.ShapeDtypeStruct((3, 2 * block, width), BF)] * 2,
        scratch_shapes=[
            pltpu.VMEM((length, 2 * HD), BF),
            pltpu.VMEM((length, 2 * HD), BF),
            pltpu.VMEM((length, 2 * HD), BF),
            pltpu.VMEM((length, 2 * HD), BF),
            pltpu.VMEM((2 * HD, length), BF),
            pltpu.VMEM((length, 2 * HD), F32),
            pltpu.VMEM((length, 2 * HD), F32),
            pltpu.VMEM((2 * HD, block), F32),
            pltpu.VMEM((block, block), F32),
            pltpu.VMEM((PIECE, block), F32),
        ],
        compiler_params=pltpu.CompilerParams(vmem_limit_bytes=VMEM_LIMIT),
        cost_estimate=pl.CostEstimate(flops=25 * length * length * width // 2, bytes_accessed=30 * block * width, transcendentals=0),
        name="attend_pull",
    )(slopes, starts, me, *[b for b in blocks for _ in range(3)], *grads, *exacts, *log_totals)


GELU_A = 0.7978845608028654
GELU_B = 0.044715


def normalize(values):
    centred = values - jnp.mean(values, axis=-1, keepdims=True)
    spread = lax.rsqrt(jnp.mean(centred * centred, axis=-1, keepdims=True) + NORM_EPS)
    return centred * spread, spread


def norm_pull(values, gain, grad):
    unit, spread = normalize(values)
    grad_unit = grad * gain
    inner = grad_unit - jnp.mean(grad_unit, axis=-1, keepdims=True)
    inner = inner - unit * jnp.mean(grad_unit * unit, axis=-1, keepdims=True)
    return spread * inner, jnp.sum(grad * unit, axis=0, keepdims=True), jnp.sum(grad, axis=0, keepdims=True)


def joined(refs, first, last):
    return jnp.concatenate([ref[0, :, first:last] for ref in refs], axis=0)


def mlp_kernel(normed_ref, mid_ref, vector_ref, bias_ref, *rest):
    weight_refs, (hidden_ref, active_ref, out_ref, next_ref, acc_ref) = rest[:8], rest[8:]
    tile = hidden_ref.shape[1]
    step = pl.program_id(0)
    hidden = dot_nn(normed_ref[...], joined(weight_refs, 0, tile)) + bias_ref[...]
    inner = jnp.tanh(GELU_A * (hidden + GELU_B * hidden * hidden * hidden))
    active = (0.5 * hidden * (1.0 + inner)).astype(BF)
    hidden_ref[...] = hidden.astype(BF)
    active_ref[...] = active
    term = dot_nt(active, joined(weight_refs, tile, 2 * tile))

    @pl.when(step == 0)
    def _():
        acc_ref[...] = term

    @pl.when(step > 0)
    def _():
        acc_ref[...] += term

    @pl.when(step == pl.num_programs(0) - 1)
    def _():
        out = mid_ref[...] + (acc_ref[...] + vector_ref[5:6])
        out_ref[...] = out
        next_ref[...] = (normalize(out)[0] * vector_ref[6:7] + vector_ref[7:8]).astype(BF)


def mlp_forward(normed, mid, vectors, bias, bundles):
    rows, features = normed.shape
    units = bias.shape[1]
    tile = 512
    whole = pl.BlockSpec((rows, features), lambda f: (0, 0))
    tiles = pl.BlockSpec((rows, tile), lambda f: (0, f))
    weight_spec = pl.BlockSpec((1, 128, 2 * tile), lambda f: (f // 2, 0, f % 2))
    return pl.pallas_call(
        mlp_kernel,
        grid=(units // tile,),
        in_specs=[whole, whole, pl.BlockSpec((8, features), lambda f: (0, 0)), pl.BlockSpec((1, tile), lambda f: (0, f))]
        + [weight_spec] * 8,
        out_specs=[tiles, tiles, whole, whole],
        out_shape=[
            jax.ShapeDtypeStruct((rows, units), BF),
            jax.ShapeDtypeStruct((rows, units), BF),
            jax.ShapeDtypeStruct((rows, features), F32),
            jax.ShapeDtypeStruct((rows, features), BF),
        ],
        scratch_shapes=[pltpu.VMEM((rows, features), F32)],
        compiler_params=pltpu.CompilerParams(vmem_limit_bytes=VMEM_LIMIT),
        cost_estimate=pl.CostEstimate(flops=4 * rows * features * units, bytes_accessed=6 * features * units, transcendentals=0),
        name="mlp_forward",
    )(normed, mid, vectors, bias, *bundles)


def mlp_pull_kernel(grad_ref, mid_ref, vector_ref, hidden_ref, *rest):
    weight_refs = rest[:8]
    grad_hidden_ref, grad_bias_ref, grad_mid_ref, grad_low_ref, sums_ref, acc_ref, low_ref = rest[8:]
    tile = hidden_ref.shape[1]
    step = pl.program_id(0)

    @pl.when(step == 0)
    def _():
        low_ref[...] = grad_ref[...].astype(BF)

    hidden = hidden_ref[...].astype(F32)
    squared = hidden * hidden
    inner = jnp.tanh(GELU_A * hidden * (1.0 + GELU_B * squared))
    slope = 0.5 * (1.0 + inner) + 0.5 * hidden * (1.0 - inner * inner) * (GELU_A * (1.0 + 3.0 * GELU_B * squared))
    grad_hidden = dot_nn(low_ref[...], joined(weight_refs, tile, 2 * tile)) * slope
    grad_bias_ref[...] = jnp.sum(grad_hidden, axis=0, keepdims=True)
    grad_hidden = grad_hidden.astype(BF)
    grad_hidden_ref[...] = grad_hidden
    term = dot_nt(grad_hidden, joined(weight_refs, 0, tile))

    @pl.when(step == 0)
    def _():
        acc_ref[...] = term

    @pl.when(step > 0)
    def _():
        acc_ref[...] += term

    @pl.when(step == pl.num_programs(0) - 1)
    def _():
        grad = grad_ref[...]
        grad_norm, grad_gain, grad_shift = norm_pull(mid_ref[...], vector_ref[3:4], acc_ref[...])
        grad_mid = grad + grad_norm
        grad_mid_ref[...] = grad_mid
        grad_low_ref[...] = grad_mid.astype(BF)
        sums_ref[...] = jnp.concatenate(
            [
                jnp.sum(grad_mid, axis=0, keepdims=True),
                grad_gain,
                grad_shift,
                jnp.sum(grad, axis=0, keepdims=True),
                jnp.zeros((4, grad.shape[1]), F32),
            ],
            axis=0,
        )


def mlp_backward(grad, mid, vectors, hidden, bundles):
    rows, features = grad.shape
    units = hidden.shape[1]
    tile = 512
    whole = pl.BlockSpec((rows, features), lambda f: (0, 0))
    tiles = pl.BlockSpec((rows, tile), lambda f: (0, f))
    eight = pl.BlockSpec((8, features), lambda f: (0, 0))
    weight_spec = pl.BlockSpec((1, 128, 2 * tile), lambda f: (f // 2, 0, f % 2))
    return pl.pallas_call(
        mlp_pull_kernel,
        grid=(units // tile,),
        in_specs=[whole, whole, eight, tiles] + [weight_spec] * 8,
        out_specs=[tiles, pl.BlockSpec((1, tile), lambda f: (0, f)), whole, whole, eight],
        out_shape=[
            jax.ShapeDtypeStruct((rows, units), BF),
            jax.ShapeDtypeStruct((1, units), F32),
            jax.ShapeDtypeStruct((rows, features), F32),
            jax.ShapeDtypeStruct((rows, features), BF),
            jax.ShapeDtypeStruct((8, features), F32),
        ],
        scratch_shapes=[pltpu.VMEM((rows, features), F32), pltpu.VMEM((rows, features), BF)],
        compiler_params=pltpu.CompilerParams(vmem_limit_bytes=VMEM_LIMIT),
        cost_estimate=pl.CostEstimate(flops=4 * rows * features * units, bytes_accessed=6 * features * units, transcendentals=0),
        name="mlp_backward",
    )(grad, mid, vectors, hidden, *bundles)


def mlp_weights_kernel(grad_ref, normed_ref, active_ref, grad_hidden_ref, *rest):
    out_refs, (grad_t_ref, normed_t_ref) = rest[:8], rest[8:]
    tile = active_ref.shape[1]

    @pl.when(pl.program_id(0) == 0)
    def _():
        grad_t_ref[...] = grad_ref[...].astype(BF).T
        normed_t_ref[...] = normed_ref[...].T

    grad_expand = dot_nn(normed_t_ref[...], grad_hidden_ref[...]).astype(BF)
    grad_reduce = dot_nn(grad_t_ref[...], active_ref[...]).astype(BF)
    for index, out_ref in enumerate(out_refs):
        here = slice(index * 128, (index + 1) * 128)
        out_ref[0, :, :tile] = grad_expand[here]
        out_ref[0, :, tile:] = grad_reduce[here]


def mlp_weight_grads(grad, normed, active, grad_hidden):
    rows, features = grad.shape
    units = active.shape[1]
    tile = 512
    whole = pl.BlockSpec((rows, features), lambda f: (0, 0))
    tiles = pl.BlockSpec((rows, tile), lambda f: (0, f))
    weight_spec = pl.BlockSpec((1, 128, 2 * tile), lambda f: (f // 2, 0, f % 2))
    return pl.pallas_call(
        mlp_weights_kernel,
        grid=(units // tile,),
        in_specs=[whole, whole, tiles, tiles],
        out_specs=[weight_spec] * 8,
        out_shape=[jax.ShapeDtypeStruct((units // 1024, 128, 2048), BF)] * 8,
        scratch_shapes=[pltpu.VMEM((features, rows), BF), pltpu.VMEM((features, rows), BF)],
        compiler_params=pltpu.CompilerParams(vmem_limit_bytes=VMEM_LIMIT),
        cost_estimate=pl.CostEstimate(flops=4 * rows * features * units, bytes_accessed=8 * features * units, transcendentals=0),
        name="mlp_weight_grads",
    )(grad, normed, active, grad_hidden)


def head_columns(refs, quarter, first, last):
    return jnp.concatenate(
        [ref[quarter if index % 2 == 0 else 1 - quarter, :, first:last] for index, ref in enumerate(refs)], axis=0
    )


def in_vmem(count):
    return [pl.BlockSpec(memory_space=pltpu.VMEM)] * count


def call_once(kernel, name, outs, args, flops):
    moved = sum(a.size * a.dtype.itemsize for a in args) + sum(a.size * a.dtype.itemsize for a in outs)
    return pl.pallas_call(
        kernel,
        in_specs=in_vmem(len(args)),
        out_specs=in_vmem(len(outs)),
        out_shape=outs,
        compiler_params=pltpu.CompilerParams(vmem_limit_bytes=VMEM_LIMIT),
        cost_estimate=pl.CostEstimate(flops=flops, bytes_accessed=moved, transcendentals=0),
        name=name,
    )(*args)


def project_kernel(rows_ref, bias_ref, *rest):
    weight_refs, out_refs = rest[:8], rest[8:]
    rows = rows_ref[...]
    for quarter in (1, 0):
        out = dot_nn(rows, head_columns(weight_refs, quarter, 0, 768)) + bias_ref[quarter:quarter + 1]
        out_refs[quarter][...] = out.astype(BF)


def project(rows, bias, pieces):
    out = jax.ShapeDtypeStruct((rows.shape[0], 768), BF)
    return call_once(project_kernel, "project", [out, out], [rows, bias, *pieces], 2 * rows.shape[0] * 1024 * 1536)


def mix_term(mixed_refs, weight_refs):
    rows = jnp.concatenate([ref[...] for ref in mixed_refs], axis=1)
    weight = jnp.concatenate([head_columns(weight_refs, quarter, 768, 1024) for quarter in range(2)], axis=1)
    return dot_nt(rows, weight)


def mix_far_kernel(mine_ref, other_ref, *rest):
    rest[8][...] = mix_term((mine_ref, other_ref), rest[:8]).astype(BF)


def mix_far(mine, other, pieces):
    out = jax.ShapeDtypeStruct((mine.shape[0], 1024), BF)
    return call_once(mix_far_kernel, "mix_far", [out], [mine, other, *pieces], 2 * mine.shape[0] * 512 * 1024)[0]


def mix_near_kernel(mine_ref, other_ref, far_ref, resid_ref, vector_ref, *rest):
    weight_refs, (mid_ref, normed_ref) = rest[:8], rest[8:]
    term = mix_term((mine_ref, other_ref), weight_refs)
    mid = resid_ref[...] + (term + far_ref[...].astype(F32) + vector_ref[2:3])
    mid_ref[...] = mid
    normed_ref[...] = (normalize(mid)[0] * vector_ref[3:4] + vector_ref[4:5]).astype(BF)


def mix_near(mine, other, far, resid, vectors, pieces):
    outs = [jax.ShapeDtypeStruct(resid.shape, F32), jax.ShapeDtypeStruct(resid.shape, BF)]
    return call_once(mix_near_kernel, "mix_near", outs, [mine, other, far, resid, vectors, *pieces], 2 * mine.shape[0] * 512 * 1024)


def unmix_kernel(grad_ref, *rest):
    weight_refs, out_refs = rest[:8], rest[8:]
    grad = grad_ref[...]
    for quarter in (1, 0):
        out_refs[quarter][...] = dot_nn(grad, head_columns(weight_refs, quarter, 768, 1024)).astype(BF)


def unmix(grad, pieces):
    out = jax.ShapeDtypeStruct((grad.shape[0], 256), BF)
    return call_once(unmix_kernel, "unmix", [out, out], [grad, *pieces], 2 * grad.shape[0] * 512 * 1024)


def unproject_term(grad_refs, weight_refs, first):
    rows = jnp.concatenate([ref[part, first:first + 512] for ref in grad_refs for part in range(3)], axis=1)
    weight = jnp.concatenate([head_columns(weight_refs, quarter, 0, 768) for quarter in range(2)], axis=1)
    return dot_nt(rows, weight)


def unproject_far_kernel(mine_ref, other_ref, *rest):
    rest[8][...] = unproject_term((mine_ref, other_ref), rest[:8], 512).astype(BF)


def unproject_far(mine, other, pieces):
    out = jax.ShapeDtypeStruct((512, 1024), BF)
    return call_once(unproject_far_kernel, "unproject_far", [out], [mine, other, *pieces], 2 * 512 * 1536 * 1024)[0]


def unproject_near_kernel(mine_ref, other_ref, far_ref, resid_ref, grad_mid_ref, vector_ref, *rest):
    weight_refs, (grad_ref, low_ref, sums_ref) = rest[:8], rest[8:]
    term = unproject_term((mine_ref, other_ref), weight_refs, 0) + far_ref[...].astype(F32)
    grad_norm, grad_gain, grad_shift = norm_pull(resid_ref[...], vector_ref[0:1], term)
    grad = grad_mid_ref[...] + grad_norm
    grad_ref[...] = grad
    low_ref[...] = grad.astype(BF)
    sums_ref[...] = jnp.concatenate([grad_gain, grad_shift, jnp.zeros((6, grad.shape[1]), F32)], axis=0)


def unproject_near(mine, other, far, resid, grad_mid, vectors, pieces):
    outs = [
        jax.ShapeDtypeStruct(resid.shape, F32),
        jax.ShapeDtypeStruct(resid.shape, BF),
        jax.ShapeDtypeStruct((8, resid.shape[1]), F32),
    ]
    args = [mine, other, far, resid, grad_mid, vectors, *pieces]
    return call_once(unproject_near_kernel, "unproject_near", outs, args, 2 * 512 * 1536 * 1024)


def head_grads_kernel(near_ref, far_ref, grad_near_ref, grad_far_ref, mine_ref, other_ref, *rest):
    mixed_refs, out_refs, bias_ref = (rest[0:2], rest[2:4]), rest[4:12], rest[12]
    rows_t = jnp.concatenate([near_ref[...], far_ref[...]], axis=0).T
    grad_t = jnp.concatenate([grad_near_ref[...], grad_far_ref[...]], axis=0).T
    for quarter, ref in enumerate((mine_ref, other_ref)):
        for part in range(4):
            if part < 3:
                term = dot_nn(rows_t, ref[part])
            else:
                term = dot_nn(grad_t, jnp.concatenate([m[...] for m in mixed_refs[quarter]], axis=0))
            term = term.astype(BF)
            for index, out_ref in enumerate(out_refs):
                place = quarter if index % 2 == 0 else 1 - quarter
                out_ref[place, :, part * 256:(part + 1) * 256] = term[index * 128:(index + 1) * 128]
        for row, part in ((0, 0), (1, 2)):
            total = jnp.sum(ref[part].astype(F32), axis=0, keepdims=True)
            bias_ref[2 * quarter + row:2 * quarter + row + 1, :] = total
    bias_ref[4:8, :] = jnp.zeros((4, 256), F32)


def head_grads(near, far, grad_near, grad_far, mine, other, mixed_mine, mixed_other):
    outs = [jax.ShapeDtypeStruct((2, 128, 1024), BF)] * 8 + [jax.ShapeDtypeStruct((8, 256), F32)]
    args = [near, far, grad_near, grad_far, mine, other, *mixed_mine, *mixed_other]
    return call_once(head_grads_kernel, "head_grads", outs, args, 2 * 1024 * 1024 * 2048)


def gather_plane(own):
    half = own.shape[0] // 2
    from_x = swap(own, XBIT)
    from_y = swap(own, YBIT)
    across = jnp.concatenate([swap(from_x[:half], YBIT), swap(from_y[half:], XBIT)], axis=0)
    out = []
    for quad in (own, from_x, from_y, across):
        out += [quad, swap(quad, CORE)]
    return out


def scatter_plane(pieces):
    own, to_x, to_y, across = [pieces[2 * i] + swap(pieces[2 * i + 1], CORE) for i in range(4)]
    half = own.shape[0] // 2
    first = own[:half] + swap(to_y[:half], YBIT) + swap(to_x[:half] + swap(across[:half], YBIT), XBIT)
    second = own[half:] + swap(to_x[half:], XBIT) + swap(to_y[half:] + swap(across[half:], XBIT), YBIT)
    return first, second


def pack_heads(project, output):
    return jnp.concatenate([project.transpose(1, 0, 2).reshape(128, 768), output.T], axis=1)


def unpack_heads(values):
    return values[:, :768].reshape(128, 3, 256).transpose(1, 0, 2), values[:, 768:].T


def pack_units(expand, reduce):
    parts = (expand.reshape(128, 2, 512), reduce.T.reshape(128, 2, 512))
    return jnp.stack(parts, axis=2).reshape(128, 2048)


def unpack_units(values):
    shaped = values.reshape(128, 2, 2, 512)
    return shaped[:, :, 0].reshape(128, 1024), shaped[:, :, 1].reshape(128, 1024).T


def fetch_heads(piece, core):
    far = swap(piece, Z1)
    return gather_plane(jnp.stack([jnp.where(core == 0, piece, far), jnp.where(core == 0, far, piece)]))


def fetch_units(piece):
    own = jnp.stack([piece, swap(piece, 1), swap(piece, 2), swap(piece, 3)])
    return own, gather_plane(own)


def fetch_small(six, project_bias, expand_bias, own, place, core):
    layers = six.shape[1]
    wide = jnp.pad(project_bias, ((0, 0), (0, 0), (0, 96)))
    piece = jnp.concatenate([six.transpose(1, 0, 2), wide, expand_bias[:, None, :], jnp.zeros((layers, 7, 128), BF)], axis=1)
    every = lax.all_gather(piece, AXES, axis=0, tiled=False).reshape(8, 4, layers, 16, 128).astype(F32)
    turned = every[jnp.arange(8) ^ own, 0]
    native = every[:, place ^ jnp.arange(4)]
    out = []
    for layer in range(layers):
        vectors = turned[:, layer, :6].transpose(1, 0, 2).reshape(6, 1024)
        following = turned[:, min(layer + 1, layers - 1), :2].transpose(1, 0, 2).reshape(2, 1024)
        pair = native[:, ::2, layer, 6:8, :32].transpose(1, 2, 0, 3).reshape(2, 2, 256)
        pair = jnp.where(core == 0, pair, pair[::-1])
        head_bias = jnp.concatenate([pair[:, 0], jnp.zeros((2, 256), F32), pair[:, 1]], axis=1)
        unit_bias = native[:, :, layer, 8].transpose(1, 0, 2).reshape(1, 4096)
        out.append((jnp.concatenate([vectors, following], axis=0), head_bias, unit_bias))
    return out


def sum_small(layers, own, core):
    turn = jnp.arange(8) ^ own
    rows = []
    for first_sums, second_sums, unit_sums, head_sums in layers:
        six = jnp.stack([first_sums[0], first_sums[1], second_sums[0], second_sums[1], second_sums[2], second_sums[3]])
        heads = head_sums[:4].reshape(2, 2, 256)
        heads = jnp.where(core == 0, heads, heads[::-1]).reshape(4, 8, 32)[:, turn]
        heads = jnp.pad(heads, ((0, 0), (0, 0), (0, 96)))
        rows += [six.reshape(6, 8, 128), unit_sums.reshape(4, 8, 128)[:, turn], heads]
    rows = jnp.concatenate(rows, axis=0).transpose(1, 0, 2)
    rows = rows.reshape(2, 2, 2, rows.shape[1], 128)
    rows = rows[:, :, 0] + swap(rows[:, :, 1], CORE)
    rows = rows[:, 0] + swap(rows[:, 1], XBIT)
    rows = rows[0] + swap(rows[1], YBIT)
    rows = rows.reshape(len(layers), 14, 128)

    def part(offset):
        return jnp.concatenate([rows[:, :6], rows[:, 6 + offset:7 + offset], rows[:, 12:14]], axis=1)

    two = swap(part(2), 2)
    base = jnp.concatenate([rows[:, :7], rows[:, 10:12]], axis=1)
    whole = base[:, :7] + two[:, :7] + swap(part(1), 1)[:, :7] + swap(part(3), 3)[:, :7]
    return whole[:, :6], whole[:, 6], base[:, 7:, :32] + two[:, 7:, :32]


def reduce_heads(pieces, core):
    first, second = (part[0].astype(F32) for part in scatter_plane(pieces))
    near = jnp.where(core == 0, first, second)
    away = jnp.where(core == 0, second, first)
    return unpack_heads(near + swap(away.astype(BF), Z1).astype(F32))


def reduce_units(pieces):
    first, second = scatter_plane(pieces)
    terms = [first[0], swap(first[1], 1), swap(second[0], 2), swap(second[1], 3)]
    return unpack_units(sum(term.astype(F32) for term in terms))


def fast_device(
    layer_input,
    first_gain,
    first_shift,
    project_weight,
    project_bias,
    output_weight,
    output_bias,
    second_gain,
    second_shift,
    expand_weight,
    expand_bias,
    reduce_weight,
    reduce_bias,
    picture_start,
    cotangent,
):
    own = lax.axis_index("dp")
    place = lax.axis_index("tensor")
    core = own & 1
    me = (2 * core + (place & 1)).astype(jnp.int32).reshape(1)
    slopes = head_slopes((place ^ (2 * core)) * 4, 4)
    starts = redeal(picture_start)[0]
    six = jnp.stack([first_gain, first_shift, output_bias, second_gain, second_shift, reduce_bias])
    small = fetch_small(six, project_bias, expand_bias, own, place, core)
    head_piece = [pack_heads(project_weight[i], output_weight[i]) for i in range(LAYERS)]
    unit_piece = [pack_units(expand_weight[i], reduce_weight[i]) for i in range(LAYERS)]
    dealt = redeal(layer_input)
    heads, units = [None] * LAYERS, [None] * LAYERS
    heads[0] = fetch_heads(head_piece[0], core)
    quad, units[0] = fetch_units(after(unit_piece[0], dealt))
    resid = turn_blocks(dealt.astype(F32), own)
    normed = layer_norm(resid, small[0][0][0], small[0][0][1]).astype(BF)
    saved = []
    for layer in range(LAYERS):
        vectors, head_bias, unit_bias = small[layer]
        pieces = heads[layer]
        far = swap(normed, Z0)
        if layer + 1 < LAYERS:
            heads[layer + 1] = fetch_heads(after(head_piece[layer + 1], quad), core)
            quad, units[layer + 1] = fetch_units(after(unit_piece[layer + 1], far))
        near_mine, near_other = project(normed, head_bias, pieces)
        got_near = swap(near_other, CORE)
        far_mine, far_other = project(far, head_bias, pieces)
        got_far = swap(far_other, CORE)
        blocks = (near_mine, far_mine, got_near, got_far)
        far_mixed, far_send, far_exact, far_log = attend(blocks, 1, slopes, starts, me)
        far_got = swap(far_send, CORE)
        far_term = swap(mix_far(far_mixed, far_got, pieces), Z0)
        near_mixed, near_send, near_exact, near_log = attend(blocks, 0, slopes, starts, me)
        near_got = swap(near_send, CORE)
        mid, normed_two = mix_near(near_mixed, near_got, far_term, resid, vectors, pieces)
        hidden, active, out, following = mlp_forward(normed_two, mid, vectors, unit_bias, units[layer])
        saved.append((
            resid, normed, far, blocks, (near_exact, far_exact), (near_log, far_log),
            (near_mixed, far_mixed), (near_got, far_got), mid, normed_two, hidden, active,
        ))
        resid, normed = out, following
        if layer == 0:
            grad = turn_blocks(redeal(after(cotangent, far_term)).astype(F32), own)
    layer_output = redeal(turn_blocks(resid.astype(BF), own))
    sums, head_grad, unit_grad = [None] * LAYERS, [None] * LAYERS, [None] * LAYERS
    for layer in reversed(range(LAYERS)):
        vectors, pieces = small[layer][0], heads[layer]
        (
            resid, normed, far, blocks, exacts, logs, mixed, mixed_got, mid, normed_two, hidden, active,
        ) = saved[layer]
        grad_hidden, unit_sums, grad_mid, grad_low, second_sums = mlp_backward(grad, mid, vectors, hidden, units[layer])
        grad_far = swap(grad_low, Z0)
        unit_pieces = mlp_weight_grads(grad, normed_two, active, grad_hidden)
        near_mine, near_other = unmix(grad_low, pieces)
        got_near = swap(near_other, CORE)
        far_mine, far_other = unmix(grad_far, pieces)
        got_far = swap(far_other, CORE)
        grads_mixed = (near_mine, far_mine, got_near, got_far)
        mine, away = attend_pull(blocks, grads_mixed, exacts, logs, slopes, starts, me)
        other = swap(away, CORE)
        far_term = swap(unproject_far(mine, other, pieces), Z0)
        *head_pieces, head_sums = head_grads(normed, far, grad_low, grad_far, mine, other, mixed, mixed_got)
        grad, grad_low, first_sums = unproject_near(mine, other, far_term, resid, grad_mid, vectors, pieces)
        sums[layer] = (first_sums, second_sums, unit_sums, head_sums)
        head_grad[layer] = reduce_heads(head_pieces, core)
        unit_grad[layer] = reduce_units(unit_pieces)
    input_grad = redeal(turn_blocks(grad_low, own))
    six, unit_sum, head_sum = sum_small(sums, own, core)
    return (
        layer_output,
        input_grad,
        six[:, 0],
        six[:, 1],
        jnp.stack([g[0] for g in head_grad]),
        head_sum,
        jnp.stack([g[1] for g in head_grad]),
        six[:, 2],
        six[:, 3],
        six[:, 4],
        jnp.stack([g[0] for g in unit_grad]),
        unit_sum,
        jnp.stack([g[1] for g in unit_grad]),
        six[:, 5],
    )


def solution(mesh):
    placed = (
        P(("dp", "tensor"), None),
        P(None, "dp"),
        P(None, "dp"),
        P(None, None, "dp", "tensor"),
        P(None, None, ("tensor", "dp")),
        P(None, "tensor", "dp"),
        P(None, "dp"),
        P(None, "dp"),
        P(None, "dp"),
        P(None, "dp", "tensor"),
        P(None, ("tensor", "dp")),
        P(None, "tensor", "dp"),
        P(None, "dp"),
        P("dp", None),
        P(("dp", "tensor"), None),
    )
    return jax.shard_map(
        fast_device if mesh_is_paired(mesh) else on_device,
        mesh=mesh,
        in_specs=placed,
        out_specs=(
            P(("dp", "tensor"), None),
            P(("dp", "tensor"), None),
            P(None, "dp"),
            P(None, "dp"),
            P(None, None, "dp", "tensor"),
            P(None, None, ("tensor", "dp")),
            P(None, "tensor", "dp"),
            P(None, "dp"),
            P(None, "dp"),
            P(None, "dp"),
            P(None, "dp", "tensor"),
            P(None, ("tensor", "dp")),
            P(None, "tensor", "dp"),
            P(None, "dp"),
        ),
        check_vma=False,
    )
```

```python
import functools

import jax
import jax.numpy as jnp
from jax import lax
from jax.experimental import pallas as pl
from jax.experimental.pallas import tpu as pltpu
from jax.sharding import PartitionSpec as P

HEADS = 16
HD = 64
LAYERS = 2
SEQ_LEN = 2048
PIECE = 256


NORM_EPS = 1e-05


def layer_norm(values, gain, shift):
    centred = values - jnp.mean(values, axis=-1, keepdims=True)
    spread = jnp.mean(centred * centred, axis=-1, keepdims=True)
    return centred * lax.rsqrt(spread + NORM_EPS) * gain + shift


def gelu_tanh(values):
    return jax.nn.gelu(values, approximate=True)


def piece_numbers(starts):
    places = jnp.arange(SEQ_LEN, dtype=jnp.int32)
    inside = (places[:, None] >= starts[None, :]) & (places[:, None] < starts[None, :] + PIECE)
    numbers = jnp.arange(1, starts.shape[0] + 1, dtype=jnp.int32)
    return jnp.sum(jnp.where(inside, numbers[None, :], 0), axis=1)


def head_slopes(first_head, count_heads):
    heads_at = (first_head + jnp.arange(count_heads, dtype=jnp.int32)).astype(jnp.float32)
    return jnp.exp2(-8.0 * (heads_at + 1.0) / HEADS)


def gather_rows(values):
    return lax.all_gather(values, "tensor", axis=0, tiled=True)


def gather_grads(values):
    return lax.all_gather(values, "tensor", axis=0, tiled=True)


def scatter_rows(values, weight):
    rows_here = values.shape[0] // lax.axis_size("tensor")

    def partial_term(offset, count_rows):
        return jnp.dot(values, weight, preferred_element_type=jnp.float32)

    return lax.psum_scatter(
        partial_term(jnp.int32(0), rows_here * lax.axis_size("tensor")).astype(jnp.bfloat16),
        "tensor",
        scatter_dimension=0,
        tiled=True,
    ).astype(jnp.float32)


def scatter_back(partial_term, rows_here):
    return lax.psum_scatter(
        partial_term(jnp.int32(0), rows_here * lax.axis_size("tensor")).astype(jnp.bfloat16),
        "tensor",
        scatter_dimension=0,
        tiled=True,
    ).astype(jnp.float32)


def block_scores(query_block, key_rows, offset, piece_ids, slopes):
    length = key_rows.shape[0]
    count_rows = query_block.shape[0]
    query_places = offset + jnp.arange(count_rows, dtype=jnp.int32)
    key_places = jnp.arange(length, dtype=jnp.int32)
    product = jnp.einsum("qhe,khe->hqk", query_block, key_rows, preferred_element_type=jnp.float32)
    distance = jnp.abs(query_places[:, None] - key_places[None, :]).astype(jnp.float32)
    scores = product * HD ** (-0.5) - slopes[:, None, None] * distance[None]
    query_pieces = lax.dynamic_slice_in_dim(piece_ids, offset, count_rows, 0)
    allowed = (key_places[None, :] <= query_places[:, None]) | (
        query_pieces[:, None] == piece_ids[None, :]
    ) & (query_pieces[:, None] > 0)
    return jnp.where(allowed[None], scores, -jnp.inf)


def sequence_forward(operands, slopes):
    queries, key_rows, value_rows, piece_ids = operands
    length = queries.shape[0]
    block_rows = min(512, length)

    def one_block(block_index):
        offset = block_index * block_rows
        query_block = lax.dynamic_slice_in_dim(queries, offset, block_rows, 0)
        scores = block_scores(query_block, key_rows, offset, piece_ids, slopes)
        row_max = jnp.max(scores, axis=-1, keepdims=True)
        raw_weights = jnp.exp(scores - row_max)
        totals = jnp.sum(raw_weights, axis=-1, keepdims=True)
        soft_weights = (raw_weights / totals).astype(jnp.bfloat16)
        attended = jnp.einsum(
            "hqk,khe->qhe", soft_weights, value_rows, preferred_element_type=jnp.float32
        )
        return (attended.astype(jnp.bfloat16), (row_max + jnp.log(totals))[..., 0])

    attended, log_total = lax.map(one_block, jnp.arange(length // block_rows, dtype=jnp.int32))
    return (attended.reshape(length, queries.shape[1], queries.shape[2]), log_total)


def sequence_backward(operands, slopes):
    queries, key_rows, value_rows, piece_ids, grad_mixed, log_total = operands
    length = queries.shape[0]
    block_rows = min(512, length)

    def one_block(carry, block_index):
        key_grad, value_grad = carry
        offset = block_index * block_rows
        query_block = lax.dynamic_slice_in_dim(queries, offset, block_rows, 0)
        grad_block = lax.dynamic_slice_in_dim(grad_mixed, offset, block_rows, 0)
        scores = block_scores(query_block, key_rows, offset, piece_ids, slopes)
        probs = jnp.exp(scores - log_total[block_index][..., None])
        soft_weights = probs.astype(jnp.bfloat16)
        value_grad = value_grad + jnp.einsum(
            "hqk,qhe->khe", soft_weights, grad_block, preferred_element_type=jnp.float32
        )
        prob_grad = jnp.einsum(
            "qhe,khe->hqk", grad_block, value_rows, preferred_element_type=jnp.float32
        )
        centred = jnp.sum(probs * prob_grad, axis=-1, keepdims=True)
        score_grad = (probs * (prob_grad - centred) * HD ** (-0.5)).astype(jnp.bfloat16)
        query_grad = jnp.einsum(
            "hqk,khe->qhe", score_grad, key_rows, preferred_element_type=jnp.float32
        )
        key_grad = key_grad + jnp.einsum(
            "hqk,qhe->khe", score_grad, query_block, preferred_element_type=jnp.float32
        )
        return ((key_grad, value_grad), query_grad)

    empty = jnp.zeros(queries.shape, jnp.float32)
    (key_grad, value_grad), query_grad = lax.scan(
        one_block, (empty, empty), jnp.arange(length // block_rows, dtype=jnp.int32)
    )
    return (query_grad.reshape(queries.shape), key_grad, value_grad)


def attend_forward(triple, piece_ids, slopes):
    width = triple.shape[2]
    count_seq = piece_ids.shape[0]
    length = piece_ids.shape[1]
    shaped = triple.reshape(3, count_seq, length, width // HD, HD)
    attended, log_total = lax.map(
        lambda operands: sequence_forward(operands, slopes),
        (shaped[0], shaped[1], shaped[2], piece_ids),
    )
    return (attended.reshape(count_seq * length, width), log_total)


def attend_backward(triple, grad_attended, log_total, piece_ids, slopes):
    width = triple.shape[2]
    count_seq = piece_ids.shape[0]
    length = piece_ids.shape[1]
    shaped = triple.reshape(3, count_seq, length, width // HD, HD)
    grad_shaped = grad_attended.reshape(count_seq, length, width // HD, HD)
    query_grad, key_grad, value_grad = lax.map(
        lambda operands: sequence_backward(operands, slopes),
        (shaped[0], shaped[1], shaped[2], piece_ids, grad_shaped, log_total),
    )
    return (
        query_grad.reshape(-1, width),
        key_grad.reshape(-1, width),
        value_grad.reshape(-1, width),
    )


def fetch_layer(
    project_weight,
    project_bias,
    output_weight,
    expand_weight,
    expand_bias,
    reduce_weight,
    small_stack,
    layer_index,
):
    return (
        lax.all_gather(project_weight[layer_index], "dp", axis=1, tiled=True),
        lax.all_gather(project_bias[layer_index], "dp", axis=1, tiled=True),
        lax.all_gather(output_weight[layer_index], "dp", axis=1, tiled=True),
        lax.all_gather(expand_weight[layer_index], "dp", axis=0, tiled=True),
        lax.all_gather(expand_bias[layer_index], "dp", axis=0, tiled=True),
        lax.all_gather(reduce_weight[layer_index], "dp", axis=1, tiled=True),
        lax.all_gather(small_stack[layer_index], "dp", axis=1, tiled=True),
    )


def forward_layer(resid, weights, piece_ids, slopes):
    w_project, bias_project, w_output, w_expand, bias_expand, w_reduce, small = weights
    vectors = small.astype(jnp.float32)
    normed = layer_norm(resid, vectors[0], vectors[1])
    gathered = gather_rows(normed.astype(jnp.bfloat16))
    product = jnp.einsum("gd,cde->cge", gathered, w_project, preferred_element_type=jnp.float32)
    biases = jnp.stack([bias_project[0], jnp.zeros_like(bias_project[0]), bias_project[1]]).astype(
        jnp.float32
    )
    triple = (product + biases[:, None, :]).astype(jnp.bfloat16)
    attended, log_total = attend_forward(triple, piece_ids, slopes)
    resid_mid = resid + (scatter_rows(attended, w_output) + vectors[2])
    normed_two = layer_norm(resid_mid, vectors[3], vectors[4])
    gathered_two = gather_rows(normed_two.astype(jnp.bfloat16))
    hidden = jnp.dot(
        gathered_two, w_expand, preferred_element_type=jnp.float32
    ) + bias_expand.astype(jnp.float32)
    active = gelu_tanh(hidden).astype(jnp.bfloat16)
    mlp_sum = scatter_rows(active, w_reduce)
    mlp_keep = (gathered_two, hidden, None)
    resid_out = resid_mid + (mlp_sum + vectors[5])
    return (resid_out, (gathered, triple, attended, log_total, resid_mid, mlp_keep))


def backward_layer(grad_out, resid, weights, kept, piece_ids, slopes):
    w_project, bias_project, w_output, w_expand, bias_expand, w_reduce, small = weights
    vectors = small.astype(jnp.float32)
    gathered, triple, attended, log_total, resid_mid, mlp_keep = kept
    rows_here = grad_out.shape[0]
    rows_in, hidden, full_weights = mlp_keep
    grad_bias_reduce = jnp.sum(grad_out, axis=0)
    active, gelu_pull = jax.vjp(gelu_tanh, hidden)
    active_low = active.astype(jnp.bfloat16)
    grad_mlp = gather_grads(grad_out.astype(jnp.bfloat16))
    grad_reduce = jnp.einsum("gf,gd->fd", active_low, grad_mlp, preferred_element_type=jnp.float32)
    grad_active = jnp.einsum("gd,fd->gf", grad_mlp, w_reduce, preferred_element_type=jnp.float32)
    (grad_hidden,) = gelu_pull(grad_active)
    grad_bias_expand = jnp.sum(grad_hidden, axis=0)
    grad_hidden_low = grad_hidden.astype(jnp.bfloat16)
    grad_expand = jnp.einsum(
        "gd,gf->df", rows_in, grad_hidden_low, preferred_element_type=jnp.float32
    )

    def expand_term(offset, count_rows):
        return jnp.einsum(
            "gf,df->gd", grad_hidden_low, w_expand, preferred_element_type=jnp.float32
        )

    grad_normed_two = scatter_back(expand_term, rows_here)
    unused_two, second_pull = jax.vjp(layer_norm, resid_mid, vectors[3], vectors[4])
    grad_from_norm, grad_gain_two, grad_shift_two = second_pull(grad_normed_two)
    grad_mid = grad_out + grad_from_norm
    grad_bias_output = jnp.sum(grad_mid, axis=0)
    grad_attn = gather_grads(grad_mid.astype(jnp.bfloat16))
    grad_output = jnp.einsum("gt,gd->td", attended, grad_attn, preferred_element_type=jnp.float32)
    grad_attended = jnp.einsum(
        "gd,td->gt", grad_attn, w_output, preferred_element_type=jnp.float32
    ).astype(jnp.bfloat16)
    query_grad, key_grad, value_grad = attend_backward(
        triple, grad_attended, log_total, piece_ids, slopes
    )
    grad_bias_project = jnp.stack([jnp.sum(query_grad, axis=0), jnp.sum(value_grad, axis=0)])
    grad_triple = jnp.stack([query_grad, key_grad, value_grad]).astype(jnp.bfloat16)
    grad_project = jnp.einsum(
        "gd,cge->cde", gathered, grad_triple, preferred_element_type=jnp.float32
    )

    def project_term(offset, count_rows):
        return jnp.einsum("cge,cde->gd", grad_triple, w_project, preferred_element_type=jnp.float32)

    grad_normed = scatter_back(project_term, rows_here)
    unused_one, first_pull = jax.vjp(layer_norm, resid, vectors[0], vectors[1])
    grad_from_first, grad_gain_one, grad_shift_one = first_pull(grad_normed)
    grad_stream = grad_mid + grad_from_first
    small_grads = jnp.stack(
        [
            grad_gain_one,
            grad_shift_one,
            grad_bias_output,
            grad_gain_two,
            grad_shift_two,
            grad_bias_reduce,
        ]
    )
    return (
        grad_stream,
        (
            grad_project,
            grad_bias_project,
            grad_output,
            grad_expand,
            grad_bias_expand,
            grad_reduce,
            small_grads,
        ),
    )


def reduce_layer(layer_grads):
    (
        grad_project,
        grad_bias_project,
        grad_output,
        grad_expand,
        grad_bias_expand,
        grad_reduce,
        small_grads,
    ) = layer_grads
    return (
        lax.psum_scatter(
            grad_project.astype(jnp.bfloat16), "dp", scatter_dimension=1, tiled=True
        ).astype(jnp.float32),
        lax.psum_scatter(
            grad_bias_project.astype(jnp.bfloat16), "dp", scatter_dimension=1, tiled=True
        ).astype(jnp.float32),
        lax.psum_scatter(
            grad_output.astype(jnp.bfloat16), "dp", scatter_dimension=1, tiled=True
        ).astype(jnp.float32),
        lax.psum_scatter(
            grad_expand.astype(jnp.bfloat16), "dp", scatter_dimension=0, tiled=True
        ).astype(jnp.float32),
        lax.psum_scatter(
            grad_bias_expand.astype(jnp.bfloat16), "dp", scatter_dimension=0, tiled=True
        ).astype(jnp.float32),
        lax.psum_scatter(
            grad_reduce.astype(jnp.bfloat16), "dp", scatter_dimension=1, tiled=True
        ).astype(jnp.float32),
        lax.psum_scatter(
            small_grads.astype(jnp.bfloat16), "dp", scatter_dimension=1, tiled=True
        ).astype(jnp.float32),
    )


def on_device(
    layer_input,
    first_gain,
    first_shift,
    project_weight,
    project_bias,
    output_weight,
    output_bias,
    second_gain,
    second_shift,
    expand_weight,
    expand_bias,
    reduce_weight,
    reduce_bias,
    picture_start,
    cotangent,
):
    small_stack = jnp.stack(
        [first_gain, first_shift, output_bias, second_gain, second_shift, reduce_bias], axis=1
    )
    piece_ids = jax.vmap(piece_numbers)(picture_start)
    heads_here = project_weight.shape[3] // HD
    slopes = head_slopes(lax.axis_index("tensor") * heads_here, heads_here)
    resid = layer_input.astype(jnp.float32)
    saved = []
    for layer_index in range(LAYERS):
        weights = fetch_layer(
            project_weight,
            project_bias,
            output_weight,
            expand_weight,
            expand_bias,
            reduce_weight,
            small_stack,
            layer_index,
        )
        resid_next, kept = forward_layer(resid, weights, piece_ids, slopes)
        saved.append((resid, weights, kept))
        resid = resid_next
    layer_output = resid.astype(jnp.bfloat16)
    grad_stream = cotangent.astype(jnp.float32)
    collected = []
    for layer_index in reversed(range(LAYERS)):
        resid_in, weights, kept = saved[layer_index]
        grad_stream, layer_grads = backward_layer(
            grad_stream, resid_in, weights, kept, piece_ids, slopes
        )
        layer_grads = reduce_layer(layer_grads)
        collected.insert(0, layer_grads)
    stacked = tuple(
        (jnp.stack([grad_entry[member] for grad_entry in collected]) for member in range(7))
    )
    (
        grad_project,
        grad_bias_project,
        grad_output,
        grad_expand,
        grad_bias_expand,
        grad_reduce,
        small_grads,
    ) = stacked
    small_grads = lax.psum(small_grads, "tensor")
    return (
        layer_output,
        grad_stream.astype(jnp.bfloat16),
        small_grads[:, 0],
        small_grads[:, 1],
        grad_project,
        grad_bias_project,
        grad_output,
        small_grads[:, 2],
        small_grads[:, 3],
        small_grads[:, 4],
        grad_expand,
        grad_bias_expand,
        grad_reduce,
        small_grads[:, 5],
    )


Z0, Z1, CORE, XBIT, YBIT = 1, 2, 4, 8, 16
AXES = ("dp", "tensor")
NEG = -1e30
BF = jnp.bfloat16
F32 = jnp.float32
VMEM_LIMIT = 56 * 1024 * 1024


def took(us):
    return pl.CostEstimate(flops=int(us * 5e8), bytes_accessed=1, transcendentals=0)


def mesh_is_paired(mesh):
    return dict(mesh.shape) == {"dp": 8, "tensor": 4}


def swap(values, mask):
    return lax.ppermute(values, AXES, [(i, i ^ mask) for i in range(32)])


def swap_some(values, masks):
    pairs = [(i, i ^ masks[(i >> 2) & 1]) for i in range(32)]
    return lax.ppermute(values, AXES, [pair for pair in pairs if pair[0] != pair[1]])


def redeal(values):
    def target(i):
        core, z1 = (i >> 2) & 1, (i >> 1) & 1
        return (i & ~6) | (z1 << 2) | (core << 1)

    return lax.ppermute(values, AXES, [(i, target(i)) for i in range(32) if target(i) != i])


def turn_index(values, own):
    shape = values.shape
    for bit in range(3):
        values = values.reshape(8 >> (bit + 1), 2, (1 << bit), *shape[1:])
        values = jnp.where((own >> bit) & 1, jnp.concatenate([values[:, 1:], values[:, :1]], axis=1), values)
    return values.reshape(shape)


def after(values, *others):
    return lax.optimization_barrier((values, *others))[0]


def after_all(values, *others):
    if not others:
        return tuple(values)
    return lax.optimization_barrier((*values, *others))[:len(values)]


def task(steps):
    next(steps)
    return steps


def advance(token, *tasks):
    made = []
    for steps in tasks:
        try:
            made += steps.send(token)
        except StopIteration:
            pass
    return made


def dot_nt(a, b):
    return lax.dot_general(a, b, (((1,), (1,)), ((), ())), preferred_element_type=F32)


def dot_nn(a, b):
    return lax.dot_general(a, b, (((1,), (0,)), ((), ())), preferred_element_type=F32)


def head_mask(shape, head):
    lane = lax.broadcasted_iota(jnp.int32, shape, 1)
    return (lane < HD) if head == 0 else (lane >= HD)


def diagonal_bias(rows, columns, first_row, first_column, start):
    key = first_row + lax.broadcasted_iota(jnp.int32, (rows, 1), 0)
    query = first_column + lax.broadcasted_iota(jnp.int32, (1, columns), 1)
    key_in = (key >= start) & (key < start + PIECE)
    query_in = (query >= start) & (query < start + PIECE)
    allowed = (key <= query) | (key_in & query_in)
    reach = (jnp.minimum(key, 2 * query - key) - first_column).astype(F32)
    return jnp.where(allowed, reach, NEG)


def ramp(rows, first_row, first_column):
    return (first_row - first_column + lax.broadcasted_iota(jnp.int32, (rows, 1), 0)).astype(F32)


def attend_kernel(block, rest_bit, slope_ref, start_ref, me_ref, *rest):
    triple_refs, rest = rest[:12], rest[12:]
    near_ref, away_ref, exact_ref, lse_ref, q_ref, k_ref, v_ref, vt_ref, acc_ref, max_ref, bias_ref, tail_ref = rest
    pair = pl.program_id(0)
    turn = pl.program_id(1)
    me = me_ref[0]
    step = (2 * turn + rest_bit) ^ me
    length = k_ref.shape[0]
    first = step * block

    def at(index):
        return pl.multiple_of((index ^ me) * block, block)

    start = start_ref[first // (length // start_ref.shape[0])]

    @pl.when(turn == 0)
    def _():
        for index in range(4):
            here = slice(index * block, (index + 1) * block)
            q_ref[here, :] = triple_refs[3 * index][...] * jnp.asarray(HD ** -0.5, BF)
            k_ref[here, :] = triple_refs[3 * index + 1][...]
            v_ref[here, :] = triple_refs[3 * index + 2][...]
        for head in range(2):
            mixed = jnp.where(head_mask((length, 2 * HD), head), v_ref[...], jnp.ones((), BF))
            vt_ref[head] = mixed.T

    bias_ref[...] = diagonal_bias(block, block, first, first, start)
    q_block = q_ref[pl.ds(at(step), block), :]
    heads = [jnp.where(head_mask(q_block.shape, head), q_block, jnp.zeros((), BF)) for head in range(2)]
    slopes = [slope_ref[2 * pair + head] for head in range(2)]
    acc_ref[...] = jnp.zeros_like(acc_ref)
    max_ref[...] = jnp.full_like(max_ref, NEG)

    def absorb(head, scores, vt):
        old = max_ref[head]
        new = jnp.maximum(old, jnp.max(scores, axis=0, keepdims=True))
        weights = jnp.exp(scores - new).astype(BF)
        acc_ref[head] = acc_ref[head] * jnp.exp(old - new) + dot_nn(vt, weights)
        max_ref[head] = new

    def full(index, carry):
        place = at(index)
        keys = k_ref[pl.ds(place, block), :]
        slant = ramp(block, index * block, first)
        for head in range(2):
            absorb(head, dot_nt(keys, heads[head]) + slopes[head] * slant, vt_ref[head, :, pl.ds(place, block)])
        return carry

    place = at(step)
    for head in range(2):
        absorb(
            head,
            dot_nt(k_ref[pl.ds(place, block), :], heads[head]) + slopes[head] * bias_ref[...],
            vt_ref[head, :, pl.ds(place, block)],
        )
    lax.fori_loop(0, step, full, 0)
    edge = first + block

    @pl.when((start < edge) & (start + PIECE > edge))
    def _():
        after = at(step + 1)
        tail_ref[...] = diagonal_bias(PIECE, block, edge, first, start)
        for head in range(2):
            absorb(
                head,
                dot_nt(k_ref[pl.ds(after, PIECE), :], heads[head]) + slopes[head] * tail_ref[...],
                vt_ref[head, :, pl.ds(after, PIECE)],
            )

    outs = []
    for head in range(2):
        acc = acc_ref[head]
        total = acc[HD:HD + 1] if head == 0 else acc[0:1]
        outs.append((acc * (1.0 / total))[head * HD:(head + 1) * HD])
        lse_ref[0, head:head + 1, :] = max_ref[head] + jnp.log(total)
    mixed = jnp.concatenate(outs, axis=0)
    exact_ref[...] = mixed
    final = mixed.T.astype(BF)

    @pl.when(turn == 0)
    def _():
        near_ref[...] = final

    @pl.when(turn == 1)
    def _():
        away_ref[...] = final


def triple_specs(block, pairs):
    specs = []
    for index in range(4):
        for part in range(3):
            specs.append(pl.BlockSpec((block, 2 * HD), functools.partial(lambda part, p, i: (0, part * pairs + p), part)))
    return specs


def attend(blocks, rest_bit, slopes, starts, me):
    block, width = blocks[0].shape[0], blocks[0].shape[1] // 3
    pairs = width // (2 * HD)
    length = 4 * block
    smem = pl.BlockSpec(memory_space=pltpu.SMEM)
    return pl.pallas_call(
        functools.partial(attend_kernel, block, rest_bit),
        grid=(pairs, 2),
        in_specs=[smem, smem, smem] + triple_specs(block, pairs),
        out_specs=[
            pl.BlockSpec((block, 2 * HD), lambda p, i: (0, p)),
            pl.BlockSpec((block, 2 * HD), lambda p, i: (0, p)),
            pl.BlockSpec((2 * HD, block), lambda p, i: (p, i)),
            pl.BlockSpec((1, 8, block), lambda p, i: (p, 0, i)),
        ],
        out_shape=[
            jax.ShapeDtypeStruct((block, width), BF),
            jax.ShapeDtypeStruct((block, width), BF),
            jax.ShapeDtypeStruct((width, 2 * block), F32),
            jax.ShapeDtypeStruct((pairs, 8, 2 * block), F32),
        ],
        scratch_shapes=[
            pltpu.VMEM((length, 2 * HD), BF),
            pltpu.VMEM((length, 2 * HD), BF),
            pltpu.VMEM((length, 2 * HD), BF),
            pltpu.VMEM((2, 2 * HD, length), BF),
            pltpu.VMEM((2, 2 * HD, block), F32),
            pltpu.VMEM((2, 1, block), F32),
            pltpu.VMEM((block, block), F32),
            pltpu.VMEM((PIECE, block), F32),
        ],
        compiler_params=pltpu.CompilerParams(vmem_limit_bytes=VMEM_LIMIT),
        cost_estimate=took(17),
        name="attend",
    )(slopes, starts, me, *[b for b in blocks for _ in range(3)])


def pull_kernel(block, pair, slope_ref, start_ref, me_ref, *rest):
    triple_refs, grad_refs, rest = rest[:12], rest[12:16], rest[16:]
    exact_refs, lse_refs, rest = rest[0:2], rest[2:4], rest[4:]
    mine_ref, away_ref, q_ref, k_ref, v_ref, g_ref, kt_ref, dk_acc, dv_acc, dqt_ref, bias_ref, tail_ref = rest
    turn = pl.program_id(0)
    me = me_ref[0]
    step = turn ^ me
    length = k_ref.shape[0]
    first = step * block
    half, bit = turn // 2, turn % 2

    def at(index):
        return pl.multiple_of((index ^ me) * block, block)

    start = start_ref[first // (length // start_ref.shape[0])]

    @pl.when(turn == 0)
    def _():
        for index in range(4):
            here = slice(index * block, (index + 1) * block)
            q_ref[here, :] = triple_refs[3 * index][...] * jnp.asarray(HD ** -0.5, BF)
            k_ref[here, :] = triple_refs[3 * index + 1][...]
            v_ref[here, :] = triple_refs[3 * index + 2][...]
            g_ref[here, :] = grad_refs[index][...]
        kt_ref[...] = k_ref[...].T
        dk_acc[...] = jnp.zeros_like(dk_acc)
        dv_acc[...] = jnp.zeros_like(dv_acc)

    bias_ref[...] = diagonal_bias(block, block, first, first, start)
    dqt_ref[...] = jnp.zeros_like(dqt_ref)
    zero = jnp.zeros((), BF)
    q_block = q_ref[pl.ds(at(step), block), :]
    g_block = g_ref[pl.ds(at(step), block), :]
    masks = [head_mask(q_block.shape, head) for head in range(2)]
    q_heads = [jnp.where(mask, q_block, zero) for mask in masks]
    g_heads = [jnp.where(mask, g_block, zero) for mask in masks]
    slopes = [slope_ref[2 * pair + head] for head in range(2)]
    lanes = pl.ds(pl.multiple_of(half * block, block), block)
    exact = jnp.where(bit == 0, exact_refs[0][:, lanes], exact_refs[1][:, lanes])
    log_total = jnp.where(bit == 0, lse_refs[0][0, :, lanes], lse_refs[1][0, :, lanes])
    product = g_block.astype(F32).T * exact
    deltas = [jnp.sum(product[head * HD:(head + 1) * HD], axis=0, keepdims=True) for head in range(2)]

    def absorb(place, rows, bias_of):
        keys = k_ref[pl.ds(place, rows), :]
        values = v_ref[pl.ds(place, rows), :]
        dk = dk_acc[pl.ds(place, rows), :]
        dv = dv_acc[pl.ds(place, rows), :]
        for head in range(2):
            scores = dot_nt(keys, q_heads[head]) + slopes[head] * bias_of
            weights = jnp.exp(scores - log_total[head:head + 1, :])
            dv = dv + dot_nn(weights.astype(BF), g_heads[head])
            grad_p = dot_nt(values, g_heads[head])
            grad_s = (weights * (grad_p - deltas[head])).astype(BF)
            dk = dk + dot_nn(grad_s, q_heads[head])
            dqt_ref[head * HD:(head + 1) * HD, :] += dot_nn(kt_ref[head * HD:(head + 1) * HD, pl.ds(place, rows)], grad_s)
        dk_acc[pl.ds(place, rows), :] = dk
        dv_acc[pl.ds(place, rows), :] = dv

    absorb(at(step), block, bias_ref[...])

    def full(index, carry):
        absorb(at(index), block, ramp(block, index * block, first))
        return carry

    lax.fori_loop(0, step, full, 0)
    edge = first + block

    @pl.when((start < edge) & (start + PIECE > edge))
    def _():
        tail_ref[...] = diagonal_bias(PIECE, block, edge, first, start)
        absorb(at(step + 1), PIECE, tail_ref[...])

    grad_q = (dqt_ref[...].T * (HD ** -0.5)).astype(BF)
    here = pl.ds(pl.multiple_of(bit * block, block), block)

    @pl.when(half == 0)
    def _():
        mine_ref[0, here, :] = grad_q

    @pl.when(half == 1)
    def _():
        away_ref[0, here, :] = grad_q

    @pl.when(turn == 3)
    def _():
        for part, ref in ((1, dk_acc), (2, dv_acc)):
            mine_ref[part] = ref[:2 * block].astype(BF)
            away_ref[part] = ref[2 * block:].astype(BF)


def attend_pull(pair, blocks, grads, exacts, log_totals, slopes, starts, me):
    block, width = blocks[0].shape[0], blocks[0].shape[1] // 3
    pairs = width // (2 * HD)
    length = 4 * block
    smem = pl.BlockSpec(memory_space=pltpu.SMEM)
    triples = [pl.BlockSpec((block, 2 * HD), functools.partial(lambda part, i: (0, part * pairs + pair), part)) for part in range(3)]
    rows = pl.BlockSpec((block, 2 * HD), lambda i: (0, pair))
    wide = pl.BlockSpec((2 * HD, 2 * block), lambda i: (pair, 0))
    sums = pl.BlockSpec((1, 8, 2 * block), lambda i: (pair, 0, 0))
    out = pl.BlockSpec((3, 2 * block, 2 * HD), lambda i: (0, 0, 0))
    return pl.pallas_call(
        functools.partial(pull_kernel, block, pair),
        grid=(4,),
        in_specs=[smem, smem, smem] + triples * 4 + [rows] * 4 + [wide] * 2 + [sums] * 2,
        out_specs=[out, out],
        out_shape=[jax.ShapeDtypeStruct((3, 2 * block, 2 * HD), BF)] * 2,
        scratch_shapes=[
            pltpu.VMEM((length, 2 * HD), BF),
            pltpu.VMEM((length, 2 * HD), BF),
            pltpu.VMEM((length, 2 * HD), BF),
            pltpu.VMEM((length, 2 * HD), BF),
            pltpu.VMEM((2 * HD, length), BF),
            pltpu.VMEM((length, 2 * HD), F32),
            pltpu.VMEM((length, 2 * HD), F32),
            pltpu.VMEM((2 * HD, block), F32),
            pltpu.VMEM((block, block), F32),
            pltpu.VMEM((PIECE, block), F32),
        ],
        compiler_params=pltpu.CompilerParams(vmem_limit_bytes=VMEM_LIMIT),
        cost_estimate=took(22),
        name="attend_pull",
    )(slopes, starts, me, *[b for b in blocks for _ in range(3)], *grads, *exacts, *log_totals)


def head_columns(refs, quarter, first, last):
    return jnp.concatenate(
        [refs[odd][chip, 1 - quarter if odd else quarter, :, first:last] for chip in range(4) for odd in range(2)], axis=0
    )


def in_vmem(count):
    return [pl.BlockSpec(memory_space=pltpu.VMEM)] * count


def call_once(kernel, name, outs, args, us, scalars=0):
    return pl.pallas_call(
        kernel,
        in_specs=[pl.BlockSpec(memory_space=pltpu.SMEM)] * scalars + in_vmem(len(args) - scalars),
        out_specs=in_vmem(len(outs)),
        out_shape=outs,
        compiler_params=pltpu.CompilerParams(vmem_limit_bytes=VMEM_LIMIT),
        cost_estimate=took(us),
        name=name,
    )(*args)


def project_kernel(rows_ref, bias_ref, *rest):
    weight_refs, out_refs = rest[:2], rest[2:]
    rows = rows_ref[...]
    for quarter in (1, 0):
        out = dot_nn(rows, head_columns(weight_refs, quarter, 0, 768)) + bias_ref[quarter:quarter + 1]
        out_refs[quarter][...] = out.astype(BF)


def project(rows, bias, pieces):
    out = jax.ShapeDtypeStruct((rows.shape[0], 768), BF)
    return call_once(project_kernel, "project", [out, out], [rows, bias, *pieces], 5)


def mix_term(mixed_refs, weight_refs):
    rows = jnp.concatenate([ref[...] for ref in mixed_refs], axis=1)
    weight = jnp.concatenate([head_columns(weight_refs, quarter, 768, 1024) for quarter in range(2)], axis=1)
    return dot_nt(rows, weight)


def mix_far_kernel(mine_ref, other_ref, *rest):
    rest[2][...] = mix_term((mine_ref, other_ref), rest[:2]).astype(BF)


def mix_far(mine, other, pieces):
    out = jax.ShapeDtypeStruct((mine.shape[0], 1024), BF)
    return call_once(mix_far_kernel, "mix_far", [out], [mine, other, *pieces], 4)[0]


def mix_near_kernel(mine_ref, other_ref, far_ref, resid_ref, vector_ref, *rest):
    weight_refs, (mid_ref, normed_ref, flip_ref) = rest[:2], rest[2:]
    term = mix_term((mine_ref, other_ref), weight_refs)
    mid = resid_ref[...] + (term + far_ref[...].astype(F32) + vector_ref[2:3])
    mid_ref[...] = mid
    normed = (normalize(mid)[0] * vector_ref[3:4] + vector_ref[4:5]).astype(BF)
    normed_ref[...] = normed
    flip_ref[...] = flipped(normed)


def mix_near(mine, other, far, resid, vectors, pieces):
    outs = [
        jax.ShapeDtypeStruct(resid.shape, F32),
        jax.ShapeDtypeStruct(resid.shape, BF),
        jax.ShapeDtypeStruct(resid.shape, BF),
    ]
    return call_once(mix_near_kernel, "mix_near", outs, [mine, other, far, resid, vectors, *pieces], 6)


def unmix_kernel(grad_ref, *rest):
    weight_refs, out_refs = rest[:2], rest[2:]
    grad = grad_ref[...]
    for quarter in (1, 0):
        out_refs[quarter][...] = dot_nn(grad, head_columns(weight_refs, quarter, 768, 1024)).astype(BF)


def unmix(grad, pieces):
    out = jax.ShapeDtypeStruct((grad.shape[0], 256), BF)
    return call_once(unmix_kernel, "unmix", [out, out], [grad, *pieces], 4)


def unproject_term(grad_refs, weight_refs, first):
    rows = jnp.concatenate(
        [ref[part, first:first + 512] for pair in grad_refs for part in range(3) for ref in pair], axis=1
    )
    weight = jnp.concatenate([head_columns(weight_refs, quarter, 0, 768) for quarter in range(2)], axis=1)
    return dot_nt(rows, weight)


def unproject_far_kernel(*rest):
    rest[6][...] = unproject_term((rest[0:2], rest[2:4]), rest[4:6], 512).astype(BF)


def unproject_far(mine, other, pieces):
    out = jax.ShapeDtypeStruct((512, 1024), BF)
    return call_once(unproject_far_kernel, "unproject_far", [out], [*mine, *other, *pieces], 6)[0]


def unproject_near_kernel(last, own_ref, *rest):
    mine, other, rest = rest[0:2], rest[2:4], rest[4:]
    far_ref, resid_ref, grad_mid_ref, vector_ref, rest = *rest[:4], rest[4:]
    weight_refs, (grad_ref, low_ref, sums_ref) = rest[:2], rest[2:]
    term = unproject_term((mine, other), weight_refs, 0) + far_ref[...].astype(F32)
    grad_norm, grad_gain, grad_shift = norm_pull(resid_ref[...], vector_ref[0:1], term)
    grad = grad_mid_ref[...] + grad_norm
    grad_ref[...] = grad
    if last:
        put_turned(low_ref, own_ref[0], grad.astype(BF))
    else:
        low_ref[...] = flipped(grad).astype(BF)
    sums_ref[...] = jnp.concatenate([grad_gain, grad_shift, jnp.zeros((6, grad.shape[1]), F32)], axis=0)


def unproject_near(last, own_keep, mine, other, far, resid, grad_mid, vectors, pieces):
    outs = [
        jax.ShapeDtypeStruct(resid.shape, F32),
        jax.ShapeDtypeStruct(resid.shape, BF),
        jax.ShapeDtypeStruct((8, resid.shape[1]), F32),
    ]
    args = [own_keep, *mine, *other, far, resid, grad_mid, vectors, *pieces]
    kernel = functools.partial(unproject_near_kernel, last)
    return call_once(kernel, "unproject_near", outs, args, 9, scalars=1)


def head_grads_kernel(near_ref, far_ref, grad_near_ref, grad_far_ref, *rest):
    pairs, rest = (rest[0:2], rest[2:4]), rest[4:]
    mixed_refs, out_refs, bias_ref = (rest[0:2], rest[2:4]), rest[4:6], rest[6]
    rows_t = jnp.concatenate([near_ref[...], far_ref[...]], axis=0).T
    grad_t = jnp.concatenate([grad_near_ref[...], grad_far_ref[...]], axis=0).T
    for quarter, refs in enumerate(pairs):
        grads = [jnp.concatenate([ref[part] for ref in refs], axis=1) for part in range(3)]
        for part in range(4):
            if part < 3:
                term = dot_nn(rows_t, grads[part])
            else:
                term = dot_nn(grad_t, jnp.concatenate([m[...] for m in mixed_refs[quarter]], axis=0))
            term = term.astype(BF)
            for index in range(8):
                chip, odd = index // 2, index % 2
                place = 1 - quarter if odd else quarter
                out_refs[odd][chip, place, :, part * 256:(part + 1) * 256] = term[index * 128:(index + 1) * 128]
        for row, part in ((0, 0), (1, 2)):
            total = jnp.sum(grads[part].astype(F32), axis=0, keepdims=True)
            bias_ref[2 * quarter + row:2 * quarter + row + 1, :] = total
    bias_ref[4:8, :] = jnp.zeros((4, 256), F32)


def head_grads(near, far, grad_near, grad_far, mine, other, mixed_mine, mixed_other):
    outs = [jax.ShapeDtypeStruct((4, 2, 128, 1024), BF)] * 2 + [jax.ShapeDtypeStruct((8, 256), F32)]
    args = [near, far, grad_near, grad_far, *mine, *other, *mixed_mine, *mixed_other]
    return call_once(head_grads_kernel, "head_grads", outs, args, 10)


GELU_A = 0.7978845608028654
GELU_B = 0.044715


def normalize(values):
    centred = values - jnp.mean(values, axis=-1, keepdims=True)
    spread = lax.rsqrt(jnp.mean(centred * centred, axis=-1, keepdims=True) + NORM_EPS)
    return centred * spread, spread


def norm_pull(values, gain, grad):
    unit, spread = normalize(values)
    grad_unit = grad * gain
    inner = grad_unit - jnp.mean(grad_unit, axis=-1, keepdims=True)
    inner = inner - unit * jnp.mean(grad_unit * unit, axis=-1, keepdims=True)
    return spread * inner, jnp.sum(grad * unit, axis=0, keepdims=True), jnp.sum(grad, axis=0, keepdims=True)


def joined(refs, first, last):
    return jnp.concatenate([ref[0, :, first:last] for ref in refs], axis=0)


def flipped(values):
    return jnp.concatenate([values[:, (block ^ 1) * 128:(block ^ 1) * 128 + 128] for block in range(8)], axis=1)


def put_turned(out_ref, own, values):
    for block in range(8):
        here = pl.ds(pl.multiple_of((block ^ own) * 128, 128), 128)
        out_ref[:, here] = values[:, block * 128:(block + 1) * 128]


def enter_kernel(own_ref, direct_ref, moved_ref, vector_ref, resid_ref, normed_ref, flip_ref):
    own, keep = own_ref[0], own_ref[1]
    for block in range(8):
        here = pl.ds(pl.multiple_of((block ^ own) * 128, 128), 128)
        rows = jnp.where(keep > 0, direct_ref[:, here].astype(F32), moved_ref[:, here].astype(F32))
        resid_ref[:, block * 128:(block + 1) * 128] = rows
    values = resid_ref[...]
    normed_ref[...] = (normalize(values)[0] * vector_ref[0:1] + vector_ref[1:2]).astype(BF)
    flip_ref[...] = flipped(values).astype(BF)


def enter(own_keep, direct, moved, vectors):
    rows, features = direct.shape
    smem = pl.BlockSpec(memory_space=pltpu.SMEM)
    vmem = pl.BlockSpec(memory_space=pltpu.VMEM)
    return pl.pallas_call(
        enter_kernel,
        in_specs=[smem, vmem, vmem, vmem],
        out_specs=[vmem, vmem, vmem],
        out_shape=[
            jax.ShapeDtypeStruct((rows, features), F32),
            jax.ShapeDtypeStruct((rows, features), BF),
            jax.ShapeDtypeStruct((rows, features), BF),
        ],
        compiler_params=pltpu.CompilerParams(vmem_limit_bytes=VMEM_LIMIT),
        cost_estimate=took(4),
        name="enter",
    )(own_keep, direct, moved, vectors)


def half_specs(tile):
    def spec(half):
        return pl.BlockSpec((2, 128, 2 * tile), lambda f: (0, 0, jnp.clip(f - 2 * half, 0, 1)))

    return [spec(half) for half in range(2) for _ in range(4)]


def by_half(step, weight_refs, body):
    @pl.when(step < 2)
    def _():
        body(weight_refs[:4])

    @pl.when(step >= 2)
    def _():
        body(weight_refs[4:])


def joined(refs, first, last):
    return jnp.concatenate([ref[core, :, first:last] for ref in refs for core in range(2)], axis=0)


GELU_A = 0.7978845608028654
GELU_B = 0.044715


def normalize(values):
    centred = values - jnp.mean(values, axis=-1, keepdims=True)
    spread = lax.rsqrt(jnp.mean(centred * centred, axis=-1, keepdims=True) + NORM_EPS)
    return centred * spread, spread


def norm_pull(values, gain, grad):
    unit, spread = normalize(values)
    grad_unit = grad * gain
    inner = grad_unit - jnp.mean(grad_unit, axis=-1, keepdims=True)
    inner = inner - unit * jnp.mean(grad_unit * unit, axis=-1, keepdims=True)
    return spread * inner, jnp.sum(grad * unit, axis=0, keepdims=True), jnp.sum(grad, axis=0, keepdims=True)


def mlp_kernel(normed_ref, other_ref, bias_ref, *rest):
    weight_refs, (hidden_ref, active_ref, near_ref, away_ref, acc_ref) = rest[:8], rest[8:]
    rows, tile = normed_ref.shape[0], hidden_ref.shape[1]
    step = pl.program_id(0)

    @pl.when(step == 0)
    def _():
        acc_ref[...] = jnp.zeros_like(acc_ref)

    def body(refs):
        expand, reduce = joined(refs, 0, tile), joined(refs, tile, 2 * tile)
        for first, ref in ((0, normed_ref), (rows, other_ref)):
            hidden = dot_nn(ref[...], expand) + bias_ref[...]
            inner = jnp.tanh(GELU_A * (hidden + GELU_B * hidden * hidden * hidden))
            active = (0.5 * hidden * (1.0 + inner)).astype(BF)
            hidden_ref[first:first + rows] = hidden.astype(BF)
            active_ref[first:first + rows] = active
            acc_ref[first:first + rows] += dot_nt(active, reduce)

    by_half(step, weight_refs, body)

    @pl.when(step == pl.num_programs(0) - 1)
    def _():
        near_ref[...] = acc_ref[:rows]
        away_ref[...] = flipped(acc_ref[rows:]).astype(BF)


def mlp_forward(normed, other, bias, weights):
    rows, features = normed.shape
    units = bias.shape[1]
    tile = 512
    whole = pl.BlockSpec((rows, features), lambda f: (0, 0))
    tiles = pl.BlockSpec((2 * rows, tile), lambda f: (0, f))
    return pl.pallas_call(
        mlp_kernel,
        grid=(units // tile,),
        in_specs=[whole, whole, pl.BlockSpec((1, tile), lambda f: (0, f))] + half_specs(tile),
        out_specs=[tiles, tiles, whole, whole],
        out_shape=[
            jax.ShapeDtypeStruct((2 * rows, units), BF),
            jax.ShapeDtypeStruct((2 * rows, units), BF),
            jax.ShapeDtypeStruct((rows, features), F32),
            jax.ShapeDtypeStruct((rows, features), BF),
        ],
        scratch_shapes=[pltpu.VMEM((2 * rows, features), F32)],
        compiler_params=pltpu.CompilerParams(vmem_limit_bytes=VMEM_LIMIT),
        cost_estimate=took(18),
        name="mlp_forward",
    )(normed, other, bias, *weights)


def mlp_close_kernel(last, own_ref, near_ref, got_ref, mid_ref, vector_ref, out_ref, next_ref):
    out = mid_ref[...] + (near_ref[...] + got_ref[...].astype(F32) + vector_ref[5:6])
    out_ref[...] = out
    if last:
        put_turned(next_ref, own_ref[0], out.astype(BF))
    else:
        next_ref[...] = (normalize(out)[0] * vector_ref[6:7] + vector_ref[7:8]).astype(BF)


def mlp_close(last, own_keep, near, got, mid, vectors):
    outs = [jax.ShapeDtypeStruct(mid.shape, F32), jax.ShapeDtypeStruct(mid.shape, BF)]
    args = [own_keep, near, got, mid, vectors]
    return call_once(functools.partial(mlp_close_kernel, last), "mlp_close", outs, args, 3, scalars=1)


def mlp_pull_kernel(grad_ref, other_ref, hidden_ref, *rest):
    weight_refs = rest[:8]
    grad_hidden_ref, grad_bias_ref, near_ref, away_ref, acc_ref, low_ref = rest[8:]
    rows, tile = grad_ref.shape[0], hidden_ref.shape[1]
    step = pl.program_id(0)

    @pl.when(step == 0)
    def _():
        low_ref[:rows] = grad_ref[...].astype(BF)
        low_ref[rows:] = other_ref[...]
        acc_ref[...] = jnp.zeros_like(acc_ref)

    def body(refs):
        expand, reduce = joined(refs, 0, tile), joined(refs, tile, 2 * tile)
        total = jnp.zeros((1, tile), F32)
        for first in (0, rows):
            here = slice(first, first + rows)
            hidden = hidden_ref[here].astype(F32)
            squared = hidden * hidden
            inner = jnp.tanh(GELU_A * hidden * (1.0 + GELU_B * squared))
            slope = 0.5 * (1.0 + inner) + 0.5 * hidden * (1.0 - inner * inner) * (GELU_A * (1.0 + 3.0 * GELU_B * squared))
            grad_hidden = dot_nn(low_ref[here], reduce) * slope
            total = total + jnp.sum(grad_hidden, axis=0, keepdims=True)
            grad_hidden = grad_hidden.astype(BF)
            grad_hidden_ref[here] = grad_hidden
            acc_ref[here] += dot_nt(grad_hidden, expand)
        grad_bias_ref[...] = total

    by_half(step, weight_refs, body)

    @pl.when(step == pl.num_programs(0) - 1)
    def _():
        near_ref[...] = acc_ref[:rows]
        away_ref[...] = flipped(acc_ref[rows:]).astype(BF)


def mlp_backward(grad, other, hidden, weights):
    rows, features = grad.shape
    units = hidden.shape[1]
    tile = 512
    whole = pl.BlockSpec((rows, features), lambda f: (0, 0))
    tiles = pl.BlockSpec((2 * rows, tile), lambda f: (0, f))
    return pl.pallas_call(
        mlp_pull_kernel,
        grid=(units // tile,),
        in_specs=[whole, whole, tiles] + half_specs(tile),
        out_specs=[tiles, pl.BlockSpec((1, tile), lambda f: (0, f)), whole, whole],
        out_shape=[
            jax.ShapeDtypeStruct((2 * rows, units), BF),
            jax.ShapeDtypeStruct((1, units), F32),
            jax.ShapeDtypeStruct((rows, features), F32),
            jax.ShapeDtypeStruct((rows, features), BF),
        ],
        scratch_shapes=[pltpu.VMEM((2 * rows, features), F32), pltpu.VMEM((2 * rows, features), BF)],
        compiler_params=pltpu.CompilerParams(vmem_limit_bytes=VMEM_LIMIT),
        cost_estimate=took(22),
        name="mlp_backward",
    )(grad, other, hidden, *weights)


def mlp_open_kernel(near_ref, got_ref, mid_ref, grad_ref, vector_ref, grad_mid_ref, grad_low_ref, sums_ref):
    grad = grad_ref[...]
    term = near_ref[...] + got_ref[...].astype(F32)
    grad_norm, grad_gain, grad_shift = norm_pull(mid_ref[...], vector_ref[3:4], term)
    grad_mid = grad + grad_norm
    grad_mid_ref[...] = grad_mid
    grad_low_ref[...] = grad_mid.astype(BF)
    rows = [jnp.sum(grad_mid, axis=0, keepdims=True), grad_gain, grad_shift, jnp.sum(grad, axis=0, keepdims=True)]
    sums_ref[...] = jnp.concatenate(rows + [jnp.zeros((4, grad.shape[1]), F32)], axis=0)


def mlp_open(near, got, mid, grad, vectors):
    outs = [
        jax.ShapeDtypeStruct(mid.shape, F32),
        jax.ShapeDtypeStruct(mid.shape, BF),
        jax.ShapeDtypeStruct((8, mid.shape[1]), F32),
    ]
    return call_once(mlp_open_kernel, "mlp_open", outs, [near, got, mid, grad, vectors], 5)


def unit_grads_kernel(second, left_ref, other_ref, right_ref, own_ref, pair_ref, single_ref, left_t_ref):
    @pl.when(pl.program_id(0) == 0)
    def _():
        left_t_ref[...] = jnp.concatenate([left_ref[...].astype(BF), other_ref[...]], axis=0).T

    grad = dot_nn(left_t_ref[...], right_ref[...]).astype(BF)
    single, direct = (1, 2) if second == "x" else (2, 1)
    for core in range(2):
        own_ref[0, core] = grad[core * 128:(core + 1) * 128]
        single_ref[0, core] = grad[(2 * single + core) * 128:(2 * single + core + 1) * 128]
        pair_ref[0, 0, core] = grad[(2 * direct + core) * 128:(2 * direct + core + 1) * 128]
        pair_ref[0, 1, core] = grad[(6 + core) * 128:(7 + core) * 128]


def unit_grads(second, left, other, right):
    rows, features = left.shape
    units = right.shape[1]
    tile = 512
    whole = pl.BlockSpec((rows, features), lambda f: (0, 0))
    out = pl.BlockSpec((1, 2, 128, tile), lambda f: (f // 2, 0, 0, f % 2))
    one = jax.ShapeDtypeStruct((2, 2, 128, 1024), BF)
    return pl.pallas_call(
        functools.partial(unit_grads_kernel, second),
        grid=(units // tile,),
        in_specs=[whole, whole, pl.BlockSpec((2 * rows, tile), lambda f: (0, f))],
        out_specs=[out, pl.BlockSpec((1, 2, 2, 128, tile), lambda f: (f // 2, 0, 0, 0, f % 2)), out],
        out_shape=[one, jax.ShapeDtypeStruct((2, 2, 2, 128, 1024), BF), one],
        scratch_shapes=[pltpu.VMEM((features, 2 * rows), BF)],
        compiler_params=pltpu.CompilerParams(vmem_limit_bytes=VMEM_LIMIT),
        cost_estimate=took(10),
        name="unit_grads",
    )(left, other, right)


def fetch_heads(piece, core, out):
    token = yield
    far = swap(after(piece, token), Z1)
    token = yield []
    far = after(far, token)
    own = jnp.stack([jnp.where(core == 0, piece, far), jnp.where(core == 0, far, piece)])
    from_x = swap(own, XBIT)
    from_y = swap(own, YBIT)
    token = yield [own]
    from_x, from_y = after_all((from_x, from_y), token)
    across = swap(from_y, XBIT)
    token = yield [from_x, from_y]
    quads = jnp.stack([own, from_x, from_y, after(across, token)])
    other = swap(quads, CORE)
    token = yield [quads]
    out += [quads, other]


def fetch_units(piece, core, first_out, second_out):
    token = yield
    piece = after(piece, token)
    same, cross = swap_some(piece, (0, Z1)), swap_some(piece, (CORE | Z1, CORE))
    token = yield []
    same, cross = after_all((same, cross), token)
    first = jnp.stack([jnp.where(core == 0, piece, same), cross])
    first_x, first_y = swap(first, XBIT), swap(first, YBIT)
    second = swap(first, Z0)
    token = yield [first]
    first_x, first_y, second = after_all((first_x, first_y, second), token)
    second_x, second_y = swap(second, XBIT), swap(second, YBIT)
    token = yield [first_x, first_y, second]
    second_x, second_y = after_all((second_x, second_y), token)
    first_across, second_across = swap(first_x, YBIT), swap(second_y, XBIT)
    token = yield [second_x, second_y]
    first_across, second_across = after_all((first_across, second_across), token)
    first_out += [first, first_x, first_y, first_across]
    second_out += [second, second_x, second_y, second_across]
    yield [first_across, second_across]


def pack_heads(project, output):
    return jnp.concatenate([project.transpose(1, 0, 2).reshape(128, 768), output.T], axis=1)


def unpack_heads(values):
    return values[:, :768].reshape(128, 3, 256).transpose(1, 0, 2), values[:, 768:].T


def pack_units(expand, reduce):
    parts = (expand.reshape(128, 2, 512), reduce.T.reshape(128, 2, 512))
    return jnp.stack(parts, axis=2).reshape(128, 2048)


def fetch_small(six, project_bias, expand_bias, own, core):
    layers = six.shape[1]
    wide = jnp.pad(project_bias, ((0, 0), (0, 0), (0, 96)))
    rows = jnp.concatenate([six.transpose(1, 0, 2), wide, expand_bias[:, None, :]], axis=1).astype(F32)[None]
    for mask in (CORE, XBIT, YBIT):
        rows = jnp.concatenate([rows, swap(rows, mask)], axis=0)
    vectors = rows[:, :, :6].transpose(1, 2, 0, 3).reshape(layers, 6, 1024)
    local = turn_index(rows[:, :, 6:], own).transpose(1, 2, 0, 3)[None]
    for mask in (Z0, Z1):
        local = jnp.concatenate([local, swap(local, mask)], axis=0)
    native = local.transpose(1, 0, 2, 3, 4)
    out = []
    for layer in range(layers):
        pair = native[layer, ::2, :2, :, :32].reshape(2, 2, 256)
        pair = jnp.where(core == 0, pair, pair[::-1])
        head_bias = jnp.concatenate([pair[:, 0], jnp.zeros((2, 256), F32), pair[:, 1]], axis=1)
        unit_bias = native[layer, :, 2].reshape(2, 1, 2048)
        unit_bias = jnp.where(core == 0, unit_bias[0], unit_bias[1])
        following = vectors[min(layer + 1, layers - 1), :2]
        out.append((jnp.concatenate([vectors[layer], following], axis=0), head_bias, unit_bias))
    return out


def spread_sums(rows):
    rows = rows.reshape(2, 2, 2, rows.shape[1], 128)
    rows = rows[:, :, 0] + swap(rows[:, :, 1], CORE)
    rows = rows[:, 0] + swap(rows[:, 1], XBIT)
    return rows[0] + swap(rows[1], YBIT)


def sum_small(layers, own, core):
    count = len(layers)
    vectors, biases = [], []
    for first_sums, second_sums, unit_sums, head_sums in layers:
        vectors += [first_sums[:2], second_sums[:4]]
        heads = head_sums[:4].reshape(2, 2, 256)
        heads = jnp.where(core == 0, heads, heads[::-1]).reshape(4, 8, 32)
        heads = jnp.pad(heads, ((0, 0), (0, 0), (0, 96)))
        units = unit_sums.reshape(2, 8, 128)
        none = jnp.zeros_like(units)
        biases += [jnp.where(core == 0, units, none), jnp.where(core == 0, none, units), heads]
    vectors = jnp.concatenate(vectors, axis=0).reshape(6 * count, 8, 128).transpose(1, 0, 2)
    biases = turn_index(jnp.concatenate(biases, axis=0).transpose(1, 0, 2), own)
    rows = spread_sums(jnp.concatenate([vectors, biases], axis=1))
    vectors, biases = rows[:6 * count].reshape(count, 6, 128), rows[6 * count:].reshape(count, 8, 128)

    def part(offset):
        return jnp.concatenate([vectors, biases[:, offset:offset + 1], biases[:, 6:8]], axis=1)

    two = swap(part(2), 2)
    whole = jnp.concatenate([vectors, biases[:, :1]], axis=1) + two[:, :7] + swap(part(1), 1)[:, :7] + swap(part(3), 3)[:, :7]
    return whole[:, :6], whole[:, 6], biases[:, 4:6, :32] + two[:, 7:, :32]


def reduce_heads(even, odd, core, out):
    token = yield
    got = swap(odd, CORE)
    token = yield []
    got = after(got, token)
    low, high = even[:2] + got[:2], even[2:] + got[2:]
    from_y = swap(high, YBIT)
    token = yield [low, high]
    from_y = after(from_y, token)
    relayed = low[1] + from_y[1]
    relay = swap(relayed, XBIT)
    token = yield [relayed]
    total = low[0] + from_y[0] + after(relay, token)
    near = jnp.where(core == 0, total[0], total[1])
    away = jnp.where(core == 0, total[1], total[0])
    far = swap(away, Z1)
    token = yield [near, away]
    out.append(unpack_heads(near.astype(F32) + after(far, token).astype(F32)))


def reduce_units(reduce_parts, expand_parts, core, out):
    yield
    own_r, pair_r, single_r = reduce_parts
    from_y = swap(pair_r, YBIT)
    yield []
    own_e, pair_e, single_e = expand_parts
    from_x = swap(pair_e, XBIT)
    token = yield []
    from_y = after(from_y, token)
    relayed_r = single_r + from_y[:, 1]
    relay_r = swap(relayed_r, XBIT)
    token = yield [relayed_r]
    from_x = after(from_x, token)
    relayed_e = single_e + from_x[:, 1]
    relay_e = swap(relayed_e, YBIT)
    token = yield [relayed_e]
    relay_r, relay_e = after_all((relay_r, relay_e), token)
    here, away = [
        jnp.stack([own_r[i] + from_y[i, 0] + relay_r[i], own_e[i] + from_x[i, 0] + relay_e[i]]) for i in range(2)
    ]
    got = swap(away, Z0)
    token = yield [here, away]
    here = here + after(got, token)
    same, cross = here[:, 0], here[:, 1]
    same_got, cross_got = swap_some(same, (0, Z1)), swap_some(cross, (CORE, CORE | Z1))
    token = yield [same, cross]
    same_got, cross_got = after_all((same_got, cross_got), token)
    out.append(jnp.where(core == 0, same, same_got).astype(F32) + cross_got.astype(F32))


def fast_device(
    layer_input,
    first_gain,
    first_shift,
    project_weight,
    project_bias,
    output_weight,
    output_bias,
    second_gain,
    second_shift,
    expand_weight,
    expand_bias,
    reduce_weight,
    reduce_bias,
    picture_start,
    cotangent,
):
    own = lax.axis_index("dp")
    place = lax.axis_index("tensor")
    core = own & 1
    keep = core == (place >> 1)
    own_keep = jnp.stack([own, keep.astype(jnp.int32)]).astype(jnp.int32)
    me = (2 * core + (place & 1)).astype(jnp.int32).reshape(1)
    slopes = head_slopes((place ^ (2 * core)) * 4, 4)

    six = jnp.stack([first_gain, first_shift, output_bias, second_gain, second_shift, reduce_bias])
    head_piece = [pack_heads(project_weight[i], output_weight[i]) for i in range(LAYERS)]
    unit_piece = [pack_units(expand_weight[i], reduce_weight[i]) for i in range(LAYERS)]
    heads, units = [[] for i in range(LAYERS)], [([], []) for i in range(LAYERS)]
    head_tasks = [task(fetch_heads(head_piece[i], core, heads[i])) for i in range(LAYERS)]
    unit_tasks = [task(fetch_units(unit_piece[i], core, *units[i])) for i in range(LAYERS)]

    advance(layer_input, head_tasks[0])
    small = fetch_small(six, project_bias, expand_bias, own, core)
    dealt = redeal(layer_input)
    starts = jnp.where(keep, picture_start, redeal(picture_start))[0]
    advance(layer_input, unit_tasks[0])
    made = advance(layer_input, head_tasks[0])
    resid, normed, unused = enter(own_keep, layer_input, after(dealt, *made), small[0][0])
    made = advance(normed, head_tasks[0])
    normed = after(normed, *made)
    advance(normed, head_tasks[0])
    saved = []
    for layer in range(LAYERS):
        vectors, head_bias, unit_bias = small[layer]
        first, last = layer == 0, layer + 1 == LAYERS
        far = swap(normed, Z0)
        if not heads[layer]:
            advance(normed, head_tasks[layer])
        pieces = heads[layer]
        near_mine, near_other = project(normed, head_bias, pieces)
        got_near = swap(near_other, CORE)
        made = advance(near_mine, unit_tasks[layer])
        far_mine, far_other = project(after(far, near_mine, *made), head_bias, pieces)
        got_far = swap(far_other, CORE)
        made = []
        if first:
            made += advance(far_mine, head_tasks[1], unit_tasks[1])
        else:
            made += advance(far_mine, unit_tasks[layer])
        blocks = after_all((near_mine, far_mine, got_near, got_far), *made)
        far_mixed, far_send, far_exact, far_log = attend(blocks, 1, slopes, starts, me)
        far_got = swap(far_send, CORE)
        far_part = mix_far(far_mixed, far_got, pieces)
        far_term = swap(far_part, Z0)
        made = advance(far_part, unit_tasks[layer])
        near_blocks = after_all(blocks, far_part, *made)
        near_mixed, near_send, near_exact, near_log = attend(near_blocks, 0, slopes, starts, me)
        near_got = swap(near_send, CORE)
        made = []
        if first:
            made += advance(near_mixed, unit_tasks[0])
        else:
            cotangent_far = redeal(after(cotangent, near_mixed))
        mid, normed_two, flip_two = mix_near(near_mixed, near_got, after(far_term, near_mixed, *made), resid, vectors, pieces)
        normed_other = swap(flip_two, CORE)
        if first:
            made = advance(mid, unit_tasks[0], head_tasks[1], unit_tasks[1])
            normed_two = after(normed_two, *made)
        hidden, active, near_out, away_out = mlp_forward(normed_two, normed_other, unit_bias, units[layer][0] + units[layer][1])
        got_out = swap(away_out, CORE)
        if not last:
            made = advance(near_out, head_tasks[layer + 1])
            got_out = after(got_out, *made)
        out, following = mlp_close(last, own_keep, near_out, got_out, mid, vectors)
        if not last:
            advance(out, head_tasks[layer + 1])
        else:
            grad, unused, flip_grad = enter(own_keep, cotangent, after(cotangent_far, out), vectors)
            grad_other = swap(flip_grad, CORE)
        saved.append((
            resid, normed, far, blocks, (near_exact, far_exact), (near_log, far_log), (near_mixed, far_mixed),
            (near_got, far_got), mid, normed_two, normed_other, hidden, active,
        ))
        resid, normed = out, following
    layer_output = jnp.where(keep, normed, redeal(normed))
    sums = [None] * LAYERS
    head_grad, unit_grad = ([[] for i in range(LAYERS)] for j in range(2))
    pending = []
    for layer in reversed(range(LAYERS)):
        vectors, pieces = small[layer][0], heads[layer]
        (
            resid, normed, far, blocks, exacts, logs, mixed, mixed_got, mid, normed_two, normed_other, hidden, active,
        ) = saved[layer]
        grad_hidden, unit_sums, near_term, away_term = mlp_backward(grad, grad_other, hidden, units[layer][0] + units[layer][1])
        got_term = after(swap(away_term, CORE), *advance(near_term, *pending[:1]))
        grad_mid, grad_low, second_sums = mlp_open(near_term, got_term, mid, grad, vectors)
        grad_far = swap(grad_low, Z0)
        made = advance(grad_low, *pending[1:])
        reduce_parts = unit_grads("x", grad, grad_other, after(active, grad_low, *made))
        near_mine, near_other = unmix(after(grad_low, reduce_parts[0]), pieces)
        got_near = swap(near_other, CORE)
        expand_parts = unit_grads("y", normed_two, normed_other, after(grad_hidden, near_mine))
        unit_task = task(reduce_units(reduce_parts, expand_parts, core, unit_grad[layer]))
        advance(None, unit_task)
        advance(None, unit_task)
        far_mine, far_other = unmix(after(grad_far, expand_parts[0]), pieces)
        got_far = swap(far_other, CORE)
        made = advance(far_mine, *pending)
        grads_mixed = after_all((near_mine, far_mine, got_near, got_far), *made)
        mine_0, away_0 = attend_pull(0, blocks, grads_mixed, exacts, logs, slopes, starts, me)
        other_0 = swap(away_0, CORE)
        made = advance(mine_0, unit_task, *pending)
        grads_mixed = after_all(grads_mixed, mine_0, *made)
        mine_1, away_1 = attend_pull(1, blocks, grads_mixed, exacts, logs, slopes, starts, me)
        other_1 = swap(away_1, CORE)
        other_1 = after(other_1, *advance(mine_1, unit_task))
        mine, other = (mine_0, mine_1), (other_0, other_1)
        far_part = unproject_far(mine, other, pieces)
        far_term = swap(far_part, Z0)
        even, odd, head_sums = head_grads(normed, far, grad_low, after(grad_far, far_part), mine, other, mixed, mixed_got)
        head_task = task(reduce_heads(even, odd, core, head_grad[layer]))
        advance(None, head_task)
        made = advance(head_sums, unit_task) if layer == 0 else [head_sums]
        grad, grad_low, first_sums = unproject_near(
            layer == 0, own_keep, mine, other, after(far_term, *made), resid, grad_mid, vectors, pieces
        )
        sums[layer] = (first_sums, second_sums, unit_sums, head_sums)
        if layer > 0:
            grad_other = swap(grad_low, CORE)
            grad = after(grad, *advance(grad, head_task))
        pending = [unit_task, head_task]
    input_far = redeal(grad_low)
    sums = after_all([row for layer in sums for row in layer], grad)
    while len(head_grad[0]) + len(unit_grad[0]) < 2:
        made = advance(grad, *pending)
    input_grad = jnp.where(keep, grad_low, input_far)
    six, unit_sum, head_sum = sum_small([sums[4 * i:4 * i + 4] for i in range(LAYERS)], own, core)
    return (
        layer_output,
        input_grad,
        six[:, 0],
        six[:, 1],
        jnp.stack([g[0][0] for g in head_grad]),
        head_sum,
        jnp.stack([g[0][1] for g in head_grad]),
        six[:, 2],
        six[:, 3],
        six[:, 4],
        jnp.stack([g[0][1] for g in unit_grad]),
        unit_sum,
        jnp.stack([g[0][0].T for g in unit_grad]),
        six[:, 5],
    )


def solution(mesh):
    placed = (
        P(("dp", "tensor"), None),
        P(None, "dp"),
        P(None, "dp"),
        P(None, None, "dp", "tensor"),
        P(None, None, ("tensor", "dp")),
        P(None, "tensor", "dp"),
        P(None, "dp"),
        P(None, "dp"),
        P(None, "dp"),
        P(None, "dp", "tensor"),
        P(None, ("tensor", "dp")),
        P(None, "tensor", "dp"),
        P(None, "dp"),
        P("dp", None),
        P(("dp", "tensor"), None),
    )
    return jax.shard_map(
        fast_device if mesh_is_paired(mesh) else on_device,
        mesh=mesh,
        in_specs=placed,
        out_specs=(
            P(("dp", "tensor"), None),
            P(("dp", "tensor"), None),
            P(None, "dp"),
            P(None, "dp"),
            P(None, None, "dp", "tensor"),
            P(None, None, ("tensor", "dp")),
            P(None, "tensor", "dp"),
            P(None, "dp"),
            P(None, "dp"),
            P(None, "dp"),
            P(None, "dp", "tensor"),
            P(None, ("tensor", "dp")),
            P(None, "tensor", "dp"),
            P(None, "dp"),
        ),
        check_vma=False,
    )
```

```python
import functools

import jax
import jax.numpy as jnp
from jax import lax
from jax.experimental import pallas as pl
from jax.experimental.pallas import tpu as pltpu
from jax.sharding import PartitionSpec as P

HEADS = 16
HD = 64
LAYERS = 2
SEQ_LEN = 2048
PIECE = 256


NORM_EPS = 1e-05


def layer_norm(values, gain, shift):
    centred = values - jnp.mean(values, axis=-1, keepdims=True)
    spread = jnp.mean(centred * centred, axis=-1, keepdims=True)
    return centred * lax.rsqrt(spread + NORM_EPS) * gain + shift


def gelu_tanh(values):
    return jax.nn.gelu(values, approximate=True)


def piece_numbers(starts):
    places = jnp.arange(SEQ_LEN, dtype=jnp.int32)
    inside = (places[:, None] >= starts[None, :]) & (places[:, None] < starts[None, :] + PIECE)
    numbers = jnp.arange(1, starts.shape[0] + 1, dtype=jnp.int32)
    return jnp.sum(jnp.where(inside, numbers[None, :], 0), axis=1)


def head_slopes(first_head, count_heads):
    heads_at = (first_head + jnp.arange(count_heads, dtype=jnp.int32)).astype(jnp.float32)
    return jnp.exp2(-8.0 * (heads_at + 1.0) / HEADS)


def gather_rows(values):
    return lax.all_gather(values, "tensor", axis=0, tiled=True)


def gather_grads(values):
    return lax.all_gather(values, "tensor", axis=0, tiled=True)


def scatter_rows(values, weight):
    rows_here = values.shape[0] // lax.axis_size("tensor")

    def partial_term(offset, count_rows):
        return jnp.dot(values, weight, preferred_element_type=jnp.float32)

    return lax.psum_scatter(
        partial_term(jnp.int32(0), rows_here * lax.axis_size("tensor")).astype(jnp.bfloat16),
        "tensor",
        scatter_dimension=0,
        tiled=True,
    ).astype(jnp.float32)


def scatter_back(partial_term, rows_here):
    return lax.psum_scatter(
        partial_term(jnp.int32(0), rows_here * lax.axis_size("tensor")).astype(jnp.bfloat16),
        "tensor",
        scatter_dimension=0,
        tiled=True,
    ).astype(jnp.float32)


def block_scores(query_block, key_rows, offset, piece_ids, slopes):
    length = key_rows.shape[0]
    count_rows = query_block.shape[0]
    query_places = offset + jnp.arange(count_rows, dtype=jnp.int32)
    key_places = jnp.arange(length, dtype=jnp.int32)
    product = jnp.einsum("qhe,khe->hqk", query_block, key_rows, preferred_element_type=jnp.float32)
    distance = jnp.abs(query_places[:, None] - key_places[None, :]).astype(jnp.float32)
    scores = product * HD ** (-0.5) - slopes[:, None, None] * distance[None]
    query_pieces = lax.dynamic_slice_in_dim(piece_ids, offset, count_rows, 0)
    allowed = (key_places[None, :] <= query_places[:, None]) | (
        query_pieces[:, None] == piece_ids[None, :]
    ) & (query_pieces[:, None] > 0)
    return jnp.where(allowed[None], scores, -jnp.inf)


def sequence_forward(operands, slopes):
    queries, key_rows, value_rows, piece_ids = operands
    length = queries.shape[0]
    block_rows = min(512, length)

    def one_block(block_index):
        offset = block_index * block_rows
        query_block = lax.dynamic_slice_in_dim(queries, offset, block_rows, 0)
        scores = block_scores(query_block, key_rows, offset, piece_ids, slopes)
        row_max = jnp.max(scores, axis=-1, keepdims=True)
        raw_weights = jnp.exp(scores - row_max)
        totals = jnp.sum(raw_weights, axis=-1, keepdims=True)
        soft_weights = (raw_weights / totals).astype(jnp.bfloat16)
        attended = jnp.einsum(
            "hqk,khe->qhe", soft_weights, value_rows, preferred_element_type=jnp.float32
        )
        return (attended.astype(jnp.bfloat16), (row_max + jnp.log(totals))[..., 0])

    attended, log_total = lax.map(one_block, jnp.arange(length // block_rows, dtype=jnp.int32))
    return (attended.reshape(length, queries.shape[1], queries.shape[2]), log_total)


def sequence_backward(operands, slopes):
    queries, key_rows, value_rows, piece_ids, grad_mixed, log_total = operands
    length = queries.shape[0]
    block_rows = min(512, length)

    def one_block(carry, block_index):
        key_grad, value_grad = carry
        offset = block_index * block_rows
        query_block = lax.dynamic_slice_in_dim(queries, offset, block_rows, 0)
        grad_block = lax.dynamic_slice_in_dim(grad_mixed, offset, block_rows, 0)
        scores = block_scores(query_block, key_rows, offset, piece_ids, slopes)
        probs = jnp.exp(scores - log_total[block_index][..., None])
        soft_weights = probs.astype(jnp.bfloat16)
        value_grad = value_grad + jnp.einsum(
            "hqk,qhe->khe", soft_weights, grad_block, preferred_element_type=jnp.float32
        )
        prob_grad = jnp.einsum(
            "qhe,khe->hqk", grad_block, value_rows, preferred_element_type=jnp.float32
        )
        centred = jnp.sum(probs * prob_grad, axis=-1, keepdims=True)
        score_grad = (probs * (prob_grad - centred) * HD ** (-0.5)).astype(jnp.bfloat16)
        query_grad = jnp.einsum(
            "hqk,khe->qhe", score_grad, key_rows, preferred_element_type=jnp.float32
        )
        key_grad = key_grad + jnp.einsum(
            "hqk,qhe->khe", score_grad, query_block, preferred_element_type=jnp.float32
        )
        return ((key_grad, value_grad), query_grad)

    empty = jnp.zeros(queries.shape, jnp.float32)
    (key_grad, value_grad), query_grad = lax.scan(
        one_block, (empty, empty), jnp.arange(length // block_rows, dtype=jnp.int32)
    )
    return (query_grad.reshape(queries.shape), key_grad, value_grad)


def attend_forward(triple, piece_ids, slopes):
    width = triple.shape[2]
    count_seq = piece_ids.shape[0]
    length = piece_ids.shape[1]
    shaped = triple.reshape(3, count_seq, length, width // HD, HD)
    attended, log_total = lax.map(
        lambda operands: sequence_forward(operands, slopes),
        (shaped[0], shaped[1], shaped[2], piece_ids),
    )
    return (attended.reshape(count_seq * length, width), log_total)


def attend_backward(triple, grad_attended, log_total, piece_ids, slopes):
    width = triple.shape[2]
    count_seq = piece_ids.shape[0]
    length = piece_ids.shape[1]
    shaped = triple.reshape(3, count_seq, length, width // HD, HD)
    grad_shaped = grad_attended.reshape(count_seq, length, width // HD, HD)
    query_grad, key_grad, value_grad = lax.map(
        lambda operands: sequence_backward(operands, slopes),
        (shaped[0], shaped[1], shaped[2], piece_ids, grad_shaped, log_total),
    )
    return (
        query_grad.reshape(-1, width),
        key_grad.reshape(-1, width),
        value_grad.reshape(-1, width),
    )


def fetch_layer(
    project_weight,
    project_bias,
    output_weight,
    expand_weight,
    expand_bias,
    reduce_weight,
    small_stack,
    layer_index,
):
    return (
        lax.all_gather(project_weight[layer_index], "dp", axis=1, tiled=True),
        lax.all_gather(project_bias[layer_index], "dp", axis=1, tiled=True),
        lax.all_gather(output_weight[layer_index], "dp", axis=1, tiled=True),
        lax.all_gather(expand_weight[layer_index], "dp", axis=0, tiled=True),
        lax.all_gather(expand_bias[layer_index], "dp", axis=0, tiled=True),
        lax.all_gather(reduce_weight[layer_index], "dp", axis=1, tiled=True),
        lax.all_gather(small_stack[layer_index], "dp", axis=1, tiled=True),
    )


def forward_layer(resid, weights, piece_ids, slopes):
    w_project, bias_project, w_output, w_expand, bias_expand, w_reduce, small = weights
    vectors = small.astype(jnp.float32)
    normed = layer_norm(resid, vectors[0], vectors[1])
    gathered = gather_rows(normed.astype(jnp.bfloat16))
    product = jnp.einsum("gd,cde->cge", gathered, w_project, preferred_element_type=jnp.float32)
    biases = jnp.stack([bias_project[0], jnp.zeros_like(bias_project[0]), bias_project[1]]).astype(
        jnp.float32
    )
    triple = (product + biases[:, None, :]).astype(jnp.bfloat16)
    attended, log_total = attend_forward(triple, piece_ids, slopes)
    resid_mid = resid + (scatter_rows(attended, w_output) + vectors[2])
    normed_two = layer_norm(resid_mid, vectors[3], vectors[4])
    gathered_two = gather_rows(normed_two.astype(jnp.bfloat16))
    hidden = jnp.dot(
        gathered_two, w_expand, preferred_element_type=jnp.float32
    ) + bias_expand.astype(jnp.float32)
    active = gelu_tanh(hidden).astype(jnp.bfloat16)
    mlp_sum = scatter_rows(active, w_reduce)
    mlp_keep = (gathered_two, hidden, None)
    resid_out = resid_mid + (mlp_sum + vectors[5])
    return (resid_out, (gathered, triple, attended, log_total, resid_mid, mlp_keep))


def backward_layer(grad_out, resid, weights, kept, piece_ids, slopes):
    w_project, bias_project, w_output, w_expand, bias_expand, w_reduce, small = weights
    vectors = small.astype(jnp.float32)
    gathered, triple, attended, log_total, resid_mid, mlp_keep = kept
    rows_here = grad_out.shape[0]
    rows_in, hidden, full_weights = mlp_keep
    grad_bias_reduce = jnp.sum(grad_out, axis=0)
    active, gelu_pull = jax.vjp(gelu_tanh, hidden)
    active_low = active.astype(jnp.bfloat16)
    grad_mlp = gather_grads(grad_out.astype(jnp.bfloat16))
    grad_reduce = jnp.einsum("gf,gd->fd", active_low, grad_mlp, preferred_element_type=jnp.float32)
    grad_active = jnp.einsum("gd,fd->gf", grad_mlp, w_reduce, preferred_element_type=jnp.float32)
    (grad_hidden,) = gelu_pull(grad_active)
    grad_bias_expand = jnp.sum(grad_hidden, axis=0)
    grad_hidden_low = grad_hidden.astype(jnp.bfloat16)
    grad_expand = jnp.einsum(
        "gd,gf->df", rows_in, grad_hidden_low, preferred_element_type=jnp.float32
    )

    def expand_term(offset, count_rows):
        return jnp.einsum(
            "gf,df->gd", grad_hidden_low, w_expand, preferred_element_type=jnp.float32
        )

    grad_normed_two = scatter_back(expand_term, rows_here)
    unused_two, second_pull = jax.vjp(layer_norm, resid_mid, vectors[3], vectors[4])
    grad_from_norm, grad_gain_two, grad_shift_two = second_pull(grad_normed_two)
    grad_mid = grad_out + grad_from_norm
    grad_bias_output = jnp.sum(grad_mid, axis=0)
    grad_attn = gather_grads(grad_mid.astype(jnp.bfloat16))
    grad_output = jnp.einsum("gt,gd->td", attended, grad_attn, preferred_element_type=jnp.float32)
    grad_attended = jnp.einsum(
        "gd,td->gt", grad_attn, w_output, preferred_element_type=jnp.float32
    ).astype(jnp.bfloat16)
    query_grad, key_grad, value_grad = attend_backward(
        triple, grad_attended, log_total, piece_ids, slopes
    )
    grad_bias_project = jnp.stack([jnp.sum(query_grad, axis=0), jnp.sum(value_grad, axis=0)])
    grad_triple = jnp.stack([query_grad, key_grad, value_grad]).astype(jnp.bfloat16)
    grad_project = jnp.einsum(
        "gd,cge->cde", gathered, grad_triple, preferred_element_type=jnp.float32
    )

    def project_term(offset, count_rows):
        return jnp.einsum("cge,cde->gd", grad_triple, w_project, preferred_element_type=jnp.float32)

    grad_normed = scatter_back(project_term, rows_here)
    unused_one, first_pull = jax.vjp(layer_norm, resid, vectors[0], vectors[1])
    grad_from_first, grad_gain_one, grad_shift_one = first_pull(grad_normed)
    grad_stream = grad_mid + grad_from_first
    small_grads = jnp.stack(
        [
            grad_gain_one,
            grad_shift_one,
            grad_bias_output,
            grad_gain_two,
            grad_shift_two,
            grad_bias_reduce,
        ]
    )
    return (
        grad_stream,
        (
            grad_project,
            grad_bias_project,
            grad_output,
            grad_expand,
            grad_bias_expand,
            grad_reduce,
            small_grads,
        ),
    )


def reduce_layer(layer_grads):
    (
        grad_project,
        grad_bias_project,
        grad_output,
        grad_expand,
        grad_bias_expand,
        grad_reduce,
        small_grads,
    ) = layer_grads
    return (
        lax.psum_scatter(
            grad_project.astype(jnp.bfloat16), "dp", scatter_dimension=1, tiled=True
        ).astype(jnp.float32),
        lax.psum_scatter(
            grad_bias_project.astype(jnp.bfloat16), "dp", scatter_dimension=1, tiled=True
        ).astype(jnp.float32),
        lax.psum_scatter(
            grad_output.astype(jnp.bfloat16), "dp", scatter_dimension=1, tiled=True
        ).astype(jnp.float32),
        lax.psum_scatter(
            grad_expand.astype(jnp.bfloat16), "dp", scatter_dimension=0, tiled=True
        ).astype(jnp.float32),
        lax.psum_scatter(
            grad_bias_expand.astype(jnp.bfloat16), "dp", scatter_dimension=0, tiled=True
        ).astype(jnp.float32),
        lax.psum_scatter(
            grad_reduce.astype(jnp.bfloat16), "dp", scatter_dimension=1, tiled=True
        ).astype(jnp.float32),
        lax.psum_scatter(
            small_grads.astype(jnp.bfloat16), "dp", scatter_dimension=1, tiled=True
        ).astype(jnp.float32),
    )


def on_device(
    layer_input,
    first_gain,
    first_shift,
    project_weight,
    project_bias,
    output_weight,
    output_bias,
    second_gain,
    second_shift,
    expand_weight,
    expand_bias,
    reduce_weight,
    reduce_bias,
    picture_start,
    cotangent,
):
    small_stack = jnp.stack(
        [first_gain, first_shift, output_bias, second_gain, second_shift, reduce_bias], axis=1
    )
    piece_ids = jax.vmap(piece_numbers)(picture_start)
    heads_here = project_weight.shape[3] // HD
    slopes = head_slopes(lax.axis_index("tensor") * heads_here, heads_here)
    resid = layer_input.astype(jnp.float32)
    saved = []
    for layer_index in range(LAYERS):
        weights = fetch_layer(
            project_weight,
            project_bias,
            output_weight,
            expand_weight,
            expand_bias,
            reduce_weight,
            small_stack,
            layer_index,
        )
        resid_next, kept = forward_layer(resid, weights, piece_ids, slopes)
        saved.append((resid, weights, kept))
        resid = resid_next
    layer_output = resid.astype(jnp.bfloat16)
    grad_stream = cotangent.astype(jnp.float32)
    collected = []
    for layer_index in reversed(range(LAYERS)):
        resid_in, weights, kept = saved[layer_index]
        grad_stream, layer_grads = backward_layer(
            grad_stream, resid_in, weights, kept, piece_ids, slopes
        )
        layer_grads = reduce_layer(layer_grads)
        collected.insert(0, layer_grads)
    stacked = tuple(
        (jnp.stack([grad_entry[member] for grad_entry in collected]) for member in range(7))
    )
    (
        grad_project,
        grad_bias_project,
        grad_output,
        grad_expand,
        grad_bias_expand,
        grad_reduce,
        small_grads,
    ) = stacked
    small_grads = lax.psum(small_grads, "tensor")
    return (
        layer_output,
        grad_stream.astype(jnp.bfloat16),
        small_grads[:, 0],
        small_grads[:, 1],
        grad_project,
        grad_bias_project,
        grad_output,
        small_grads[:, 2],
        small_grads[:, 3],
        small_grads[:, 4],
        grad_expand,
        grad_bias_expand,
        grad_reduce,
        small_grads[:, 5],
    )


Z0, Z1, CORE, XBIT, YBIT = 1, 2, 4, 8, 16
AXES = ("dp", "tensor")
NEG = -1e30
BF = jnp.bfloat16
F32 = jnp.float32
VMEM_LIMIT = 56 * 1024 * 1024


def took(us):
    return pl.CostEstimate(flops=int(us * 5e8), bytes_accessed=1, transcendentals=0)


def mesh_is_paired(mesh):
    return dict(mesh.shape) == {"dp": 8, "tensor": 4}


def swap(values, mask):
    return lax.ppermute(values, AXES, [(i, i ^ mask) for i in range(32)])


def swap_some(values, masks):
    pairs = [(i, i ^ masks[(i >> 2) & 1]) for i in range(32)]
    return lax.ppermute(values, AXES, [pair for pair in pairs if pair[0] != pair[1]])


def redeal(values):
    def target(i):
        core, z1 = (i >> 2) & 1, (i >> 1) & 1
        return (i & ~6) | (z1 << 2) | (core << 1)

    return lax.ppermute(values, AXES, [(i, target(i)) for i in range(32) if target(i) != i])


CHIPS = [[0, 2, 4, 6], [1, 3, 5, 7]]


def plane_gather(values):
    return lax.all_gather(values, "dp", axis_index_groups=CHIPS, axis=0, tiled=False)


def plane_scatter(values):
    return lax.psum_scatter(values, "dp", axis_index_groups=CHIPS, scatter_dimension=0, tiled=False)


def turn_index(values, own):
    shape = values.shape
    for bit in range(3):
        values = values.reshape(8 >> (bit + 1), 2, (1 << bit), *shape[1:])
        values = jnp.where((own >> bit) & 1, jnp.concatenate([values[:, 1:], values[:, :1]], axis=1), values)
    return values.reshape(shape)


def after(values, *others):
    return lax.optimization_barrier((values, *others))[0]


def after_all(values, *others):
    if not others:
        return tuple(values)
    return lax.optimization_barrier((*values, *others))[:len(values)]


def task(steps):
    next(steps)
    return steps


def advance(token, *tasks):
    made = []
    for steps in tasks:
        try:
            made += steps.send(token)
        except StopIteration:
            pass
    return made


def dot_nt(a, b):
    return lax.dot_general(a, b, (((1,), (1,)), ((), ())), preferred_element_type=F32)


def dot_nn(a, b):
    return lax.dot_general(a, b, (((1,), (0,)), ((), ())), preferred_element_type=F32)


def head_mask(shape, head):
    lane = lax.broadcasted_iota(jnp.int32, shape, 1)
    return (lane < HD) if head == 0 else (lane >= HD)


def diagonal_bias(rows, columns, first_row, first_column, start):
    key = first_row + lax.broadcasted_iota(jnp.int32, (rows, 1), 0)
    query = first_column + lax.broadcasted_iota(jnp.int32, (1, columns), 1)
    key_in = (key >= start) & (key < start + PIECE)
    query_in = (query >= start) & (query < start + PIECE)
    allowed = (key <= query) | (key_in & query_in)
    reach = (jnp.minimum(key, 2 * query - key) - first_column).astype(F32)
    return jnp.where(allowed, reach, NEG)


def ramp(rows, first_row, first_column):
    return (first_row - first_column + lax.broadcasted_iota(jnp.int32, (rows, 1), 0)).astype(F32)


def attend_kernel(block, rest_bit, slope_ref, start_ref, me_ref, *rest):
    triple_refs, rest = rest[:12], rest[12:]
    near_ref, away_ref, exact_ref, lse_ref, q_ref, k_ref, v_ref, vt_ref, acc_ref, max_ref, bias_ref, tail_ref = rest
    pair = pl.program_id(0)
    turn = pl.program_id(1)
    me = me_ref[0]
    step = (2 * turn + rest_bit) ^ me
    length = k_ref.shape[0]
    first = step * block

    def at(index):
        return pl.multiple_of((index ^ me) * block, block)

    start = start_ref[first // (length // start_ref.shape[0])]

    @pl.when(turn == 0)
    def _():
        for index in range(4):
            here = slice(index * block, (index + 1) * block)
            q_ref[here, :] = triple_refs[3 * index][...] * jnp.asarray(HD ** -0.5, BF)
            k_ref[here, :] = triple_refs[3 * index + 1][...]
            v_ref[here, :] = triple_refs[3 * index + 2][...]
        for head in range(2):
            mixed = jnp.where(head_mask((length, 2 * HD), head), v_ref[...], jnp.ones((), BF))
            vt_ref[head] = mixed.T

    bias_ref[...] = diagonal_bias(block, block, first, first, start)
    q_block = q_ref[pl.ds(at(step), block), :]
    heads = [jnp.where(head_mask(q_block.shape, head), q_block, jnp.zeros((), BF)) for head in range(2)]
    slopes = [slope_ref[2 * pair + head] for head in range(2)]
    acc_ref[...] = jnp.zeros_like(acc_ref)
    max_ref[...] = jnp.full_like(max_ref, NEG)

    def absorb(head, scores, vt):
        old = max_ref[head]
        new = jnp.maximum(old, jnp.max(scores, axis=0, keepdims=True))
        weights = jnp.exp(scores - new).astype(BF)
        acc_ref[head] = acc_ref[head] * jnp.exp(old - new) + dot_nn(vt, weights)
        max_ref[head] = new

    def full(index, carry):
        place = at(index)
        keys = k_ref[pl.ds(place, block), :]
        slant = ramp(block, index * block, first)
        for head in range(2):
            absorb(head, dot_nt(keys, heads[head]) + slopes[head] * slant, vt_ref[head, :, pl.ds(place, block)])
        return carry

    place = at(step)
    for head in range(2):
        absorb(
            head,
            dot_nt(k_ref[pl.ds(place, block), :], heads[head]) + slopes[head] * bias_ref[...],
            vt_ref[head, :, pl.ds(place, block)],
        )
    lax.fori_loop(0, step, full, 0)
    edge = first + block

    @pl.when((start < edge) & (start + PIECE > edge))
    def _():
        after = at(step + 1)
        tail_ref[...] = diagonal_bias(PIECE, block, edge, first, start)
        for head in range(2):
            absorb(
                head,
                dot_nt(k_ref[pl.ds(after, PIECE), :], heads[head]) + slopes[head] * tail_ref[...],
                vt_ref[head, :, pl.ds(after, PIECE)],
            )

    outs = []
    for head in range(2):
        acc = acc_ref[head]
        total = acc[HD:HD + 1] if head == 0 else acc[0:1]
        outs.append((acc * (1.0 / total))[head * HD:(head + 1) * HD])
        lse_ref[0, head:head + 1, :] = max_ref[head] + jnp.log(total)
    mixed = jnp.concatenate(outs, axis=0)
    exact_ref[...] = mixed
    final = mixed.T.astype(BF)

    @pl.when(turn == 0)
    def _():
        near_ref[...] = final

    @pl.when(turn == 1)
    def _():
        away_ref[...] = final


def triple_specs(block, pairs):
    specs = []
    for index in range(4):
        for part in range(3):
            specs.append(pl.BlockSpec((block, 2 * HD), functools.partial(lambda part, p, i: (0, part * pairs + p), part)))
    return specs


def attend(blocks, rest_bit, slopes, starts, me):
    block, width = blocks[0].shape[0], blocks[0].shape[1] // 3
    pairs = width // (2 * HD)
    length = 4 * block
    smem = pl.BlockSpec(memory_space=pltpu.SMEM)
    return pl.pallas_call(
        functools.partial(attend_kernel, block, rest_bit),
        grid=(pairs, 2),
        in_specs=[smem, smem, smem] + triple_specs(block, pairs),
        out_specs=[
            pl.BlockSpec((block, 2 * HD), lambda p, i: (0, p)),
            pl.BlockSpec((block, 2 * HD), lambda p, i: (0, p)),
            pl.BlockSpec((2 * HD, block), lambda p, i: (p, i)),
            pl.BlockSpec((1, 8, block), lambda p, i: (p, 0, i)),
        ],
        out_shape=[
            jax.ShapeDtypeStruct((block, width), BF),
            jax.ShapeDtypeStruct((block, width), BF),
            jax.ShapeDtypeStruct((width, 2 * block), F32),
            jax.ShapeDtypeStruct((pairs, 8, 2 * block), F32),
        ],
        scratch_shapes=[
            pltpu.VMEM((length, 2 * HD), BF),
            pltpu.VMEM((length, 2 * HD), BF),
            pltpu.VMEM((length, 2 * HD), BF),
            pltpu.VMEM((2, 2 * HD, length), BF),
            pltpu.VMEM((2, 2 * HD, block), F32),
            pltpu.VMEM((2, 1, block), F32),
            pltpu.VMEM((block, block), F32),
            pltpu.VMEM((PIECE, block), F32),
        ],
        compiler_params=pltpu.CompilerParams(vmem_limit_bytes=VMEM_LIMIT),
        cost_estimate=took(17),
        name="attend",
    )(slopes, starts, me, *[b for b in blocks for _ in range(3)])


def pull_kernel(block, pair, slope_ref, start_ref, me_ref, *rest):
    triple_refs, grad_refs, rest = rest[:12], rest[12:16], rest[16:]
    exact_refs, lse_refs, rest = rest[0:2], rest[2:4], rest[4:]
    mine_ref, away_ref, q_ref, k_ref, v_ref, g_ref, kt_ref, dk_acc, dv_acc, dqt_ref, bias_ref, tail_ref = rest
    turn = pl.program_id(0)
    me = me_ref[0]
    step = turn ^ me
    length = k_ref.shape[0]
    first = step * block
    half, bit = turn // 2, turn % 2

    def at(index):
        return pl.multiple_of((index ^ me) * block, block)

    start = start_ref[first // (length // start_ref.shape[0])]

    @pl.when(turn == 0)
    def _():
        for index in range(4):
            here = slice(index * block, (index + 1) * block)
            q_ref[here, :] = triple_refs[3 * index][...] * jnp.asarray(HD ** -0.5, BF)
            k_ref[here, :] = triple_refs[3 * index + 1][...]
            v_ref[here, :] = triple_refs[3 * index + 2][...]
            g_ref[here, :] = grad_refs[index][...]
        kt_ref[...] = k_ref[...].T
        dk_acc[...] = jnp.zeros_like(dk_acc)
        dv_acc[...] = jnp.zeros_like(dv_acc)

    bias_ref[...] = diagonal_bias(block, block, first, first, start)
    dqt_ref[...] = jnp.zeros_like(dqt_ref)
    zero = jnp.zeros((), BF)
    q_block = q_ref[pl.ds(at(step), block), :]
    g_block = g_ref[pl.ds(at(step), block), :]
    masks = [head_mask(q_block.shape, head) for head in range(2)]
    q_heads = [jnp.where(mask, q_block, zero) for mask in masks]
    g_heads = [jnp.where(mask, g_block, zero) for mask in masks]
    slopes = [slope_ref[2 * pair + head] for head in range(2)]
    lanes = pl.ds(pl.multiple_of(half * block, block), block)
    exact = jnp.where(bit == 0, exact_refs[0][:, lanes], exact_refs[1][:, lanes])
    log_total = jnp.where(bit == 0, lse_refs[0][0, :, lanes], lse_refs[1][0, :, lanes])
    product = g_block.astype(F32).T * exact
    deltas = [jnp.sum(product[head * HD:(head + 1) * HD], axis=0, keepdims=True) for head in range(2)]

    def absorb(place, rows, bias_of):
        keys = k_ref[pl.ds(place, rows), :]
        values = v_ref[pl.ds(place, rows), :]
        dk = dk_acc[pl.ds(place, rows), :]
        dv = dv_acc[pl.ds(place, rows), :]
        for head in range(2):
            scores = dot_nt(keys, q_heads[head]) + slopes[head] * bias_of
            weights = jnp.exp(scores - log_total[head:head + 1, :])
            dv = dv + dot_nn(weights.astype(BF), g_heads[head])
            grad_p = dot_nt(values, g_heads[head])
            grad_s = (weights * (grad_p - deltas[head])).astype(BF)
            dk = dk + dot_nn(grad_s, q_heads[head])
            dqt_ref[head * HD:(head + 1) * HD, :] += dot_nn(kt_ref[head * HD:(head + 1) * HD, pl.ds(place, rows)], grad_s)
        dk_acc[pl.ds(place, rows), :] = dk
        dv_acc[pl.ds(place, rows), :] = dv

    absorb(at(step), block, bias_ref[...])

    def full(index, carry):
        absorb(at(index), block, ramp(block, index * block, first))
        return carry

    lax.fori_loop(0, step, full, 0)
    edge = first + block

    @pl.when((start < edge) & (start + PIECE > edge))
    def _():
        tail_ref[...] = diagonal_bias(PIECE, block, edge, first, start)
        absorb(at(step + 1), PIECE, tail_ref[...])

    grad_q = (dqt_ref[...].T * (HD ** -0.5)).astype(BF)
    here = pl.ds(pl.multiple_of(bit * block, block), block)

    @pl.when(half == 0)
    def _():
        mine_ref[0, here, :] = grad_q

    @pl.when(half == 1)
    def _():
        away_ref[0, here, :] = grad_q

    @pl.when(turn == 3)
    def _():
        for part, ref in ((1, dk_acc), (2, dv_acc)):
            mine_ref[part] = ref[:2 * block].astype(BF)
            away_ref[part] = ref[2 * block:].astype(BF)


def attend_pull(pair, blocks, grads, exacts, log_totals, slopes, starts, me):
    block, width = blocks[0].shape[0], blocks[0].shape[1] // 3
    pairs = width // (2 * HD)
    length = 4 * block
    smem = pl.BlockSpec(memory_space=pltpu.SMEM)
    triples = [pl.BlockSpec((block, 2 * HD), functools.partial(lambda part, i: (0, part * pairs + pair), part)) for part in range(3)]
    rows = pl.BlockSpec((block, 2 * HD), lambda i: (0, pair))
    wide = pl.BlockSpec((2 * HD, 2 * block), lambda i: (pair, 0))
    sums = pl.BlockSpec((1, 8, 2 * block), lambda i: (pair, 0, 0))
    out = pl.BlockSpec((3, 2 * block, 2 * HD), lambda i: (0, 0, 0))
    return pl.pallas_call(
        functools.partial(pull_kernel, block, pair),
        grid=(4,),
        in_specs=[smem, smem, smem] + triples * 4 + [rows] * 4 + [wide] * 2 + [sums] * 2,
        out_specs=[out, out],
        out_shape=[jax.ShapeDtypeStruct((3, 2 * block, 2 * HD), BF)] * 2,
        scratch_shapes=[
            pltpu.VMEM((length, 2 * HD), BF),
            pltpu.VMEM((length, 2 * HD), BF),
            pltpu.VMEM((length, 2 * HD), BF),
            pltpu.VMEM((length, 2 * HD), BF),
            pltpu.VMEM((2 * HD, length), BF),
            pltpu.VMEM((length, 2 * HD), F32),
            pltpu.VMEM((length, 2 * HD), F32),
            pltpu.VMEM((2 * HD, block), F32),
            pltpu.VMEM((block, block), F32),
            pltpu.VMEM((PIECE, block), F32),
        ],
        compiler_params=pltpu.CompilerParams(vmem_limit_bytes=VMEM_LIMIT),
        cost_estimate=took(22),
        name="attend_pull",
    )(slopes, starts, me, *[b for b in blocks for _ in range(3)], *grads, *exacts, *log_totals)


def head_columns(refs, quarter, first, last):
    return jnp.concatenate(
        [refs[odd][chip ^ refs[2][0], 1 - quarter if odd else quarter, :, first:last] for chip in range(4) for odd in range(2)],
        axis=0,
    )


def placed(arrays):
    return [
        pl.BlockSpec(memory_space=pltpu.SMEM if a.dtype == jnp.int32 else pltpu.VMEM) for a in arrays
    ]


def call_once(kernel, name, outs, args, us):
    return pl.pallas_call(
        kernel,
        in_specs=placed(args),
        out_specs=placed(outs),
        out_shape=outs,
        compiler_params=pltpu.CompilerParams(vmem_limit_bytes=VMEM_LIMIT),
        cost_estimate=took(us),
        name=name,
    )(*args)


def project_kernel(rows_ref, bias_ref, *rest):
    weight_refs, out_refs = rest[:3], rest[3:]
    rows = rows_ref[...]
    for quarter in (1, 0):
        out = dot_nn(rows, head_columns(weight_refs, quarter, 0, 768)) + bias_ref[quarter:quarter + 1]
        out_refs[quarter][...] = out.astype(BF)


def project(rows, bias, pieces):
    out = jax.ShapeDtypeStruct((rows.shape[0], 768), BF)
    return call_once(project_kernel, "project", [out, out], [rows, bias, *pieces], 5)


def mix_term(mixed_refs, weight_refs):
    rows = jnp.concatenate([ref[...] for ref in mixed_refs], axis=1)
    weight = jnp.concatenate([head_columns(weight_refs, quarter, 768, 1024) for quarter in range(2)], axis=1)
    return dot_nt(rows, weight)


def mix_far_kernel(mine_ref, other_ref, *rest):
    rest[3][...] = mix_term((mine_ref, other_ref), rest[:3]).astype(BF)


def mix_far(mine, other, pieces):
    out = jax.ShapeDtypeStruct((mine.shape[0], 1024), BF)
    return call_once(mix_far_kernel, "mix_far", [out], [mine, other, *pieces], 4)[0]


def mix_near_kernel(mine_ref, other_ref, far_ref, resid_ref, vector_ref, *rest):
    weight_refs, (mid_ref, normed_ref, flip_ref) = rest[:3], rest[3:]
    term = mix_term((mine_ref, other_ref), weight_refs)
    mid = resid_ref[...] + (term + far_ref[...].astype(F32) + vector_ref[2:3])
    mid_ref[...] = mid
    normed = (normalize(mid)[0] * vector_ref[3:4] + vector_ref[4:5]).astype(BF)
    normed_ref[...] = normed
    flip_ref[...] = flipped(normed)


def mix_near(mine, other, far, resid, vectors, pieces):
    outs = [
        jax.ShapeDtypeStruct(resid.shape, F32),
        jax.ShapeDtypeStruct(resid.shape, BF),
        jax.ShapeDtypeStruct(resid.shape, BF),
    ]
    return call_once(mix_near_kernel, "mix_near", outs, [mine, other, far, resid, vectors, *pieces], 6)


def unmix_kernel(grad_ref, *rest):
    weight_refs, out_refs = rest[:3], rest[3:]
    grad = grad_ref[...]
    for quarter in (1, 0):
        out_refs[quarter][...] = dot_nn(grad, head_columns(weight_refs, quarter, 768, 1024)).astype(BF)


def unmix(grad, pieces):
    out = jax.ShapeDtypeStruct((grad.shape[0], 256), BF)
    return call_once(unmix_kernel, "unmix", [out, out], [grad, *pieces], 4)


def unproject_term(grad_refs, weight_refs, first):
    rows = jnp.concatenate(
        [ref[part, first:first + 512] for pair in grad_refs for part in range(3) for ref in pair], axis=1
    )
    weight = jnp.concatenate([head_columns(weight_refs, quarter, 0, 768) for quarter in range(2)], axis=1)
    return dot_nt(rows, weight)


def unproject_far_kernel(*rest):
    rest[7][...] = unproject_term((rest[0:2], rest[2:4]), rest[4:7], 512).astype(BF)


def unproject_far(mine, other, pieces):
    out = jax.ShapeDtypeStruct((512, 1024), BF)
    return call_once(unproject_far_kernel, "unproject_far", [out], [*mine, *other, *pieces], 6)[0]


def unproject_near_kernel(last, own_ref, *rest):
    mine, other, rest = rest[0:2], rest[2:4], rest[4:]
    far_ref, resid_ref, grad_mid_ref, vector_ref, rest = *rest[:4], rest[4:]
    weight_refs, (grad_ref, low_ref, sums_ref) = rest[:3], rest[3:]
    term = unproject_term((mine, other), weight_refs, 0) + far_ref[...].astype(F32)
    grad_norm, grad_gain, grad_shift = norm_pull(resid_ref[...], vector_ref[0:1], term)
    grad = grad_mid_ref[...] + grad_norm
    grad_ref[...] = grad
    if last:
        put_turned(low_ref, own_ref[0], grad.astype(BF))
    else:
        low_ref[...] = flipped(grad).astype(BF)
    sums_ref[...] = jnp.concatenate([grad_gain, grad_shift, jnp.zeros((6, grad.shape[1]), F32)], axis=0)


def unproject_near(last, own_keep, mine, other, far, resid, grad_mid, vectors, pieces):
    outs = [
        jax.ShapeDtypeStruct(resid.shape, F32),
        jax.ShapeDtypeStruct(resid.shape, BF),
        jax.ShapeDtypeStruct((8, resid.shape[1]), F32),
    ]
    args = [own_keep, *mine, *other, far, resid, grad_mid, vectors, *pieces]
    kernel = functools.partial(unproject_near_kernel, last)
    return call_once(kernel, "unproject_near", outs, args, 9)


def head_grads_kernel(turn_ref, near_ref, far_ref, grad_near_ref, grad_far_ref, *rest):
    pairs, rest = (rest[0:2], rest[2:4]), rest[4:]
    mixed_refs, out_refs, bias_ref = (rest[0:2], rest[2:4]), rest[4:6], rest[6]
    rows_t = jnp.concatenate([near_ref[...], far_ref[...]], axis=0).T
    grad_t = jnp.concatenate([grad_near_ref[...], grad_far_ref[...]], axis=0).T
    for quarter, refs in enumerate(pairs):
        grads = [jnp.concatenate([ref[part] for ref in refs], axis=1) for part in range(3)]
        for part in range(4):
            if part < 3:
                term = dot_nn(rows_t, grads[part])
            else:
                term = dot_nn(grad_t, jnp.concatenate([m[...] for m in mixed_refs[quarter]], axis=0))
            term = term.astype(BF)
            for index in range(8):
                chip, odd = index // 2, index % 2
                place = 1 - quarter if odd else quarter
                out_refs[odd][chip ^ turn_ref[0], place, :, part * 256:(part + 1) * 256] = term[index * 128:(index + 1) * 128]
        for row, part in ((0, 0), (1, 2)):
            total = jnp.sum(grads[part].astype(F32), axis=0, keepdims=True)
            bias_ref[2 * quarter + row:2 * quarter + row + 1, :] = total
    bias_ref[4:8, :] = jnp.zeros((4, 256), F32)


def head_grads(turn, near, far, grad_near, grad_far, mine, other, mixed_mine, mixed_other):
    outs = [jax.ShapeDtypeStruct((4, 2, 128, 1024), BF)] * 2 + [jax.ShapeDtypeStruct((8, 256), F32)]
    args = [turn, near, far, grad_near, grad_far, *mine, *other, *mixed_mine, *mixed_other]
    return call_once(head_grads_kernel, "head_grads", outs, args, 10)


GELU_A = 0.7978845608028654
GELU_B = 0.044715


def normalize(values):
    centred = values - jnp.mean(values, axis=-1, keepdims=True)
    spread = lax.rsqrt(jnp.mean(centred * centred, axis=-1, keepdims=True) + NORM_EPS)
    return centred * spread, spread


def norm_pull(values, gain, grad):
    unit, spread = normalize(values)
    grad_unit = grad * gain
    inner = grad_unit - jnp.mean(grad_unit, axis=-1, keepdims=True)
    inner = inner - unit * jnp.mean(grad_unit * unit, axis=-1, keepdims=True)
    return spread * inner, jnp.sum(grad * unit, axis=0, keepdims=True), jnp.sum(grad, axis=0, keepdims=True)


def flipped(values):
    return jnp.concatenate([values[:, (block ^ 1) * 128:(block ^ 1) * 128 + 128] for block in range(8)], axis=1)


def put_turned(out_ref, own, values):
    for block in range(8):
        here = pl.ds(pl.multiple_of((block ^ own) * 128, 128), 128)
        out_ref[:, here] = values[:, block * 128:(block + 1) * 128]


def enter_kernel(own_ref, direct_ref, moved_ref, vector_ref, resid_ref, normed_ref, flip_ref):
    own, keep = own_ref[0], own_ref[1]
    for block in range(8):
        here = pl.ds(pl.multiple_of((block ^ own) * 128, 128), 128)
        rows = jnp.where(keep > 0, direct_ref[:, here].astype(F32), moved_ref[:, here].astype(F32))
        resid_ref[:, block * 128:(block + 1) * 128] = rows
    values = resid_ref[...]
    normed_ref[...] = (normalize(values)[0] * vector_ref[0:1] + vector_ref[1:2]).astype(BF)
    flip_ref[...] = flipped(values).astype(BF)


def enter(own_keep, direct, moved, vectors):
    rows, features = direct.shape
    smem = pl.BlockSpec(memory_space=pltpu.SMEM)
    vmem = pl.BlockSpec(memory_space=pltpu.VMEM)
    return pl.pallas_call(
        enter_kernel,
        in_specs=[smem, vmem, vmem, vmem],
        out_specs=[vmem, vmem, vmem],
        out_shape=[
            jax.ShapeDtypeStruct((rows, features), F32),
            jax.ShapeDtypeStruct((rows, features), BF),
            jax.ShapeDtypeStruct((rows, features), BF),
        ],
        compiler_params=pltpu.CompilerParams(vmem_limit_bytes=VMEM_LIMIT),
        cost_estimate=took(4),
        name="enter",
    )(own_keep, direct, moved, vectors)


def half_specs(tile, weights):
    def spec(half, chip, whole):
        def index(f, turn):
            column = jnp.clip(f - 2 * half, 0, 1)
            return (chip ^ turn[0], 0, 0, column) if whole else (0, 0, column)

        return pl.BlockSpec((None, 2, 128, 2 * tile) if whole else (2, 128, 2 * tile), index)

    return [spec(half, chip, len(weights[half]) == 1) for half in range(2) for chip in range(4)]


def half_arrays(weights):
    return [array for half in weights for array in (half if len(half) == 4 else half * 4)]


def by_half(step, weight_refs, body):
    @pl.when(step < 2)
    def _():
        body(weight_refs[:4])

    @pl.when(step >= 2)
    def _():
        body(weight_refs[4:])


def joined(refs, first, last):
    return jnp.concatenate([ref[core, :, first:last] for ref in refs for core in range(2)], axis=0)


def mlp_kernel(turn_ref, normed_ref, other_ref, bias_ref, *rest):
    weight_refs, (hidden_ref, active_ref, near_ref, away_ref, acc_ref) = rest[:8], rest[8:]
    rows, tile = normed_ref.shape[0], hidden_ref.shape[1]
    step = pl.program_id(0)

    @pl.when(step == 0)
    def _():
        acc_ref[...] = jnp.zeros_like(acc_ref)

    def body(refs):
        expand, reduce = joined(refs, 0, tile), joined(refs, tile, 2 * tile)
        for first, ref in ((0, normed_ref), (rows, other_ref)):
            hidden = dot_nn(ref[...], expand) + bias_ref[...]
            inner = jnp.tanh(GELU_A * (hidden + GELU_B * hidden * hidden * hidden))
            active = (0.5 * hidden * (1.0 + inner)).astype(BF)
            hidden_ref[first:first + rows] = hidden.astype(BF)
            active_ref[first:first + rows] = active
            acc_ref[first:first + rows] += dot_nt(active, reduce)

    by_half(step, weight_refs, body)

    @pl.when(step == pl.num_programs(0) - 1)
    def _():
        near_ref[...] = acc_ref[:rows]
        away_ref[...] = flipped(acc_ref[rows:]).astype(BF)


def mlp_forward(turn, normed, other, bias, weights):
    rows, features = normed.shape
    units = bias.shape[1]
    tile = 512
    whole = pl.BlockSpec((rows, features), lambda f, turn: (0, 0))
    tiles = pl.BlockSpec((2 * rows, tile), lambda f, turn: (0, f))
    return pl.pallas_call(
        mlp_kernel,
        grid_spec=pltpu.PrefetchScalarGridSpec(
            num_scalar_prefetch=1,
            grid=(units // tile,),
            in_specs=[whole, whole, pl.BlockSpec((1, tile), lambda f, turn: (0, f))] + half_specs(tile, weights),
            out_specs=[tiles, tiles, whole, whole],
            scratch_shapes=[pltpu.VMEM((2 * rows, features), F32)],
        ),
        out_shape=[
            jax.ShapeDtypeStruct((2 * rows, units), BF),
            jax.ShapeDtypeStruct((2 * rows, units), BF),
            jax.ShapeDtypeStruct((rows, features), F32),
            jax.ShapeDtypeStruct((rows, features), BF),
        ],
        compiler_params=pltpu.CompilerParams(vmem_limit_bytes=VMEM_LIMIT),
        cost_estimate=took(18),
        name="mlp_forward",
    )(turn, normed, other, bias, *half_arrays(weights))


def mlp_close_kernel(last, own_ref, near_ref, got_ref, mid_ref, vector_ref, out_ref, next_ref):
    out = mid_ref[...] + (near_ref[...] + got_ref[...].astype(F32) + vector_ref[5:6])
    out_ref[...] = out
    if last:
        put_turned(next_ref, own_ref[0], out.astype(BF))
    else:
        next_ref[...] = (normalize(out)[0] * vector_ref[6:7] + vector_ref[7:8]).astype(BF)


def mlp_close(last, own_keep, near, got, mid, vectors):
    outs = [jax.ShapeDtypeStruct(mid.shape, F32), jax.ShapeDtypeStruct(mid.shape, BF)]
    args = [own_keep, near, got, mid, vectors]
    return call_once(functools.partial(mlp_close_kernel, last), "mlp_close", outs, args, 3)


def mlp_pull_kernel(turn_ref, grad_ref, other_ref, hidden_ref, *rest):
    weight_refs = rest[:8]
    grad_hidden_ref, grad_bias_ref, near_ref, away_ref, acc_ref, low_ref = rest[8:]
    rows, tile = grad_ref.shape[0], hidden_ref.shape[1]
    step = pl.program_id(0)

    @pl.when(step == 0)
    def _():
        low_ref[:rows] = grad_ref[...].astype(BF)
        low_ref[rows:] = other_ref[...]
        acc_ref[...] = jnp.zeros_like(acc_ref)

    def body(refs):
        expand, reduce = joined(refs, 0, tile), joined(refs, tile, 2 * tile)
        total = jnp.zeros((1, tile), F32)
        for first in (0, rows):
            here = slice(first, first + rows)
            hidden = hidden_ref[here].astype(F32)
            squared = hidden * hidden
            inner = jnp.tanh(GELU_A * hidden * (1.0 + GELU_B * squared))
            slope = 0.5 * (1.0 + inner) + 0.5 * hidden * (1.0 - inner * inner) * (GELU_A * (1.0 + 3.0 * GELU_B * squared))
            grad_hidden = dot_nn(low_ref[here], reduce) * slope
            total = total + jnp.sum(grad_hidden, axis=0, keepdims=True)
            grad_hidden = grad_hidden.astype(BF)
            grad_hidden_ref[here] = grad_hidden
            acc_ref[here] += dot_nt(grad_hidden, expand)
        grad_bias_ref[...] = total

    by_half(step, weight_refs, body)

    @pl.when(step == pl.num_programs(0) - 1)
    def _():
        near_ref[...] = acc_ref[:rows]
        away_ref[...] = flipped(acc_ref[rows:]).astype(BF)


def mlp_backward(turn, grad, other, hidden, weights):
    rows, features = grad.shape
    units = hidden.shape[1]
    tile = 512
    whole = pl.BlockSpec((rows, features), lambda f, turn: (0, 0))
    tiles = pl.BlockSpec((2 * rows, tile), lambda f, turn: (0, f))
    return pl.pallas_call(
        mlp_pull_kernel,
        grid_spec=pltpu.PrefetchScalarGridSpec(
            num_scalar_prefetch=1,
            grid=(units // tile,),
            in_specs=[whole, whole, tiles] + half_specs(tile, weights),
            out_specs=[tiles, pl.BlockSpec((1, tile), lambda f, turn: (0, f)), whole, whole],
            scratch_shapes=[pltpu.VMEM((2 * rows, features), F32), pltpu.VMEM((2 * rows, features), BF)],
        ),
        out_shape=[
            jax.ShapeDtypeStruct((2 * rows, units), BF),
            jax.ShapeDtypeStruct((1, units), F32),
            jax.ShapeDtypeStruct((rows, features), F32),
            jax.ShapeDtypeStruct((rows, features), BF),
        ],
        compiler_params=pltpu.CompilerParams(vmem_limit_bytes=VMEM_LIMIT),
        cost_estimate=took(22),
        name="mlp_backward",
    )(turn, grad, other, hidden, *half_arrays(weights))


def mlp_open_kernel(near_ref, got_ref, mid_ref, grad_ref, vector_ref, grad_mid_ref, grad_low_ref, sums_ref):
    grad = grad_ref[...]
    term = near_ref[...] + got_ref[...].astype(F32)
    grad_norm, grad_gain, grad_shift = norm_pull(mid_ref[...], vector_ref[3:4], term)
    grad_mid = grad + grad_norm
    grad_mid_ref[...] = grad_mid
    grad_low_ref[...] = grad_mid.astype(BF)
    rows = [jnp.sum(grad_mid, axis=0, keepdims=True), grad_gain, grad_shift, jnp.sum(grad, axis=0, keepdims=True)]
    sums_ref[...] = jnp.concatenate(rows + [jnp.zeros((4, grad.shape[1]), F32)], axis=0)


def mlp_open(near, got, mid, grad, vectors):
    outs = [
        jax.ShapeDtypeStruct(mid.shape, F32),
        jax.ShapeDtypeStruct(mid.shape, BF),
        jax.ShapeDtypeStruct((8, mid.shape[1]), F32),
    ]
    return call_once(mlp_open_kernel, "mlp_open", outs, [near, got, mid, grad, vectors], 5)


def unit_grads_kernel(second, left_ref, other_ref, right_ref, own_ref, pair_ref, single_ref, left_t_ref):
    @pl.when(pl.program_id(0) == 0)
    def _():
        left_t_ref[...] = jnp.concatenate([left_ref[...].astype(BF), other_ref[...]], axis=0).T

    grad = dot_nn(left_t_ref[...], right_ref[...]).astype(BF)
    single, direct = (1, 2) if second == "x" else (2, 1)
    for core in range(2):
        own_ref[0, core] = grad[core * 128:(core + 1) * 128]
        single_ref[0, core] = grad[(2 * single + core) * 128:(2 * single + core + 1) * 128]
        pair_ref[0, 0, core] = grad[(2 * direct + core) * 128:(2 * direct + core + 1) * 128]
        pair_ref[0, 1, core] = grad[(6 + core) * 128:(7 + core) * 128]


def unit_grads(second, left, other, right):
    rows, features = left.shape
    units = right.shape[1]
    tile = 512
    whole = pl.BlockSpec((rows, features), lambda f: (0, 0))
    out = pl.BlockSpec((1, 2, 128, tile), lambda f: (f // 2, 0, 0, f % 2))
    one = jax.ShapeDtypeStruct((2, 2, 128, 1024), BF)
    return pl.pallas_call(
        functools.partial(unit_grads_kernel, second),
        grid=(units // tile,),
        in_specs=[whole, whole, pl.BlockSpec((2 * rows, tile), lambda f: (0, f))],
        out_specs=[out, pl.BlockSpec((1, 2, 2, 128, tile), lambda f: (f // 2, 0, 0, 0, f % 2)), out],
        out_shape=[one, jax.ShapeDtypeStruct((2, 2, 2, 128, 1024), BF), one],
        scratch_shapes=[pltpu.VMEM((features, 2 * rows), BF)],
        compiler_params=pltpu.CompilerParams(vmem_limit_bytes=VMEM_LIMIT),
        cost_estimate=took(10),
        name="unit_grads",
    )(left, other, right)


def unit_grads_whole_kernel(turn_ref, left_ref, other_ref, right_ref, out_ref, left_t_ref):
    @pl.when(pl.program_id(0) == 0)
    def _():
        left_t_ref[...] = jnp.concatenate([left_ref[...].astype(BF), other_ref[...]], axis=0).T

    grad = dot_nn(left_t_ref[...], right_ref[...]).astype(BF)
    for chip in range(4):
        for core in range(2):
            first = (2 * chip + core) * 128
            out_ref[chip ^ turn_ref[0], 0, core] = grad[first:first + 128]


def unit_grads_whole(turn, left, other, right):
    rows, features = left.shape
    units = right.shape[1]
    tile = 512
    whole = pl.BlockSpec((rows, features), lambda f: (0, 0))
    return pl.pallas_call(
        unit_grads_whole_kernel,
        grid=(units // tile,),
        in_specs=[
            pl.BlockSpec(memory_space=pltpu.SMEM),
            whole,
            whole,
            pl.BlockSpec((2 * rows, tile), lambda f: (0, f)),
        ],
        out_specs=pl.BlockSpec((4, 1, 2, 128, tile), lambda f: (0, f // 2, 0, 0, f % 2)),
        out_shape=jax.ShapeDtypeStruct((4, 2, 2, 128, 1024), BF),
        scratch_shapes=[pltpu.VMEM((features, 2 * rows), BF)],
        compiler_params=pltpu.CompilerParams(vmem_limit_bytes=VMEM_LIMIT),
        cost_estimate=took(10),
        name="unit_grads_whole",
    )(turn, left, other, right)


MESH = pl.DeviceIdType.MESH


def flip(index, bit):
    return index + bit - 2 * bit * ((index // bit) % 2)


def peer(mask):
    dp, tensor = lax.axis_index("dp"), lax.axis_index("tensor")
    for bit in (1, 2):
        tensor = flip(tensor, bit) if mask & bit else tensor
        dp = flip(dp, bit) if mask & (CORE * bit) else dp
    dp = flip(dp, 4) if mask & YBIT else dp
    return {"dp": dp, "tensor": tensor}


def xor_block(block, own):
    return sum(bit * ((block // bit + own // bit) % 2) for bit in (1, 2, 4))


def greet(masks):
    barrier = pltpu.get_barrier_semaphore()
    for mask in masks:
        pl.semaphore_signal(barrier, inc=1, device_id=peer(mask), device_id_type=MESH)
    pl.semaphore_wait(barrier, len(masks))


def project_rows(rows, weight_refs, bias_ref, layer, out_refs):
    for quarter in (1, 0):
        weight = jnp.concatenate(
            [weight_refs[odd][chip, 1 - quarter if odd else quarter, :, 0:768] for chip in range(4) for odd in range(2)],
            axis=0,
        )
        out_refs[quarter][...] = (dot_nn(rows, weight) + bias_ref[layer, quarter:quarter + 1]).astype(BF)


SMALL_ROWS = 11


def start_kernel(
    layers, x_ref, project_ref, output_ref, expand_ref, reduce_ref, small_ref,
    resid_ref, normed_ref, far_ref, even_ref, odd_ref, first_ref, vector_ref, head_bias_ref, unit_bias_ref,
    near_mine_ref, far_mine_ref, got_near_ref, got_far_ref,
    came_ref, piece_ref, every_ref, near_other_ref, far_other_ref, local_sem, send_sem, recv_sem,
):
    own, place = lax.axis_index("dp"), lax.axis_index("tensor")
    core = own % 2
    keep = core == place // 2
    count = [0]

    def copy(source, target, device):
        index = count[0]
        count[0] += 1
        return pltpu.make_async_remote_copy(
            src_ref=source, dst_ref=target, send_sem=send_sem.at[index], recv_sem=recv_sem.at[index],
            device_id=device, device_id_type=MESH,
        )

    greet((1, 2, 4, 6, 8, 16))
    tokens = copy(x_ref, came_ref, peer(CORE | Z1))
    stay = pltpu.make_async_copy(x_ref, came_ref, local_sem)

    @pl.when(keep)
    def _():
        stay.start()

    @pl.when(jnp.logical_not(keep))
    def _():
        tokens.start()

    for part in range(3):
        even_ref[0, core, :, part * 256:(part + 1) * 256] = project_ref[0, part]
    even_ref[0, core, :, 768:1024] = output_ref[0].T
    along = copy(even_ref.at[0, core], even_ref.at[0, 1 - core], peer(Z1))
    along.start()
    every_ref[0, 0] = small_ref[...]
    smalls = [
        (copy(every_ref.at[0, pl.ds(0, width)], every_ref.at[0, pl.ds(width, width)], peer(mask)))
        for width, mask in ((1, CORE), (2, XBIT), (4, YBIT))
    ]
    smalls += [
        copy(every_ref.at[pl.ds(0, width)], every_ref.at[pl.ds(width, width)], peer(mask)) for width, mask in ((1, Z0), (2, Z1))
    ]
    smalls[0].start()
    for half in range(2):
        here = slice(half * 512, (half + 1) * 512)
        piece_ref[:, half * 1024:half * 1024 + 512] = expand_ref[0, :, here]
        piece_ref[:, half * 1024 + 512:half * 1024 + 1024] = reduce_ref[0, here, :].T
    cross = copy(piece_ref, first_ref.at[1], {
        "dp": flip(own, 1), "tensor": place + (1 - core) * (flip(place, 2) - place)
    })
    same = copy(piece_ref, first_ref.at[0], peer(Z1))

    @pl.when(core == 0)
    def _():
        first_ref[0] = piece_ref[...]

    for step in range(1, 5):
        smalls[step - 1].wait()
        smalls[step].start()
    along.wait()
    over_x = copy(even_ref.at[0], even_ref.at[1], peer(XBIT))
    over_y = copy(even_ref.at[0], even_ref.at[2], peer(YBIT))
    over_x.start()
    over_y.start()
    cores = [copy(even_ref.at[chip], odd_ref.at[chip], peer(CORE)) for chip in range(4)]
    cores[0].start()
    smalls[4].wait()
    for layer in range(layers):
        base = layer * SMALL_ROWS
        later = min(layer + 1, layers - 1) * SMALL_ROWS
        rows = [base + row for row in range(6)] + [later, later + 1]
        for row, source in enumerate(rows):
            vector_ref[layer, row:row + 1, :] = jnp.concatenate(
                [every_ref[0, block, source:source + 1, :] for block in range(8)], axis=1
            )
        for quarter in range(2):
            which = 2 * (core + quarter - 2 * core * quarter)
            total = every_ref[which, 0, base + 6:base + 10, :]
            for block in range(1, 8):
                total = total + every_ref[which, block, base + 6:base + 10, :]
            head_bias_ref[layer, quarter:quarter + 1, :] = jnp.concatenate(
                [total[0:1], total[1:2], jnp.zeros((1, 256), F32), total[2:3], total[3:4]], axis=1
            )
            for block in range(8):
                unit_bias_ref[layer, :, quarter * 1024 + block * 128:quarter * 1024 + (block + 1) * 128] = every_ref[
                    2 * core + quarter, xor_block(block, own), base + 10:base + 11, :
                ]
    over_y.wait()
    over_x.wait()
    across = copy(even_ref.at[2], even_ref.at[3], peer(XBIT))
    across.start()
    cores[1].start()
    cores[2].start()

    @pl.when(keep)
    def _():
        stay.wait()

    @pl.when(jnp.logical_not(keep))
    def _():
        tokens.wait()

    for block in range(8):
        here = pl.ds(pl.multiple_of(xor_block(block, own) * 128, 128), 128)
        resid_ref[:, block * 128:(block + 1) * 128] = came_ref[:, here].astype(F32)
    normed = (normalize(resid_ref[...])[0] * vector_ref[0, 0:1] + vector_ref[0, 1:2]).astype(BF)
    normed_ref[...] = normed
    beside = copy(normed_ref, far_ref, peer(Z0))
    beside.start()
    cross.start()

    @pl.when(core == 1)
    def _():
        same.start()

    across.wait()
    cores[3].start()
    for one in cores:
        one.wait()
    weights = (even_ref, odd_ref)
    project_rows(normed_ref[...], weights, head_bias_ref, 0, (near_mine_ref, near_other_ref))
    back_near = copy(near_other_ref, got_near_ref, peer(CORE))
    back_near.start()
    beside.wait()
    project_rows(far_ref[...], weights, head_bias_ref, 0, (far_mine_ref, far_other_ref))
    back_far = copy(far_other_ref, got_far_ref, peer(CORE))
    back_far.start()
    cross.wait()

    @pl.when(core == 1)
    def _():
        same.wait()

    back_near.wait()
    back_far.wait()


def start(x, project_weight, output_weight, expand_weight, reduce_weight, small, layers):
    rows, features = x.shape
    vmem = pl.BlockSpec(memory_space=pltpu.VMEM)

    triple = jax.ShapeDtypeStruct((rows, 768), BF)
    heads = jax.ShapeDtypeStruct((4, 2, 128, 1024), BF)
    outs = [
        jax.ShapeDtypeStruct((rows, features), F32),
        jax.ShapeDtypeStruct((rows, features), BF),
        jax.ShapeDtypeStruct((rows, features), BF),
        heads,
        heads,
        jax.ShapeDtypeStruct((2, 128, 2048), BF),
        jax.ShapeDtypeStruct((layers, 8, features), F32),
        jax.ShapeDtypeStruct((layers, 2, 768), F32),
        jax.ShapeDtypeStruct((layers, 1, 2048), F32),
        triple,
        triple,
        triple,
        triple,
    ]
    copies = 19
    return pl.pallas_call(
        functools.partial(start_kernel, layers),
        in_specs=[vmem] * 6,
        out_specs=[vmem] * len(outs),
        out_shape=outs,
        scratch_shapes=[
            pltpu.VMEM((rows, features), BF),
            pltpu.VMEM((128, 2048), BF),
            pltpu.VMEM((4, 8, *small.shape), F32),
            pltpu.VMEM((rows, 768), BF),
            pltpu.VMEM((rows, 768), BF),
            pltpu.SemaphoreType.DMA,
            pltpu.SemaphoreType.DMA((copies,)),
            pltpu.SemaphoreType.DMA((copies,)),
        ],
        compiler_params=pltpu.CompilerParams(vmem_limit_bytes=VMEM_LIMIT, collective_id=0, has_side_effects=True),
        cost_estimate=took(60),
        name="start",
    )(x, project_weight, output_weight, expand_weight, reduce_weight, small)


def fetch_heads(piece, core, turn, out):
    token = yield
    far = swap(after(piece, token), Z1)
    token = yield []
    far = after(far, token)
    own = jnp.stack([jnp.where(core == 0, piece, far), jnp.where(core == 0, far, piece)])
    from_x = swap(own, XBIT)
    from_y = swap(own, YBIT)
    token = yield [own]
    from_x, from_y = after_all((from_x, from_y), token)
    across = swap(from_y, XBIT)
    token = yield [from_x, from_y]
    quads = jnp.stack([own, from_x, from_y, after(across, token)])
    other = swap(quads, CORE)
    token = yield [quads]
    out += [quads, other, turn]


def fetch_units_near(first, first_out, second_out):
    token = yield
    first = after(first, token)
    first_x, first_y, second = swap(first, XBIT), swap(first, YBIT), swap(first, Z0)
    token = yield []
    first_x, first_y, second = after_all((first_x, first_y, second), token)
    yield from join_units(first, first_x, first_y, second, first_out, second_out)


def fetch_units(piece, core, first_out, second_out):
    token = yield
    piece = after(piece, token)
    pair = jnp.stack([piece, swap(piece, CORE)])
    far = swap_some(pair, (0, Z1))
    token = yield [pair]
    first = jnp.where(core == 0, pair, after(far, token))
    token = yield [first]
    second = swap(after(first, token), Z0)
    token = yield []
    first, second = after_all((first, second), token)
    first_x, first_y = swap(first, XBIT), swap(first, YBIT)
    token = yield [second]
    first_x, first_y = after_all((first_x, first_y), token)
    yield from join_units(first, first_x, first_y, second, first_out, second_out)


def join_units(first, first_x, first_y, second, first_out, second_out):
    second_x, second_y = swap(second, XBIT), swap(second, YBIT)
    token = yield [first_x, first_y, second]
    second_x, second_y = after_all((second_x, second_y), token)
    first_across, second_across = swap(first_x, YBIT), swap(second_y, XBIT)
    token = yield [second_x, second_y]
    first_across, second_across = after_all((first_across, second_across), token)
    first_out += [first, first_x, first_y, first_across]
    second_out += [second, second_x, second_y, second_across]
    yield [first_across, second_across]


def pack_heads(project, output):
    return jnp.concatenate([project.transpose(1, 0, 2).reshape(128, 768), output.T], axis=1)


def unpack_heads(values):
    return values[:, :768].reshape(128, 3, 256).transpose(1, 0, 2), values[:, 768:].T


def pack_units(expand, reduce):
    parts = (expand.reshape(128, 2, 512), reduce.T.reshape(128, 2, 512))
    return jnp.stack(parts, axis=2).reshape(128, 2048)


def small_rows(six, project_bias, expand_bias, own):
    layers = six.shape[1]
    wide = jnp.zeros((layers, 2, 256), F32)
    wide = lax.dynamic_update_slice(wide, project_bias.astype(F32), (0, 0, own * 32))
    rows = jnp.concatenate(
        [six.transpose(1, 0, 2).astype(F32), wide.reshape(layers, 4, 128), expand_bias[:, None, :].astype(F32)], axis=1
    )
    return jnp.pad(rows.reshape(layers * SMALL_ROWS, 128), ((0, -layers * SMALL_ROWS % 8), (0, 0)))


def pack_kernel(count, own_ref, *rest):
    out_ref, own = rest[-1], own_ref[0]
    core = own % 2
    out_ref[...] = jnp.zeros_like(out_ref)
    for layer in range(count):
        first_ref, second_ref, unit_ref, head_ref = rest[4 * layer:4 * layer + 4]
        for place in range(8):
            here = slice(place * 128, (place + 1) * 128)
            out_ref[place, 6 * layer:6 * layer + 2, :] = first_ref[0:2, here]
            out_ref[place, 6 * layer + 2:6 * layer + 6, :] = second_ref[0:4, here]
            base = 6 * count + 12 * layer
            for quarter in range(2):
                lane = pl.multiple_of(quarter * 1024 + (place ^ own) * 128, 128)
                out_ref[place, pl.ds(base + 2 * core + quarter, 1), :] = unit_ref[0:1, pl.ds(lane, 128)]
                row = base + 4 + 4 * (quarter ^ core)
                for half in range(2):
                    out_ref[place, pl.ds(row + 2 * half, 2), :] = head_ref[2 * quarter:2 * quarter + 2, half * 128:(half + 1) * 128]


def sum_small(layers, own, own_keep, token):
    count = len(layers)
    rows = 18 * count
    args = [own_keep] + [array for layer in layers for array in layer]
    rows = call_once(
        functools.partial(pack_kernel, count), "pack", [jax.ShapeDtypeStruct((8, rows, 128), F32)], args, 3
    )[0]
    rows = after(rows, token)
    for mask in (CORE, XBIT, YBIT):
        bit = rows.reshape(-1, 2, 18 * count, 128)
        rows = bit[:, 0] + swap(bit[:, 1], mask)
    vectors, biases = rows[0, :6 * count], rows[0, 6 * count:].reshape(count, 12, 128)

    def part(offset, *more):
        return jnp.concatenate([vectors, biases[:, offset], *more], axis=0)

    two = swap(part(2, biases[:, 8:].reshape(4 * count, 128)), 2)
    whole = part(0) + two[:7 * count] + swap(part(1), 1) + swap(part(3), 3)
    heads = biases[:, 4:8] + two[7 * count:].reshape(count, 4, 128)
    heads = heads.reshape(count, 2, 2, 128).transpose(0, 2, 1, 3).reshape(count, 2, 256)
    heads = lax.dynamic_slice_in_dim(heads, own * 32, 32, 2)
    return whole[:6 * count].reshape(count, 6, 128), whole[6 * count:], heads


def reduce_heads(even, odd, core, out):
    token = yield
    got = swap(odd, CORE)
    token = yield []
    got = after(got, token)
    low, high = even[:2] + got[:2], even[2:] + got[2:]
    from_y = swap(high, YBIT)
    token = yield [low, high]
    from_y = after(from_y, token)
    relayed = low[1] + from_y[1]
    relay = swap(relayed, XBIT)
    token = yield [relayed]
    total = low[0] + from_y[0] + after(relay, token)
    yield from close_heads(total, core, out)


def close_heads(total, core, out):
    near = jnp.where(core == 0, total[0], total[1])
    away = jnp.where(core == 0, total[1], total[0])
    far = swap(away, Z1)
    token = yield [near, away]
    out.append(unpack_heads(near.astype(F32) + after(far, token).astype(F32)))
    yield list(out[-1])


def reduce_units(reduce_parts, expand_parts, core, out):
    yield
    own_r, pair_r, single_r = reduce_parts
    from_y = swap(pair_r, YBIT)
    yield []
    own_e, pair_e, single_e = expand_parts
    from_x = swap(pair_e, XBIT)
    token = yield []
    from_y = after(from_y, token)
    relayed_r = single_r + from_y[:, 1]
    relay_r = swap(relayed_r, XBIT)
    token = yield [relayed_r]
    from_x = after(from_x, token)
    relayed_e = single_e + from_x[:, 1]
    relay_e = swap(relayed_e, YBIT)
    token = yield [relayed_e]
    relay_r, relay_e = after_all((relay_r, relay_e), token)
    totals = [
        jnp.stack([own_r[i] + from_y[i, 0] + relay_r[i], own_e[i] + from_x[i, 0] + relay_e[i]]) for i in range(2)
    ]
    yield from close_units(*totals, core, out)


def close_units(here, away, core, out):
    got = swap(away, Z0)
    token = yield [here, away]
    here = here + after(got, token)
    same, cross = here[:, 0], here[:, 1]
    same_got, cross_got = swap_some(same, (0, Z1)), swap_some(cross, (CORE, CORE | Z1))
    token = yield [same, cross]
    same_got, cross_got = after_all((same_got, cross_got), token)
    out.append(jnp.where(core == 0, same, same_got).astype(F32) + cross_got.astype(F32))
    yield [out[-1]]


def fast_device(
    layer_input,
    first_gain,
    first_shift,
    project_weight,
    project_bias,
    output_weight,
    output_bias,
    second_gain,
    second_shift,
    expand_weight,
    expand_bias,
    reduce_weight,
    reduce_bias,
    picture_start,
    cotangent,
):
    own = lax.axis_index("dp")
    place = lax.axis_index("tensor")
    core = own & 1
    keep = core == (place >> 1)
    own_keep = jnp.stack([own, keep.astype(jnp.int32)]).astype(jnp.int32)
    me = (2 * core + (place & 1)).astype(jnp.int32).reshape(1)
    slopes = head_slopes((place ^ (2 * core)) * 4, 4)

    six = jnp.stack([first_gain, first_shift, output_bias, second_gain, second_shift, reduce_bias])
    turn = jnp.zeros((1,), jnp.int32)
    resid, normed, far, even, odd, ready, vectors_of, head_bias_of, unit_bias_of, *blocks = start(
        layer_input, project_weight, output_weight, expand_weight, reduce_weight,
        small_rows(six, project_bias, expand_bias, own), LAYERS,
    )
    near_mine, far_mine, got_near, got_far = blocks
    small = [(vectors_of[i], head_bias_of[i], unit_bias_of[i]) for i in range(LAYERS)]
    starts = jnp.where(keep, picture_start, redeal(picture_start))[0]
    heads, units = [[] for i in range(LAYERS)], [([], []) for i in range(LAYERS)]
    heads[0] += [even, odd, turn]
    head_tasks, unit_tasks = [None], [task(fetch_units_near(ready, *units[0]))]
    for layer in range(1, LAYERS):
        weights = after_all((project_weight, output_weight, expand_weight, reduce_weight), far_mine)
        head_piece = pack_heads(weights[0][layer], weights[1][layer])
        unit_piece = pack_units(weights[2][layer], weights[3][layer])
        head_tasks.append(task(fetch_heads(head_piece, core, turn, heads[layer])))
        unit_tasks.append(task(fetch_units(unit_piece, core, *units[layer])))
    saved = []
    for layer in range(LAYERS):
        vectors, head_bias, unit_bias = small[layer]
        first, last = layer == 0, layer + 1 == LAYERS
        if not first:
            far = swap(normed, Z0)
            while not heads[layer]:
                advance(normed, head_tasks[layer])
            near_mine, near_other = project(normed, head_bias, heads[layer])
            got_near = swap(near_other, CORE)
            far_mine, far_other = project(after(far, near_mine), head_bias, heads[layer])
            got_far = swap(far_other, CORE)
        pieces = heads[layer]
        made = advance(far_mine, unit_tasks[layer])
        if first:
            made += advance(far_mine, unit_tasks[1])
        blocks = after_all((near_mine, far_mine, got_near, got_far), *made)
        far_mixed, far_send, far_exact, far_log = attend(blocks, 1, slopes, starts, me)
        far_got = swap(far_send, CORE)
        far_part = mix_far(far_mixed, far_got, pieces)
        far_term = swap(far_part, Z0)
        made = advance(far_part, unit_tasks[layer])
        near_blocks = after_all(blocks, far_part, *made)
        near_mixed, near_send, near_exact, near_log = attend(near_blocks, 0, slopes, starts, me)
        near_got = swap(near_send, CORE)
        made = advance(near_mixed, unit_tasks[layer])
        if first:
            made += advance(near_mixed, unit_tasks[1])
        if last:
            cotangent_far = redeal(after(cotangent, near_mixed))
        mid, normed_two, flip_two = mix_near(near_mixed, near_got, after(far_term, near_mixed, *made), resid, vectors, pieces)
        normed_other = swap(flip_two, CORE)
        if last:
            grad, unused, flip_grad = enter(own_keep, cotangent, after(cotangent_far, mid), vectors)
            grad_other = swap(flip_grad, CORE)
            normed_two = after(normed_two, grad)
        if first:
            made = advance(mid, unit_tasks[0])
            advance(mid, unit_tasks[1], head_tasks[1])
            normed_two = after(normed_two, *made)
        hidden, active, near_out, away_out = mlp_forward(turn, normed_two, normed_other, unit_bias, units[layer])
        got_out = swap(away_out, CORE)
        if not last:
            got_out = after(got_out, *advance(near_out, head_tasks[layer + 1]))
        out, following = mlp_close(last, own_keep, near_out, got_out, mid, vectors)
        if not last:
            advance(out, head_tasks[layer + 1])
            advance(out, unit_tasks[layer + 1])
        saved.append((
            resid, normed, far, blocks, (near_exact, far_exact), (near_log, far_log), (near_mixed, far_mixed),
            (near_got, far_got), mid, normed_two, normed_other, hidden, active,
        ))
        resid, normed = out, following
    layer_output = jnp.where(keep, normed, redeal(normed))
    grad = after(grad, normed)
    sums = [None] * LAYERS
    head_grad, unit_grad = ([[] for i in range(LAYERS)] for j in range(2))
    pending = []
    for layer in reversed(range(LAYERS)):
        vectors, pieces = small[layer][0], heads[layer]
        (
            resid, normed, far, blocks, exacts, logs, mixed, mixed_got, mid, normed_two, normed_other, hidden, active,
        ) = saved[layer]
        grad_hidden, unit_sums, near_term, away_term = mlp_backward(turn, grad, grad_other, hidden, units[layer])
        got_term = after(swap(away_term, CORE), *advance(near_term, *pending))
        grad_mid, grad_low, second_sums = mlp_open(near_term, got_term, mid, grad, vectors)
        grad_far = swap(grad_low, Z0)
        first = layer == 0
        reduce_parts = unit_grads("x", grad, grad_other, after(active, grad_low))
        made = advance(reduce_parts[0], *pending)
        near_mine, near_other = unmix(after(grad_low, reduce_parts[0], *made), pieces)
        got_near = swap(near_other, CORE)
        expand_parts = unit_grads("y", normed_two, normed_other, after(grad_hidden, near_mine))
        unit_task = task(reduce_units(reduce_parts, expand_parts, core, unit_grad[layer]))
        advance(None, unit_task)
        advance(None, unit_task)
        far_mine, far_other = unmix(after(grad_far, expand_parts[0]), pieces)
        got_far = swap(far_other, CORE)
        made = advance(far_mine, *pending)
        grads_mixed = after_all((near_mine, far_mine, got_near, got_far), *made)
        mine_0, away_0 = attend_pull(0, blocks, grads_mixed, exacts, logs, slopes, starts, me)
        other_0 = swap(away_0, CORE)
        made = advance(mine_0, unit_task)
        grads_mixed = after_all(grads_mixed, mine_0, *made)
        mine_1, away_1 = attend_pull(1, blocks, grads_mixed, exacts, logs, slopes, starts, me)
        other_1 = swap(away_1, CORE)
        other_1 = after(other_1, *advance(mine_1, unit_task))
        mine, other = (mine_0, mine_1), (other_0, other_1)
        far_part = unproject_far(mine, other, pieces)
        far_term = swap(far_part, Z0)
        even, odd, head_sums = head_grads(
            turn, normed, far, grad_low, after(grad_far, far_part), mine, other, mixed, mixed_got
        )
        head_task = task(reduce_heads(even, odd, core, head_grad[layer]))
        advance(None, head_task)
        made = advance(head_sums, unit_task)
        grad, grad_low, first_sums = unproject_near(
            first, own_keep, mine, other, after(far_term, *made), resid, grad_mid, vectors, pieces
        )
        sums[layer] = (first_sums, second_sums, unit_sums, head_sums)
        if not first:
            grad_other = swap(grad_low, CORE)
            grad = after(grad, *advance(grad, head_task))
        pending = [unit_task, head_task]
    input_far = redeal(grad_low)
    made = advance(grad, *pending)
    six, unit_sum, head_sum = sum_small(sums, own, own_keep, made[0])
    while len(head_grad[0]) + len(unit_grad[0]) < 2:
        advance(grad, *pending)
    input_grad = jnp.where(keep, grad_low, input_far)
    return (
        layer_output,
        input_grad,
        six[:, 0],
        six[:, 1],
        jnp.stack([g[0][0] for g in head_grad]),
        head_sum,
        jnp.stack([g[0][1] for g in head_grad]),
        six[:, 2],
        six[:, 3],
        six[:, 4],
        jnp.stack([g[0][1] for g in unit_grad]),
        unit_sum,
        jnp.stack([g[0][0].T for g in unit_grad]),
        six[:, 5],
    )


def solution(mesh):
    placed = (
        P(("dp", "tensor"), None),
        P(None, "dp"),
        P(None, "dp"),
        P(None, None, "dp", "tensor"),
        P(None, None, ("tensor", "dp")),
        P(None, "tensor", "dp"),
        P(None, "dp"),
        P(None, "dp"),
        P(None, "dp"),
        P(None, "dp", "tensor"),
        P(None, ("tensor", "dp")),
        P(None, "tensor", "dp"),
        P(None, "dp"),
        P("dp", None),
        P(("dp", "tensor"), None),
    )
    return jax.shard_map(
        fast_device if mesh_is_paired(mesh) else on_device,
        mesh=mesh,
        in_specs=placed,
        out_specs=(
            P(("dp", "tensor"), None),
            P(("dp", "tensor"), None),
            P(None, "dp"),
            P(None, "dp"),
            P(None, None, "dp", "tensor"),
            P(None, None, ("tensor", "dp")),
            P(None, "tensor", "dp"),
            P(None, "dp"),
            P(None, "dp"),
            P(None, "dp"),
            P(None, "dp", "tensor"),
            P(None, ("tensor", "dp")),
            P(None, "tensor", "dp"),
            P(None, "dp"),
        ),
        check_vma=False,
    )
```

```python
import functools

import jax
import jax.numpy as jnp
from jax import lax
from jax.experimental import pallas as pl
from jax.experimental.pallas import tpu as pltpu
from jax.sharding import PartitionSpec as P

HEADS = 16
HD = 64
LAYERS = 2
SEQ_LEN = 2048
PIECE = 256


NORM_EPS = 1e-05


def layer_norm(values, gain, shift):
    centred = values - jnp.mean(values, axis=-1, keepdims=True)
    spread = jnp.mean(centred * centred, axis=-1, keepdims=True)
    return centred * lax.rsqrt(spread + NORM_EPS) * gain + shift


def gelu_tanh(values):
    return jax.nn.gelu(values, approximate=True)


def piece_numbers(starts):
    places = jnp.arange(SEQ_LEN, dtype=jnp.int32)
    inside = (places[:, None] >= starts[None, :]) & (places[:, None] < starts[None, :] + PIECE)
    numbers = jnp.arange(1, starts.shape[0] + 1, dtype=jnp.int32)
    return jnp.sum(jnp.where(inside, numbers[None, :], 0), axis=1)


def head_slopes(first_head, count_heads):
    heads_at = (first_head + jnp.arange(count_heads, dtype=jnp.int32)).astype(jnp.float32)
    return jnp.exp2(-8.0 * (heads_at + 1.0) / HEADS)


def gather_rows(values):
    return lax.all_gather(values, "tensor", axis=0, tiled=True)


def gather_grads(values):
    return lax.all_gather(values, "tensor", axis=0, tiled=True)


def scatter_rows(values, weight):
    rows_here = values.shape[0] // lax.axis_size("tensor")

    def partial_term(offset, count_rows):
        return jnp.dot(values, weight, preferred_element_type=jnp.float32)

    return lax.psum_scatter(
        partial_term(jnp.int32(0), rows_here * lax.axis_size("tensor")).astype(jnp.bfloat16),
        "tensor",
        scatter_dimension=0,
        tiled=True,
    ).astype(jnp.float32)


def scatter_back(partial_term, rows_here):
    return lax.psum_scatter(
        partial_term(jnp.int32(0), rows_here * lax.axis_size("tensor")).astype(jnp.bfloat16),
        "tensor",
        scatter_dimension=0,
        tiled=True,
    ).astype(jnp.float32)


def block_scores(query_block, key_rows, offset, piece_ids, slopes):
    length = key_rows.shape[0]
    count_rows = query_block.shape[0]
    query_places = offset + jnp.arange(count_rows, dtype=jnp.int32)
    key_places = jnp.arange(length, dtype=jnp.int32)
    product = jnp.einsum("qhe,khe->hqk", query_block, key_rows, preferred_element_type=jnp.float32)
    distance = jnp.abs(query_places[:, None] - key_places[None, :]).astype(jnp.float32)
    scores = product * HD ** (-0.5) - slopes[:, None, None] * distance[None]
    query_pieces = lax.dynamic_slice_in_dim(piece_ids, offset, count_rows, 0)
    allowed = (key_places[None, :] <= query_places[:, None]) | (
        query_pieces[:, None] == piece_ids[None, :]
    ) & (query_pieces[:, None] > 0)
    return jnp.where(allowed[None], scores, -jnp.inf)


def sequence_forward(operands, slopes):
    queries, key_rows, value_rows, piece_ids = operands
    length = queries.shape[0]
    block_rows = min(512, length)

    def one_block(block_index):
        offset = block_index * block_rows
        query_block = lax.dynamic_slice_in_dim(queries, offset, block_rows, 0)
        scores = block_scores(query_block, key_rows, offset, piece_ids, slopes)
        row_max = jnp.max(scores, axis=-1, keepdims=True)
        raw_weights = jnp.exp(scores - row_max)
        totals = jnp.sum(raw_weights, axis=-1, keepdims=True)
        soft_weights = (raw_weights / totals).astype(jnp.bfloat16)
        attended = jnp.einsum(
            "hqk,khe->qhe", soft_weights, value_rows, preferred_element_type=jnp.float32
        )
        return (attended.astype(jnp.bfloat16), (row_max + jnp.log(totals))[..., 0])

    attended, log_total = lax.map(one_block, jnp.arange(length // block_rows, dtype=jnp.int32))
    return (attended.reshape(length, queries.shape[1], queries.shape[2]), log_total)


def sequence_backward(operands, slopes):
    queries, key_rows, value_rows, piece_ids, grad_mixed, log_total = operands
    length = queries.shape[0]
    block_rows = min(512, length)

    def one_block(carry, block_index):
        key_grad, value_grad = carry
        offset = block_index * block_rows
        query_block = lax.dynamic_slice_in_dim(queries, offset, block_rows, 0)
        grad_block = lax.dynamic_slice_in_dim(grad_mixed, offset, block_rows, 0)
        scores = block_scores(query_block, key_rows, offset, piece_ids, slopes)
        probs = jnp.exp(scores - log_total[block_index][..., None])
        soft_weights = probs.astype(jnp.bfloat16)
        value_grad = value_grad + jnp.einsum(
            "hqk,qhe->khe", soft_weights, grad_block, preferred_element_type=jnp.float32
        )
        prob_grad = jnp.einsum(
            "qhe,khe->hqk", grad_block, value_rows, preferred_element_type=jnp.float32
        )
        centred = jnp.sum(probs * prob_grad, axis=-1, keepdims=True)
        score_grad = (probs * (prob_grad - centred) * HD ** (-0.5)).astype(jnp.bfloat16)
        query_grad = jnp.einsum(
            "hqk,khe->qhe", score_grad, key_rows, preferred_element_type=jnp.float32
        )
        key_grad = key_grad + jnp.einsum(
            "hqk,qhe->khe", score_grad, query_block, preferred_element_type=jnp.float32
        )
        return ((key_grad, value_grad), query_grad)

    empty = jnp.zeros(queries.shape, jnp.float32)
    (key_grad, value_grad), query_grad = lax.scan(
        one_block, (empty, empty), jnp.arange(length // block_rows, dtype=jnp.int32)
    )
    return (query_grad.reshape(queries.shape), key_grad, value_grad)


def attend_forward(triple, piece_ids, slopes):
    width = triple.shape[2]
    count_seq = piece_ids.shape[0]
    length = piece_ids.shape[1]
    shaped = triple.reshape(3, count_seq, length, width // HD, HD)
    attended, log_total = lax.map(
        lambda operands: sequence_forward(operands, slopes),
        (shaped[0], shaped[1], shaped[2], piece_ids),
    )
    return (attended.reshape(count_seq * length, width), log_total)


def attend_backward(triple, grad_attended, log_total, piece_ids, slopes):
    width = triple.shape[2]
    count_seq = piece_ids.shape[0]
    length = piece_ids.shape[1]
    shaped = triple.reshape(3, count_seq, length, width // HD, HD)
    grad_shaped = grad_attended.reshape(count_seq, length, width // HD, HD)
    query_grad, key_grad, value_grad = lax.map(
        lambda operands: sequence_backward(operands, slopes),
        (shaped[0], shaped[1], shaped[2], piece_ids, grad_shaped, log_total),
    )
    return (
        query_grad.reshape(-1, width),
        key_grad.reshape(-1, width),
        value_grad.reshape(-1, width),
    )


def fetch_layer(
    project_weight,
    project_bias,
    output_weight,
    expand_weight,
    expand_bias,
    reduce_weight,
    small_stack,
    layer_index,
):
    return (
        lax.all_gather(project_weight[layer_index], "dp", axis=1, tiled=True),
        lax.all_gather(project_bias[layer_index], "dp", axis=1, tiled=True),
        lax.all_gather(output_weight[layer_index], "dp", axis=1, tiled=True),
        lax.all_gather(expand_weight[layer_index], "dp", axis=0, tiled=True),
        lax.all_gather(expand_bias[layer_index], "dp", axis=0, tiled=True),
        lax.all_gather(reduce_weight[layer_index], "dp", axis=1, tiled=True),
        lax.all_gather(small_stack[layer_index], "dp", axis=1, tiled=True),
    )


def forward_layer(resid, weights, piece_ids, slopes):
    w_project, bias_project, w_output, w_expand, bias_expand, w_reduce, small = weights
    vectors = small.astype(jnp.float32)
    normed = layer_norm(resid, vectors[0], vectors[1])
    gathered = gather_rows(normed.astype(jnp.bfloat16))
    product = jnp.einsum("gd,cde->cge", gathered, w_project, preferred_element_type=jnp.float32)
    biases = jnp.stack([bias_project[0], jnp.zeros_like(bias_project[0]), bias_project[1]]).astype(
        jnp.float32
    )
    triple = (product + biases[:, None, :]).astype(jnp.bfloat16)
    attended, log_total = attend_forward(triple, piece_ids, slopes)
    resid_mid = resid + (scatter_rows(attended, w_output) + vectors[2])
    normed_two = layer_norm(resid_mid, vectors[3], vectors[4])
    gathered_two = gather_rows(normed_two.astype(jnp.bfloat16))
    hidden = jnp.dot(
        gathered_two, w_expand, preferred_element_type=jnp.float32
    ) + bias_expand.astype(jnp.float32)
    active = gelu_tanh(hidden).astype(jnp.bfloat16)
    mlp_sum = scatter_rows(active, w_reduce)
    mlp_keep = (gathered_two, hidden, None)
    resid_out = resid_mid + (mlp_sum + vectors[5])
    return (resid_out, (gathered, triple, attended, log_total, resid_mid, mlp_keep))


def backward_layer(grad_out, resid, weights, kept, piece_ids, slopes):
    w_project, bias_project, w_output, w_expand, bias_expand, w_reduce, small = weights
    vectors = small.astype(jnp.float32)
    gathered, triple, attended, log_total, resid_mid, mlp_keep = kept
    rows_here = grad_out.shape[0]
    rows_in, hidden, full_weights = mlp_keep
    grad_bias_reduce = jnp.sum(grad_out, axis=0)
    active, gelu_pull = jax.vjp(gelu_tanh, hidden)
    active_low = active.astype(jnp.bfloat16)
    grad_mlp = gather_grads(grad_out.astype(jnp.bfloat16))
    grad_reduce = jnp.einsum("gf,gd->fd", active_low, grad_mlp, preferred_element_type=jnp.float32)
    grad_active = jnp.einsum("gd,fd->gf", grad_mlp, w_reduce, preferred_element_type=jnp.float32)
    (grad_hidden,) = gelu_pull(grad_active)
    grad_bias_expand = jnp.sum(grad_hidden, axis=0)
    grad_hidden_low = grad_hidden.astype(jnp.bfloat16)
    grad_expand = jnp.einsum(
        "gd,gf->df", rows_in, grad_hidden_low, preferred_element_type=jnp.float32
    )

    def expand_term(offset, count_rows):
        return jnp.einsum(
            "gf,df->gd", grad_hidden_low, w_expand, preferred_element_type=jnp.float32
        )

    grad_normed_two = scatter_back(expand_term, rows_here)
    unused_two, second_pull = jax.vjp(layer_norm, resid_mid, vectors[3], vectors[4])
    grad_from_norm, grad_gain_two, grad_shift_two = second_pull(grad_normed_two)
    grad_mid = grad_out + grad_from_norm
    grad_bias_output = jnp.sum(grad_mid, axis=0)
    grad_attn = gather_grads(grad_mid.astype(jnp.bfloat16))
    grad_output = jnp.einsum("gt,gd->td", attended, grad_attn, preferred_element_type=jnp.float32)
    grad_attended = jnp.einsum(
        "gd,td->gt", grad_attn, w_output, preferred_element_type=jnp.float32
    ).astype(jnp.bfloat16)
    query_grad, key_grad, value_grad = attend_backward(
        triple, grad_attended, log_total, piece_ids, slopes
    )
    grad_bias_project = jnp.stack([jnp.sum(query_grad, axis=0), jnp.sum(value_grad, axis=0)])
    grad_triple = jnp.stack([query_grad, key_grad, value_grad]).astype(jnp.bfloat16)
    grad_project = jnp.einsum(
        "gd,cge->cde", gathered, grad_triple, preferred_element_type=jnp.float32
    )

    def project_term(offset, count_rows):
        return jnp.einsum("cge,cde->gd", grad_triple, w_project, preferred_element_type=jnp.float32)

    grad_normed = scatter_back(project_term, rows_here)
    unused_one, first_pull = jax.vjp(layer_norm, resid, vectors[0], vectors[1])
    grad_from_first, grad_gain_one, grad_shift_one = first_pull(grad_normed)
    grad_stream = grad_mid + grad_from_first
    small_grads = jnp.stack(
        [
            grad_gain_one,
            grad_shift_one,
            grad_bias_output,
            grad_gain_two,
            grad_shift_two,
            grad_bias_reduce,
        ]
    )
    return (
        grad_stream,
        (
            grad_project,
            grad_bias_project,
            grad_output,
            grad_expand,
            grad_bias_expand,
            grad_reduce,
            small_grads,
        ),
    )


def reduce_layer(layer_grads):
    (
        grad_project,
        grad_bias_project,
        grad_output,
        grad_expand,
        grad_bias_expand,
        grad_reduce,
        small_grads,
    ) = layer_grads
    return (
        lax.psum_scatter(
            grad_project.astype(jnp.bfloat16), "dp", scatter_dimension=1, tiled=True
        ).astype(jnp.float32),
        lax.psum_scatter(
            grad_bias_project.astype(jnp.bfloat16), "dp", scatter_dimension=1, tiled=True
        ).astype(jnp.float32),
        lax.psum_scatter(
            grad_output.astype(jnp.bfloat16), "dp", scatter_dimension=1, tiled=True
        ).astype(jnp.float32),
        lax.psum_scatter(
            grad_expand.astype(jnp.bfloat16), "dp", scatter_dimension=0, tiled=True
        ).astype(jnp.float32),
        lax.psum_scatter(
            grad_bias_expand.astype(jnp.bfloat16), "dp", scatter_dimension=0, tiled=True
        ).astype(jnp.float32),
        lax.psum_scatter(
            grad_reduce.astype(jnp.bfloat16), "dp", scatter_dimension=1, tiled=True
        ).astype(jnp.float32),
        lax.psum_scatter(
            small_grads.astype(jnp.bfloat16), "dp", scatter_dimension=1, tiled=True
        ).astype(jnp.float32),
    )


def on_device(
    layer_input,
    first_gain,
    first_shift,
    project_weight,
    project_bias,
    output_weight,
    output_bias,
    second_gain,
    second_shift,
    expand_weight,
    expand_bias,
    reduce_weight,
    reduce_bias,
    picture_start,
    cotangent,
):
    small_stack = jnp.stack(
        [first_gain, first_shift, output_bias, second_gain, second_shift, reduce_bias], axis=1
    )
    piece_ids = jax.vmap(piece_numbers)(picture_start)
    heads_here = project_weight.shape[3] // HD
    slopes = head_slopes(lax.axis_index("tensor") * heads_here, heads_here)
    resid = layer_input.astype(jnp.float32)
    saved = []
    for layer_index in range(LAYERS):
        weights = fetch_layer(
            project_weight,
            project_bias,
            output_weight,
            expand_weight,
            expand_bias,
            reduce_weight,
            small_stack,
            layer_index,
        )
        resid_next, kept = forward_layer(resid, weights, piece_ids, slopes)
        saved.append((resid, weights, kept))
        resid = resid_next
    layer_output = resid.astype(jnp.bfloat16)
    grad_stream = cotangent.astype(jnp.float32)
    collected = []
    for layer_index in reversed(range(LAYERS)):
        resid_in, weights, kept = saved[layer_index]
        grad_stream, layer_grads = backward_layer(
            grad_stream, resid_in, weights, kept, piece_ids, slopes
        )
        layer_grads = reduce_layer(layer_grads)
        collected.insert(0, layer_grads)
    stacked = tuple(
        (jnp.stack([grad_entry[member] for grad_entry in collected]) for member in range(7))
    )
    (
        grad_project,
        grad_bias_project,
        grad_output,
        grad_expand,
        grad_bias_expand,
        grad_reduce,
        small_grads,
    ) = stacked
    small_grads = lax.psum(small_grads, "tensor")
    return (
        layer_output,
        grad_stream.astype(jnp.bfloat16),
        small_grads[:, 0],
        small_grads[:, 1],
        grad_project,
        grad_bias_project,
        grad_output,
        small_grads[:, 2],
        small_grads[:, 3],
        small_grads[:, 4],
        grad_expand,
        grad_bias_expand,
        grad_reduce,
        small_grads[:, 5],
    )


Z0, Z1, CORE, XBIT, YBIT = 1, 2, 4, 8, 16
AXES = ("dp", "tensor")
NEG = -1e30
BF = jnp.bfloat16
F32 = jnp.float32
VMEM_LIMIT = 24 * 1024 * 1024


def took(us):
    return pl.CostEstimate(flops=int(us * 5e8), bytes_accessed=1, transcendentals=0)


def mesh_is_paired(mesh):
    return dict(mesh.shape) == {"dp": 8, "tensor": 4}


def swap(values, mask):
    return lax.ppermute(values, AXES, [(i, i ^ mask) for i in range(32)])


def swap_some(values, masks):
    pairs = [(i, i ^ masks[(i >> 2) & 1]) for i in range(32)]
    return lax.ppermute(values, AXES, [pair for pair in pairs if pair[0] != pair[1]])


def redeal(values):
    def target(i):
        core, z1 = (i >> 2) & 1, (i >> 1) & 1
        return (i & ~6) | (z1 << 2) | (core << 1)

    return lax.ppermute(values, AXES, [(i, target(i)) for i in range(32) if target(i) != i])


CHIPS = [[0, 2, 4, 6], [1, 3, 5, 7]]


def plane_gather(values):
    return lax.all_gather(values, "dp", axis_index_groups=CHIPS, axis=0, tiled=False)


def plane_scatter(values):
    return lax.psum_scatter(values, "dp", axis_index_groups=CHIPS, scatter_dimension=0, tiled=False)


def turn_index(values, own):
    shape = values.shape
    for bit in range(3):
        values = values.reshape(8 >> (bit + 1), 2, (1 << bit), *shape[1:])
        values = jnp.where((own >> bit) & 1, jnp.concatenate([values[:, 1:], values[:, :1]], axis=1), values)
    return values.reshape(shape)


def after(values, *others):
    return lax.optimization_barrier((values, *others))[0]


def after_all(values, *others):
    if not others:
        return tuple(values)
    return lax.optimization_barrier((*values, *others))[:len(values)]


def task(steps):
    next(steps)
    return steps


def advance(token, *tasks):
    made = []
    for steps in tasks:
        try:
            made += steps.send(token)
        except StopIteration:
            pass
    return made


def dot_nt(a, b):
    return lax.dot_general(a, b, (((1,), (1,)), ((), ())), preferred_element_type=F32)


def dot_nn(a, b):
    return lax.dot_general(a, b, (((1,), (0,)), ((), ())), preferred_element_type=F32)


def head_mask(shape, head):
    lane = lax.broadcasted_iota(jnp.int32, shape, 1)
    return (lane < HD) if head == 0 else (lane >= HD)


def diagonal_bias(rows, columns, first_row, first_column, start):
    key = first_row + lax.broadcasted_iota(jnp.int32, (rows, 1), 0)
    query = first_column + lax.broadcasted_iota(jnp.int32, (1, columns), 1)
    key_in = (key >= start) & (key < start + PIECE)
    query_in = (query >= start) & (query < start + PIECE)
    allowed = (key <= query) | (key_in & query_in)
    reach = (jnp.minimum(key, 2 * query - key) - first_column).astype(F32)
    return jnp.where(allowed, reach, NEG)


def ramp(rows, first_row, first_column):
    return (first_row - first_column + lax.broadcasted_iota(jnp.int32, (rows, 1), 0)).astype(F32)


def attend_kernel(block, rest_bit, slope_ref, start_ref, me_ref, *rest):
    triple_refs, rest = rest[:12], rest[12:]
    near_ref, away_ref, exact_ref, lse_ref, q_ref, k_ref, v_ref, vt_ref, acc_ref, max_ref, bias_ref, tail_ref = rest
    pair = pl.program_id(0)
    turn = pl.program_id(1)
    me = me_ref[0]
    step = (2 * turn + rest_bit) ^ me
    length = k_ref.shape[0]
    first = step * block

    def at(index):
        return pl.multiple_of((index ^ me) * block, block)

    start = start_ref[first // (length // start_ref.shape[0])]

    @pl.when(turn == 0)
    def _():
        for index in range(4):
            here = slice(index * block, (index + 1) * block)
            q_ref[here, :] = triple_refs[3 * index][...] * jnp.asarray(HD ** -0.5, BF)
            k_ref[here, :] = triple_refs[3 * index + 1][...]
            v_ref[here, :] = triple_refs[3 * index + 2][...]
        for head in range(2):
            mixed = jnp.where(head_mask((length, 2 * HD), head), v_ref[...], jnp.ones((), BF))
            vt_ref[head] = mixed.T

    bias_ref[...] = diagonal_bias(block, block, first, first, start)
    q_block = q_ref[pl.ds(at(step), block), :]
    heads = [jnp.where(head_mask(q_block.shape, head), q_block, jnp.zeros((), BF)) for head in range(2)]
    slopes = [slope_ref[2 * pair + head] for head in range(2)]
    acc_ref[...] = jnp.zeros_like(acc_ref)
    max_ref[...] = jnp.full_like(max_ref, NEG)

    def absorb(head, scores, vt):
        old = max_ref[head]
        new = jnp.maximum(old, jnp.max(scores, axis=0, keepdims=True))
        weights = jnp.exp(scores - new).astype(BF)
        acc_ref[head] = acc_ref[head] * jnp.exp(old - new) + dot_nn(vt, weights)
        max_ref[head] = new

    def full(index, carry):
        place = at(index)
        keys = k_ref[pl.ds(place, block), :]
        slant = ramp(block, index * block, first)
        for head in range(2):
            absorb(head, dot_nt(keys, heads[head]) + slopes[head] * slant, vt_ref[head, :, pl.ds(place, block)])
        return carry

    place = at(step)
    for head in range(2):
        absorb(
            head,
            dot_nt(k_ref[pl.ds(place, block), :], heads[head]) + slopes[head] * bias_ref[...],
            vt_ref[head, :, pl.ds(place, block)],
        )
    lax.fori_loop(0, step, full, 0)
    edge = first + block

    @pl.when((start < edge) & (start + PIECE > edge))
    def _():
        after = at(step + 1)
        tail_ref[...] = diagonal_bias(PIECE, block, edge, first, start)
        for head in range(2):
            absorb(
                head,
                dot_nt(k_ref[pl.ds(after, PIECE), :], heads[head]) + slopes[head] * tail_ref[...],
                vt_ref[head, :, pl.ds(after, PIECE)],
            )

    outs = []
    for head in range(2):
        acc = acc_ref[head]
        total = acc[HD:HD + 1] if head == 0 else acc[0:1]
        outs.append((acc * (1.0 / total))[head * HD:(head + 1) * HD])
        lse_ref[0, head:head + 1, :] = max_ref[head] + jnp.log(total)
    mixed = jnp.concatenate(outs, axis=0)
    exact_ref[...] = mixed
    final = mixed.T.astype(BF)

    @pl.when(turn == 0)
    def _():
        near_ref[...] = final

    @pl.when(turn == 1)
    def _():
        away_ref[...] = final


def triple_specs(block, pairs):
    specs = []
    for index in range(4):
        for part in range(3):
            specs.append(pl.BlockSpec((block, 2 * HD), functools.partial(lambda part, p, i: (0, part * pairs + p), part)))
    return specs


def attend(blocks, rest_bit, slopes, starts, me):
    block, width = blocks[0].shape[0], blocks[0].shape[1] // 3
    pairs = width // (2 * HD)
    length = 4 * block
    smem = pl.BlockSpec(memory_space=pltpu.SMEM)
    return pl.pallas_call(
        functools.partial(attend_kernel, block, rest_bit),
        grid=(pairs, 2),
        in_specs=[smem, smem, smem] + triple_specs(block, pairs),
        out_specs=[
            pl.BlockSpec((block, 2 * HD), lambda p, i: (0, p)),
            pl.BlockSpec((block, 2 * HD), lambda p, i: (0, p)),
            pl.BlockSpec((2 * HD, block), lambda p, i: (p, i)),
            pl.BlockSpec((1, 8, block), lambda p, i: (p, 0, i)),
        ],
        out_shape=[
            jax.ShapeDtypeStruct((block, width), BF),
            jax.ShapeDtypeStruct((block, width), BF),
            jax.ShapeDtypeStruct((width, 2 * block), F32),
            jax.ShapeDtypeStruct((pairs, 8, 2 * block), F32),
        ],
        scratch_shapes=[
            pltpu.VMEM((length, 2 * HD), BF),
            pltpu.VMEM((length, 2 * HD), BF),
            pltpu.VMEM((length, 2 * HD), BF),
            pltpu.VMEM((2, 2 * HD, length), BF),
            pltpu.VMEM((2, 2 * HD, block), F32),
            pltpu.VMEM((2, 1, block), F32),
            pltpu.VMEM((block, block), F32),
            pltpu.VMEM((PIECE, block), F32),
        ],
        compiler_params=pltpu.CompilerParams(vmem_limit_bytes=VMEM_LIMIT),
        cost_estimate=took(17),
        name="attend",
    )(slopes, starts, me, *[b for b in blocks for _ in range(3)])


def pull_kernel(block, pair, slope_ref, start_ref, me_ref, *rest):
    triple_refs, grad_refs, rest = rest[:12], rest[12:16], rest[16:]
    exact_refs, lse_refs, rest = rest[0:2], rest[2:4], rest[4:]
    mine_ref, away_ref, q_ref, k_ref, v_ref, g_ref, kt_ref, dk_acc, dv_acc, dqt_ref, bias_ref, tail_ref = rest
    turn = pl.program_id(0)
    me = me_ref[0]
    step = turn ^ me
    length = k_ref.shape[0]
    first = step * block
    half, bit = turn // 2, turn % 2

    def at(index):
        return pl.multiple_of((index ^ me) * block, block)

    start = start_ref[first // (length // start_ref.shape[0])]

    @pl.when(turn == 0)
    def _():
        for index in range(4):
            here = slice(index * block, (index + 1) * block)
            q_ref[here, :] = triple_refs[3 * index][...] * jnp.asarray(HD ** -0.5, BF)
            k_ref[here, :] = triple_refs[3 * index + 1][...]
            v_ref[here, :] = triple_refs[3 * index + 2][...]
            g_ref[here, :] = grad_refs[index][...]
        kt_ref[...] = k_ref[...].T
        dk_acc[...] = jnp.zeros_like(dk_acc)
        dv_acc[...] = jnp.zeros_like(dv_acc)

    bias_ref[...] = diagonal_bias(block, block, first, first, start)
    dqt_ref[...] = jnp.zeros_like(dqt_ref)
    zero = jnp.zeros((), BF)
    q_block = q_ref[pl.ds(at(step), block), :]
    g_block = g_ref[pl.ds(at(step), block), :]
    masks = [head_mask(q_block.shape, head) for head in range(2)]
    q_heads = [jnp.where(mask, q_block, zero) for mask in masks]
    g_heads = [jnp.where(mask, g_block, zero) for mask in masks]
    slopes = [slope_ref[2 * pair + head] for head in range(2)]
    lanes = pl.ds(pl.multiple_of(half * block, block), block)
    exact = jnp.where(bit == 0, exact_refs[0][:, lanes], exact_refs[1][:, lanes])
    log_total = jnp.where(bit == 0, lse_refs[0][0, :, lanes], lse_refs[1][0, :, lanes])
    product = g_block.astype(F32).T * exact
    deltas = [jnp.sum(product[head * HD:(head + 1) * HD], axis=0, keepdims=True) for head in range(2)]

    def absorb(place, rows, bias_of):
        keys = k_ref[pl.ds(place, rows), :]
        values = v_ref[pl.ds(place, rows), :]
        dk = dk_acc[pl.ds(place, rows), :]
        dv = dv_acc[pl.ds(place, rows), :]
        for head in range(2):
            scores = dot_nt(keys, q_heads[head]) + slopes[head] * bias_of
            weights = jnp.exp(scores - log_total[head:head + 1, :])
            dv = dv + dot_nn(weights.astype(BF), g_heads[head])
            grad_p = dot_nt(values, g_heads[head])
            grad_s = (weights * (grad_p - deltas[head])).astype(BF)
            dk = dk + dot_nn(grad_s, q_heads[head])
            dqt_ref[head * HD:(head + 1) * HD, :] += dot_nn(kt_ref[head * HD:(head + 1) * HD, pl.ds(place, rows)], grad_s)
        dk_acc[pl.ds(place, rows), :] = dk
        dv_acc[pl.ds(place, rows), :] = dv

    absorb(at(step), block, bias_ref[...])

    def full(index, carry):
        absorb(at(index), block, ramp(block, index * block, first))
        return carry

    lax.fori_loop(0, step, full, 0)
    edge = first + block

    @pl.when((start < edge) & (start + PIECE > edge))
    def _():
        tail_ref[...] = diagonal_bias(PIECE, block, edge, first, start)
        absorb(at(step + 1), PIECE, tail_ref[...])

    grad_q = (dqt_ref[...].T * (HD ** -0.5)).astype(BF)
    here = pl.ds(pl.multiple_of(bit * block, block), block)

    @pl.when(half == 0)
    def _():
        mine_ref[0, here, :] = grad_q

    @pl.when(half == 1)
    def _():
        away_ref[0, here, :] = grad_q

    @pl.when(turn == 3)
    def _():
        for part, ref in ((1, dk_acc), (2, dv_acc)):
            mine_ref[part] = ref[:2 * block].astype(BF)
            away_ref[part] = ref[2 * block:].astype(BF)


def attend_pull(pair, blocks, grads, exacts, log_totals, slopes, starts, me):
    block, width = blocks[0].shape[0], blocks[0].shape[1] // 3
    pairs = width // (2 * HD)
    length = 4 * block
    smem = pl.BlockSpec(memory_space=pltpu.SMEM)
    triples = [pl.BlockSpec((block, 2 * HD), functools.partial(lambda part, i: (0, part * pairs + pair), part)) for part in range(3)]
    rows = pl.BlockSpec((block, 2 * HD), lambda i: (0, pair))
    wide = pl.BlockSpec((2 * HD, 2 * block), lambda i: (pair, 0))
    sums = pl.BlockSpec((1, 8, 2 * block), lambda i: (pair, 0, 0))
    out = pl.BlockSpec((3, 2 * block, 2 * HD), lambda i: (0, 0, 0))
    return pl.pallas_call(
        functools.partial(pull_kernel, block, pair),
        grid=(4,),
        in_specs=[smem, smem, smem] + triples * 4 + [rows] * 4 + [wide] * 2 + [sums] * 2,
        out_specs=[out, out],
        out_shape=[jax.ShapeDtypeStruct((3, 2 * block, 2 * HD), BF)] * 2,
        scratch_shapes=[
            pltpu.VMEM((length, 2 * HD), BF),
            pltpu.VMEM((length, 2 * HD), BF),
            pltpu.VMEM((length, 2 * HD), BF),
            pltpu.VMEM((length, 2 * HD), BF),
            pltpu.VMEM((2 * HD, length), BF),
            pltpu.VMEM((length, 2 * HD), F32),
            pltpu.VMEM((length, 2 * HD), F32),
            pltpu.VMEM((2 * HD, block), F32),
            pltpu.VMEM((block, block), F32),
            pltpu.VMEM((PIECE, block), F32),
        ],
        compiler_params=pltpu.CompilerParams(vmem_limit_bytes=VMEM_LIMIT),
        cost_estimate=took(22),
        name="attend_pull",
    )(slopes, starts, me, *[b for b in blocks for _ in range(3)], *grads, *exacts, *log_totals)


def head_columns(refs, quarter, first, last):
    return jnp.concatenate(
        [refs[odd][chip ^ refs[2][0], 1 - quarter if odd else quarter, :, first:last] for chip in range(4) for odd in range(2)],
        axis=0,
    )


def placed(arrays):
    return [
        pl.BlockSpec(memory_space=pltpu.SMEM if a.dtype == jnp.int32 else pltpu.VMEM) for a in arrays
    ]


def call_once(kernel, name, outs, args, us):
    return pl.pallas_call(
        kernel,
        in_specs=placed(args),
        out_specs=placed(outs),
        out_shape=outs,
        compiler_params=pltpu.CompilerParams(vmem_limit_bytes=VMEM_LIMIT),
        cost_estimate=took(us),
        name=name,
    )(*args)


def project_kernel(rows_ref, bias_ref, *rest):
    weight_refs, out_refs = rest[:3], rest[3:]
    rows = rows_ref[...]
    for quarter in (1, 0):
        out = dot_nn(rows, head_columns(weight_refs, quarter, 0, 768)) + bias_ref[quarter:quarter + 1]
        out_refs[quarter][...] = out.astype(BF)


def project(rows, bias, pieces):
    out = jax.ShapeDtypeStruct((rows.shape[0], 768), BF)
    return call_once(project_kernel, "project", [out, out], [rows, bias, *pieces], 5)


def mix_term(mixed_refs, weight_refs):
    rows = jnp.concatenate([ref[...] for ref in mixed_refs], axis=1)
    weight = jnp.concatenate([head_columns(weight_refs, quarter, 768, 1024) for quarter in range(2)], axis=1)
    return dot_nt(rows, weight)


def mix_far_kernel(mine_ref, other_ref, *rest):
    rest[3][...] = mix_term((mine_ref, other_ref), rest[:3]).astype(BF)


def mix_far(mine, other, pieces):
    out = jax.ShapeDtypeStruct((mine.shape[0], 1024), BF)
    return call_once(mix_far_kernel, "mix_far", [out], [mine, other, *pieces], 4)[0]


def mix_near_kernel(mine_ref, other_ref, far_ref, resid_ref, vector_ref, *rest):
    weight_refs, (mid_ref, normed_ref, flip_ref) = rest[:3], rest[3:]
    term = mix_term((mine_ref, other_ref), weight_refs)
    mid = resid_ref[...] + (term + far_ref[...].astype(F32) + vector_ref[2:3])
    mid_ref[...] = mid
    normed = (normalize(mid)[0] * vector_ref[3:4] + vector_ref[4:5]).astype(BF)
    normed_ref[...] = normed
    flip_ref[...] = flipped(normed)


def mix_near(mine, other, far, resid, vectors, pieces):
    outs = [
        jax.ShapeDtypeStruct(resid.shape, F32),
        jax.ShapeDtypeStruct(resid.shape, BF),
        jax.ShapeDtypeStruct(resid.shape, BF),
    ]
    return call_once(mix_near_kernel, "mix_near", outs, [mine, other, far, resid, vectors, *pieces], 6)


def unmix_kernel(grad_ref, *rest):
    weight_refs, out_refs = rest[:3], rest[3:]
    grad = grad_ref[...]
    for quarter in (1, 0):
        out_refs[quarter][...] = dot_nn(grad, head_columns(weight_refs, quarter, 768, 1024)).astype(BF)


def unmix(grad, pieces):
    out = jax.ShapeDtypeStruct((grad.shape[0], 256), BF)
    return call_once(unmix_kernel, "unmix", [out, out], [grad, *pieces], 4)


def unproject_term(grad_refs, weight_refs, first):
    rows = jnp.concatenate(
        [ref[part, first:first + 512] for pair in grad_refs for part in range(3) for ref in pair], axis=1
    )
    weight = jnp.concatenate([head_columns(weight_refs, quarter, 0, 768) for quarter in range(2)], axis=1)
    return dot_nt(rows, weight)


def unproject_far_kernel(*rest):
    rest[7][...] = unproject_term((rest[0:2], rest[2:4]), rest[4:7], 512).astype(BF)


def unproject_far(mine, other, pieces):
    out = jax.ShapeDtypeStruct((512, 1024), BF)
    return call_once(unproject_far_kernel, "unproject_far", [out], [*mine, *other, *pieces], 6)[0]


def unproject_near_kernel(last, own_ref, *rest):
    mine, other, rest = rest[0:2], rest[2:4], rest[4:]
    far_ref, resid_ref, grad_mid_ref, vector_ref, rest = *rest[:4], rest[4:]
    weight_refs, (grad_ref, low_ref, sums_ref) = rest[:3], rest[3:]
    term = unproject_term((mine, other), weight_refs, 0) + far_ref[...].astype(F32)
    grad_norm, grad_gain, grad_shift = norm_pull(resid_ref[...], vector_ref[0:1], term)
    grad = grad_mid_ref[...] + grad_norm
    grad_ref[...] = grad
    if last:
        put_turned(low_ref, own_ref[0], grad.astype(BF))
    else:
        low_ref[...] = flipped(grad).astype(BF)
    sums_ref[...] = jnp.concatenate([grad_gain, grad_shift, jnp.zeros((6, grad.shape[1]), F32)], axis=0)


def unproject_near(last, own_keep, mine, other, far, resid, grad_mid, vectors, pieces):
    outs = [
        jax.ShapeDtypeStruct(resid.shape, F32),
        jax.ShapeDtypeStruct(resid.shape, BF),
        jax.ShapeDtypeStruct((8, resid.shape[1]), F32),
    ]
    args = [own_keep, *mine, *other, far, resid, grad_mid, vectors, *pieces]
    kernel = functools.partial(unproject_near_kernel, last)
    return call_once(kernel, "unproject_near", outs, args, 9)


def head_grads_kernel(turn_ref, near_ref, far_ref, grad_near_ref, grad_far_ref, *rest):
    pairs, rest = (rest[0:2], rest[2:4]), rest[4:]
    mixed_refs, out_refs, bias_ref = (rest[0:2], rest[2:4]), rest[4:6], rest[6]
    rows_t = jnp.concatenate([near_ref[...], far_ref[...]], axis=0).T
    grad_t = jnp.concatenate([grad_near_ref[...], grad_far_ref[...]], axis=0).T
    for quarter, refs in enumerate(pairs):
        grads = [jnp.concatenate([ref[part] for ref in refs], axis=1) for part in range(3)]
        for part in range(4):
            if part < 3:
                term = dot_nn(rows_t, grads[part])
            else:
                term = dot_nn(grad_t, jnp.concatenate([m[...] for m in mixed_refs[quarter]], axis=0))
            term = term.astype(BF)
            for index in range(8):
                chip, odd = index // 2, index % 2
                place = 1 - quarter if odd else quarter
                out_refs[odd][chip ^ turn_ref[0], place, :, part * 256:(part + 1) * 256] = term[index * 128:(index + 1) * 128]
        for row, part in ((0, 0), (1, 2)):
            total = jnp.sum(grads[part].astype(F32), axis=0, keepdims=True)
            bias_ref[2 * quarter + row:2 * quarter + row + 1, :] = total
    bias_ref[4:8, :] = jnp.zeros((4, 256), F32)


def head_grads(turn, near, far, grad_near, grad_far, mine, other, mixed_mine, mixed_other):
    outs = [jax.ShapeDtypeStruct((4, 2, 128, 1024), BF)] * 2 + [jax.ShapeDtypeStruct((8, 256), F32)]
    args = [turn, near, far, grad_near, grad_far, *mine, *other, *mixed_mine, *mixed_other]
    return call_once(head_grads_kernel, "head_grads", outs, args, 10)


GELU_A = 0.7978845608028654
GELU_B = 0.044715


def normalize(values):
    centred = values - jnp.mean(values, axis=-1, keepdims=True)
    spread = lax.rsqrt(jnp.mean(centred * centred, axis=-1, keepdims=True) + NORM_EPS)
    return centred * spread, spread


def norm_pull(values, gain, grad):
    unit, spread = normalize(values)
    grad_unit = grad * gain
    inner = grad_unit - jnp.mean(grad_unit, axis=-1, keepdims=True)
    inner = inner - unit * jnp.mean(grad_unit * unit, axis=-1, keepdims=True)
    return spread * inner, jnp.sum(grad * unit, axis=0, keepdims=True), jnp.sum(grad, axis=0, keepdims=True)


def flipped(values):
    return jnp.concatenate([values[:, (block ^ 1) * 128:(block ^ 1) * 128 + 128] for block in range(8)], axis=1)


def put_turned(out_ref, own, values):
    for block in range(8):
        here = pl.ds(pl.multiple_of((block ^ own) * 128, 128), 128)
        out_ref[:, here] = values[:, block * 128:(block + 1) * 128]


def enter_kernel(own_ref, direct_ref, moved_ref, vector_ref, resid_ref, normed_ref, flip_ref):
    own, keep = own_ref[0], own_ref[1]
    for block in range(8):
        here = pl.ds(pl.multiple_of((block ^ own) * 128, 128), 128)
        rows = jnp.where(keep > 0, direct_ref[:, here].astype(F32), moved_ref[:, here].astype(F32))
        resid_ref[:, block * 128:(block + 1) * 128] = rows
    values = resid_ref[...]
    normed_ref[...] = (normalize(values)[0] * vector_ref[0:1] + vector_ref[1:2]).astype(BF)
    flip_ref[...] = flipped(values).astype(BF)


def enter(own_keep, direct, moved, vectors):
    rows, features = direct.shape
    smem = pl.BlockSpec(memory_space=pltpu.SMEM)
    vmem = pl.BlockSpec(memory_space=pltpu.VMEM)
    return pl.pallas_call(
        enter_kernel,
        in_specs=[smem, vmem, vmem, vmem],
        out_specs=[vmem, vmem, vmem],
        out_shape=[
            jax.ShapeDtypeStruct((rows, features), F32),
            jax.ShapeDtypeStruct((rows, features), BF),
            jax.ShapeDtypeStruct((rows, features), BF),
        ],
        compiler_params=pltpu.CompilerParams(vmem_limit_bytes=VMEM_LIMIT),
        cost_estimate=took(4),
        name="enter",
    )(own_keep, direct, moved, vectors)


def half_specs(tile, weights):
    def spec(half, chip, whole):
        def index(f, turn):
            column = jnp.clip(f - 2 * half, 0, 1)
            return (chip ^ turn[0], 0, 0, column) if whole else (0, 0, column)

        return pl.BlockSpec((None, 2, 128, 2 * tile) if whole else (2, 128, 2 * tile), index)

    return [spec(half, chip, len(weights[half]) == 1) for half in range(2) for chip in range(4)]


def half_arrays(weights):
    return [array for half in weights for array in (half if len(half) == 4 else half * 4)]


def by_half(step, weight_refs, body):
    @pl.when(step < 2)
    def _():
        body(weight_refs[:4])

    @pl.when(step >= 2)
    def _():
        body(weight_refs[4:])


def joined(refs, first, last):
    return jnp.concatenate([ref[core, :, first:last] for ref in refs for core in range(2)], axis=0)


def mlp_kernel(turn_ref, normed_ref, other_ref, bias_ref, *rest):
    weight_refs, (hidden_ref, active_ref, near_ref, away_ref, acc_ref) = rest[:8], rest[8:]
    rows, tile = normed_ref.shape[0], hidden_ref.shape[1]
    step = pl.program_id(0)

    @pl.when(step == 0)
    def _():
        acc_ref[...] = jnp.zeros_like(acc_ref)

    def body(refs):
        expand, reduce = joined(refs, 0, tile), joined(refs, tile, 2 * tile)
        for first, ref in ((0, normed_ref), (rows, other_ref)):
            hidden = dot_nn(ref[...], expand) + bias_ref[...]
            inner = jnp.tanh(GELU_A * (hidden + GELU_B * hidden * hidden * hidden))
            active = (0.5 * hidden * (1.0 + inner)).astype(BF)
            hidden_ref[first:first + rows] = hidden.astype(BF)
            active_ref[first:first + rows] = active
            acc_ref[first:first + rows] += dot_nt(active, reduce)

    by_half(step, weight_refs, body)

    @pl.when(step == pl.num_programs(0) - 1)
    def _():
        near_ref[...] = acc_ref[:rows]
        away_ref[...] = flipped(acc_ref[rows:]).astype(BF)


def mlp_forward(turn, normed, other, bias, weights):
    rows, features = normed.shape
    units = bias.shape[1]
    tile = 512
    whole = pl.BlockSpec((rows, features), lambda f, turn: (0, 0))
    tiles = pl.BlockSpec((2 * rows, tile), lambda f, turn: (0, f))
    return pl.pallas_call(
        mlp_kernel,
        grid_spec=pltpu.PrefetchScalarGridSpec(
            num_scalar_prefetch=1,
            grid=(units // tile,),
            in_specs=[whole, whole, pl.BlockSpec((1, tile), lambda f, turn: (0, f))] + half_specs(tile, weights),
            out_specs=[tiles, tiles, whole, whole],
            scratch_shapes=[pltpu.VMEM((2 * rows, features), F32)],
        ),
        out_shape=[
            jax.ShapeDtypeStruct((2 * rows, units), BF),
            jax.ShapeDtypeStruct((2 * rows, units), BF),
            jax.ShapeDtypeStruct((rows, features), F32),
            jax.ShapeDtypeStruct((rows, features), BF),
        ],
        compiler_params=pltpu.CompilerParams(vmem_limit_bytes=VMEM_LIMIT),
        cost_estimate=took(18),
        name="mlp_forward",
    )(turn, normed, other, bias, *half_arrays(weights))


def mlp_close_kernel(last, own_ref, near_ref, got_ref, mid_ref, vector_ref, out_ref, next_ref):
    out = mid_ref[...] + (near_ref[...] + got_ref[...].astype(F32) + vector_ref[5:6])
    out_ref[...] = out
    if last:
        put_turned(next_ref, own_ref[0], out.astype(BF))
    else:
        next_ref[...] = (normalize(out)[0] * vector_ref[6:7] + vector_ref[7:8]).astype(BF)


def mlp_close(last, own_keep, near, got, mid, vectors):
    outs = [jax.ShapeDtypeStruct(mid.shape, F32), jax.ShapeDtypeStruct(mid.shape, BF)]
    args = [own_keep, near, got, mid, vectors]
    return call_once(functools.partial(mlp_close_kernel, last), "mlp_close", outs, args, 3)


def mlp_pull_kernel(turn_ref, grad_ref, other_ref, hidden_ref, *rest):
    weight_refs = rest[:8]
    grad_hidden_ref, grad_bias_ref, near_ref, away_ref, acc_ref, low_ref = rest[8:]
    rows, tile = grad_ref.shape[0], hidden_ref.shape[1]
    step = pl.program_id(0)

    @pl.when(step == 0)
    def _():
        low_ref[:rows] = grad_ref[...].astype(BF)
        low_ref[rows:] = other_ref[...]
        acc_ref[...] = jnp.zeros_like(acc_ref)

    def body(refs):
        expand, reduce = joined(refs, 0, tile), joined(refs, tile, 2 * tile)
        total = jnp.zeros((1, tile), F32)
        for first in (0, rows):
            here = slice(first, first + rows)
            hidden = hidden_ref[here].astype(F32)
            squared = hidden * hidden
            inner = jnp.tanh(GELU_A * hidden * (1.0 + GELU_B * squared))
            slope = 0.5 * (1.0 + inner) + 0.5 * hidden * (1.0 - inner * inner) * (GELU_A * (1.0 + 3.0 * GELU_B * squared))
            grad_hidden = dot_nn(low_ref[here], reduce) * slope
            total = total + jnp.sum(grad_hidden, axis=0, keepdims=True)
            grad_hidden = grad_hidden.astype(BF)
            grad_hidden_ref[here] = grad_hidden
            acc_ref[here] += dot_nt(grad_hidden, expand)
        grad_bias_ref[...] = total

    by_half(step, weight_refs, body)

    @pl.when(step == pl.num_programs(0) - 1)
    def _():
        near_ref[...] = acc_ref[:rows]
        away_ref[...] = flipped(acc_ref[rows:]).astype(BF)


def mlp_backward(turn, grad, other, hidden, weights):
    rows, features = grad.shape
    units = hidden.shape[1]
    tile = 512
    whole = pl.BlockSpec((rows, features), lambda f, turn: (0, 0))
    tiles = pl.BlockSpec((2 * rows, tile), lambda f, turn: (0, f))
    return pl.pallas_call(
        mlp_pull_kernel,
        grid_spec=pltpu.PrefetchScalarGridSpec(
            num_scalar_prefetch=1,
            grid=(units // tile,),
            in_specs=[whole, whole, tiles] + half_specs(tile, weights),
            out_specs=[tiles, pl.BlockSpec((1, tile), lambda f, turn: (0, f)), whole, whole],
            scratch_shapes=[pltpu.VMEM((2 * rows, features), F32), pltpu.VMEM((2 * rows, features), BF)],
        ),
        out_shape=[
            jax.ShapeDtypeStruct((2 * rows, units), BF),
            jax.ShapeDtypeStruct((1, units), F32),
            jax.ShapeDtypeStruct((rows, features), F32),
            jax.ShapeDtypeStruct((rows, features), BF),
        ],
        compiler_params=pltpu.CompilerParams(vmem_limit_bytes=VMEM_LIMIT),
        cost_estimate=took(22),
        name="mlp_backward",
    )(turn, grad, other, hidden, *half_arrays(weights))


def mlp_open_kernel(near_ref, got_ref, mid_ref, grad_ref, vector_ref, grad_mid_ref, grad_low_ref, sums_ref):
    grad = grad_ref[...]
    term = near_ref[...] + got_ref[...].astype(F32)
    grad_norm, grad_gain, grad_shift = norm_pull(mid_ref[...], vector_ref[3:4], term)
    grad_mid = grad + grad_norm
    grad_mid_ref[...] = grad_mid
    grad_low_ref[...] = grad_mid.astype(BF)
    rows = [jnp.sum(grad_mid, axis=0, keepdims=True), grad_gain, grad_shift, jnp.sum(grad, axis=0, keepdims=True)]
    sums_ref[...] = jnp.concatenate(rows + [jnp.zeros((4, grad.shape[1]), F32)], axis=0)


def mlp_open(near, got, mid, grad, vectors):
    outs = [
        jax.ShapeDtypeStruct(mid.shape, F32),
        jax.ShapeDtypeStruct(mid.shape, BF),
        jax.ShapeDtypeStruct((8, mid.shape[1]), F32),
    ]
    return call_once(mlp_open_kernel, "mlp_open", outs, [near, got, mid, grad, vectors], 5)


def unit_grads_kernel(second, left_ref, other_ref, right_ref, own_ref, pair_ref, single_ref, left_t_ref):
    @pl.when(pl.program_id(0) == 0)
    def _():
        left_t_ref[...] = jnp.concatenate([left_ref[...].astype(BF), other_ref[...]], axis=0).T

    grad = dot_nn(left_t_ref[...], right_ref[...]).astype(BF)
    single, direct = (1, 2) if second == "x" else (2, 1)
    for core in range(2):
        own_ref[0, core] = grad[core * 128:(core + 1) * 128]
        single_ref[0, core] = grad[(2 * single + core) * 128:(2 * single + core + 1) * 128]
        pair_ref[0, 0, core] = grad[(2 * direct + core) * 128:(2 * direct + core + 1) * 128]
        pair_ref[0, 1, core] = grad[(6 + core) * 128:(7 + core) * 128]


def unit_grads(second, left, other, right):
    rows, features = left.shape
    units = right.shape[1]
    tile = 512
    whole = pl.BlockSpec((rows, features), lambda f: (0, 0))
    out = pl.BlockSpec((1, 2, 128, tile), lambda f: (f // 2, 0, 0, f % 2))
    one = jax.ShapeDtypeStruct((2, 2, 128, 1024), BF)
    return pl.pallas_call(
        functools.partial(unit_grads_kernel, second),
        grid=(units // tile,),
        in_specs=[whole, whole, pl.BlockSpec((2 * rows, tile), lambda f: (0, f))],
        out_specs=[out, pl.BlockSpec((1, 2, 2, 128, tile), lambda f: (f // 2, 0, 0, 0, f % 2)), out],
        out_shape=[one, jax.ShapeDtypeStruct((2, 2, 2, 128, 1024), BF), one],
        scratch_shapes=[pltpu.VMEM((features, 2 * rows), BF)],
        compiler_params=pltpu.CompilerParams(vmem_limit_bytes=VMEM_LIMIT),
        cost_estimate=took(10),
        name="unit_grads",
    )(left, other, right)


def unit_grads_whole_kernel(turn_ref, left_ref, other_ref, right_ref, out_ref, left_t_ref):
    @pl.when(pl.program_id(0) == 0)
    def _():
        left_t_ref[...] = jnp.concatenate([left_ref[...].astype(BF), other_ref[...]], axis=0).T

    grad = dot_nn(left_t_ref[...], right_ref[...]).astype(BF)
    for chip in range(4):
        for core in range(2):
            first = (2 * chip + core) * 128
            out_ref[chip ^ turn_ref[0], 0, core] = grad[first:first + 128]


def unit_grads_whole(turn, left, other, right):
    rows, features = left.shape
    units = right.shape[1]
    tile = 512
    whole = pl.BlockSpec((rows, features), lambda f: (0, 0))
    return pl.pallas_call(
        unit_grads_whole_kernel,
        grid=(units // tile,),
        in_specs=[
            pl.BlockSpec(memory_space=pltpu.SMEM),
            whole,
            whole,
            pl.BlockSpec((2 * rows, tile), lambda f: (0, f)),
        ],
        out_specs=pl.BlockSpec((4, 1, 2, 128, tile), lambda f: (0, f // 2, 0, 0, f % 2)),
        out_shape=jax.ShapeDtypeStruct((4, 2, 2, 128, 1024), BF),
        scratch_shapes=[pltpu.VMEM((features, 2 * rows), BF)],
        compiler_params=pltpu.CompilerParams(vmem_limit_bytes=VMEM_LIMIT),
        cost_estimate=took(10),
        name="unit_grads_whole",
    )(turn, left, other, right)


MESH = pl.DeviceIdType.MESH


def flip(index, bit):
    return index + bit - 2 * bit * ((index // bit) % 2)


def peer(mask):
    dp, tensor = lax.axis_index("dp"), lax.axis_index("tensor")
    for bit in (1, 2):
        tensor = flip(tensor, bit) if mask & bit else tensor
        dp = flip(dp, bit) if mask & (CORE * bit) else dp
    dp = flip(dp, 4) if mask & YBIT else dp
    return {"dp": dp, "tensor": tensor}


def xor_block(block, own):
    return sum(bit * ((block // bit + own // bit) % 2) for bit in (1, 2, 4))


def greet(masks):
    barrier = pltpu.get_barrier_semaphore()
    for mask in masks:
        pl.semaphore_signal(barrier, inc=1, device_id=peer(mask), device_id_type=MESH)
    pl.semaphore_wait(barrier, len(masks))


def project_rows(rows, weight_refs, bias_ref, layer, out_refs):
    for quarter in (1, 0):
        weight = jnp.concatenate(
            [weight_refs[odd][chip, 1 - quarter if odd else quarter, :, 0:768] for chip in range(4) for odd in range(2)],
            axis=0,
        )
        out_refs[quarter][...] = (dot_nn(rows, weight) + bias_ref[layer, quarter:quarter + 1]).astype(BF)


SMALL_ROWS = 11


def start_kernel(
    layers, x_ref, project_ref, output_ref, expand_ref, reduce_ref, small_ref,
    resid_ref, normed_ref, far_ref, even_ref, odd_ref, first_ref, first_x_ref, first_y_ref, second_ref, vector_ref, head_bias_ref, unit_bias_ref,
    near_mine_ref, far_mine_ref, got_near_ref, got_far_ref,
    came_ref, piece_ref, every_ref, near_other_ref, far_other_ref, local_sem, send_sem, recv_sem,
):
    own, place = lax.axis_index("dp"), lax.axis_index("tensor")
    core = own % 2
    keep = core == place // 2
    count = [0]

    def copy(source, target, device):
        index = count[0]
        count[0] += 1
        return pltpu.make_async_remote_copy(
            src_ref=source, dst_ref=target, send_sem=send_sem.at[index], recv_sem=recv_sem.at[index],
            device_id=device, device_id_type=MESH,
        )

    greet((1, 2, 4, 6, 8, 16))
    tokens = copy(x_ref, came_ref, peer(CORE | Z1))
    stay = pltpu.make_async_copy(x_ref, came_ref, local_sem)

    @pl.when(keep)
    def _():
        stay.start()

    @pl.when(jnp.logical_not(keep))
    def _():
        tokens.start()

    for part in range(3):
        even_ref[0, core, :, part * 256:(part + 1) * 256] = project_ref[0, part]
    even_ref[0, core, :, 768:1024] = output_ref[0].T
    along = copy(even_ref.at[0, core], even_ref.at[0, 1 - core], peer(Z1))
    along.start()
    every_ref[0, 0] = small_ref[...]
    smalls = [
        (copy(every_ref.at[0, pl.ds(0, width)], every_ref.at[0, pl.ds(width, width)], peer(mask)))
        for width, mask in ((1, CORE), (2, XBIT), (4, YBIT))
    ]
    smalls += [
        copy(every_ref.at[pl.ds(0, width)], every_ref.at[pl.ds(width, width)], peer(mask)) for width, mask in ((1, Z0), (2, Z1))
    ]
    smalls[0].start()
    for half in range(2):
        here = slice(half * 512, (half + 1) * 512)
        piece_ref[:, half * 1024:half * 1024 + 512] = expand_ref[0, :, here]
        piece_ref[:, half * 1024 + 512:half * 1024 + 1024] = reduce_ref[0, here, :].T
    cross = copy(piece_ref, first_ref.at[1], {
        "dp": flip(own, 1), "tensor": place + (1 - core) * (flip(place, 2) - place)
    })
    same = copy(piece_ref, first_ref.at[0], peer(Z1))

    @pl.when(core == 0)
    def _():
        first_ref[0] = piece_ref[...]

    for step in range(1, 5):
        smalls[step - 1].wait()
        smalls[step].start()
    along.wait()
    over_x = copy(even_ref.at[0], even_ref.at[1], peer(XBIT))
    over_y = copy(even_ref.at[0], even_ref.at[2], peer(YBIT))
    over_x.start()
    over_y.start()
    cores = [copy(even_ref.at[chip], odd_ref.at[chip], peer(CORE)) for chip in range(4)]
    cores[0].start()
    smalls[4].wait()
    for layer in range(layers):
        base = layer * SMALL_ROWS
        later = min(layer + 1, layers - 1) * SMALL_ROWS
        rows = [base + row for row in range(6)] + [later, later + 1]
        for row, source in enumerate(rows):
            vector_ref[layer, row:row + 1, :] = jnp.concatenate(
                [every_ref[0, block, source:source + 1, :] for block in range(8)], axis=1
            )
        for quarter in range(2):
            which = 2 * (core + quarter - 2 * core * quarter)
            total = every_ref[which, 0, base + 6:base + 10, :]
            for block in range(1, 8):
                total = total + every_ref[which, block, base + 6:base + 10, :]
            head_bias_ref[layer, quarter:quarter + 1, :] = jnp.concatenate(
                [total[0:1], total[1:2], jnp.zeros((1, 256), F32), total[2:3], total[3:4]], axis=1
            )
            for block in range(8):
                unit_bias_ref[layer, :, quarter * 1024 + block * 128:quarter * 1024 + (block + 1) * 128] = every_ref[
                    2 * core + quarter, xor_block(block, own), base + 10:base + 11, :
                ]
    @pl.when(keep)
    def _():
        stay.wait()

    @pl.when(jnp.logical_not(keep))
    def _():
        tokens.wait()

    for block in range(8):
        here = pl.ds(pl.multiple_of(xor_block(block, own) * 128, 128), 128)
        resid_ref[:, block * 128:(block + 1) * 128] = came_ref[:, here].astype(F32)
    normed = (normalize(resid_ref[...])[0] * vector_ref[0, 0:1] + vector_ref[0, 1:2]).astype(BF)
    normed_ref[...] = normed
    beside = copy(normed_ref, far_ref, peer(Z0))
    beside.start()
    cross.start()

    @pl.when(core == 1)
    def _():
        same.start()

    over_y.wait()
    over_x.wait()
    across = copy(even_ref.at[2], even_ref.at[3], peer(XBIT))
    across.start()
    cores[1].start()
    cores[2].start()
    across.wait()
    cores[3].start()
    for one in cores:
        one.wait()
    weights = (even_ref, odd_ref)
    project_rows(normed_ref[...], weights, head_bias_ref, 0, (near_mine_ref, near_other_ref))
    back_near = copy(near_other_ref, got_near_ref, peer(CORE))
    back_near.start()
    cross.wait()

    @pl.when(core == 1)
    def _():
        same.wait()

    units = [copy(first_ref, target, peer(mask)) for target, mask in ((first_x_ref, XBIT), (first_y_ref, YBIT), (second_ref, Z0))]
    for one in units:
        one.start()
    beside.wait()
    project_rows(far_ref[...], weights, head_bias_ref, 0, (far_mine_ref, far_other_ref))
    back_far = copy(far_other_ref, got_far_ref, peer(CORE))
    back_far.start()
    back_near.wait()
    back_far.wait()
    for one in units:
        one.wait()


def start(x, project_weight, output_weight, expand_weight, reduce_weight, small, layers):
    rows, features = x.shape
    vmem = pl.BlockSpec(memory_space=pltpu.VMEM)

    triple = jax.ShapeDtypeStruct((rows, 768), BF)
    heads = jax.ShapeDtypeStruct((4, 2, 128, 1024), BF)
    outs = [
        jax.ShapeDtypeStruct((rows, features), F32),
        jax.ShapeDtypeStruct((rows, features), BF),
        jax.ShapeDtypeStruct((rows, features), BF),
        heads,
        heads,
        *[jax.ShapeDtypeStruct((2, 128, 2048), BF)] * 4,
        jax.ShapeDtypeStruct((layers, 8, features), F32),
        jax.ShapeDtypeStruct((layers, 2, 768), F32),
        jax.ShapeDtypeStruct((layers, 1, 2048), F32),
        triple,
        triple,
        triple,
        triple,
    ]
    copies = 22
    return pl.pallas_call(
        functools.partial(start_kernel, layers),
        in_specs=[vmem] * 6,
        out_specs=[vmem] * len(outs),
        out_shape=outs,
        scratch_shapes=[
            pltpu.VMEM((rows, features), BF),
            pltpu.VMEM((128, 2048), BF),
            pltpu.VMEM((4, 8, *small.shape), F32),
            pltpu.VMEM((rows, 768), BF),
            pltpu.VMEM((rows, 768), BF),
            pltpu.SemaphoreType.DMA,
            pltpu.SemaphoreType.DMA((copies,)),
            pltpu.SemaphoreType.DMA((copies,)),
        ],
        compiler_params=pltpu.CompilerParams(vmem_limit_bytes=VMEM_LIMIT, collective_id=0, has_side_effects=True),
        cost_estimate=took(60),
        name="start",
    )(x, project_weight, output_weight, expand_weight, reduce_weight, small)


def finish_kernel(
    layers, grad_ref, even_ref, odd_ref, here_ref, away_ref, *rest,
):
    sums, rest = rest[:4 * layers], rest[4 * layers:]
    grad_out_ref, project_ref, output_ref, reduce_ref, expand_ref, small_ref, rest = *rest[:6], rest[6:]
    odd_got, y_send, y_got, x_send, x_got, relay_send, relay_got, z_send, z_got, away_got, part_ref, part_got, rest = *rest[:12], rest[12:]
    rows_ref, core_got, x_rows, y_rows, near_send, near_got, far_send, far_got, local_sem, send_sem, recv_sem = rest
    own, place = lax.axis_index("dp"), lax.axis_index("tensor")
    core = own % 2
    keep = core == place // 2
    count = [0]

    def copy(source, target, device):
        index = count[0]
        count[0] += 1
        return pltpu.make_async_remote_copy(
            src_ref=source, dst_ref=target, send_sem=send_sem.at[index], recv_sem=recv_sem.at[index],
            device_id=device, device_id_type=MESH,
        )

    greet((1, 2, 4, 6, 8, 16))
    across = copy(odd_ref, odd_got, peer(CORE))
    across.start()
    beside = copy(away_ref, away_got, peer(Z0))
    beside.start()
    tokens = copy(grad_ref, grad_out_ref, peer(CORE | Z1))
    stay = pltpu.make_async_copy(grad_ref, grad_out_ref, local_sem)

    @pl.when(keep)
    def _():
        stay.start()

    @pl.when(jnp.logical_not(keep))
    def _():
        tokens.start()

    vectors = 6 * layers
    rows_ref[...] = jnp.zeros_like(rows_ref)
    for layer in range(layers):
        first_ref, second_ref, unit_ref, head_ref = sums[4 * layer:4 * layer + 4]
        base = vectors + 12 * layer
        for block in range(8):
            slot = (block % 2) * 4 + (block // 2 % 2) * 2 + block // 4
            lanes = slice(block * 128, (block + 1) * 128)
            rows_ref[slot, 6 * layer:6 * layer + 2, :] = first_ref[0:2, lanes]
            rows_ref[slot, 6 * layer + 2:6 * layer + 6, :] = second_ref[0:4, lanes]
            for quarter in range(2):
                lane = pl.multiple_of(quarter * 1024 + xor_block(block, own) * 128, 128)
                rows_ref[slot, pl.ds(base + 2 * core + quarter, 1), :] = unit_ref[0:1, pl.ds(lane, 128)]
                row = base + 4 + 4 * (quarter + core - 2 * quarter * core)
                for half in range(2):
                    rows_ref[slot, pl.ds(row + 2 * half, 2), :] = head_ref[
                        2 * quarter:2 * quarter + 2, half * 128:(half + 1) * 128
                    ]
    hop = copy(rows_ref.at[pl.ds(4, 4)], core_got, peer(CORE))
    hop.start()
    hop.wait()
    rows_ref[0:4] = rows_ref[0:4] + core_got[...]
    hop = copy(rows_ref.at[pl.ds(2, 2)], x_rows, peer(XBIT))
    hop.start()
    across.wait()
    for chip in range(4):
        for quarter in range(2):
            odd_got[chip, quarter] = odd_got[chip, quarter] + even_ref[chip, quarter]
    y_send[0], y_send[1] = odd_got[2, 0], odd_got[3, 0]
    x_send[0], x_send[1] = odd_got[1, 1], odd_got[3, 1]
    over_y = copy(y_send, y_got, peer(YBIT))
    over_x = copy(x_send, x_got, peer(XBIT))
    over_y.start()
    over_x.start()
    hop.wait()
    rows_ref[0:2] = rows_ref[0:2] + x_rows[...]
    hop = copy(rows_ref.at[pl.ds(1, 1)], y_rows, peer(YBIT))
    hop.start()
    hop.wait()
    rows_ref[0] = rows_ref[0] + y_rows[0]
    near_send[...] = jnp.zeros_like(near_send)
    far_send[...] = jnp.zeros_like(far_send)
    near_send[0:vectors, :] = rows_ref[0, 0:vectors, :]
    for layer in range(layers):
        base = vectors + 12 * layer
        near_send[vectors + 2 * layer:vectors + 2 * layer + 1, :] = rows_ref[0, base + 1:base + 2, :]
        near_send[vectors + 2 * layer + 1:vectors + 2 * layer + 2, :] = rows_ref[0, base + 3:base + 4, :]
    hop = copy(near_send, near_got, peer(Z0))
    hop.start()
    over_y.wait()
    over_x.wait()
    relay_send[0] = odd_got[1, 0] + y_got[1]
    relay_send[1] = odd_got[2, 1] + x_got[1]
    relays = [copy(relay_send.at[i], relay_got.at[i], peer(mask)) for i, mask in ((0, XBIT), (1, YBIT))]
    for one in relays:
        one.start()
    beside.wait()
    for kind in range(2):
        for side in range(2):
            part_ref[side, kind] = here_ref[kind, side] + away_got[kind, side]
    crossing = copy(part_ref.at[1], part_got.at[1], {
        "dp": flip(own, 1), "tensor": place + core * (flip(place, 2) - place)
    })
    crossing.start()
    along = copy(part_ref.at[0], part_got.at[0], peer(Z1))

    @pl.when(core == 1)
    def _():
        along.start()

    @pl.when(core == 0)
    def _():
        part_got[0] = part_ref[0]

    for one in relays:
        one.wait()
    total = [odd_got[0, 0] + y_got[0] + relay_got[0], odd_got[0, 1] + x_got[0] + relay_got[1]]
    z_send[core] = total[0]
    z_send[1 - core] = total[1]
    heads = copy(z_send.at[1], z_got, peer(Z1))
    heads.start()
    hop.wait()
    far_send[0:vectors, :] = rows_ref[0, 0:vectors, :] + near_got[0:vectors, :]
    for layer in range(layers):
        base = vectors + 12 * layer
        far_send[vectors + layer:vectors + layer + 1, :] = (
            rows_ref[0, base + 2:base + 3, :] + near_got[vectors + 2 * layer + 1:vectors + 2 * layer + 2, :]
        )
        far_send[vectors + layers + 4 * layer:vectors + layers + 4 * layer + 4, :] = rows_ref[0, base + 8:base + 12, :]
    hop = copy(far_send, far_got, peer(Z1))
    hop.start()
    crossing.wait()

    @pl.when(core == 1)
    def _():
        along.wait()

    reduce_ref[...] = (part_got[0, 0].astype(F32) + part_got[1, 0].astype(F32)).T
    expand_ref[...] = part_got[0, 1].astype(F32) + part_got[1, 1].astype(F32)
    hop.wait()
    small_ref[0:vectors, :] = far_send[0:vectors, :] + far_got[0:vectors, :]
    for layer in range(layers):
        base = vectors + 12 * layer
        row = vectors + layer
        small_ref[row:row + 1, :] = (
            rows_ref[0, base:base + 1, :] + near_got[vectors + 2 * layer:vectors + 2 * layer + 1, :] + far_got[row:row + 1, :]
        )
        row = vectors + layers + 4 * layer
        small_ref[row:row + 4, :] = rows_ref[0, base + 4:base + 8, :] + far_got[row:row + 4, :]
    heads.wait()
    for part in range(3):
        here = slice(part * 256, (part + 1) * 256)
        project_ref[part] = z_send[0, :, here].astype(F32) + z_got[:, here].astype(F32)
    output_ref[...] = (z_send[0, :, 768:].astype(F32) + z_got[:, 768:].astype(F32)).T

    @pl.when(keep)
    def _():
        stay.wait()

    @pl.when(jnp.logical_not(keep))
    def _():
        tokens.wait()


def finish(grad, even, odd, here, away, sums):
    layers = len(sums)
    vmem = pl.BlockSpec(memory_space=pltpu.VMEM)
    rows = 18 * layers
    args = [grad, even, odd, here, away, *[array for layer in sums for array in layer]]
    small = 8 * (-(-11 * layers // 8))
    outs = [
        jax.ShapeDtypeStruct(grad.shape, BF),
        jax.ShapeDtypeStruct((3, 128, 256), F32),
        jax.ShapeDtypeStruct((256, 128), F32),
        jax.ShapeDtypeStruct((1024, 128), F32),
        jax.ShapeDtypeStruct((128, 1024), F32),
        jax.ShapeDtypeStruct((small, 128), F32),
    ]
    one = (128, 1024)
    copies = 15
    return pl.pallas_call(
        functools.partial(finish_kernel, layers),
        in_specs=[vmem] * len(args),
        out_specs=[vmem] * len(outs),
        out_shape=outs,
        scratch_shapes=[
            pltpu.VMEM((4, 2, *one), BF),
            *[pltpu.VMEM((2, *one), BF)] * 7,
            pltpu.VMEM(one, BF),
            *[pltpu.VMEM((2, 2, *one), BF)] * 3,
            pltpu.VMEM((8, rows, 128), F32),
            pltpu.VMEM((4, rows, 128), F32),
            pltpu.VMEM((2, rows, 128), F32),
            pltpu.VMEM((1, rows, 128), F32),
            *[pltpu.VMEM((small, 128), F32)] * 4,
            pltpu.SemaphoreType.DMA,
            pltpu.SemaphoreType.DMA((copies,)),
            pltpu.SemaphoreType.DMA((copies,)),
        ],
        compiler_params=pltpu.CompilerParams(vmem_limit_bytes=VMEM_LIMIT, collective_id=1, has_side_effects=True),
        cost_estimate=took(50),
        name="finish",
    )(*args)


def fetch_heads(piece, core, turn, out):
    token = yield
    far = swap(after(piece, token), Z1)
    token = yield []
    far = after(far, token)
    own = jnp.stack([jnp.where(core == 0, piece, far), jnp.where(core == 0, far, piece)])
    from_x = swap(own, XBIT)
    from_y = swap(own, YBIT)
    token = yield [own]
    from_x, from_y = after_all((from_x, from_y), token)
    across = swap(from_y, XBIT)
    token = yield [from_x, from_y]
    quads = jnp.stack([own, from_x, from_y, after(across, token)])
    other = swap(quads, CORE)
    token = yield [quads]
    out += [quads, other, turn]


def fetch_units(piece, core, first_out, second_out):
    token = yield
    piece = after(piece, token)
    pair = jnp.stack([piece, swap(piece, CORE)])
    far = swap_some(pair, (0, Z1))
    token = yield [pair]
    first = jnp.where(core == 0, pair, after(far, token))
    token = yield [first]
    second = swap(after(first, token), Z0)
    token = yield []
    second = after(second, token)
    token = yield [second]
    first = after(first, token)
    first_x, first_y = swap(first, XBIT), swap(first, YBIT)
    token = yield []
    steps = join_units(first, first_x, first_y, second, first_out, second_out)
    next(steps)
    made = steps.send(token)
    while made is not None:
        token = yield made
        made = next_made(steps, token)


def next_made(steps, token):
    try:
        return steps.send(token)
    except StopIteration:
        return None


def join_units(first, first_x, first_y, second, first_out, second_out):
    token = yield
    first, first_x, first_y, second = after_all((first, first_x, first_y, second), token)
    second_x, second_y = swap(second, XBIT), swap(second, YBIT)
    token = yield [first_x, first_y, second]
    second_x, second_y = after_all((second_x, second_y), token)
    first_across, second_across = swap(first_x, YBIT), swap(second_y, XBIT)
    token = yield [second_x, second_y]
    first_across, second_across = after_all((first_across, second_across), token)
    first_out += [first, first_x, first_y, first_across]
    second_out += [second, second_x, second_y, second_across]
    yield [first_across, second_across]


def pack_heads(project, output):
    return jnp.concatenate([project.transpose(1, 0, 2).reshape(128, 768), output.T], axis=1)


def unpack_heads(values):
    return values[:, :768].reshape(128, 3, 256).transpose(1, 0, 2), values[:, 768:].T


def pack_units(expand, reduce):
    parts = (expand.reshape(128, 2, 512), reduce.T.reshape(128, 2, 512))
    return jnp.stack(parts, axis=2).reshape(128, 2048)


def small_rows(six, project_bias, expand_bias, own):
    layers = six.shape[1]
    wide = jnp.zeros((layers, 2, 256), F32)
    wide = lax.dynamic_update_slice(wide, project_bias.astype(F32), (0, 0, own * 32))
    rows = jnp.concatenate(
        [six.transpose(1, 0, 2).astype(F32), wide.reshape(layers, 4, 128), expand_bias[:, None, :].astype(F32)], axis=1
    )
    return jnp.pad(rows.reshape(layers * SMALL_ROWS, 128), ((0, -layers * SMALL_ROWS % 8), (0, 0)))


def reduce_heads(even, odd, core, out):
    token = yield
    got = swap(odd, CORE)
    token = yield []
    got = after(got, token)
    low, high = even[:2] + got[:2], even[2:] + got[2:]
    from_y = swap(high, YBIT)
    token = yield [low, high]
    from_y = after(from_y, token)
    relayed = low[1] + from_y[1]
    relay = swap(relayed, XBIT)
    token = yield [relayed]
    total = low[0] + from_y[0] + after(relay, token)
    yield from close_heads(total, core, out)


def close_heads(total, core, out):
    near = jnp.where(core == 0, total[0], total[1])
    away = jnp.where(core == 0, total[1], total[0])
    far = swap(away, Z1)
    token = yield [near, away]
    out.append(unpack_heads(near.astype(F32) + after(far, token).astype(F32)))
    yield list(out[-1])


def reduce_units(reduce_parts, expand_parts, core, out):
    yield
    own_r, pair_r, single_r = reduce_parts
    from_y = swap(pair_r, YBIT)
    yield []
    own_e, pair_e, single_e = expand_parts
    from_x = swap(pair_e, XBIT)
    token = yield []
    from_y = after(from_y, token)
    relayed_r = single_r + from_y[:, 1]
    relay_r = swap(relayed_r, XBIT)
    token = yield [relayed_r]
    from_x = after(from_x, token)
    relayed_e = single_e + from_x[:, 1]
    relay_e = swap(relayed_e, YBIT)
    token = yield [relayed_e]
    relay_r, relay_e = after_all((relay_r, relay_e), token)
    totals = [
        jnp.stack([own_r[i] + from_y[i, 0] + relay_r[i], own_e[i] + from_x[i, 0] + relay_e[i]]) for i in range(2)
    ]
    if core is None:
        out += totals
        yield totals
        return
    yield from close_units(*totals, core, out)


def close_units(here, away, core, out):
    got = swap(away, Z0)
    token = yield [here, away]
    here = here + after(got, token)
    same, cross = here[:, 0], here[:, 1]
    same_got, cross_got = swap_some(same, (0, Z1)), swap_some(cross, (CORE, CORE | Z1))
    token = yield [same, cross]
    same_got, cross_got = after_all((same_got, cross_got), token)
    out.append(jnp.where(core == 0, same, same_got).astype(F32) + cross_got.astype(F32))
    yield [out[-1]]


def fast_device(
    layer_input,
    first_gain,
    first_shift,
    project_weight,
    project_bias,
    output_weight,
    output_bias,
    second_gain,
    second_shift,
    expand_weight,
    expand_bias,
    reduce_weight,
    reduce_bias,
    picture_start,
    cotangent,
):
    own = lax.axis_index("dp")
    place = lax.axis_index("tensor")
    core = own & 1
    keep = core == (place >> 1)
    own_keep = jnp.stack([own, keep.astype(jnp.int32)]).astype(jnp.int32)
    me = (2 * core + (place & 1)).astype(jnp.int32).reshape(1)
    slopes = head_slopes((place ^ (2 * core)) * 4, 4)

    six = jnp.stack([first_gain, first_shift, output_bias, second_gain, second_shift, reduce_bias])
    turn = jnp.zeros((1,), jnp.int32)
    resid, normed, far, even, odd, first_pieces, first_x, first_y, second, vectors_of, head_bias_of, unit_bias_of, *blocks = start(
        layer_input, project_weight, output_weight, expand_weight, reduce_weight,
        small_rows(six, project_bias, expand_bias, own), LAYERS,
    )
    near_mine, far_mine, got_near, got_far = blocks
    small = [(vectors_of[i], head_bias_of[i], unit_bias_of[i]) for i in range(LAYERS)]
    starts = jnp.where(keep, picture_start, redeal(picture_start))[0]
    heads, units = [[] for i in range(LAYERS)], [([], []) for i in range(LAYERS)]
    heads[0] += [even, odd, turn]
    head_tasks, unit_tasks = [None], [task(join_units(first_pieces, first_x, first_y, second, *units[0]))]
    for layer in range(1, LAYERS):
        weights = after_all((project_weight, output_weight, expand_weight, reduce_weight), far_mine)
        head_piece = pack_heads(weights[0][layer], weights[1][layer])
        unit_piece = pack_units(weights[2][layer], weights[3][layer])
        head_tasks.append(task(fetch_heads(head_piece, core, turn, heads[layer])))
        unit_tasks.append(task(fetch_units(unit_piece, core, *units[layer])))
    saved = []
    for layer in range(LAYERS):
        vectors, head_bias, unit_bias = small[layer]
        first, last = layer == 0, layer + 1 == LAYERS
        if not first:
            far = swap(normed, Z0)
            while not heads[layer]:
                advance(normed, head_tasks[layer])
            near_mine, near_other = project(normed, head_bias, heads[layer])
            got_near = swap(near_other, CORE)
            far_mine, far_other = project(after(far, near_mine), head_bias, heads[layer])
            got_far = swap(far_other, CORE)
        pieces = heads[layer]
        made = advance(far_mine, unit_tasks[layer])
        if first:
            made += advance(far_mine, unit_tasks[1])
            made += [far_piece for far_piece in (head_piece,)]
        blocks = after_all((near_mine, far_mine, got_near, got_far), *made)
        far_mixed, far_send, far_exact, far_log = attend(blocks, 1, slopes, starts, me)
        far_got = swap(far_send, CORE)
        far_part = mix_far(far_mixed, far_got, pieces)
        far_term = swap(far_part, Z0)
        made = advance(far_part, unit_tasks[layer])
        near_blocks = after_all(blocks, far_part, *made)
        near_mixed, near_send, near_exact, near_log = attend(near_blocks, 0, slopes, starts, me)
        near_got = swap(near_send, CORE)
        made = advance(near_mixed, unit_tasks[layer])
        if first:
            made += advance(near_mixed, unit_tasks[1])
        if last:
            cotangent_far = redeal(after(cotangent, near_mixed))
        mid, normed_two, flip_two = mix_near(near_mixed, near_got, after(far_term, near_mixed, *made), resid, vectors, pieces)
        normed_other = swap(flip_two, CORE)
        if last:
            grad, unused, flip_grad = enter(own_keep, cotangent, after(cotangent_far, mid), vectors)
            grad_other = swap(flip_grad, CORE)
            normed_two = after(normed_two, grad)
        if first:
            advance(mid, unit_tasks[1], head_tasks[1])
        hidden, active, near_out, away_out = mlp_forward(turn, normed_two, normed_other, unit_bias, units[layer])
        got_out = swap(away_out, CORE)
        if not last:
            got_out = after(got_out, *advance(near_out, head_tasks[layer + 1], unit_tasks[layer + 1]))
        out, following = mlp_close(last, own_keep, near_out, got_out, mid, vectors)
        if not last:
            advance(out, head_tasks[layer + 1])
            advance(out, unit_tasks[layer + 1])
        saved.append((
            resid, normed, far, blocks, (near_exact, far_exact), (near_log, far_log), (near_mixed, far_mixed),
            (near_got, far_got), mid, normed_two, normed_other, hidden, active,
        ))
        resid, normed = out, following
    layer_output = jnp.where(keep, normed, redeal(normed))
    grad = after(grad, normed)
    sums = [None] * LAYERS
    head_grad, unit_grad = ([[] for i in range(LAYERS)] for j in range(2))
    pending = []
    for layer in reversed(range(LAYERS)):
        vectors, pieces = small[layer][0], heads[layer]
        (
            resid, normed, far, blocks, exacts, logs, mixed, mixed_got, mid, normed_two, normed_other, hidden, active,
        ) = saved[layer]
        grad_hidden, unit_sums, near_term, away_term = mlp_backward(turn, grad, grad_other, hidden, units[layer])
        got_term = after(swap(away_term, CORE), *advance(near_term, *pending))
        grad_mid, grad_low, second_sums = mlp_open(near_term, got_term, mid, grad, vectors)
        grad_far = swap(grad_low, Z0)
        first = layer == 0
        reduce_parts = unit_grads("x", grad, grad_other, after(active, grad_low))
        made = advance(reduce_parts[0], *pending)
        near_mine, near_other = unmix(after(grad_low, reduce_parts[0], *made), pieces)
        got_near = swap(near_other, CORE)
        expand_parts = unit_grads("y", normed_two, normed_other, after(grad_hidden, near_mine))
        unit_task = task(reduce_units(reduce_parts, expand_parts, None if first else core, unit_grad[layer]))
        advance(None, unit_task)
        advance(None, unit_task)
        far_mine, far_other = unmix(after(grad_far, expand_parts[0]), pieces)
        got_far = swap(far_other, CORE)
        made = advance(far_mine, *pending)
        grads_mixed = after_all((near_mine, far_mine, got_near, got_far), *made)
        mine_0, away_0 = attend_pull(0, blocks, grads_mixed, exacts, logs, slopes, starts, me)
        other_0 = swap(away_0, CORE)
        made = advance(mine_0, unit_task)
        grads_mixed = after_all(grads_mixed, mine_0, *made)
        mine_1, away_1 = attend_pull(1, blocks, grads_mixed, exacts, logs, slopes, starts, me)
        other_1 = swap(away_1, CORE)
        other_1 = after(other_1, *advance(mine_1, unit_task))
        mine, other = (mine_0, mine_1), (other_0, other_1)
        far_part = unproject_far(mine, other, pieces)
        far_term = swap(far_part, Z0)
        even, odd, head_sums = head_grads(
            turn, normed, far, grad_low, after(grad_far, far_part), mine, other, mixed, mixed_got
        )
        if not first:
            head_task = task(reduce_heads(even, odd, core, head_grad[layer]))
            advance(None, head_task)
        made = advance(head_sums, unit_task)
        grad, grad_low, first_sums = unproject_near(
            first, own_keep, mine, other, after(far_term, *made), resid, grad_mid, vectors, pieces
        )
        sums[layer] = (first_sums, second_sums, unit_sums, head_sums)
        if not first:
            grad_other = swap(grad_low, CORE)
            grad = after(grad, *advance(grad, head_task))
        pending = [unit_task, head_task]
    input_grad, *grads, small_sums = finish(grad_low, even, odd, *unit_grad[0], sums)
    head_grad[0], unit_grad[0] = [grads[:2]], [grads[2:]]
    unit_grad[1:] = [[(g[0][0].T, g[0][1])] for g in unit_grad[1:]]
    six = small_sums[:6 * LAYERS].reshape(LAYERS, 6, 128)
    unit_sum = small_sums[6 * LAYERS:7 * LAYERS]
    head_sum = small_sums[7 * LAYERS:11 * LAYERS].reshape(LAYERS, 2, 2, 128).transpose(0, 2, 1, 3).reshape(LAYERS, 2, 256)
    head_sum = lax.dynamic_slice_in_dim(head_sum, own * 32, 32, 2)
    return (
        layer_output,
        input_grad,
        six[:, 0],
        six[:, 1],
        jnp.stack([g[0][0] for g in head_grad]),
        head_sum,
        jnp.stack([g[0][1] for g in head_grad]),
        six[:, 2],
        six[:, 3],
        six[:, 4],
        jnp.stack([g[0][1] for g in unit_grad]),
        unit_sum,
        jnp.stack([g[0][0] for g in unit_grad]),
        six[:, 5],
    )


def solution(mesh):
    placed = (
        P(("dp", "tensor"), None),
        P(None, "dp"),
        P(None, "dp"),
        P(None, None, "dp", "tensor"),
        P(None, None, ("tensor", "dp")),
        P(None, "tensor", "dp"),
        P(None, "dp"),
        P(None, "dp"),
        P(None, "dp"),
        P(None, "dp", "tensor"),
        P(None, ("tensor", "dp")),
        P(None, "tensor", "dp"),
        P(None, "dp"),
        P("dp", None),
        P(("dp", "tensor"), None),
    )
    return jax.shard_map(
        fast_device if mesh_is_paired(mesh) else on_device,
        mesh=mesh,
        in_specs=placed,
        out_specs=(
            P(("dp", "tensor"), None),
            P(("dp", "tensor"), None),
            P(None, "dp"),
            P(None, "dp"),
            P(None, None, "dp", "tensor"),
            P(None, None, ("tensor", "dp")),
            P(None, "tensor", "dp"),
            P(None, "dp"),
            P(None, "dp"),
            P(None, "dp"),
            P(None, "dp", "tensor"),
            P(None, ("tensor", "dp")),
            P(None, "tensor", "dp"),
            P(None, "dp"),
        ),
        check_vma=False,
    )
```

```python
import functools

import jax
import jax.numpy as jnp
from jax import lax
from jax.experimental import pallas as pl
from jax.experimental.pallas import tpu as pltpu
from jax.sharding import PartitionSpec as P

HEADS = 16
HD = 64
LAYERS = 2
SEQ_LEN = 2048
PIECE = 256


NORM_EPS = 1e-05


def layer_norm(values, gain, shift):
    centred = values - jnp.mean(values, axis=-1, keepdims=True)
    spread = jnp.mean(centred * centred, axis=-1, keepdims=True)
    return centred * lax.rsqrt(spread + NORM_EPS) * gain + shift


def gelu_tanh(values):
    return jax.nn.gelu(values, approximate=True)


def piece_numbers(starts):
    places = jnp.arange(SEQ_LEN, dtype=jnp.int32)
    inside = (places[:, None] >= starts[None, :]) & (places[:, None] < starts[None, :] + PIECE)
    numbers = jnp.arange(1, starts.shape[0] + 1, dtype=jnp.int32)
    return jnp.sum(jnp.where(inside, numbers[None, :], 0), axis=1)


def head_slopes(first_head, count_heads):
    heads_at = (first_head + jnp.arange(count_heads, dtype=jnp.int32)).astype(jnp.float32)
    return jnp.exp2(-8.0 * (heads_at + 1.0) / HEADS)


def gather_rows(values):
    return lax.all_gather(values, "tensor", axis=0, tiled=True)


def gather_grads(values):
    return lax.all_gather(values, "tensor", axis=0, tiled=True)


def scatter_rows(values, weight):
    rows_here = values.shape[0] // lax.axis_size("tensor")

    def partial_term(offset, count_rows):
        return jnp.dot(values, weight, preferred_element_type=jnp.float32)

    return lax.psum_scatter(
        partial_term(jnp.int32(0), rows_here * lax.axis_size("tensor")).astype(jnp.bfloat16),
        "tensor",
        scatter_dimension=0,
        tiled=True,
    ).astype(jnp.float32)


def scatter_back(partial_term, rows_here):
    return lax.psum_scatter(
        partial_term(jnp.int32(0), rows_here * lax.axis_size("tensor")).astype(jnp.bfloat16),
        "tensor",
        scatter_dimension=0,
        tiled=True,
    ).astype(jnp.float32)


def block_scores(query_block, key_rows, offset, piece_ids, slopes):
    length = key_rows.shape[0]
    count_rows = query_block.shape[0]
    query_places = offset + jnp.arange(count_rows, dtype=jnp.int32)
    key_places = jnp.arange(length, dtype=jnp.int32)
    product = jnp.einsum("qhe,khe->hqk", query_block, key_rows, preferred_element_type=jnp.float32)
    distance = jnp.abs(query_places[:, None] - key_places[None, :]).astype(jnp.float32)
    scores = product * HD ** (-0.5) - slopes[:, None, None] * distance[None]
    query_pieces = lax.dynamic_slice_in_dim(piece_ids, offset, count_rows, 0)
    allowed = (key_places[None, :] <= query_places[:, None]) | (
        query_pieces[:, None] == piece_ids[None, :]
    ) & (query_pieces[:, None] > 0)
    return jnp.where(allowed[None], scores, -jnp.inf)


def sequence_forward(operands, slopes):
    queries, key_rows, value_rows, piece_ids = operands
    length = queries.shape[0]
    block_rows = min(512, length)

    def one_block(block_index):
        offset = block_index * block_rows
        query_block = lax.dynamic_slice_in_dim(queries, offset, block_rows, 0)
        scores = block_scores(query_block, key_rows, offset, piece_ids, slopes)
        row_max = jnp.max(scores, axis=-1, keepdims=True)
        raw_weights = jnp.exp(scores - row_max)
        totals = jnp.sum(raw_weights, axis=-1, keepdims=True)
        soft_weights = (raw_weights / totals).astype(jnp.bfloat16)
        attended = jnp.einsum(
            "hqk,khe->qhe", soft_weights, value_rows, preferred_element_type=jnp.float32
        )
        return (attended.astype(jnp.bfloat16), (row_max + jnp.log(totals))[..., 0])

    attended, log_total = lax.map(one_block, jnp.arange(length // block_rows, dtype=jnp.int32))
    return (attended.reshape(length, queries.shape[1], queries.shape[2]), log_total)


def sequence_backward(operands, slopes):
    queries, key_rows, value_rows, piece_ids, grad_mixed, log_total = operands
    length = queries.shape[0]
    block_rows = min(512, length)

    def one_block(carry, block_index):
        key_grad, value_grad = carry
        offset = block_index * block_rows
        query_block = lax.dynamic_slice_in_dim(queries, offset, block_rows, 0)
        grad_block = lax.dynamic_slice_in_dim(grad_mixed, offset, block_rows, 0)
        scores = block_scores(query_block, key_rows, offset, piece_ids, slopes)
        probs = jnp.exp(scores - log_total[block_index][..., None])
        soft_weights = probs.astype(jnp.bfloat16)
        value_grad = value_grad + jnp.einsum(
            "hqk,qhe->khe", soft_weights, grad_block, preferred_element_type=jnp.float32
        )
        prob_grad = jnp.einsum(
            "qhe,khe->hqk", grad_block, value_rows, preferred_element_type=jnp.float32
        )
        centred = jnp.sum(probs * prob_grad, axis=-1, keepdims=True)
        score_grad = (probs * (prob_grad - centred) * HD ** (-0.5)).astype(jnp.bfloat16)
        query_grad = jnp.einsum(
            "hqk,khe->qhe", score_grad, key_rows, preferred_element_type=jnp.float32
        )
        key_grad = key_grad + jnp.einsum(
            "hqk,qhe->khe", score_grad, query_block, preferred_element_type=jnp.float32
        )
        return ((key_grad, value_grad), query_grad)

    empty = jnp.zeros(queries.shape, jnp.float32)
    (key_grad, value_grad), query_grad = lax.scan(
        one_block, (empty, empty), jnp.arange(length // block_rows, dtype=jnp.int32)
    )
    return (query_grad.reshape(queries.shape), key_grad, value_grad)


def attend_forward(triple, piece_ids, slopes):
    width = triple.shape[2]
    count_seq = piece_ids.shape[0]
    length = piece_ids.shape[1]
    shaped = triple.reshape(3, count_seq, length, width // HD, HD)
    attended, log_total = lax.map(
        lambda operands: sequence_forward(operands, slopes),
        (shaped[0], shaped[1], shaped[2], piece_ids),
    )
    return (attended.reshape(count_seq * length, width), log_total)


def attend_backward(triple, grad_attended, log_total, piece_ids, slopes):
    width = triple.shape[2]
    count_seq = piece_ids.shape[0]
    length = piece_ids.shape[1]
    shaped = triple.reshape(3, count_seq, length, width // HD, HD)
    grad_shaped = grad_attended.reshape(count_seq, length, width // HD, HD)
    query_grad, key_grad, value_grad = lax.map(
        lambda operands: sequence_backward(operands, slopes),
        (shaped[0], shaped[1], shaped[2], piece_ids, grad_shaped, log_total),
    )
    return (
        query_grad.reshape(-1, width),
        key_grad.reshape(-1, width),
        value_grad.reshape(-1, width),
    )


def fetch_layer(
    project_weight,
    project_bias,
    output_weight,
    expand_weight,
    expand_bias,
    reduce_weight,
    small_stack,
    layer_index,
):
    return (
        lax.all_gather(project_weight[layer_index], "dp", axis=1, tiled=True),
        lax.all_gather(project_bias[layer_index], "dp", axis=1, tiled=True),
        lax.all_gather(output_weight[layer_index], "dp", axis=1, tiled=True),
        lax.all_gather(expand_weight[layer_index], "dp", axis=0, tiled=True),
        lax.all_gather(expand_bias[layer_index], "dp", axis=0, tiled=True),
        lax.all_gather(reduce_weight[layer_index], "dp", axis=1, tiled=True),
        lax.all_gather(small_stack[layer_index], "dp", axis=1, tiled=True),
    )


def forward_layer(resid, weights, piece_ids, slopes):
    w_project, bias_project, w_output, w_expand, bias_expand, w_reduce, small = weights
    vectors = small.astype(jnp.float32)
    normed = layer_norm(resid, vectors[0], vectors[1])
    gathered = gather_rows(normed.astype(jnp.bfloat16))
    product = jnp.einsum("gd,cde->cge", gathered, w_project, preferred_element_type=jnp.float32)
    biases = jnp.stack([bias_project[0], jnp.zeros_like(bias_project[0]), bias_project[1]]).astype(
        jnp.float32
    )
    triple = (product + biases[:, None, :]).astype(jnp.bfloat16)
    attended, log_total = attend_forward(triple, piece_ids, slopes)
    resid_mid = resid + (scatter_rows(attended, w_output) + vectors[2])
    normed_two = layer_norm(resid_mid, vectors[3], vectors[4])
    gathered_two = gather_rows(normed_two.astype(jnp.bfloat16))
    hidden = jnp.dot(
        gathered_two, w_expand, preferred_element_type=jnp.float32
    ) + bias_expand.astype(jnp.float32)
    active = gelu_tanh(hidden).astype(jnp.bfloat16)
    mlp_sum = scatter_rows(active, w_reduce)
    mlp_keep = (gathered_two, hidden, None)
    resid_out = resid_mid + (mlp_sum + vectors[5])
    return (resid_out, (gathered, triple, attended, log_total, resid_mid, mlp_keep))


def backward_layer(grad_out, resid, weights, kept, piece_ids, slopes):
    w_project, bias_project, w_output, w_expand, bias_expand, w_reduce, small = weights
    vectors = small.astype(jnp.float32)
    gathered, triple, attended, log_total, resid_mid, mlp_keep = kept
    rows_here = grad_out.shape[0]
    rows_in, hidden, full_weights = mlp_keep
    grad_bias_reduce = jnp.sum(grad_out, axis=0)
    active, gelu_pull = jax.vjp(gelu_tanh, hidden)
    active_low = active.astype(jnp.bfloat16)
    grad_mlp = gather_grads(grad_out.astype(jnp.bfloat16))
    grad_reduce = jnp.einsum("gf,gd->fd", active_low, grad_mlp, preferred_element_type=jnp.float32)
    grad_active = jnp.einsum("gd,fd->gf", grad_mlp, w_reduce, preferred_element_type=jnp.float32)
    (grad_hidden,) = gelu_pull(grad_active)
    grad_bias_expand = jnp.sum(grad_hidden, axis=0)
    grad_hidden_low = grad_hidden.astype(jnp.bfloat16)
    grad_expand = jnp.einsum(
        "gd,gf->df", rows_in, grad_hidden_low, preferred_element_type=jnp.float32
    )

    def expand_term(offset, count_rows):
        return jnp.einsum(
            "gf,df->gd", grad_hidden_low, w_expand, preferred_element_type=jnp.float32
        )

    grad_normed_two = scatter_back(expand_term, rows_here)
    unused_two, second_pull = jax.vjp(layer_norm, resid_mid, vectors[3], vectors[4])
    grad_from_norm, grad_gain_two, grad_shift_two = second_pull(grad_normed_two)
    grad_mid = grad_out + grad_from_norm
    grad_bias_output = jnp.sum(grad_mid, axis=0)
    grad_attn = gather_grads(grad_mid.astype(jnp.bfloat16))
    grad_output = jnp.einsum("gt,gd->td", attended, grad_attn, preferred_element_type=jnp.float32)
    grad_attended = jnp.einsum(
        "gd,td->gt", grad_attn, w_output, preferred_element_type=jnp.float32
    ).astype(jnp.bfloat16)
    query_grad, key_grad, value_grad = attend_backward(
        triple, grad_attended, log_total, piece_ids, slopes
    )
    grad_bias_project = jnp.stack([jnp.sum(query_grad, axis=0), jnp.sum(value_grad, axis=0)])
    grad_triple = jnp.stack([query_grad, key_grad, value_grad]).astype(jnp.bfloat16)
    grad_project = jnp.einsum(
        "gd,cge->cde", gathered, grad_triple, preferred_element_type=jnp.float32
    )

    def project_term(offset, count_rows):
        return jnp.einsum("cge,cde->gd", grad_triple, w_project, preferred_element_type=jnp.float32)

    grad_normed = scatter_back(project_term, rows_here)
    unused_one, first_pull = jax.vjp(layer_norm, resid, vectors[0], vectors[1])
    grad_from_first, grad_gain_one, grad_shift_one = first_pull(grad_normed)
    grad_stream = grad_mid + grad_from_first
    small_grads = jnp.stack(
        [
            grad_gain_one,
            grad_shift_one,
            grad_bias_output,
            grad_gain_two,
            grad_shift_two,
            grad_bias_reduce,
        ]
    )
    return (
        grad_stream,
        (
            grad_project,
            grad_bias_project,
            grad_output,
            grad_expand,
            grad_bias_expand,
            grad_reduce,
            small_grads,
        ),
    )


def reduce_layer(layer_grads):
    (
        grad_project,
        grad_bias_project,
        grad_output,
        grad_expand,
        grad_bias_expand,
        grad_reduce,
        small_grads,
    ) = layer_grads
    return (
        lax.psum_scatter(
            grad_project.astype(jnp.bfloat16), "dp", scatter_dimension=1, tiled=True
        ).astype(jnp.float32),
        lax.psum_scatter(
            grad_bias_project.astype(jnp.bfloat16), "dp", scatter_dimension=1, tiled=True
        ).astype(jnp.float32),
        lax.psum_scatter(
            grad_output.astype(jnp.bfloat16), "dp", scatter_dimension=1, tiled=True
        ).astype(jnp.float32),
        lax.psum_scatter(
            grad_expand.astype(jnp.bfloat16), "dp", scatter_dimension=0, tiled=True
        ).astype(jnp.float32),
        lax.psum_scatter(
            grad_bias_expand.astype(jnp.bfloat16), "dp", scatter_dimension=0, tiled=True
        ).astype(jnp.float32),
        lax.psum_scatter(
            grad_reduce.astype(jnp.bfloat16), "dp", scatter_dimension=1, tiled=True
        ).astype(jnp.float32),
        lax.psum_scatter(
            small_grads.astype(jnp.bfloat16), "dp", scatter_dimension=1, tiled=True
        ).astype(jnp.float32),
    )


def on_device(
    layer_input,
    first_gain,
    first_shift,
    project_weight,
    project_bias,
    output_weight,
    output_bias,
    second_gain,
    second_shift,
    expand_weight,
    expand_bias,
    reduce_weight,
    reduce_bias,
    picture_start,
    cotangent,
):
    small_stack = jnp.stack(
        [first_gain, first_shift, output_bias, second_gain, second_shift, reduce_bias], axis=1
    )
    piece_ids = jax.vmap(piece_numbers)(picture_start)
    heads_here = project_weight.shape[3] // HD
    slopes = head_slopes(lax.axis_index("tensor") * heads_here, heads_here)
    resid = layer_input.astype(jnp.float32)
    saved = []
    for layer_index in range(LAYERS):
        weights = fetch_layer(
            project_weight,
            project_bias,
            output_weight,
            expand_weight,
            expand_bias,
            reduce_weight,
            small_stack,
            layer_index,
        )
        resid_next, kept = forward_layer(resid, weights, piece_ids, slopes)
        saved.append((resid, weights, kept))
        resid = resid_next
    layer_output = resid.astype(jnp.bfloat16)
    grad_stream = cotangent.astype(jnp.float32)
    collected = []
    for layer_index in reversed(range(LAYERS)):
        resid_in, weights, kept = saved[layer_index]
        grad_stream, layer_grads = backward_layer(
            grad_stream, resid_in, weights, kept, piece_ids, slopes
        )
        layer_grads = reduce_layer(layer_grads)
        collected.insert(0, layer_grads)
    stacked = tuple(
        (jnp.stack([grad_entry[member] for grad_entry in collected]) for member in range(7))
    )
    (
        grad_project,
        grad_bias_project,
        grad_output,
        grad_expand,
        grad_bias_expand,
        grad_reduce,
        small_grads,
    ) = stacked
    small_grads = lax.psum(small_grads, "tensor")
    return (
        layer_output,
        grad_stream.astype(jnp.bfloat16),
        small_grads[:, 0],
        small_grads[:, 1],
        grad_project,
        grad_bias_project,
        grad_output,
        small_grads[:, 2],
        small_grads[:, 3],
        small_grads[:, 4],
        grad_expand,
        grad_bias_expand,
        grad_reduce,
        small_grads[:, 5],
    )


Z0, Z1, CORE, XBIT, YBIT = 1, 2, 4, 8, 16
AXES = ("dp", "tensor")
NEG = -1e30
BF = jnp.bfloat16
F32 = jnp.float32
VMEM_LIMIT = 24 * 1024 * 1024


def took(us):
    return pl.CostEstimate(flops=int(us * 5e8), bytes_accessed=1, transcendentals=0)


def mesh_is_paired(mesh):
    return dict(mesh.shape) == {"dp": 8, "tensor": 4}


def swap(values, mask):
    return lax.ppermute(values, AXES, [(i, i ^ mask) for i in range(32)])


def swap_some(values, masks):
    pairs = [(i, i ^ masks[(i >> 2) & 1]) for i in range(32)]
    return lax.ppermute(values, AXES, [pair for pair in pairs if pair[0] != pair[1]])


def redeal(values):
    def target(i):
        core, z1 = (i >> 2) & 1, (i >> 1) & 1
        return (i & ~6) | (z1 << 2) | (core << 1)

    return lax.ppermute(values, AXES, [(i, target(i)) for i in range(32) if target(i) != i])


CHIPS = [[0, 2, 4, 6], [1, 3, 5, 7]]


def plane_gather(values):
    return lax.all_gather(values, "dp", axis_index_groups=CHIPS, axis=0, tiled=False)


def plane_scatter(values):
    return lax.psum_scatter(values, "dp", axis_index_groups=CHIPS, scatter_dimension=0, tiled=False)


def turn_index(values, own):
    shape = values.shape
    for bit in range(3):
        values = values.reshape(8 >> (bit + 1), 2, (1 << bit), *shape[1:])
        values = jnp.where((own >> bit) & 1, jnp.concatenate([values[:, 1:], values[:, :1]], axis=1), values)
    return values.reshape(shape)


def after(values, *others):
    return lax.optimization_barrier((values, *others))[0]


def after_all(values, *others):
    if not others:
        return tuple(values)
    return lax.optimization_barrier((*values, *others))[:len(values)]


def task(steps):
    next(steps)
    return steps


def advance(token, *tasks):
    made = []
    for steps in tasks:
        try:
            made += steps.send(token)
        except StopIteration:
            pass
    return made


def dot_nt(a, b):
    return lax.dot_general(a, b, (((1,), (1,)), ((), ())), preferred_element_type=F32)


def dot_nn(a, b):
    return lax.dot_general(a, b, (((1,), (0,)), ((), ())), preferred_element_type=F32)


def head_mask(shape, head):
    lane = lax.broadcasted_iota(jnp.int32, shape, 1)
    return (lane < HD) if head == 0 else (lane >= HD)


def diagonal_bias(rows, columns, first_row, first_column, start):
    key = first_row + lax.broadcasted_iota(jnp.int32, (rows, 1), 0)
    query = first_column + lax.broadcasted_iota(jnp.int32, (1, columns), 1)
    key_in = (key >= start) & (key < start + PIECE)
    query_in = (query >= start) & (query < start + PIECE)
    allowed = (key <= query) | (key_in & query_in)
    reach = (jnp.minimum(key, 2 * query - key) - first_column).astype(F32)
    return jnp.where(allowed, reach, NEG)


def ramp(rows, first_row, first_column):
    return (first_row - first_column + lax.broadcasted_iota(jnp.int32, (rows, 1), 0)).astype(F32)


def attend_kernel(block, rest_bit, slope_ref, start_ref, me_ref, *rest):
    triple_refs, rest = rest[:12], rest[12:]
    near_ref, away_ref, exact_ref, lse_ref, q_ref, k_ref, v_ref, vt_ref, acc_ref, max_ref, bias_ref, tail_ref = rest
    pair = pl.program_id(0)
    turn = pl.program_id(1)
    me = me_ref[0]
    step = (2 * turn + rest_bit) ^ me
    length = k_ref.shape[0]
    first = step * block

    def at(index):
        return pl.multiple_of((index ^ me) * block, block)

    start = start_ref[first // (length // start_ref.shape[0])]

    @pl.when(turn == 0)
    def _():
        for index in range(4):
            here = slice(index * block, (index + 1) * block)
            q_ref[here, :] = triple_refs[3 * index][...] * jnp.asarray(HD ** -0.5, BF)
            k_ref[here, :] = triple_refs[3 * index + 1][...]
            v_ref[here, :] = triple_refs[3 * index + 2][...]
        for head in range(2):
            mixed = jnp.where(head_mask((length, 2 * HD), head), v_ref[...], jnp.ones((), BF))
            vt_ref[head] = mixed.T

    bias_ref[...] = diagonal_bias(block, block, first, first, start)
    q_block = q_ref[pl.ds(at(step), block), :]
    heads = [jnp.where(head_mask(q_block.shape, head), q_block, jnp.zeros((), BF)) for head in range(2)]
    slopes = [slope_ref[2 * pair + head] for head in range(2)]
    acc_ref[...] = jnp.zeros_like(acc_ref)
    max_ref[...] = jnp.full_like(max_ref, NEG)

    def absorb(head, scores, vt):
        old = max_ref[head]
        new = jnp.maximum(old, jnp.max(scores, axis=0, keepdims=True))
        weights = jnp.exp(scores - new).astype(BF)
        acc_ref[head] = acc_ref[head] * jnp.exp(old - new) + dot_nn(vt, weights)
        max_ref[head] = new

    def full(index, carry):
        place = at(index)
        keys = k_ref[pl.ds(place, block), :]
        slant = ramp(block, index * block, first)
        for head in range(2):
            absorb(head, dot_nt(keys, heads[head]) + slopes[head] * slant, vt_ref[head, :, pl.ds(place, block)])
        return carry

    place = at(step)
    for head in range(2):
        absorb(
            head,
            dot_nt(k_ref[pl.ds(place, block), :], heads[head]) + slopes[head] * bias_ref[...],
            vt_ref[head, :, pl.ds(place, block)],
        )
    lax.fori_loop(0, step, full, 0)
    edge = first + block

    @pl.when((start < edge) & (start + PIECE > edge))
    def _():
        after = at(step + 1)
        tail_ref[...] = diagonal_bias(PIECE, block, edge, first, start)
        for head in range(2):
            absorb(
                head,
                dot_nt(k_ref[pl.ds(after, PIECE), :], heads[head]) + slopes[head] * tail_ref[...],
                vt_ref[head, :, pl.ds(after, PIECE)],
            )

    outs = []
    for head in range(2):
        acc = acc_ref[head]
        total = acc[HD:HD + 1] if head == 0 else acc[0:1]
        outs.append((acc * (1.0 / total))[head * HD:(head + 1) * HD])
        lse_ref[0, head:head + 1, :] = max_ref[head] + jnp.log(total)
    mixed = jnp.concatenate(outs, axis=0)
    exact_ref[...] = mixed
    final = mixed.T.astype(BF)

    @pl.when(turn == 0)
    def _():
        near_ref[...] = final

    @pl.when(turn == 1)
    def _():
        away_ref[...] = final


def triple_specs(block, pairs):
    specs = []
    for index in range(4):
        for part in range(3):
            specs.append(pl.BlockSpec((block, 2 * HD), functools.partial(lambda part, p, i: (0, part * pairs + p), part)))
    return specs


def attend(blocks, rest_bit, slopes, starts, me):
    block, width = blocks[0].shape[0], blocks[0].shape[1] // 3
    pairs = width // (2 * HD)
    length = 4 * block
    smem = pl.BlockSpec(memory_space=pltpu.SMEM)
    return pl.pallas_call(
        functools.partial(attend_kernel, block, rest_bit),
        grid=(pairs, 2),
        in_specs=[smem, smem, smem] + triple_specs(block, pairs),
        out_specs=[
            pl.BlockSpec((block, 2 * HD), lambda p, i: (0, p)),
            pl.BlockSpec((block, 2 * HD), lambda p, i: (0, p)),
            pl.BlockSpec((2 * HD, block), lambda p, i: (p, i)),
            pl.BlockSpec((1, 8, block), lambda p, i: (p, 0, i)),
        ],
        out_shape=[
            jax.ShapeDtypeStruct((block, width), BF),
            jax.ShapeDtypeStruct((block, width), BF),
            jax.ShapeDtypeStruct((width, 2 * block), F32),
            jax.ShapeDtypeStruct((pairs, 8, 2 * block), F32),
        ],
        scratch_shapes=[
            pltpu.VMEM((length, 2 * HD), BF),
            pltpu.VMEM((length, 2 * HD), BF),
            pltpu.VMEM((length, 2 * HD), BF),
            pltpu.VMEM((2, 2 * HD, length), BF),
            pltpu.VMEM((2, 2 * HD, block), F32),
            pltpu.VMEM((2, 1, block), F32),
            pltpu.VMEM((block, block), F32),
            pltpu.VMEM((PIECE, block), F32),
        ],
        compiler_params=pltpu.CompilerParams(vmem_limit_bytes=VMEM_LIMIT),
        cost_estimate=took(17),
        name="attend",
    )(slopes, starts, me, *[b for b in blocks for _ in range(3)])


def pull_kernel(block, pair, slope_ref, start_ref, me_ref, *rest):
    triple_refs, grad_refs, rest = rest[:12], rest[12:16], rest[16:]
    exact_refs, lse_refs, rest = rest[0:2], rest[2:4], rest[4:]
    mine_ref, away_ref, q_ref, k_ref, v_ref, g_ref, kt_ref, dk_acc, dv_acc, dqt_ref, bias_ref, tail_ref = rest
    turn = pl.program_id(0)
    me = me_ref[0]
    step = turn ^ me
    length = k_ref.shape[0]
    first = step * block
    half, bit = turn // 2, turn % 2

    def at(index):
        return pl.multiple_of((index ^ me) * block, block)

    start = start_ref[first // (length // start_ref.shape[0])]

    @pl.when(turn == 0)
    def _():
        for index in range(4):
            here = slice(index * block, (index + 1) * block)
            q_ref[here, :] = triple_refs[3 * index][...] * jnp.asarray(HD ** -0.5, BF)
            k_ref[here, :] = triple_refs[3 * index + 1][...]
            v_ref[here, :] = triple_refs[3 * index + 2][...]
            g_ref[here, :] = grad_refs[index][...]
        kt_ref[...] = k_ref[...].T
        dk_acc[...] = jnp.zeros_like(dk_acc)
        dv_acc[...] = jnp.zeros_like(dv_acc)

    bias_ref[...] = diagonal_bias(block, block, first, first, start)
    dqt_ref[...] = jnp.zeros_like(dqt_ref)
    zero = jnp.zeros((), BF)
    q_block = q_ref[pl.ds(at(step), block), :]
    g_block = g_ref[pl.ds(at(step), block), :]
    masks = [head_mask(q_block.shape, head) for head in range(2)]
    q_heads = [jnp.where(mask, q_block, zero) for mask in masks]
    g_heads = [jnp.where(mask, g_block, zero) for mask in masks]
    slopes = [slope_ref[2 * pair + head] for head in range(2)]
    lanes = pl.ds(pl.multiple_of(half * block, block), block)
    exact = jnp.where(bit == 0, exact_refs[0][:, lanes], exact_refs[1][:, lanes])
    log_total = jnp.where(bit == 0, lse_refs[0][0, :, lanes], lse_refs[1][0, :, lanes])
    product = g_block.astype(F32).T * exact
    deltas = [jnp.sum(product[head * HD:(head + 1) * HD], axis=0, keepdims=True) for head in range(2)]

    def absorb(place, rows, bias_of):
        keys = k_ref[pl.ds(place, rows), :]
        values = v_ref[pl.ds(place, rows), :]
        dk = dk_acc[pl.ds(place, rows), :]
        dv = dv_acc[pl.ds(place, rows), :]
        for head in range(2):
            scores = dot_nt(keys, q_heads[head]) + slopes[head] * bias_of
            weights = jnp.exp(scores - log_total[head:head + 1, :])
            dv = dv + dot_nn(weights.astype(BF), g_heads[head])
            grad_p = dot_nt(values, g_heads[head])
            grad_s = (weights * (grad_p - deltas[head])).astype(BF)
            dk = dk + dot_nn(grad_s, q_heads[head])
            dqt_ref[head * HD:(head + 1) * HD, :] += dot_nn(kt_ref[head * HD:(head + 1) * HD, pl.ds(place, rows)], grad_s)
        dk_acc[pl.ds(place, rows), :] = dk
        dv_acc[pl.ds(place, rows), :] = dv

    absorb(at(step), block, bias_ref[...])

    def full(index, carry):
        absorb(at(index), block, ramp(block, index * block, first))
        return carry

    lax.fori_loop(0, step, full, 0)
    edge = first + block

    @pl.when((start < edge) & (start + PIECE > edge))
    def _():
        tail_ref[...] = diagonal_bias(PIECE, block, edge, first, start)
        absorb(at(step + 1), PIECE, tail_ref[...])

    grad_q = (dqt_ref[...].T * (HD ** -0.5)).astype(BF)
    here = pl.ds(pl.multiple_of(bit * block, block), block)

    @pl.when(half == 0)
    def _():
        mine_ref[0, here, :] = grad_q

    @pl.when(half == 1)
    def _():
        away_ref[0, here, :] = grad_q

    @pl.when(turn == 3)
    def _():
        for part, ref in ((1, dk_acc), (2, dv_acc)):
            mine_ref[part] = ref[:2 * block].astype(BF)
            away_ref[part] = ref[2 * block:].astype(BF)


def attend_pull(pair, blocks, grads, exacts, log_totals, slopes, starts, me):
    block, width = blocks[0].shape[0], blocks[0].shape[1] // 3
    pairs = width // (2 * HD)
    length = 4 * block
    smem = pl.BlockSpec(memory_space=pltpu.SMEM)
    triples = [pl.BlockSpec((block, 2 * HD), functools.partial(lambda part, i: (0, part * pairs + pair), part)) for part in range(3)]
    rows = pl.BlockSpec((block, 2 * HD), lambda i: (0, pair))
    wide = pl.BlockSpec((2 * HD, 2 * block), lambda i: (pair, 0))
    sums = pl.BlockSpec((1, 8, 2 * block), lambda i: (pair, 0, 0))
    out = pl.BlockSpec((3, 2 * block, 2 * HD), lambda i: (0, 0, 0))
    return pl.pallas_call(
        functools.partial(pull_kernel, block, pair),
        grid=(4,),
        in_specs=[smem, smem, smem] + triples * 4 + [rows] * 4 + [wide] * 2 + [sums] * 2,
        out_specs=[out, out],
        out_shape=[jax.ShapeDtypeStruct((3, 2 * block, 2 * HD), BF)] * 2,
        scratch_shapes=[
            pltpu.VMEM((length, 2 * HD), BF),
            pltpu.VMEM((length, 2 * HD), BF),
            pltpu.VMEM((length, 2 * HD), BF),
            pltpu.VMEM((length, 2 * HD), BF),
            pltpu.VMEM((2 * HD, length), BF),
            pltpu.VMEM((length, 2 * HD), F32),
            pltpu.VMEM((length, 2 * HD), F32),
            pltpu.VMEM((2 * HD, block), F32),
            pltpu.VMEM((block, block), F32),
            pltpu.VMEM((PIECE, block), F32),
        ],
        compiler_params=pltpu.CompilerParams(vmem_limit_bytes=VMEM_LIMIT),
        cost_estimate=took(22),
        name="attend_pull",
    )(slopes, starts, me, *[b for b in blocks for _ in range(3)], *grads, *exacts, *log_totals)


def head_columns(refs, quarter, first, last):
    return jnp.concatenate(
        [refs[odd][chip ^ refs[2][0], 1 - quarter if odd else quarter, :, first:last] for chip in range(4) for odd in range(2)],
        axis=0,
    )


def placed(arrays):
    return [
        pl.BlockSpec(memory_space=pltpu.SMEM if a.dtype == jnp.int32 else pltpu.VMEM) for a in arrays
    ]


def call_once(kernel, name, outs, args, us):
    return pl.pallas_call(
        kernel,
        in_specs=placed(args),
        out_specs=placed(outs),
        out_shape=outs,
        compiler_params=pltpu.CompilerParams(vmem_limit_bytes=VMEM_LIMIT),
        cost_estimate=took(us),
        name=name,
    )(*args)


def project_kernel(rows_ref, bias_ref, *rest):
    weight_refs, out_refs = rest[:3], rest[3:]
    rows = rows_ref[...]
    for quarter in (1, 0):
        out = dot_nn(rows, head_columns(weight_refs, quarter, 0, 768)) + bias_ref[quarter:quarter + 1]
        out_refs[quarter][...] = out.astype(BF)


def project(rows, bias, pieces):
    out = jax.ShapeDtypeStruct((rows.shape[0], 768), BF)
    return call_once(project_kernel, "project", [out, out], [rows, bias, *pieces], 5)


def mix_term(mixed_refs, weight_refs):
    rows = jnp.concatenate([ref[...] for ref in mixed_refs], axis=1)
    weight = jnp.concatenate([head_columns(weight_refs, quarter, 768, 1024) for quarter in range(2)], axis=1)
    return dot_nt(rows, weight)


def mix_far_kernel(mine_ref, other_ref, *rest):
    rest[3][...] = mix_term((mine_ref, other_ref), rest[:3]).astype(BF)


def mix_far(mine, other, pieces):
    out = jax.ShapeDtypeStruct((mine.shape[0], 1024), BF)
    return call_once(mix_far_kernel, "mix_far", [out], [mine, other, *pieces], 4)[0]


def mix_near_kernel(mine_ref, other_ref, far_ref, resid_ref, vector_ref, *rest):
    weight_refs, (mid_ref, normed_ref, flip_ref) = rest[:3], rest[3:]
    term = mix_term((mine_ref, other_ref), weight_refs)
    mid = resid_ref[...] + (term + far_ref[...].astype(F32) + vector_ref[2:3])
    mid_ref[...] = mid
    normed = (normalize(mid)[0] * vector_ref[3:4] + vector_ref[4:5]).astype(BF)
    normed_ref[...] = normed
    flip_ref[...] = flipped(normed)


def mix_near(mine, other, far, resid, vectors, pieces):
    outs = [
        jax.ShapeDtypeStruct(resid.shape, F32),
        jax.ShapeDtypeStruct(resid.shape, BF),
        jax.ShapeDtypeStruct(resid.shape, BF),
    ]
    return call_once(mix_near_kernel, "mix_near", outs, [mine, other, far, resid, vectors, *pieces], 6)


def unmix_kernel(grad_ref, *rest):
    weight_refs, out_refs = rest[:3], rest[3:]
    grad = grad_ref[...]
    for quarter in (1, 0):
        out_refs[quarter][...] = dot_nn(grad, head_columns(weight_refs, quarter, 768, 1024)).astype(BF)


def unmix(grad, pieces):
    out = jax.ShapeDtypeStruct((grad.shape[0], 256), BF)
    return call_once(unmix_kernel, "unmix", [out, out], [grad, *pieces], 4)


def unproject_term(grad_refs, weight_refs, first):
    rows = jnp.concatenate(
        [ref[part, first:first + 512] for pair in grad_refs for part in range(3) for ref in pair], axis=1
    )
    weight = jnp.concatenate([head_columns(weight_refs, quarter, 0, 768) for quarter in range(2)], axis=1)
    return dot_nt(rows, weight)


def unproject_far_kernel(*rest):
    rest[7][...] = unproject_term((rest[0:2], rest[2:4]), rest[4:7], 512).astype(BF)


def unproject_far(mine, other, pieces):
    out = jax.ShapeDtypeStruct((512, 1024), BF)
    return call_once(unproject_far_kernel, "unproject_far", [out], [*mine, *other, *pieces], 6)[0]


def unproject_near_kernel(last, own_ref, *rest):
    mine, other, rest = rest[0:2], rest[2:4], rest[4:]
    far_ref, resid_ref, grad_mid_ref, vector_ref, rest = *rest[:4], rest[4:]
    weight_refs, (grad_ref, low_ref, sums_ref) = rest[:3], rest[3:]
    term = unproject_term((mine, other), weight_refs, 0) + far_ref[...].astype(F32)
    grad_norm, grad_gain, grad_shift = norm_pull(resid_ref[...], vector_ref[0:1], term)
    grad = grad_mid_ref[...] + grad_norm
    grad_ref[...] = grad
    if last:
        put_turned(low_ref, own_ref[0], grad.astype(BF))
    else:
        low_ref[...] = flipped(grad).astype(BF)
    sums_ref[...] = jnp.concatenate([grad_gain, grad_shift, jnp.zeros((6, grad.shape[1]), F32)], axis=0)


def unproject_near(last, own_keep, mine, other, far, resid, grad_mid, vectors, pieces):
    outs = [
        jax.ShapeDtypeStruct(resid.shape, F32),
        jax.ShapeDtypeStruct(resid.shape, BF),
        jax.ShapeDtypeStruct((8, resid.shape[1]), F32),
    ]
    args = [own_keep, *mine, *other, far, resid, grad_mid, vectors, *pieces]
    kernel = functools.partial(unproject_near_kernel, last)
    return call_once(kernel, "unproject_near", outs, args, 9)


def head_grads_kernel(turn_ref, near_ref, far_ref, grad_near_ref, grad_far_ref, *rest):
    pairs, rest = (rest[0:2], rest[2:4]), rest[4:]
    mixed_refs, out_refs, bias_ref = (rest[0:2], rest[2:4]), rest[4:6], rest[6]
    rows_t = jnp.concatenate([near_ref[...], far_ref[...]], axis=0).T
    grad_t = jnp.concatenate([grad_near_ref[...], grad_far_ref[...]], axis=0).T
    for quarter, refs in enumerate(pairs):
        grads = [jnp.concatenate([ref[part] for ref in refs], axis=1) for part in range(3)]
        for part in range(4):
            if part < 3:
                term = dot_nn(rows_t, grads[part])
            else:
                term = dot_nn(grad_t, jnp.concatenate([m[...] for m in mixed_refs[quarter]], axis=0))
            term = term.astype(BF)
            for index in range(8):
                chip, odd = index // 2, index % 2
                place = 1 - quarter if odd else quarter
                out_refs[odd][chip ^ turn_ref[0], place, :, part * 256:(part + 1) * 256] = term[index * 128:(index + 1) * 128]
        for row, part in ((0, 0), (1, 2)):
            total = jnp.sum(grads[part].astype(F32), axis=0, keepdims=True)
            bias_ref[2 * quarter + row:2 * quarter + row + 1, :] = total
    bias_ref[4:8, :] = jnp.zeros((4, 256), F32)


def head_grads(turn, near, far, grad_near, grad_far, mine, other, mixed_mine, mixed_other):
    outs = [jax.ShapeDtypeStruct((4, 2, 128, 1024), BF)] * 2 + [jax.ShapeDtypeStruct((8, 256), F32)]
    args = [turn, near, far, grad_near, grad_far, *mine, *other, *mixed_mine, *mixed_other]
    return call_once(head_grads_kernel, "head_grads", outs, args, 10)


GELU_A = 0.7978845608028654
GELU_B = 0.044715


def normalize(values):
    centred = values - jnp.mean(values, axis=-1, keepdims=True)
    spread = lax.rsqrt(jnp.mean(centred * centred, axis=-1, keepdims=True) + NORM_EPS)
    return centred * spread, spread


def norm_pull(values, gain, grad):
    unit, spread = normalize(values)
    grad_unit = grad * gain
    inner = grad_unit - jnp.mean(grad_unit, axis=-1, keepdims=True)
    inner = inner - unit * jnp.mean(grad_unit * unit, axis=-1, keepdims=True)
    return spread * inner, jnp.sum(grad * unit, axis=0, keepdims=True), jnp.sum(grad, axis=0, keepdims=True)


def flipped(values):
    return jnp.concatenate([values[:, (block ^ 1) * 128:(block ^ 1) * 128 + 128] for block in range(8)], axis=1)


def put_turned(out_ref, own, values):
    for block in range(8):
        here = pl.ds(pl.multiple_of((block ^ own) * 128, 128), 128)
        out_ref[:, here] = values[:, block * 128:(block + 1) * 128]


def enter_kernel(own_ref, direct_ref, moved_ref, vector_ref, resid_ref, normed_ref, flip_ref):
    own, keep = own_ref[0], own_ref[1]
    for block in range(8):
        here = pl.ds(pl.multiple_of((block ^ own) * 128, 128), 128)
        rows = jnp.where(keep > 0, direct_ref[:, here].astype(F32), moved_ref[:, here].astype(F32))
        resid_ref[:, block * 128:(block + 1) * 128] = rows
    values = resid_ref[...]
    normed_ref[...] = (normalize(values)[0] * vector_ref[0:1] + vector_ref[1:2]).astype(BF)
    flip_ref[...] = flipped(values).astype(BF)


def enter(own_keep, direct, moved, vectors):
    rows, features = direct.shape
    smem = pl.BlockSpec(memory_space=pltpu.SMEM)
    vmem = pl.BlockSpec(memory_space=pltpu.VMEM)
    return pl.pallas_call(
        enter_kernel,
        in_specs=[smem, vmem, vmem, vmem],
        out_specs=[vmem, vmem, vmem],
        out_shape=[
            jax.ShapeDtypeStruct((rows, features), F32),
            jax.ShapeDtypeStruct((rows, features), BF),
            jax.ShapeDtypeStruct((rows, features), BF),
        ],
        compiler_params=pltpu.CompilerParams(vmem_limit_bytes=VMEM_LIMIT),
        cost_estimate=took(4),
        name="enter",
    )(own_keep, direct, moved, vectors)


def half_specs(tile, weights):
    def spec(half, chip, whole):
        def index(f, turn):
            column = jnp.clip(f - 2 * half, 0, 1)
            return (chip ^ turn[0], 0, 0, column) if whole else (0, 0, column)

        return pl.BlockSpec((None, 2, 128, 2 * tile) if whole else (2, 128, 2 * tile), index)

    return [spec(half, chip, len(weights[half]) == 1) for half in range(2) for chip in range(4)]


def half_arrays(weights):
    return [array for half in weights for array in (half if len(half) == 4 else half * 4)]


def by_half(step, weight_refs, body):
    @pl.when(step < 2)
    def _():
        body(weight_refs[:4])

    @pl.when(step >= 2)
    def _():
        body(weight_refs[4:])


def joined(refs, first, last):
    return jnp.concatenate([ref[core, :, first:last] for ref in refs for core in range(2)], axis=0)


def mlp_kernel(turn_ref, normed_ref, other_ref, bias_ref, *rest):
    weight_refs, (hidden_ref, active_ref, near_ref, away_ref, acc_ref) = rest[:8], rest[8:]
    rows, tile = normed_ref.shape[0], hidden_ref.shape[1]
    step = pl.program_id(0)

    @pl.when(step == 0)
    def _():
        acc_ref[...] = jnp.zeros_like(acc_ref)

    def body(refs):
        expand, reduce = joined(refs, 0, tile), joined(refs, tile, 2 * tile)
        for first, ref in ((0, normed_ref), (rows, other_ref)):
            hidden = dot_nn(ref[...], expand) + bias_ref[...]
            inner = jnp.tanh(GELU_A * (hidden + GELU_B * hidden * hidden * hidden))
            active = (0.5 * hidden * (1.0 + inner)).astype(BF)
            hidden_ref[first:first + rows] = hidden.astype(BF)
            active_ref[first:first + rows] = active
            acc_ref[first:first + rows] += dot_nt(active, reduce)

    by_half(step, weight_refs, body)

    @pl.when(step == pl.num_programs(0) - 1)
    def _():
        near_ref[...] = acc_ref[:rows]
        away_ref[...] = flipped(acc_ref[rows:]).astype(BF)


def mlp_forward(turn, normed, other, bias, weights):
    rows, features = normed.shape
    units = bias.shape[1]
    tile = 512
    whole = pl.BlockSpec((rows, features), lambda f, turn: (0, 0))
    tiles = pl.BlockSpec((2 * rows, tile), lambda f, turn: (0, f))
    return pl.pallas_call(
        mlp_kernel,
        grid_spec=pltpu.PrefetchScalarGridSpec(
            num_scalar_prefetch=1,
            grid=(units // tile,),
            in_specs=[whole, whole, pl.BlockSpec((1, tile), lambda f, turn: (0, f))] + half_specs(tile, weights),
            out_specs=[tiles, tiles, whole, whole],
            scratch_shapes=[pltpu.VMEM((2 * rows, features), F32)],
        ),
        out_shape=[
            jax.ShapeDtypeStruct((2 * rows, units), BF),
            jax.ShapeDtypeStruct((2 * rows, units), BF),
            jax.ShapeDtypeStruct((rows, features), F32),
            jax.ShapeDtypeStruct((rows, features), BF),
        ],
        compiler_params=pltpu.CompilerParams(vmem_limit_bytes=VMEM_LIMIT),
        cost_estimate=took(18),
        name="mlp_forward",
    )(turn, normed, other, bias, *half_arrays(weights))


def mlp_close_kernel(last, own_ref, near_ref, got_ref, mid_ref, vector_ref, out_ref, next_ref):
    out = mid_ref[...] + (near_ref[...] + got_ref[...].astype(F32) + vector_ref[5:6])
    out_ref[...] = out
    if last:
        put_turned(next_ref, own_ref[0], out.astype(BF))
    else:
        next_ref[...] = (normalize(out)[0] * vector_ref[6:7] + vector_ref[7:8]).astype(BF)


def mlp_close(last, own_keep, near, got, mid, vectors):
    outs = [jax.ShapeDtypeStruct(mid.shape, F32), jax.ShapeDtypeStruct(mid.shape, BF)]
    args = [own_keep, near, got, mid, vectors]
    return call_once(functools.partial(mlp_close_kernel, last), "mlp_close", outs, args, 3)


def mlp_pull_kernel(turn_ref, grad_ref, other_ref, hidden_ref, *rest):
    weight_refs = rest[:8]
    grad_hidden_ref, grad_bias_ref, near_ref, away_ref, acc_ref, low_ref = rest[8:]
    rows, tile = grad_ref.shape[0], hidden_ref.shape[1]
    step = pl.program_id(0)

    @pl.when(step == 0)
    def _():
        low_ref[:rows] = grad_ref[...].astype(BF)
        low_ref[rows:] = other_ref[...]
        acc_ref[...] = jnp.zeros_like(acc_ref)

    def body(refs):
        expand, reduce = joined(refs, 0, tile), joined(refs, tile, 2 * tile)
        total = jnp.zeros((1, tile), F32)
        for first in (0, rows):
            here = slice(first, first + rows)
            hidden = hidden_ref[here].astype(F32)
            squared = hidden * hidden
            inner = jnp.tanh(GELU_A * hidden * (1.0 + GELU_B * squared))
            slope = 0.5 * (1.0 + inner) + 0.5 * hidden * (1.0 - inner * inner) * (GELU_A * (1.0 + 3.0 * GELU_B * squared))
            grad_hidden = dot_nn(low_ref[here], reduce) * slope
            total = total + jnp.sum(grad_hidden, axis=0, keepdims=True)
            grad_hidden = grad_hidden.astype(BF)
            grad_hidden_ref[here] = grad_hidden
            acc_ref[here] += dot_nt(grad_hidden, expand)
        grad_bias_ref[...] = total

    by_half(step, weight_refs, body)

    @pl.when(step == pl.num_programs(0) - 1)
    def _():
        near_ref[...] = acc_ref[:rows]
        away_ref[...] = flipped(acc_ref[rows:]).astype(BF)


def mlp_backward(turn, grad, other, hidden, weights):
    rows, features = grad.shape
    units = hidden.shape[1]
    tile = 512
    whole = pl.BlockSpec((rows, features), lambda f, turn: (0, 0))
    tiles = pl.BlockSpec((2 * rows, tile), lambda f, turn: (0, f))
    return pl.pallas_call(
        mlp_pull_kernel,
        grid_spec=pltpu.PrefetchScalarGridSpec(
            num_scalar_prefetch=1,
            grid=(units // tile,),
            in_specs=[whole, whole, tiles] + half_specs(tile, weights),
            out_specs=[tiles, pl.BlockSpec((1, tile), lambda f, turn: (0, f)), whole, whole],
            scratch_shapes=[pltpu.VMEM((2 * rows, features), F32), pltpu.VMEM((2 * rows, features), BF)],
        ),
        out_shape=[
            jax.ShapeDtypeStruct((2 * rows, units), BF),
            jax.ShapeDtypeStruct((1, units), F32),
            jax.ShapeDtypeStruct((rows, features), F32),
            jax.ShapeDtypeStruct((rows, features), BF),
        ],
        compiler_params=pltpu.CompilerParams(vmem_limit_bytes=VMEM_LIMIT),
        cost_estimate=took(22),
        name="mlp_backward",
    )(turn, grad, other, hidden, *half_arrays(weights))


def mlp_open_kernel(near_ref, got_ref, mid_ref, grad_ref, vector_ref, grad_mid_ref, grad_low_ref, sums_ref):
    grad = grad_ref[...]
    term = near_ref[...] + got_ref[...].astype(F32)
    grad_norm, grad_gain, grad_shift = norm_pull(mid_ref[...], vector_ref[3:4], term)
    grad_mid = grad + grad_norm
    grad_mid_ref[...] = grad_mid
    grad_low_ref[...] = grad_mid.astype(BF)
    rows = [jnp.sum(grad_mid, axis=0, keepdims=True), grad_gain, grad_shift, jnp.sum(grad, axis=0, keepdims=True)]
    sums_ref[...] = jnp.concatenate(rows + [jnp.zeros((4, grad.shape[1]), F32)], axis=0)


def mlp_open(near, got, mid, grad, vectors):
    outs = [
        jax.ShapeDtypeStruct(mid.shape, F32),
        jax.ShapeDtypeStruct(mid.shape, BF),
        jax.ShapeDtypeStruct((8, mid.shape[1]), F32),
    ]
    return call_once(mlp_open_kernel, "mlp_open", outs, [near, got, mid, grad, vectors], 5)


def unit_grads_kernel(second, left_ref, other_ref, right_ref, own_ref, pair_ref, single_ref, left_t_ref):
    @pl.when(pl.program_id(0) == 0)
    def _():
        left_t_ref[...] = jnp.concatenate([left_ref[...].astype(BF), other_ref[...]], axis=0).T

    grad = dot_nn(left_t_ref[...], right_ref[...]).astype(BF)
    single, direct = (1, 2) if second == "x" else (2, 1)
    for core in range(2):
        own_ref[0, core] = grad[core * 128:(core + 1) * 128]
        single_ref[0, core] = grad[(2 * single + core) * 128:(2 * single + core + 1) * 128]
        pair_ref[0, 0, core] = grad[(2 * direct + core) * 128:(2 * direct + core + 1) * 128]
        pair_ref[0, 1, core] = grad[(6 + core) * 128:(7 + core) * 128]


def unit_grads(second, left, other, right):
    rows, features = left.shape
    units = right.shape[1]
    tile = 512
    whole = pl.BlockSpec((rows, features), lambda f: (0, 0))
    out = pl.BlockSpec((1, 2, 128, tile), lambda f: (f // 2, 0, 0, f % 2))
    one = jax.ShapeDtypeStruct((2, 2, 128, 1024), BF)
    return pl.pallas_call(
        functools.partial(unit_grads_kernel, second),
        grid=(units // tile,),
        in_specs=[whole, whole, pl.BlockSpec((2 * rows, tile), lambda f: (0, f))],
        out_specs=[out, pl.BlockSpec((1, 2, 2, 128, tile), lambda f: (f // 2, 0, 0, 0, f % 2)), out],
        out_shape=[one, jax.ShapeDtypeStruct((2, 2, 2, 128, 1024), BF), one],
        scratch_shapes=[pltpu.VMEM((features, 2 * rows), BF)],
        compiler_params=pltpu.CompilerParams(vmem_limit_bytes=VMEM_LIMIT),
        cost_estimate=took(10),
        name="unit_grads",
    )(left, other, right)


def unit_grads_whole_kernel(turn_ref, left_ref, other_ref, right_ref, out_ref, left_t_ref):
    @pl.when(pl.program_id(0) == 0)
    def _():
        left_t_ref[...] = jnp.concatenate([left_ref[...].astype(BF), other_ref[...]], axis=0).T

    grad = dot_nn(left_t_ref[...], right_ref[...]).astype(BF)
    for chip in range(4):
        for core in range(2):
            first = (2 * chip + core) * 128
            out_ref[chip ^ turn_ref[0], 0, core] = grad[first:first + 128]


def unit_grads_whole(turn, left, other, right):
    rows, features = left.shape
    units = right.shape[1]
    tile = 512
    whole = pl.BlockSpec((rows, features), lambda f: (0, 0))
    return pl.pallas_call(
        unit_grads_whole_kernel,
        grid=(units // tile,),
        in_specs=[
            pl.BlockSpec(memory_space=pltpu.SMEM),
            whole,
            whole,
            pl.BlockSpec((2 * rows, tile), lambda f: (0, f)),
        ],
        out_specs=pl.BlockSpec((4, 1, 2, 128, tile), lambda f: (0, f // 2, 0, 0, f % 2)),
        out_shape=jax.ShapeDtypeStruct((4, 2, 2, 128, 1024), BF),
        scratch_shapes=[pltpu.VMEM((features, 2 * rows), BF)],
        compiler_params=pltpu.CompilerParams(vmem_limit_bytes=VMEM_LIMIT),
        cost_estimate=took(10),
        name="unit_grads_whole",
    )(turn, left, other, right)


MESH = pl.DeviceIdType.MESH


def flip(index, bit):
    return index + bit - 2 * bit * ((index // bit) % 2)


def peer(mask):
    dp, tensor = lax.axis_index("dp"), lax.axis_index("tensor")
    for bit in (1, 2):
        tensor = flip(tensor, bit) if mask & bit else tensor
        dp = flip(dp, bit) if mask & (CORE * bit) else dp
    dp = flip(dp, 4) if mask & YBIT else dp
    return {"dp": dp, "tensor": tensor}


def xor_block(block, own):
    return sum(bit * ((block // bit + own // bit) % 2) for bit in (1, 2, 4))


def greet(masks):
    barrier = pltpu.get_barrier_semaphore()
    for mask in masks:
        pl.semaphore_signal(barrier, inc=1, device_id=peer(mask), device_id_type=MESH)
    pl.semaphore_wait(barrier, len(masks))


def project_rows(rows, weight_refs, bias_ref, layer, out_refs):
    for quarter in (1, 0):
        weight = jnp.concatenate(
            [weight_refs[odd][chip, 1 - quarter if odd else quarter, :, 0:768] for chip in range(4) for odd in range(2)],
            axis=0,
        )
        out_refs[quarter][...] = (dot_nn(rows, weight) + bias_ref[layer, quarter:quarter + 1]).astype(BF)


SMALL_ROWS = 11


def start_kernel(
    layers, x_ref, project_ref, output_ref, expand_ref, reduce_ref,
    *rest,
):
    six_refs, bias_ref, unit_row_ref, rest = rest[:6], rest[6], rest[7], rest[8:]
    (
    resid_ref, normed_ref, far_ref, even_ref, odd_ref, first_ref, heads_ref, pairs_ref, vector_ref, head_bias_ref, unit_bias_ref,
    near_mine_ref, far_mine_ref, got_near_ref, got_far_ref,
    came_ref, piece_ref, every_ref, near_other_ref, far_other_ref, local_sem, send_sem, recv_sem,
    ) = rest
    own, place = lax.axis_index("dp"), lax.axis_index("tensor")
    core = own % 2
    keep = core == place // 2
    count = [0]

    def copy(source, target, device):
        index = count[0]
        count[0] += 1
        return pltpu.make_async_remote_copy(
            src_ref=source, dst_ref=target, send_sem=send_sem.at[index], recv_sem=recv_sem.at[index],
            device_id=device, device_id_type=MESH,
        )

    greet((1, 2, 4, 6, 8, 16))
    tokens = copy(x_ref, came_ref, peer(CORE | Z1))
    stay = pltpu.make_async_copy(x_ref, came_ref, local_sem)

    @pl.when(keep)
    def _():
        stay.start()

    @pl.when(jnp.logical_not(keep))
    def _():
        tokens.start()

    def pack_heads_into(target, layer):
        for part in range(3):
            target[:, part * 256:(part + 1) * 256] = project_ref[layer, part]
        target[:, 768:1024] = output_ref[layer].T

    def pack_units_into(target, layer):
        for half in range(2):
            here = slice(half * 512, (half + 1) * 512)
            target[:, half * 1024:half * 1024 + 512] = expand_ref[layer, :, here]
            target[:, half * 1024 + 512:half * 1024 + 1024] = reduce_ref[layer, here, :].T

    pack_heads_into(even_ref.at[0, core], 0)
    along = copy(even_ref.at[0, core], even_ref.at[0, 1 - core], peer(Z1))
    along.start()
    every_ref[0, 0] = jnp.zeros(every_ref.shape[2:], F32)
    lane = lax.broadcasted_iota(jnp.int32, (1, 128), 1)
    for layer in range(layers):
        base = layer * SMALL_ROWS
        for row, ref in enumerate(six_refs):
            every_ref[0, 0, base + row:base + row + 1, :] = ref[layer:layer + 1, :].astype(F32)
        for part in range(2):
            ours = jnp.where(lane // 32 == own % 4, bias_ref[layer, part:part + 1, :].astype(F32), 0.0)
            every_ref[0, 0, pl.ds(base + 6 + 2 * part + own // 4, 1), :] = ours
        every_ref[0, 0, base + 10:base + 11, :] = unit_row_ref[layer:layer + 1, :].astype(F32)
    smalls = [
        (copy(every_ref.at[0, pl.ds(0, width)], every_ref.at[0, pl.ds(width, width)], peer(mask)))
        for width, mask in ((1, CORE), (2, XBIT), (4, YBIT))
    ]
    smalls += [
        copy(every_ref.at[pl.ds(0, width)], every_ref.at[pl.ds(width, width)], peer(mask)) for width, mask in ((1, Z0), (2, Z1))
    ]
    smalls[0].start()
    pack_units_into(piece_ref, 0)
    cross = copy(piece_ref, first_ref.at[1], {
        "dp": flip(own, 1), "tensor": place + (1 - core) * (flip(place, 2) - place)
    })
    same = copy(piece_ref, first_ref.at[0], peer(Z1))

    @pl.when(core == 0)
    def _():
        first_ref[0] = piece_ref[...]

    for step in range(1, 5):
        smalls[step - 1].wait()
        smalls[step].start()
    along.wait()
    over_x = copy(even_ref.at[0], even_ref.at[1], peer(XBIT))
    over_y = copy(even_ref.at[0], even_ref.at[2], peer(YBIT))
    over_x.start()
    over_y.start()
    cores = [copy(even_ref.at[chip], odd_ref.at[chip], peer(CORE)) for chip in range(4)]
    cores[0].start()
    smalls[4].wait()
    for layer in range(layers):
        base = layer * SMALL_ROWS
        later = min(layer + 1, layers - 1) * SMALL_ROWS
        rows = [base + row for row in range(6)] + [later, later + 1]
        for row, source in enumerate(rows):
            vector_ref[layer, row:row + 1, :] = jnp.concatenate(
                [every_ref[0, block, source:source + 1, :] for block in range(8)], axis=1
            )
        for quarter in range(2):
            which = 2 * (core + quarter - 2 * core * quarter)
            total = every_ref[which, 0, base + 6:base + 10, :]
            for block in range(1, 8):
                total = total + every_ref[which, block, base + 6:base + 10, :]
            head_bias_ref[layer, quarter:quarter + 1, :] = jnp.concatenate(
                [total[0:1], total[1:2], jnp.zeros((1, 256), F32), total[2:3], total[3:4]], axis=1
            )
            for block in range(8):
                unit_bias_ref[layer, :, quarter * 1024 + block * 128:quarter * 1024 + (block + 1) * 128] = every_ref[
                    2 * core + quarter, xor_block(block, own), base + 10:base + 11, :
                ]
    @pl.when(keep)
    def _():
        stay.wait()

    @pl.when(jnp.logical_not(keep))
    def _():
        tokens.wait()

    for block in range(8):
        here = pl.ds(pl.multiple_of(xor_block(block, own) * 128, 128), 128)
        resid_ref[:, block * 128:(block + 1) * 128] = came_ref[:, here].astype(F32)
    normed = (normalize(resid_ref[...])[0] * vector_ref[0, 0:1] + vector_ref[0, 1:2]).astype(BF)
    normed_ref[...] = normed
    beside = copy(normed_ref, far_ref, peer(Z0))
    beside.start()
    cross.start()

    @pl.when(core == 1)
    def _():
        same.start()

    ahead = []
    for layer in range(1, layers):
        pack_heads_into(heads_ref.at[layer - 1], layer)
        pack_units_into(pairs_ref.at[layer - 1, 0], layer)
        ahead.append(copy(pairs_ref.at[layer - 1, 0], pairs_ref.at[layer - 1, 1], peer(CORE)))
    for one in ahead:
        one.start()
    over_y.wait()
    over_x.wait()
    across = copy(even_ref.at[2], even_ref.at[3], peer(XBIT))
    across.start()
    cores[1].start()
    cores[2].start()
    across.wait()
    cores[3].start()
    for one in cores:
        one.wait()
    weights = (even_ref, odd_ref)
    project_rows(normed_ref[...], weights, head_bias_ref, 0, (near_mine_ref, near_other_ref))
    back_near = copy(near_other_ref, got_near_ref, peer(CORE))
    back_near.start()
    beside.wait()
    project_rows(far_ref[...], weights, head_bias_ref, 0, (far_mine_ref, far_other_ref))
    back_far = copy(far_other_ref, got_far_ref, peer(CORE))
    back_far.start()
    back_near.wait()
    back_far.wait()
    cross.wait()

    @pl.when(core == 1)
    def _():
        same.wait()

    for one in ahead:
        one.wait()


def start(x, project_weight, output_weight, expand_weight, reduce_weight, six, project_bias, expand_bias):
    rows, features = x.shape
    layers = expand_bias.shape[0]
    small = 8 * (-(-SMALL_ROWS * layers // 8))
    project_bias = jnp.tile(project_bias, (1, 1, 4))
    vmem = pl.BlockSpec(memory_space=pltpu.VMEM)

    triple = jax.ShapeDtypeStruct((rows, 768), BF)
    heads = jax.ShapeDtypeStruct((4, 2, 128, 1024), BF)
    outs = [
        jax.ShapeDtypeStruct((rows, features), F32),
        jax.ShapeDtypeStruct((rows, features), BF),
        jax.ShapeDtypeStruct((rows, features), BF),
        heads,
        heads,
        jax.ShapeDtypeStruct((2, 128, 2048), BF),
        jax.ShapeDtypeStruct((layers - 1, 128, 1024), BF),
        jax.ShapeDtypeStruct((layers - 1, 2, 128, 2048), BF),
        jax.ShapeDtypeStruct((layers, 8, features), F32),
        jax.ShapeDtypeStruct((layers, 2, 768), F32),
        jax.ShapeDtypeStruct((layers, 1, 2048), F32),
        triple,
        triple,
        triple,
        triple,
    ]
    copies = 19 + layers - 1
    return pl.pallas_call(
        functools.partial(start_kernel, layers),
        in_specs=[vmem] * 13,
        out_specs=[vmem] * len(outs),
        out_shape=outs,
        scratch_shapes=[
            pltpu.VMEM((rows, features), BF),
            pltpu.VMEM((128, 2048), BF),
            pltpu.VMEM((4, 8, small, 128), F32),
            pltpu.VMEM((rows, 768), BF),
            pltpu.VMEM((rows, 768), BF),
            pltpu.SemaphoreType.DMA,
            pltpu.SemaphoreType.DMA((copies,)),
            pltpu.SemaphoreType.DMA((copies,)),
        ],
        compiler_params=pltpu.CompilerParams(vmem_limit_bytes=VMEM_LIMIT, collective_id=0, has_side_effects=True),
        cost_estimate=took(60),
        name="start",
    )(x, project_weight, output_weight, expand_weight, reduce_weight, *six, project_bias, expand_bias)


def finish_kernel(
    layers, grad_ref, even_ref, odd_ref, here_ref, away_ref, *rest,
):
    sums, rest = rest[:4 * layers], rest[4 * layers:]
    grad_out_ref, project_ref, output_ref, reduce_ref, expand_ref, small_ref, rest = *rest[:6], rest[6:]
    odd_got, y_send, y_got, x_send, x_got, relay_send, relay_got, z_send, z_got, away_got, part_ref, part_got, rest = *rest[:12], rest[12:]
    rows_ref, core_got, x_rows, y_rows, near_send, near_got, far_send, far_got, local_sem, send_sem, recv_sem = rest
    own, place = lax.axis_index("dp"), lax.axis_index("tensor")
    core = own % 2
    keep = core == place // 2
    count = [0]

    def copy(source, target, device):
        index = count[0]
        count[0] += 1
        return pltpu.make_async_remote_copy(
            src_ref=source, dst_ref=target, send_sem=send_sem.at[index], recv_sem=recv_sem.at[index],
            device_id=device, device_id_type=MESH,
        )

    greet((1, 2, 4, 6, 8, 16))
    across = copy(odd_ref, odd_got, peer(CORE))
    across.start()
    beside = copy(away_ref, away_got, peer(Z0))
    beside.start()
    tokens = copy(grad_ref, grad_out_ref, peer(CORE | Z1))
    stay = pltpu.make_async_copy(grad_ref, grad_out_ref, local_sem)

    @pl.when(keep)
    def _():
        stay.start()

    @pl.when(jnp.logical_not(keep))
    def _():
        tokens.start()

    vectors = 6 * layers
    rows_ref[...] = jnp.zeros_like(rows_ref)
    for layer in range(layers):
        first_ref, second_ref, unit_ref, head_ref = sums[4 * layer:4 * layer + 4]
        base = vectors + 12 * layer
        for block in range(8):
            slot = (block % 2) * 4 + (block // 2 % 2) * 2 + block // 4
            lanes = slice(block * 128, (block + 1) * 128)
            rows_ref[slot, 6 * layer:6 * layer + 2, :] = first_ref[0:2, lanes]
            rows_ref[slot, 6 * layer + 2:6 * layer + 6, :] = second_ref[0:4, lanes]
            for quarter in range(2):
                lane = pl.multiple_of(quarter * 1024 + xor_block(block, own) * 128, 128)
                rows_ref[slot, pl.ds(base + 2 * core + quarter, 1), :] = unit_ref[0:1, pl.ds(lane, 128)]
                row = base + 4 + 4 * (quarter + core - 2 * quarter * core)
                for half in range(2):
                    rows_ref[slot, pl.ds(row + 2 * half, 2), :] = head_ref[
                        2 * quarter:2 * quarter + 2, half * 128:(half + 1) * 128
                    ]
    hop = copy(rows_ref.at[pl.ds(4, 4)], core_got, peer(CORE))
    hop.start()
    hop.wait()
    rows_ref[0:4] = rows_ref[0:4] + core_got[...]
    hop = copy(rows_ref.at[pl.ds(2, 2)], x_rows, peer(XBIT))
    hop.start()
    across.wait()
    for chip in range(4):
        for quarter in range(2):
            odd_got[chip, quarter] = odd_got[chip, quarter] + even_ref[chip, quarter]
    y_send[0], y_send[1] = odd_got[2, 0], odd_got[3, 0]
    x_send[0], x_send[1] = odd_got[1, 1], odd_got[3, 1]
    over_y = copy(y_send, y_got, peer(YBIT))
    over_x = copy(x_send, x_got, peer(XBIT))
    over_y.start()
    over_x.start()
    hop.wait()
    rows_ref[0:2] = rows_ref[0:2] + x_rows[...]
    hop = copy(rows_ref.at[pl.ds(1, 1)], y_rows, peer(YBIT))
    hop.start()
    hop.wait()
    rows_ref[0] = rows_ref[0] + y_rows[0]
    near_send[...] = jnp.zeros_like(near_send)
    far_send[...] = jnp.zeros_like(far_send)
    near_send[0:vectors, :] = rows_ref[0, 0:vectors, :]
    for layer in range(layers):
        base = vectors + 12 * layer
        near_send[vectors + 2 * layer:vectors + 2 * layer + 1, :] = rows_ref[0, base + 1:base + 2, :]
        near_send[vectors + 2 * layer + 1:vectors + 2 * layer + 2, :] = rows_ref[0, base + 3:base + 4, :]
    hop = copy(near_send, near_got, peer(Z0))
    hop.start()
    over_y.wait()
    over_x.wait()
    relay_send[0] = odd_got[1, 0] + y_got[1]
    relay_send[1] = odd_got[2, 1] + x_got[1]
    relays = [copy(relay_send.at[i], relay_got.at[i], peer(mask)) for i, mask in ((0, XBIT), (1, YBIT))]
    for one in relays:
        one.start()
    beside.wait()
    for kind in range(2):
        for side in range(2):
            part_ref[side, kind] = here_ref[kind, side] + away_got[kind, side]
    crossing = copy(part_ref.at[1], part_got.at[1], {
        "dp": flip(own, 1), "tensor": place + core * (flip(place, 2) - place)
    })
    crossing.start()
    along = copy(part_ref.at[0], part_got.at[0], peer(Z1))

    @pl.when(core == 1)
    def _():
        along.start()

    @pl.when(core == 0)
    def _():
        part_got[0] = part_ref[0]

    for one in relays:
        one.wait()
    total = [odd_got[0, 0] + y_got[0] + relay_got[0], odd_got[0, 1] + x_got[0] + relay_got[1]]
    z_send[core] = total[0]
    z_send[1 - core] = total[1]
    heads = copy(z_send.at[1], z_got, peer(Z1))
    heads.start()
    hop.wait()
    far_send[0:vectors, :] = rows_ref[0, 0:vectors, :] + near_got[0:vectors, :]
    for layer in range(layers):
        base = vectors + 12 * layer
        far_send[vectors + layer:vectors + layer + 1, :] = (
            rows_ref[0, base + 2:base + 3, :] + near_got[vectors + 2 * layer + 1:vectors + 2 * layer + 2, :]
        )
        far_send[vectors + layers + 4 * layer:vectors + layers + 4 * layer + 4, :] = rows_ref[0, base + 8:base + 12, :]
    hop = copy(far_send, far_got, peer(Z1))
    hop.start()
    crossing.wait()

    @pl.when(core == 1)
    def _():
        along.wait()

    reduce_ref[...] = (part_got[0, 0].astype(F32) + part_got[1, 0].astype(F32)).T
    expand_ref[...] = part_got[0, 1].astype(F32) + part_got[1, 1].astype(F32)
    hop.wait()
    small_ref[0:vectors, :] = far_send[0:vectors, :] + far_got[0:vectors, :]
    for layer in range(layers):
        base = vectors + 12 * layer
        row = vectors + layer
        small_ref[row:row + 1, :] = (
            rows_ref[0, base:base + 1, :] + near_got[vectors + 2 * layer:vectors + 2 * layer + 1, :] + far_got[row:row + 1, :]
        )
        row = vectors + layers + 4 * layer
        small_ref[row:row + 4, :] = rows_ref[0, base + 4:base + 8, :] + far_got[row:row + 4, :]
    heads.wait()
    for part in range(3):
        here = slice(part * 256, (part + 1) * 256)
        project_ref[part] = z_send[0, :, here].astype(F32) + z_got[:, here].astype(F32)
    output_ref[...] = (z_send[0, :, 768:].astype(F32) + z_got[:, 768:].astype(F32)).T

    @pl.when(keep)
    def _():
        stay.wait()

    @pl.when(jnp.logical_not(keep))
    def _():
        tokens.wait()


def finish(grad, even, odd, here, away, sums):
    layers = len(sums)
    vmem = pl.BlockSpec(memory_space=pltpu.VMEM)
    rows = 18 * layers
    args = [grad, even, odd, here, away, *[array for layer in sums for array in layer]]
    small = 8 * (-(-11 * layers // 8))
    outs = [
        jax.ShapeDtypeStruct(grad.shape, BF),
        jax.ShapeDtypeStruct((3, 128, 256), F32),
        jax.ShapeDtypeStruct((256, 128), F32),
        jax.ShapeDtypeStruct((1024, 128), F32),
        jax.ShapeDtypeStruct((128, 1024), F32),
        jax.ShapeDtypeStruct((small, 128), F32),
    ]
    one = (128, 1024)
    copies = 15
    return pl.pallas_call(
        functools.partial(finish_kernel, layers),
        in_specs=[vmem] * len(args),
        out_specs=[vmem] * len(outs),
        out_shape=outs,
        scratch_shapes=[
            pltpu.VMEM((4, 2, *one), BF),
            *[pltpu.VMEM((2, *one), BF)] * 7,
            pltpu.VMEM(one, BF),
            *[pltpu.VMEM((2, 2, *one), BF)] * 3,
            pltpu.VMEM((8, rows, 128), F32),
            pltpu.VMEM((4, rows, 128), F32),
            pltpu.VMEM((2, rows, 128), F32),
            pltpu.VMEM((1, rows, 128), F32),
            *[pltpu.VMEM((small, 128), F32)] * 4,
            pltpu.SemaphoreType.DMA,
            pltpu.SemaphoreType.DMA((copies,)),
            pltpu.SemaphoreType.DMA((copies,)),
        ],
        compiler_params=pltpu.CompilerParams(vmem_limit_bytes=VMEM_LIMIT, collective_id=1, has_side_effects=True),
        cost_estimate=took(50),
        name="finish",
    )(*args)


def fetch_heads(piece, core, turn, out):
    token = yield
    far = swap(after(piece, token), Z1)
    token = yield []
    far = after(far, token)
    own = jnp.stack([jnp.where(core == 0, piece, far), jnp.where(core == 0, far, piece)])
    from_x = swap(own, XBIT)
    from_y = swap(own, YBIT)
    token = yield [own]
    from_x, from_y = after_all((from_x, from_y), token)
    across = swap(from_y, XBIT)
    token = yield [from_x, from_y]
    quads = jnp.stack([own, from_x, from_y, after(across, token)])
    other = swap(quads, CORE)
    token = yield [quads]
    out += [quads, other, turn]


def join_units(first, first_x, first_y, second, first_out, second_out):
    second_x, second_y = swap(second, XBIT), swap(second, YBIT)
    token = yield [first_x, first_y, second]
    first_x, second_x, second_y = after_all((first_x, second_x, second_y), token)
    first_across, second_across = swap(first_x, YBIT), swap(second_y, XBIT)
    token = yield [second_x, second_y]
    first_across, second_across = after_all((first_across, second_across), token)
    first_out += [first, first_x, first_y, first_across]
    second_out += [second, second_x, second_y, second_across]
    yield [first_across, second_across]


def fetch_units_near(first, first_out, second_out):
    token = yield
    first = after(first, token)
    first_x, first_y, second = swap(first, XBIT), swap(first, YBIT), swap(first, Z0)
    token = yield []
    first_x, first_y, second = after_all((first_x, first_y, second), token)
    yield from join_units(first, first_x, first_y, second, first_out, second_out)


def fetch_units(pair, core, first_out, second_out):
    token = yield
    far = swap_some(after(pair, token), (0, Z1))
    token = yield []
    first = jnp.where(core == 0, pair, after(far, token))
    second = swap(first, Z0)
    token = yield [first]
    second = after(second, token)
    token = yield [second]
    first = after(first, token)
    first_x, first_y = swap(first, XBIT), swap(first, YBIT)
    token = yield []
    first_x, first_y = after_all((first_x, first_y), token)
    yield from join_units(first, first_x, first_y, second, first_out, second_out)


def unpack_heads(values):
    return values[:, :768].reshape(128, 3, 256).transpose(1, 0, 2), values[:, 768:].T


def reduce_heads(even, odd, core, out):
    token = yield
    got = swap(odd, CORE)
    token = yield []
    got = after(got, token)
    low, high = even[:2] + got[:2], even[2:] + got[2:]
    from_y = swap(high, YBIT)
    token = yield [low, high]
    from_y = after(from_y, token)
    relayed = low[1] + from_y[1]
    relay = swap(relayed, XBIT)
    token = yield [relayed]
    total = low[0] + from_y[0] + after(relay, token)
    yield from close_heads(total, core, out)


def close_heads(total, core, out):
    near = jnp.where(core == 0, total[0], total[1])
    away = jnp.where(core == 0, total[1], total[0])
    far = swap(away, Z1)
    token = yield [near, away]
    out.append(unpack_heads(near.astype(F32) + after(far, token).astype(F32)))
    yield list(out[-1])


def reduce_units(reduce_parts, expand_parts, core, out):
    yield
    own_r, pair_r, single_r = reduce_parts
    from_y = swap(pair_r, YBIT)
    yield []
    own_e, pair_e, single_e = expand_parts
    from_x = swap(pair_e, XBIT)
    token = yield []
    from_y = after(from_y, token)
    relayed_r = single_r + from_y[:, 1]
    relay_r = swap(relayed_r, XBIT)
    token = yield [relayed_r]
    from_x = after(from_x, token)
    relayed_e = single_e + from_x[:, 1]
    relay_e = swap(relayed_e, YBIT)
    token = yield [relayed_e]
    relay_r, relay_e = after_all((relay_r, relay_e), token)
    totals = [
        jnp.stack([own_r[i] + from_y[i, 0] + relay_r[i], own_e[i] + from_x[i, 0] + relay_e[i]]) for i in range(2)
    ]
    if core is None:
        out += totals
        yield totals
        return
    yield from close_units(*totals, core, out)


def close_units(here, away, core, out):
    got = swap(away, Z0)
    token = yield [here, away]
    here = here + after(got, token)
    token = yield [here]
    here = after(here, token)
    same, cross = here[:, 0], here[:, 1]
    same_got, cross_got = swap_some(same, (0, Z1)), swap_some(cross, (CORE, CORE | Z1))
    token = yield [same, cross]
    same_got, cross_got = after_all((same_got, cross_got), token)
    out.append(jnp.where(core == 0, same, same_got).astype(F32) + cross_got.astype(F32))
    yield [out[-1]]


def fast_device(
    layer_input,
    first_gain,
    first_shift,
    project_weight,
    project_bias,
    output_weight,
    output_bias,
    second_gain,
    second_shift,
    expand_weight,
    expand_bias,
    reduce_weight,
    reduce_bias,
    picture_start,
    cotangent,
):
    own = lax.axis_index("dp")
    place = lax.axis_index("tensor")
    core = own & 1
    keep = core == (place >> 1)
    own_keep = jnp.stack([own, keep.astype(jnp.int32)]).astype(jnp.int32)
    me = (2 * core + (place & 1)).astype(jnp.int32).reshape(1)
    slopes = head_slopes((place ^ (2 * core)) * 4, 4)

    turn = jnp.zeros((1,), jnp.int32)
    resid, normed, far, even, odd, first_pieces, own_heads, own_units, vectors_of, head_bias_of, unit_bias_of, *blocks = start(
        layer_input, project_weight, output_weight, expand_weight, reduce_weight,
        (first_gain, first_shift, output_bias, second_gain, second_shift, reduce_bias), project_bias, expand_bias,
    )
    near_mine, far_mine, got_near, got_far = blocks
    small = [(vectors_of[i], head_bias_of[i], unit_bias_of[i]) for i in range(LAYERS)]
    starts = jnp.where(keep, picture_start, redeal(picture_start))[0]
    heads, units = [[] for i in range(LAYERS)], [([], []) for i in range(LAYERS)]
    heads[0] += [even, odd, turn]
    head_tasks, unit_tasks = [None], [task(fetch_units_near(first_pieces, *units[0]))]
    for layer in range(1, LAYERS):
        head_tasks.append(task(fetch_heads(own_heads[layer - 1], core, turn, heads[layer])))
        unit_tasks.append(task(fetch_units(own_units[layer - 1], core, *units[layer])))
    saved = []
    for layer in range(LAYERS):
        vectors, head_bias, unit_bias = small[layer]
        first, last = layer == 0, layer + 1 == LAYERS
        if not first:
            far = swap(normed, Z0)
            while not heads[layer]:
                advance(normed, head_tasks[layer])
            near_mine, near_other = project(normed, head_bias, heads[layer])
            got_near = swap(near_other, CORE)
            far_mine, far_other = project(after(far, near_mine), head_bias, heads[layer])
            got_far = swap(far_other, CORE)
        pieces = heads[layer]
        made = advance(far_mine, unit_tasks[layer])
        blocks = after_all((near_mine, far_mine, got_near, got_far), *made)
        if last:
            cotangent_far = redeal(after(cotangent, far_mine))
        far_mixed, far_send, far_exact, far_log = attend(blocks, 1, slopes, starts, me)
        far_got = swap(far_send, CORE)
        far_part = mix_far(far_mixed, far_got, pieces)
        far_term = swap(far_part, Z0)
        made = advance(far_part, unit_tasks[layer])
        if last:
            grad, unused, flip_grad = enter(own_keep, cotangent, after(cotangent_far, far_part), vectors)
            grad_other = swap(flip_grad, CORE)
            made.append(grad)
        near_blocks = after_all(blocks, far_part, *made)
        near_mixed, near_send, near_exact, near_log = attend(near_blocks, 0, slopes, starts, me)
        near_got = swap(near_send, CORE)
        made = advance(near_mixed, unit_tasks[layer])
        if first:
            advance(near_mixed, unit_tasks[1], head_tasks[1])
        mid, normed_two, flip_two = mix_near(near_mixed, near_got, after(far_term, near_mixed, *made), resid, vectors, pieces)
        normed_other = swap(flip_two, CORE)
        if first:
            made = advance(mid, unit_tasks[0])
            made += advance(mid, unit_tasks[1], head_tasks[1])
            normed_two = after(normed_two, *made)
        hidden, active, near_out, away_out = mlp_forward(turn, normed_two, normed_other, unit_bias, units[layer])
        got_out = swap(away_out, CORE)
        if not last:
            got_out = after(got_out, *advance(near_out, head_tasks[layer + 1], unit_tasks[layer + 1]))
        out, following = mlp_close(last, own_keep, near_out, got_out, mid, vectors)
        if not last:
            advance(out, head_tasks[layer + 1])
            advance(out, unit_tasks[layer + 1])
        saved.append((
            resid, normed, far, blocks, (near_exact, far_exact), (near_log, far_log), (near_mixed, far_mixed),
            (near_got, far_got), mid, normed_two, normed_other, hidden, active,
        ))
        resid, normed = out, following
    layer_output = jnp.where(keep, normed, redeal(normed))
    grad = after(grad, normed)
    sums = [None] * LAYERS
    head_grad, unit_grad = ([[] for i in range(LAYERS)] for j in range(2))
    pending = []
    for layer in reversed(range(LAYERS)):
        vectors, pieces = small[layer][0], heads[layer]
        (
            resid, normed, far, blocks, exacts, logs, mixed, mixed_got, mid, normed_two, normed_other, hidden, active,
        ) = saved[layer]
        grad_hidden, unit_sums, near_term, away_term = mlp_backward(turn, grad, grad_other, hidden, units[layer])
        got_term = after(swap(away_term, CORE), *advance(near_term, *pending))
        grad_mid, grad_low, second_sums = mlp_open(near_term, got_term, mid, grad, vectors)
        grad_far = swap(grad_low, Z0)
        first = layer == 0
        reduce_parts = unit_grads("x", grad, grad_other, after(active, grad_low))
        near_mine, near_other = unmix(after(grad_low, reduce_parts[0]), pieces)
        got_near = swap(near_other, CORE)
        expand_parts = unit_grads("y", normed_two, normed_other, after(grad_hidden, near_mine))
        unit_task = task(reduce_units(reduce_parts, expand_parts, None if first else core, unit_grad[layer]))
        advance(None, unit_task)
        advance(None, unit_task)
        far_mine, far_other = unmix(after(grad_far, expand_parts[0]), pieces)
        got_far = swap(far_other, CORE)
        made = advance(far_mine, *pending)
        grads_mixed = after_all((near_mine, far_mine, got_near, got_far), *made)
        mine_0, away_0 = attend_pull(0, blocks, grads_mixed, exacts, logs, slopes, starts, me)
        other_0 = swap(away_0, CORE)
        made = advance(mine_0, unit_task)
        grads_mixed = after_all(grads_mixed, mine_0, *made)
        mine_1, away_1 = attend_pull(1, blocks, grads_mixed, exacts, logs, slopes, starts, me)
        other_1 = swap(away_1, CORE)
        made = advance(mine_1, unit_task, *pending)
        other_1 = after(other_1, *made, *([layer_output] if layer == LAYERS - 1 else []))
        mine, other = (mine_0, mine_1), (other_0, other_1)
        far_part = unproject_far(mine, other, pieces)
        far_term = swap(far_part, Z0)
        even, odd, head_sums = head_grads(
            turn, normed, far, grad_low, after(grad_far, far_part), mine, other, mixed, mixed_got
        )
        if not first:
            head_task = task(reduce_heads(even, odd, core, head_grad[layer]))
            advance(None, head_task)
        made = advance(head_sums, unit_task)
        grad, grad_low, first_sums = unproject_near(
            first, own_keep, mine, other, after(far_term, *made), resid, grad_mid, vectors, pieces
        )
        sums[layer] = (first_sums, second_sums, unit_sums, head_sums)
        if not first:
            grad_other = swap(grad_low, CORE)
            grad = after(grad, *advance(grad, head_task))
        pending = [unit_task, head_task]
    input_grad, *grads, small_sums = finish(grad_low, even, odd, *unit_grad[0], sums)
    head_grad[0], unit_grad[0] = [grads[:2]], [grads[2:]]
    unit_grad[1:] = [[(g[0][0].T, g[0][1])] for g in unit_grad[1:]]
    six = small_sums[:6 * LAYERS].reshape(LAYERS, 6, 128)
    unit_sum = small_sums[6 * LAYERS:7 * LAYERS]
    head_sum = small_sums[7 * LAYERS:11 * LAYERS].reshape(LAYERS, 2, 2, 128).transpose(0, 2, 1, 3).reshape(LAYERS, 2, 256)
    head_sum = lax.dynamic_slice_in_dim(head_sum, own * 32, 32, 2)
    return (
        layer_output,
        input_grad,
        six[:, 0],
        six[:, 1],
        jnp.stack([g[0][0] for g in head_grad]),
        head_sum,
        jnp.stack([g[0][1] for g in head_grad]),
        six[:, 2],
        six[:, 3],
        six[:, 4],
        jnp.stack([g[0][1] for g in unit_grad]),
        unit_sum,
        jnp.stack([g[0][0] for g in unit_grad]),
        six[:, 5],
    )


def solution(mesh):
    placed = (
        P(("dp", "tensor"), None),
        P(None, "dp"),
        P(None, "dp"),
        P(None, None, "dp", "tensor"),
        P(None, None, ("tensor", "dp")),
        P(None, "tensor", "dp"),
        P(None, "dp"),
        P(None, "dp"),
        P(None, "dp"),
        P(None, "dp", "tensor"),
        P(None, ("tensor", "dp")),
        P(None, "tensor", "dp"),
        P(None, "dp"),
        P("dp", None),
        P(("dp", "tensor"), None),
    )
    return jax.shard_map(
        fast_device if mesh_is_paired(mesh) else on_device,
        mesh=mesh,
        in_specs=placed,
        out_specs=(
            P(("dp", "tensor"), None),
            P(("dp", "tensor"), None),
            P(None, "dp"),
            P(None, "dp"),
            P(None, None, "dp", "tensor"),
            P(None, None, ("tensor", "dp")),
            P(None, "tensor", "dp"),
            P(None, "dp"),
            P(None, "dp"),
            P(None, "dp"),
            P(None, "dp", "tensor"),
            P(None, ("tensor", "dp")),
            P(None, "tensor", "dp"),
            P(None, "dp"),
        ),
        check_vma=False,
    )
```

```python
import functools

import jax
import jax.numpy as jnp
from jax import lax
from jax.experimental import pallas as pl
from jax.experimental.pallas import tpu as pltpu
from jax.sharding import PartitionSpec as P

HEADS = 16
HD = 64
LAYERS = 2
SEQ_LEN = 2048
PIECE = 256


NORM_EPS = 1e-05


def layer_norm(values, gain, shift):
    centred = values - jnp.mean(values, axis=-1, keepdims=True)
    spread = jnp.mean(centred * centred, axis=-1, keepdims=True)
    return centred * lax.rsqrt(spread + NORM_EPS) * gain + shift


def gelu_tanh(values):
    return jax.nn.gelu(values, approximate=True)


def piece_numbers(starts):
    places = jnp.arange(SEQ_LEN, dtype=jnp.int32)
    inside = (places[:, None] >= starts[None, :]) & (places[:, None] < starts[None, :] + PIECE)
    numbers = jnp.arange(1, starts.shape[0] + 1, dtype=jnp.int32)
    return jnp.sum(jnp.where(inside, numbers[None, :], 0), axis=1)


def head_slopes(first_head, count_heads):
    heads_at = (first_head + jnp.arange(count_heads, dtype=jnp.int32)).astype(jnp.float32)
    return jnp.exp2(-8.0 * (heads_at + 1.0) / HEADS)


def gather_rows(values):
    return lax.all_gather(values, "tensor", axis=0, tiled=True)


def gather_grads(values):
    return lax.all_gather(values, "tensor", axis=0, tiled=True)


def scatter_rows(values, weight):
    rows_here = values.shape[0] // lax.axis_size("tensor")

    def partial_term(offset, count_rows):
        return jnp.dot(values, weight, preferred_element_type=jnp.float32)

    return lax.psum_scatter(
        partial_term(jnp.int32(0), rows_here * lax.axis_size("tensor")).astype(jnp.bfloat16),
        "tensor",
        scatter_dimension=0,
        tiled=True,
    ).astype(jnp.float32)


def scatter_back(partial_term, rows_here):
    return lax.psum_scatter(
        partial_term(jnp.int32(0), rows_here * lax.axis_size("tensor")).astype(jnp.bfloat16),
        "tensor",
        scatter_dimension=0,
        tiled=True,
    ).astype(jnp.float32)


def block_scores(query_block, key_rows, offset, piece_ids, slopes):
    length = key_rows.shape[0]
    count_rows = query_block.shape[0]
    query_places = offset + jnp.arange(count_rows, dtype=jnp.int32)
    key_places = jnp.arange(length, dtype=jnp.int32)
    product = jnp.einsum("qhe,khe->hqk", query_block, key_rows, preferred_element_type=jnp.float32)
    distance = jnp.abs(query_places[:, None] - key_places[None, :]).astype(jnp.float32)
    scores = product * HD ** (-0.5) - slopes[:, None, None] * distance[None]
    query_pieces = lax.dynamic_slice_in_dim(piece_ids, offset, count_rows, 0)
    allowed = (key_places[None, :] <= query_places[:, None]) | (
        query_pieces[:, None] == piece_ids[None, :]
    ) & (query_pieces[:, None] > 0)
    return jnp.where(allowed[None], scores, -jnp.inf)


def sequence_forward(operands, slopes):
    queries, key_rows, value_rows, piece_ids = operands
    length = queries.shape[0]
    block_rows = min(512, length)

    def one_block(block_index):
        offset = block_index * block_rows
        query_block = lax.dynamic_slice_in_dim(queries, offset, block_rows, 0)
        scores = block_scores(query_block, key_rows, offset, piece_ids, slopes)
        row_max = jnp.max(scores, axis=-1, keepdims=True)
        raw_weights = jnp.exp(scores - row_max)
        totals = jnp.sum(raw_weights, axis=-1, keepdims=True)
        soft_weights = (raw_weights / totals).astype(jnp.bfloat16)
        attended = jnp.einsum(
            "hqk,khe->qhe", soft_weights, value_rows, preferred_element_type=jnp.float32
        )
        return (attended.astype(jnp.bfloat16), (row_max + jnp.log(totals))[..., 0])

    attended, log_total = lax.map(one_block, jnp.arange(length // block_rows, dtype=jnp.int32))
    return (attended.reshape(length, queries.shape[1], queries.shape[2]), log_total)


def sequence_backward(operands, slopes):
    queries, key_rows, value_rows, piece_ids, grad_mixed, log_total = operands
    length = queries.shape[0]
    block_rows = min(512, length)

    def one_block(carry, block_index):
        key_grad, value_grad = carry
        offset = block_index * block_rows
        query_block = lax.dynamic_slice_in_dim(queries, offset, block_rows, 0)
        grad_block = lax.dynamic_slice_in_dim(grad_mixed, offset, block_rows, 0)
        scores = block_scores(query_block, key_rows, offset, piece_ids, slopes)
        probs = jnp.exp(scores - log_total[block_index][..., None])
        soft_weights = probs.astype(jnp.bfloat16)
        value_grad = value_grad + jnp.einsum(
            "hqk,qhe->khe", soft_weights, grad_block, preferred_element_type=jnp.float32
        )
        prob_grad = jnp.einsum(
            "qhe,khe->hqk", grad_block, value_rows, preferred_element_type=jnp.float32
        )
        centred = jnp.sum(probs * prob_grad, axis=-1, keepdims=True)
        score_grad = (probs * (prob_grad - centred) * HD ** (-0.5)).astype(jnp.bfloat16)
        query_grad = jnp.einsum(
            "hqk,khe->qhe", score_grad, key_rows, preferred_element_type=jnp.float32
        )
        key_grad = key_grad + jnp.einsum(
            "hqk,qhe->khe", score_grad, query_block, preferred_element_type=jnp.float32
        )
        return ((key_grad, value_grad), query_grad)

    empty = jnp.zeros(queries.shape, jnp.float32)
    (key_grad, value_grad), query_grad = lax.scan(
        one_block, (empty, empty), jnp.arange(length // block_rows, dtype=jnp.int32)
    )
    return (query_grad.reshape(queries.shape), key_grad, value_grad)


def attend_forward(triple, piece_ids, slopes):
    width = triple.shape[2]
    count_seq = piece_ids.shape[0]
    length = piece_ids.shape[1]
    shaped = triple.reshape(3, count_seq, length, width // HD, HD)
    attended, log_total = lax.map(
        lambda operands: sequence_forward(operands, slopes),
        (shaped[0], shaped[1], shaped[2], piece_ids),
    )
    return (attended.reshape(count_seq * length, width), log_total)


def attend_backward(triple, grad_attended, log_total, piece_ids, slopes):
    width = triple.shape[2]
    count_seq = piece_ids.shape[0]
    length = piece_ids.shape[1]
    shaped = triple.reshape(3, count_seq, length, width // HD, HD)
    grad_shaped = grad_attended.reshape(count_seq, length, width // HD, HD)
    query_grad, key_grad, value_grad = lax.map(
        lambda operands: sequence_backward(operands, slopes),
        (shaped[0], shaped[1], shaped[2], piece_ids, grad_shaped, log_total),
    )
    return (
        query_grad.reshape(-1, width),
        key_grad.reshape(-1, width),
        value_grad.reshape(-1, width),
    )


def fetch_layer(
    project_weight,
    project_bias,
    output_weight,
    expand_weight,
    expand_bias,
    reduce_weight,
    small_stack,
    layer_index,
):
    return (
        lax.all_gather(project_weight[layer_index], "dp", axis=1, tiled=True),
        lax.all_gather(project_bias[layer_index], "dp", axis=1, tiled=True),
        lax.all_gather(output_weight[layer_index], "dp", axis=1, tiled=True),
        lax.all_gather(expand_weight[layer_index], "dp", axis=0, tiled=True),
        lax.all_gather(expand_bias[layer_index], "dp", axis=0, tiled=True),
        lax.all_gather(reduce_weight[layer_index], "dp", axis=1, tiled=True),
        lax.all_gather(small_stack[layer_index], "dp", axis=1, tiled=True),
    )


def forward_layer(resid, weights, piece_ids, slopes):
    w_project, bias_project, w_output, w_expand, bias_expand, w_reduce, small = weights
    vectors = small.astype(jnp.float32)
    normed = layer_norm(resid, vectors[0], vectors[1])
    gathered = gather_rows(normed.astype(jnp.bfloat16))
    product = jnp.einsum("gd,cde->cge", gathered, w_project, preferred_element_type=jnp.float32)
    biases = jnp.stack([bias_project[0], jnp.zeros_like(bias_project[0]), bias_project[1]]).astype(
        jnp.float32
    )
    triple = (product + biases[:, None, :]).astype(jnp.bfloat16)
    attended, log_total = attend_forward(triple, piece_ids, slopes)
    resid_mid = resid + (scatter_rows(attended, w_output) + vectors[2])
    normed_two = layer_norm(resid_mid, vectors[3], vectors[4])
    gathered_two = gather_rows(normed_two.astype(jnp.bfloat16))
    hidden = jnp.dot(
        gathered_two, w_expand, preferred_element_type=jnp.float32
    ) + bias_expand.astype(jnp.float32)
    active = gelu_tanh(hidden).astype(jnp.bfloat16)
    mlp_sum = scatter_rows(active, w_reduce)
    mlp_keep = (gathered_two, hidden, None)
    resid_out = resid_mid + (mlp_sum + vectors[5])
    return (resid_out, (gathered, triple, attended, log_total, resid_mid, mlp_keep))


def backward_layer(grad_out, resid, weights, kept, piece_ids, slopes):
    w_project, bias_project, w_output, w_expand, bias_expand, w_reduce, small = weights
    vectors = small.astype(jnp.float32)
    gathered, triple, attended, log_total, resid_mid, mlp_keep = kept
    rows_here = grad_out.shape[0]
    rows_in, hidden, full_weights = mlp_keep
    grad_bias_reduce = jnp.sum(grad_out, axis=0)
    active, gelu_pull = jax.vjp(gelu_tanh, hidden)
    active_low = active.astype(jnp.bfloat16)
    grad_mlp = gather_grads(grad_out.astype(jnp.bfloat16))
    grad_reduce = jnp.einsum("gf,gd->fd", active_low, grad_mlp, preferred_element_type=jnp.float32)
    grad_active = jnp.einsum("gd,fd->gf", grad_mlp, w_reduce, preferred_element_type=jnp.float32)
    (grad_hidden,) = gelu_pull(grad_active)
    grad_bias_expand = jnp.sum(grad_hidden, axis=0)
    grad_hidden_low = grad_hidden.astype(jnp.bfloat16)
    grad_expand = jnp.einsum(
        "gd,gf->df", rows_in, grad_hidden_low, preferred_element_type=jnp.float32
    )

    def expand_term(offset, count_rows):
        return jnp.einsum(
            "gf,df->gd", grad_hidden_low, w_expand, preferred_element_type=jnp.float32
        )

    grad_normed_two = scatter_back(expand_term, rows_here)
    unused_two, second_pull = jax.vjp(layer_norm, resid_mid, vectors[3], vectors[4])
    grad_from_norm, grad_gain_two, grad_shift_two = second_pull(grad_normed_two)
    grad_mid = grad_out + grad_from_norm
    grad_bias_output = jnp.sum(grad_mid, axis=0)
    grad_attn = gather_grads(grad_mid.astype(jnp.bfloat16))
    grad_output = jnp.einsum("gt,gd->td", attended, grad_attn, preferred_element_type=jnp.float32)
    grad_attended = jnp.einsum(
        "gd,td->gt", grad_attn, w_output, preferred_element_type=jnp.float32
    ).astype(jnp.bfloat16)
    query_grad, key_grad, value_grad = attend_backward(
        triple, grad_attended, log_total, piece_ids, slopes
    )
    grad_bias_project = jnp.stack([jnp.sum(query_grad, axis=0), jnp.sum(value_grad, axis=0)])
    grad_triple = jnp.stack([query_grad, key_grad, value_grad]).astype(jnp.bfloat16)
    grad_project = jnp.einsum(
        "gd,cge->cde", gathered, grad_triple, preferred_element_type=jnp.float32
    )

    def project_term(offset, count_rows):
        return jnp.einsum("cge,cde->gd", grad_triple, w_project, preferred_element_type=jnp.float32)

    grad_normed = scatter_back(project_term, rows_here)
    unused_one, first_pull = jax.vjp(layer_norm, resid, vectors[0], vectors[1])
    grad_from_first, grad_gain_one, grad_shift_one = first_pull(grad_normed)
    grad_stream = grad_mid + grad_from_first
    small_grads = jnp.stack(
        [
            grad_gain_one,
            grad_shift_one,
            grad_bias_output,
            grad_gain_two,
            grad_shift_two,
            grad_bias_reduce,
        ]
    )
    return (
        grad_stream,
        (
            grad_project,
            grad_bias_project,
            grad_output,
            grad_expand,
            grad_bias_expand,
            grad_reduce,
            small_grads,
        ),
    )


def reduce_layer(layer_grads):
    (
        grad_project,
        grad_bias_project,
        grad_output,
        grad_expand,
        grad_bias_expand,
        grad_reduce,
        small_grads,
    ) = layer_grads
    return (
        lax.psum_scatter(
            grad_project.astype(jnp.bfloat16), "dp", scatter_dimension=1, tiled=True
        ).astype(jnp.float32),
        lax.psum_scatter(
            grad_bias_project.astype(jnp.bfloat16), "dp", scatter_dimension=1, tiled=True
        ).astype(jnp.float32),
        lax.psum_scatter(
            grad_output.astype(jnp.bfloat16), "dp", scatter_dimension=1, tiled=True
        ).astype(jnp.float32),
        lax.psum_scatter(
            grad_expand.astype(jnp.bfloat16), "dp", scatter_dimension=0, tiled=True
        ).astype(jnp.float32),
        lax.psum_scatter(
            grad_bias_expand.astype(jnp.bfloat16), "dp", scatter_dimension=0, tiled=True
        ).astype(jnp.float32),
        lax.psum_scatter(
            grad_reduce.astype(jnp.bfloat16), "dp", scatter_dimension=1, tiled=True
        ).astype(jnp.float32),
        lax.psum_scatter(
            small_grads.astype(jnp.bfloat16), "dp", scatter_dimension=1, tiled=True
        ).astype(jnp.float32),
    )


def on_device(
    layer_input,
    first_gain,
    first_shift,
    project_weight,
    project_bias,
    output_weight,
    output_bias,
    second_gain,
    second_shift,
    expand_weight,
    expand_bias,
    reduce_weight,
    reduce_bias,
    picture_start,
    cotangent,
):
    small_stack = jnp.stack(
        [first_gain, first_shift, output_bias, second_gain, second_shift, reduce_bias], axis=1
    )
    piece_ids = jax.vmap(piece_numbers)(picture_start)
    heads_here = project_weight.shape[3] // HD
    slopes = head_slopes(lax.axis_index("tensor") * heads_here, heads_here)
    resid = layer_input.astype(jnp.float32)
    saved = []
    for layer_index in range(LAYERS):
        weights = fetch_layer(
            project_weight,
            project_bias,
            output_weight,
            expand_weight,
            expand_bias,
            reduce_weight,
            small_stack,
            layer_index,
        )
        resid_next, kept = forward_layer(resid, weights, piece_ids, slopes)
        saved.append((resid, weights, kept))
        resid = resid_next
    layer_output = resid.astype(jnp.bfloat16)
    grad_stream = cotangent.astype(jnp.float32)
    collected = []
    for layer_index in reversed(range(LAYERS)):
        resid_in, weights, kept = saved[layer_index]
        grad_stream, layer_grads = backward_layer(
            grad_stream, resid_in, weights, kept, piece_ids, slopes
        )
        layer_grads = reduce_layer(layer_grads)
        collected.insert(0, layer_grads)
    stacked = tuple(
        (jnp.stack([grad_entry[member] for grad_entry in collected]) for member in range(7))
    )
    (
        grad_project,
        grad_bias_project,
        grad_output,
        grad_expand,
        grad_bias_expand,
        grad_reduce,
        small_grads,
    ) = stacked
    small_grads = lax.psum(small_grads, "tensor")
    return (
        layer_output,
        grad_stream.astype(jnp.bfloat16),
        small_grads[:, 0],
        small_grads[:, 1],
        grad_project,
        grad_bias_project,
        grad_output,
        small_grads[:, 2],
        small_grads[:, 3],
        small_grads[:, 4],
        grad_expand,
        grad_bias_expand,
        grad_reduce,
        small_grads[:, 5],
    )


Z0, Z1, CORE, XBIT, YBIT = 1, 2, 4, 8, 16
AXES = ("dp", "tensor")
NEG = -1e30
BF = jnp.bfloat16
F32 = jnp.float32
VMEM_LIMIT = 24 * 1024 * 1024


def took(us):
    return pl.CostEstimate(flops=int(us * 5e8), bytes_accessed=1, transcendentals=0)


def mesh_is_paired(mesh):
    return dict(mesh.shape) == {"dp": 8, "tensor": 4}


def swap(values, mask):
    return lax.ppermute(values, AXES, [(i, i ^ mask) for i in range(32)])


def swap_some(values, masks):
    pairs = [(i, i ^ masks[(i >> 2) & 1]) for i in range(32)]
    return lax.ppermute(values, AXES, [pair for pair in pairs if pair[0] != pair[1]])


def redeal(values):
    def target(i):
        core, z1 = (i >> 2) & 1, (i >> 1) & 1
        return (i & ~6) | (z1 << 2) | (core << 1)

    return lax.ppermute(values, AXES, [(i, target(i)) for i in range(32) if target(i) != i])


CHIPS = [[0, 2, 4, 6], [1, 3, 5, 7]]


def plane_gather(values):
    return lax.all_gather(values, "dp", axis_index_groups=CHIPS, axis=0, tiled=False)


def plane_scatter(values):
    return lax.psum_scatter(values, "dp", axis_index_groups=CHIPS, scatter_dimension=0, tiled=False)


def turn_index(values, own):
    shape = values.shape
    for bit in range(3):
        values = values.reshape(8 >> (bit + 1), 2, (1 << bit), *shape[1:])
        values = jnp.where((own >> bit) & 1, jnp.concatenate([values[:, 1:], values[:, :1]], axis=1), values)
    return values.reshape(shape)


def after(values, *others):
    return lax.optimization_barrier((values, *others))[0]


def after_all(values, *others):
    if not others:
        return tuple(values)
    return lax.optimization_barrier((*values, *others))[:len(values)]


def task(steps):
    next(steps)
    return steps


def advance(token, *tasks):
    made = []
    for steps in tasks:
        try:
            made += steps.send(token)
        except StopIteration:
            pass
    return made


def dot_nt(a, b):
    return lax.dot_general(a, b, (((1,), (1,)), ((), ())), preferred_element_type=F32)


def dot_nn(a, b):
    return lax.dot_general(a, b, (((1,), (0,)), ((), ())), preferred_element_type=F32)


def head_mask(shape, head):
    lane = lax.broadcasted_iota(jnp.int32, shape, 1)
    return (lane < HD) if head == 0 else (lane >= HD)


def diagonal_bias(rows, columns, first_row, first_column, start):
    key = first_row + lax.broadcasted_iota(jnp.int32, (rows, 1), 0)
    query = first_column + lax.broadcasted_iota(jnp.int32, (1, columns), 1)
    key_in = (key >= start) & (key < start + PIECE)
    query_in = (query >= start) & (query < start + PIECE)
    allowed = (key <= query) | (key_in & query_in)
    reach = (jnp.minimum(key, 2 * query - key) - first_column).astype(F32)
    return jnp.where(allowed, reach, NEG)


def ramp(rows, first_row, first_column):
    return (first_row - first_column + lax.broadcasted_iota(jnp.int32, (rows, 1), 0)).astype(F32)


def attend_kernel(block, rest_bit, slope_ref, start_ref, me_ref, *rest):
    triple_refs, rest = rest[:12], rest[12:]
    near_ref, away_ref, exact_ref, lse_ref, q_ref, k_ref, v_ref, vt_ref, acc_ref, max_ref, bias_ref, tail_ref = rest
    pair = pl.program_id(0)
    turn = pl.program_id(1)
    me = me_ref[0]
    step = (2 * turn + rest_bit) ^ me
    length = k_ref.shape[0]
    first = step * block

    def at(index):
        return pl.multiple_of((index ^ me) * block, block)

    start = start_ref[first // (length // start_ref.shape[0])]

    @pl.when(turn == 0)
    def _():
        for index in range(4):
            here = slice(index * block, (index + 1) * block)
            q_ref[here, :] = triple_refs[3 * index][...] * jnp.asarray(HD ** -0.5, BF)
            k_ref[here, :] = triple_refs[3 * index + 1][...]
            v_ref[here, :] = triple_refs[3 * index + 2][...]
        for head in range(2):
            mixed = jnp.where(head_mask((length, 2 * HD), head), v_ref[...], jnp.ones((), BF))
            vt_ref[head] = mixed.T

    bias_ref[...] = diagonal_bias(block, block, first, first, start)
    q_block = q_ref[pl.ds(at(step), block), :]
    heads = [jnp.where(head_mask(q_block.shape, head), q_block, jnp.zeros((), BF)) for head in range(2)]
    slopes = [slope_ref[2 * pair + head] for head in range(2)]
    acc_ref[...] = jnp.zeros_like(acc_ref)
    max_ref[...] = jnp.full_like(max_ref, NEG)

    def absorb(head, scores, vt):
        old = max_ref[head]
        new = jnp.maximum(old, jnp.max(scores, axis=0, keepdims=True))
        weights = jnp.exp(scores - new).astype(BF)
        acc_ref[head] = acc_ref[head] * jnp.exp(old - new) + dot_nn(vt, weights)
        max_ref[head] = new

    def full(index, carry):
        place = at(index)
        keys = k_ref[pl.ds(place, block), :]
        slant = ramp(block, index * block, first)
        for head in range(2):
            absorb(head, dot_nt(keys, heads[head]) + slopes[head] * slant, vt_ref[head, :, pl.ds(place, block)])
        return carry

    place = at(step)
    for head in range(2):
        absorb(
            head,
            dot_nt(k_ref[pl.ds(place, block), :], heads[head]) + slopes[head] * bias_ref[...],
            vt_ref[head, :, pl.ds(place, block)],
        )
    lax.fori_loop(0, step, full, 0)
    edge = first + block

    @pl.when((start < edge) & (start + PIECE > edge))
    def _():
        after = at(step + 1)
        tail_ref[...] = diagonal_bias(PIECE, block, edge, first, start)
        for head in range(2):
            absorb(
                head,
                dot_nt(k_ref[pl.ds(after, PIECE), :], heads[head]) + slopes[head] * tail_ref[...],
                vt_ref[head, :, pl.ds(after, PIECE)],
            )

    outs = []
    for head in range(2):
        acc = acc_ref[head]
        total = acc[HD:HD + 1] if head == 0 else acc[0:1]
        outs.append((acc * (1.0 / total))[head * HD:(head + 1) * HD])
        lse_ref[0, head:head + 1, :] = max_ref[head] + jnp.log(total)
    mixed = jnp.concatenate(outs, axis=0)
    exact_ref[...] = mixed
    final = mixed.T.astype(BF)

    @pl.when(turn == 0)
    def _():
        near_ref[...] = final

    @pl.when(turn == 1)
    def _():
        away_ref[...] = final


def triple_specs(block, pairs):
    specs = []
    for index in range(4):
        for part in range(3):
            specs.append(pl.BlockSpec((block, 2 * HD), functools.partial(lambda part, p, i: (0, part * pairs + p), part)))
    return specs


def attend(blocks, rest_bit, slopes, starts, me):
    block, width = blocks[0].shape[0], blocks[0].shape[1] // 3
    pairs = width // (2 * HD)
    length = 4 * block
    smem = pl.BlockSpec(memory_space=pltpu.SMEM)
    return pl.pallas_call(
        functools.partial(attend_kernel, block, rest_bit),
        grid=(pairs, 2),
        in_specs=[smem, smem, smem] + triple_specs(block, pairs),
        out_specs=[
            pl.BlockSpec((block, 2 * HD), lambda p, i: (0, p)),
            pl.BlockSpec((block, 2 * HD), lambda p, i: (0, p)),
            pl.BlockSpec((2 * HD, block), lambda p, i: (p, i)),
            pl.BlockSpec((1, 8, block), lambda p, i: (p, 0, i)),
        ],
        out_shape=[
            jax.ShapeDtypeStruct((block, width), BF),
            jax.ShapeDtypeStruct((block, width), BF),
            jax.ShapeDtypeStruct((width, 2 * block), F32),
            jax.ShapeDtypeStruct((pairs, 8, 2 * block), F32),
        ],
        scratch_shapes=[
            pltpu.VMEM((length, 2 * HD), BF),
            pltpu.VMEM((length, 2 * HD), BF),
            pltpu.VMEM((length, 2 * HD), BF),
            pltpu.VMEM((2, 2 * HD, length), BF),
            pltpu.VMEM((2, 2 * HD, block), F32),
            pltpu.VMEM((2, 1, block), F32),
            pltpu.VMEM((block, block), F32),
            pltpu.VMEM((PIECE, block), F32),
        ],
        compiler_params=pltpu.CompilerParams(vmem_limit_bytes=VMEM_LIMIT),
        cost_estimate=took(17),
        name="attend",
    )(slopes, starts, me, *[b for b in blocks for _ in range(3)])


def pull_kernel(block, pair, slope_ref, start_ref, me_ref, *rest):
    triple_refs, grad_refs, rest = rest[:12], rest[12:16], rest[16:]
    exact_refs, lse_refs, rest = rest[0:2], rest[2:4], rest[4:]
    mine_ref, away_ref, q_ref, k_ref, v_ref, g_ref, kt_ref, dk_acc, dv_acc, dqt_ref, bias_ref, tail_ref = rest
    turn = pl.program_id(0)
    me = me_ref[0]
    step = turn ^ me
    length = k_ref.shape[0]
    first = step * block
    half, bit = turn // 2, turn % 2

    def at(index):
        return pl.multiple_of((index ^ me) * block, block)

    start = start_ref[first // (length // start_ref.shape[0])]

    @pl.when(turn == 0)
    def _():
        for index in range(4):
            here = slice(index * block, (index + 1) * block)
            q_ref[here, :] = triple_refs[3 * index][...] * jnp.asarray(HD ** -0.5, BF)
            k_ref[here, :] = triple_refs[3 * index + 1][...]
            v_ref[here, :] = triple_refs[3 * index + 2][...]
            g_ref[here, :] = grad_refs[index][...]
        kt_ref[...] = k_ref[...].T
        dk_acc[...] = jnp.zeros_like(dk_acc)
        dv_acc[...] = jnp.zeros_like(dv_acc)

    bias_ref[...] = diagonal_bias(block, block, first, first, start)
    dqt_ref[...] = jnp.zeros_like(dqt_ref)
    zero = jnp.zeros((), BF)
    q_block = q_ref[pl.ds(at(step), block), :]
    g_block = g_ref[pl.ds(at(step), block), :]
    masks = [head_mask(q_block.shape, head) for head in range(2)]
    q_heads = [jnp.where(mask, q_block, zero) for mask in masks]
    g_heads = [jnp.where(mask, g_block, zero) for mask in masks]
    slopes = [slope_ref[2 * pair + head] for head in range(2)]
    lanes = pl.ds(pl.multiple_of(half * block, block), block)
    exact = jnp.where(bit == 0, exact_refs[0][:, lanes], exact_refs[1][:, lanes])
    log_total = jnp.where(bit == 0, lse_refs[0][0, :, lanes], lse_refs[1][0, :, lanes])
    product = g_block.astype(F32).T * exact
    deltas = [jnp.sum(product[head * HD:(head + 1) * HD], axis=0, keepdims=True) for head in range(2)]

    def absorb(place, rows, bias_of):
        keys = k_ref[pl.ds(place, rows), :]
        values = v_ref[pl.ds(place, rows), :]
        dk = dk_acc[pl.ds(place, rows), :]
        dv = dv_acc[pl.ds(place, rows), :]
        for head in range(2):
            scores = dot_nt(keys, q_heads[head]) + slopes[head] * bias_of
            weights = jnp.exp(scores - log_total[head:head + 1, :])
            dv = dv + dot_nn(weights.astype(BF), g_heads[head])
            grad_p = dot_nt(values, g_heads[head])
            grad_s = (weights * (grad_p - deltas[head])).astype(BF)
            dk = dk + dot_nn(grad_s, q_heads[head])
            dqt_ref[head * HD:(head + 1) * HD, :] += dot_nn(kt_ref[head * HD:(head + 1) * HD, pl.ds(place, rows)], grad_s)
        dk_acc[pl.ds(place, rows), :] = dk
        dv_acc[pl.ds(place, rows), :] = dv

    absorb(at(step), block, bias_ref[...])

    def full(index, carry):
        absorb(at(index), block, ramp(block, index * block, first))
        return carry

    lax.fori_loop(0, step, full, 0)
    edge = first + block

    @pl.when((start < edge) & (start + PIECE > edge))
    def _():
        tail_ref[...] = diagonal_bias(PIECE, block, edge, first, start)
        absorb(at(step + 1), PIECE, tail_ref[...])

    grad_q = (dqt_ref[...].T * (HD ** -0.5)).astype(BF)
    here = pl.ds(pl.multiple_of(bit * block, block), block)

    @pl.when(half == 0)
    def _():
        mine_ref[0, here, :] = grad_q

    @pl.when(half == 1)
    def _():
        away_ref[0, here, :] = grad_q

    @pl.when(turn == 3)
    def _():
        for part, ref in ((1, dk_acc), (2, dv_acc)):
            mine_ref[part] = ref[:2 * block].astype(BF)
            away_ref[part] = ref[2 * block:].astype(BF)


def attend_pull(pair, blocks, grads, exacts, log_totals, slopes, starts, me):
    block, width = blocks[0].shape[0], blocks[0].shape[1] // 3
    pairs = width // (2 * HD)
    length = 4 * block
    smem = pl.BlockSpec(memory_space=pltpu.SMEM)
    triples = [pl.BlockSpec((block, 2 * HD), functools.partial(lambda part, i: (0, part * pairs + pair), part)) for part in range(3)]
    rows = pl.BlockSpec((block, 2 * HD), lambda i: (0, pair))
    wide = pl.BlockSpec((2 * HD, 2 * block), lambda i: (pair, 0))
    sums = pl.BlockSpec((1, 8, 2 * block), lambda i: (pair, 0, 0))
    out = pl.BlockSpec((3, 2 * block, 2 * HD), lambda i: (0, 0, 0))
    return pl.pallas_call(
        functools.partial(pull_kernel, block, pair),
        grid=(4,),
        in_specs=[smem, smem, smem] + triples * 4 + [rows] * 4 + [wide] * 2 + [sums] * 2,
        out_specs=[out, out],
        out_shape=[jax.ShapeDtypeStruct((3, 2 * block, 2 * HD), BF)] * 2,
        scratch_shapes=[
            pltpu.VMEM((length, 2 * HD), BF),
            pltpu.VMEM((length, 2 * HD), BF),
            pltpu.VMEM((length, 2 * HD), BF),
            pltpu.VMEM((length, 2 * HD), BF),
            pltpu.VMEM((2 * HD, length), BF),
            pltpu.VMEM((length, 2 * HD), F32),
            pltpu.VMEM((length, 2 * HD), F32),
            pltpu.VMEM((2 * HD, block), F32),
            pltpu.VMEM((block, block), F32),
            pltpu.VMEM((PIECE, block), F32),
        ],
        compiler_params=pltpu.CompilerParams(vmem_limit_bytes=VMEM_LIMIT),
        cost_estimate=took(22),
        name="attend_pull",
    )(slopes, starts, me, *[b for b in blocks for _ in range(3)], *grads, *exacts, *log_totals)


def head_columns(refs, quarter, first, last):
    return jnp.concatenate(
        [refs[odd][chip ^ refs[2][0], 1 - quarter if odd else quarter, :, first:last] for chip in range(4) for odd in range(2)],
        axis=0,
    )


def placed(arrays):
    return [
        pl.BlockSpec(memory_space=pltpu.SMEM if a.dtype == jnp.int32 else pltpu.VMEM) for a in arrays
    ]


def call_once(kernel, name, outs, args, us):
    return pl.pallas_call(
        kernel,
        in_specs=placed(args),
        out_specs=placed(outs),
        out_shape=outs,
        compiler_params=pltpu.CompilerParams(vmem_limit_bytes=VMEM_LIMIT),
        cost_estimate=took(us),
        name=name,
    )(*args)


def project_kernel(rows_ref, bias_ref, *rest):
    weight_refs, out_refs = rest[:3], rest[3:]
    rows = rows_ref[...]
    for quarter in (1, 0):
        out = dot_nn(rows, head_columns(weight_refs, quarter, 0, 768)) + bias_ref[quarter:quarter + 1]
        out_refs[quarter][...] = out.astype(BF)


def project(rows, bias, pieces):
    out = jax.ShapeDtypeStruct((rows.shape[0], 768), BF)
    return call_once(project_kernel, "project", [out, out], [rows, bias, *pieces], 5)


def mix_term(mixed_refs, weight_refs):
    rows = jnp.concatenate([ref[...] for ref in mixed_refs], axis=1)
    weight = jnp.concatenate([head_columns(weight_refs, quarter, 768, 1024) for quarter in range(2)], axis=1)
    return dot_nt(rows, weight)


def mix_far_kernel(mine_ref, other_ref, *rest):
    rest[3][...] = mix_term((mine_ref, other_ref), rest[:3]).astype(BF)


def mix_far(mine, other, pieces):
    out = jax.ShapeDtypeStruct((mine.shape[0], 1024), BF)
    return call_once(mix_far_kernel, "mix_far", [out], [mine, other, *pieces], 4)[0]


def mix_near_kernel(mine_ref, other_ref, far_ref, resid_ref, vector_ref, *rest):
    weight_refs, (mid_ref, normed_ref, flip_ref) = rest[:3], rest[3:]
    term = mix_term((mine_ref, other_ref), weight_refs)
    mid = resid_ref[...] + (term + far_ref[...].astype(F32) + vector_ref[2:3])
    mid_ref[...] = mid
    normed = (normalize(mid)[0] * vector_ref[3:4] + vector_ref[4:5]).astype(BF)
    normed_ref[...] = normed
    flip_ref[...] = flipped(normed)


def mix_near(mine, other, far, resid, vectors, pieces):
    outs = [
        jax.ShapeDtypeStruct(resid.shape, F32),
        jax.ShapeDtypeStruct(resid.shape, BF),
        jax.ShapeDtypeStruct(resid.shape, BF),
    ]
    return call_once(mix_near_kernel, "mix_near", outs, [mine, other, far, resid, vectors, *pieces], 6)


def unmix_kernel(grad_ref, *rest):
    weight_refs, out_refs = rest[:3], rest[3:]
    grad = grad_ref[...]
    for quarter in (1, 0):
        out_refs[quarter][...] = dot_nn(grad, head_columns(weight_refs, quarter, 768, 1024)).astype(BF)


def unmix(grad, pieces):
    out = jax.ShapeDtypeStruct((grad.shape[0], 256), BF)
    return call_once(unmix_kernel, "unmix", [out, out], [grad, *pieces], 4)


def unproject_term(grad_refs, weight_refs, first):
    rows = jnp.concatenate(
        [ref[part, first:first + 512] for pair in grad_refs for part in range(3) for ref in pair], axis=1
    )
    weight = jnp.concatenate([head_columns(weight_refs, quarter, 0, 768) for quarter in range(2)], axis=1)
    return dot_nt(rows, weight)


def unproject_far_kernel(*rest):
    rest[7][...] = unproject_term((rest[0:2], rest[2:4]), rest[4:7], 512).astype(BF)


def unproject_far(mine, other, pieces):
    out = jax.ShapeDtypeStruct((512, 1024), BF)
    return call_once(unproject_far_kernel, "unproject_far", [out], [*mine, *other, *pieces], 6)[0]


def unproject_near_kernel(last, own_ref, *rest):
    mine, other, rest = rest[0:2], rest[2:4], rest[4:]
    far_ref, resid_ref, grad_mid_ref, vector_ref, rest = *rest[:4], rest[4:]
    weight_refs, (grad_ref, low_ref, sums_ref) = rest[:3], rest[3:]
    term = unproject_term((mine, other), weight_refs, 0) + far_ref[...].astype(F32)
    grad_norm, grad_gain, grad_shift = norm_pull(resid_ref[...], vector_ref[0:1], term)
    grad = grad_mid_ref[...] + grad_norm
    grad_ref[...] = grad
    if last:
        put_turned(low_ref, own_ref[0], grad.astype(BF))
    else:
        low_ref[...] = flipped(grad).astype(BF)
    sums_ref[...] = jnp.concatenate([grad_gain, grad_shift, jnp.zeros((6, grad.shape[1]), F32)], axis=0)


def unproject_near(last, own_keep, mine, other, far, resid, grad_mid, vectors, pieces):
    outs = [
        jax.ShapeDtypeStruct(resid.shape, F32),
        jax.ShapeDtypeStruct(resid.shape, BF),
        jax.ShapeDtypeStruct((8, resid.shape[1]), F32),
    ]
    args = [own_keep, *mine, *other, far, resid, grad_mid, vectors, *pieces]
    kernel = functools.partial(unproject_near_kernel, last)
    return call_once(kernel, "unproject_near", outs, args, 9)


def head_grads_kernel(turn_ref, near_ref, far_ref, grad_near_ref, grad_far_ref, *rest):
    pairs, rest = (rest[0:2], rest[2:4]), rest[4:]
    mixed_refs, out_refs, bias_ref = (rest[0:2], rest[2:4]), rest[4:6], rest[6]
    rows_t = jnp.concatenate([near_ref[...], far_ref[...]], axis=0).T
    grad_t = jnp.concatenate([grad_near_ref[...], grad_far_ref[...]], axis=0).T
    for quarter, refs in enumerate(pairs):
        grads = [jnp.concatenate([ref[part] for ref in refs], axis=1) for part in range(3)]
        for part in range(4):
            if part < 3:
                term = dot_nn(rows_t, grads[part])
            else:
                term = dot_nn(grad_t, jnp.concatenate([m[...] for m in mixed_refs[quarter]], axis=0))
            term = term.astype(BF)
            for index in range(8):
                chip, odd = index // 2, index % 2
                place = 1 - quarter if odd else quarter
                out_refs[odd][chip ^ turn_ref[0], place, :, part * 256:(part + 1) * 256] = term[index * 128:(index + 1) * 128]
        for row, part in ((0, 0), (1, 2)):
            total = jnp.sum(grads[part].astype(F32), axis=0, keepdims=True)
            bias_ref[2 * quarter + row:2 * quarter + row + 1, :] = total
    bias_ref[4:8, :] = jnp.zeros((4, 256), F32)


def head_grads(turn, near, far, grad_near, grad_far, mine, other, mixed_mine, mixed_other):
    outs = [jax.ShapeDtypeStruct((4, 2, 128, 1024), BF)] * 2 + [jax.ShapeDtypeStruct((8, 256), F32)]
    args = [turn, near, far, grad_near, grad_far, *mine, *other, *mixed_mine, *mixed_other]
    return call_once(head_grads_kernel, "head_grads", outs, args, 10)


GELU_A = 0.7978845608028654
GELU_B = 0.044715


def normalize(values):
    centred = values - jnp.mean(values, axis=-1, keepdims=True)
    spread = lax.rsqrt(jnp.mean(centred * centred, axis=-1, keepdims=True) + NORM_EPS)
    return centred * spread, spread


def norm_pull(values, gain, grad):
    unit, spread = normalize(values)
    grad_unit = grad * gain
    inner = grad_unit - jnp.mean(grad_unit, axis=-1, keepdims=True)
    inner = inner - unit * jnp.mean(grad_unit * unit, axis=-1, keepdims=True)
    return spread * inner, jnp.sum(grad * unit, axis=0, keepdims=True), jnp.sum(grad, axis=0, keepdims=True)


def flipped(values):
    return jnp.concatenate([values[:, (block ^ 1) * 128:(block ^ 1) * 128 + 128] for block in range(8)], axis=1)


def put_turned(out_ref, own, values):
    for block in range(8):
        here = pl.ds(pl.multiple_of((block ^ own) * 128, 128), 128)
        out_ref[:, here] = values[:, block * 128:(block + 1) * 128]


def enter_kernel(own_ref, direct_ref, moved_ref, vector_ref, resid_ref, normed_ref, flip_ref):
    own, keep = own_ref[0], own_ref[1]
    for block in range(8):
        here = pl.ds(pl.multiple_of((block ^ own) * 128, 128), 128)
        rows = jnp.where(keep > 0, direct_ref[:, here].astype(F32), moved_ref[:, here].astype(F32))
        resid_ref[:, block * 128:(block + 1) * 128] = rows
    values = resid_ref[...]
    normed_ref[...] = (normalize(values)[0] * vector_ref[0:1] + vector_ref[1:2]).astype(BF)
    flip_ref[...] = flipped(values).astype(BF)


def enter(own_keep, direct, moved, vectors):
    rows, features = direct.shape
    smem = pl.BlockSpec(memory_space=pltpu.SMEM)
    vmem = pl.BlockSpec(memory_space=pltpu.VMEM)
    return pl.pallas_call(
        enter_kernel,
        in_specs=[smem, vmem, vmem, vmem],
        out_specs=[vmem, vmem, vmem],
        out_shape=[
            jax.ShapeDtypeStruct((rows, features), F32),
            jax.ShapeDtypeStruct((rows, features), BF),
            jax.ShapeDtypeStruct((rows, features), BF),
        ],
        compiler_params=pltpu.CompilerParams(vmem_limit_bytes=VMEM_LIMIT),
        cost_estimate=took(4),
        name="enter",
    )(own_keep, direct, moved, vectors)


def half_specs(tile, weights):
    def spec(half, chip, whole):
        def index(f, turn):
            column = jnp.clip(f - 2 * half, 0, 1)
            return (chip ^ turn[0], 0, 0, column) if whole else (0, 0, column)

        return pl.BlockSpec((None, 2, 128, 2 * tile) if whole else (2, 128, 2 * tile), index)

    return [spec(half, chip, len(weights[half]) == 1) for half in range(2) for chip in range(4)]


def half_arrays(weights):
    return [array for half in weights for array in (half if len(half) == 4 else half * 4)]


def by_half(step, weight_refs, body):
    @pl.when(step < 2)
    def _():
        body(weight_refs[:4])

    @pl.when(step >= 2)
    def _():
        body(weight_refs[4:])


def joined(refs, first, last):
    return jnp.concatenate([ref[core, :, first:last] for ref in refs for core in range(2)], axis=0)


def mlp_kernel(turn_ref, normed_ref, other_ref, bias_ref, *rest):
    weight_refs, (hidden_ref, active_ref, near_ref, away_ref, acc_ref) = rest[:8], rest[8:]
    rows, tile = normed_ref.shape[0], hidden_ref.shape[1]
    step = pl.program_id(0)

    @pl.when(step == 0)
    def _():
        acc_ref[...] = jnp.zeros_like(acc_ref)

    def body(refs):
        expand, reduce = joined(refs, 0, tile), joined(refs, tile, 2 * tile)
        for first, ref in ((0, normed_ref), (rows, other_ref)):
            hidden = dot_nn(ref[...], expand) + bias_ref[...]
            inner = jnp.tanh(GELU_A * (hidden + GELU_B * hidden * hidden * hidden))
            active = (0.5 * hidden * (1.0 + inner)).astype(BF)
            hidden_ref[first:first + rows] = hidden.astype(BF)
            active_ref[first:first + rows] = active
            acc_ref[first:first + rows] += dot_nt(active, reduce)

    by_half(step, weight_refs, body)

    @pl.when(step == pl.num_programs(0) - 1)
    def _():
        near_ref[...] = acc_ref[:rows]
        away_ref[...] = flipped(acc_ref[rows:]).astype(BF)


def mlp_forward(turn, normed, other, bias, weights):
    rows, features = normed.shape
    units = bias.shape[1]
    tile = 512
    whole = pl.BlockSpec((rows, features), lambda f, turn: (0, 0))
    tiles = pl.BlockSpec((2 * rows, tile), lambda f, turn: (0, f))
    return pl.pallas_call(
        mlp_kernel,
        grid_spec=pltpu.PrefetchScalarGridSpec(
            num_scalar_prefetch=1,
            grid=(units // tile,),
            in_specs=[whole, whole, pl.BlockSpec((1, tile), lambda f, turn: (0, f))] + half_specs(tile, weights),
            out_specs=[tiles, tiles, whole, whole],
            scratch_shapes=[pltpu.VMEM((2 * rows, features), F32)],
        ),
        out_shape=[
            jax.ShapeDtypeStruct((2 * rows, units), BF),
            jax.ShapeDtypeStruct((2 * rows, units), BF),
            jax.ShapeDtypeStruct((rows, features), F32),
            jax.ShapeDtypeStruct((rows, features), BF),
        ],
        compiler_params=pltpu.CompilerParams(vmem_limit_bytes=VMEM_LIMIT),
        cost_estimate=took(18),
        name="mlp_forward",
    )(turn, normed, other, bias, *half_arrays(weights))


def mlp_close_kernel(last, own_ref, near_ref, got_ref, mid_ref, vector_ref, out_ref, next_ref):
    out = mid_ref[...] + (near_ref[...] + got_ref[...].astype(F32) + vector_ref[5:6])
    out_ref[...] = out
    if last:
        put_turned(next_ref, own_ref[0], out.astype(BF))
    else:
        next_ref[...] = (normalize(out)[0] * vector_ref[6:7] + vector_ref[7:8]).astype(BF)


def mlp_close(last, own_keep, near, got, mid, vectors):
    outs = [jax.ShapeDtypeStruct(mid.shape, F32), jax.ShapeDtypeStruct(mid.shape, BF)]
    args = [own_keep, near, got, mid, vectors]
    return call_once(functools.partial(mlp_close_kernel, last), "mlp_close", outs, args, 3)


def mlp_pull_kernel(turn_ref, grad_ref, other_ref, hidden_ref, *rest):
    weight_refs = rest[:8]
    grad_hidden_ref, grad_bias_ref, near_ref, away_ref, acc_ref, low_ref = rest[8:]
    rows, tile = grad_ref.shape[0], hidden_ref.shape[1]
    step = pl.program_id(0)

    @pl.when(step == 0)
    def _():
        low_ref[:rows] = grad_ref[...].astype(BF)
        low_ref[rows:] = other_ref[...]
        acc_ref[...] = jnp.zeros_like(acc_ref)

    def body(refs):
        expand, reduce = joined(refs, 0, tile), joined(refs, tile, 2 * tile)
        total = jnp.zeros((1, tile), F32)
        for first in (0, rows):
            here = slice(first, first + rows)
            hidden = hidden_ref[here].astype(F32)
            squared = hidden * hidden
            inner = jnp.tanh(GELU_A * hidden * (1.0 + GELU_B * squared))
            slope = 0.5 * (1.0 + inner) + 0.5 * hidden * (1.0 - inner * inner) * (GELU_A * (1.0 + 3.0 * GELU_B * squared))
            grad_hidden = dot_nn(low_ref[here], reduce) * slope
            total = total + jnp.sum(grad_hidden, axis=0, keepdims=True)
            grad_hidden = grad_hidden.astype(BF)
            grad_hidden_ref[here] = grad_hidden
            acc_ref[here] += dot_nt(grad_hidden, expand)
        grad_bias_ref[...] = total

    by_half(step, weight_refs, body)

    @pl.when(step == pl.num_programs(0) - 1)
    def _():
        near_ref[...] = acc_ref[:rows]
        away_ref[...] = flipped(acc_ref[rows:]).astype(BF)


def mlp_backward(turn, grad, other, hidden, weights):
    rows, features = grad.shape
    units = hidden.shape[1]
    tile = 512
    whole = pl.BlockSpec((rows, features), lambda f, turn: (0, 0))
    tiles = pl.BlockSpec((2 * rows, tile), lambda f, turn: (0, f))
    return pl.pallas_call(
        mlp_pull_kernel,
        grid_spec=pltpu.PrefetchScalarGridSpec(
            num_scalar_prefetch=1,
            grid=(units // tile,),
            in_specs=[whole, whole, tiles] + half_specs(tile, weights),
            out_specs=[tiles, pl.BlockSpec((1, tile), lambda f, turn: (0, f)), whole, whole],
            scratch_shapes=[pltpu.VMEM((2 * rows, features), F32), pltpu.VMEM((2 * rows, features), BF)],
        ),
        out_shape=[
            jax.ShapeDtypeStruct((2 * rows, units), BF),
            jax.ShapeDtypeStruct((1, units), F32),
            jax.ShapeDtypeStruct((rows, features), F32),
            jax.ShapeDtypeStruct((rows, features), BF),
        ],
        compiler_params=pltpu.CompilerParams(vmem_limit_bytes=VMEM_LIMIT),
        cost_estimate=took(22),
        name="mlp_backward",
    )(turn, grad, other, hidden, *half_arrays(weights))


def mlp_open_kernel(near_ref, got_ref, mid_ref, grad_ref, vector_ref, grad_mid_ref, grad_low_ref, sums_ref):
    grad = grad_ref[...]
    term = near_ref[...] + got_ref[...].astype(F32)
    grad_norm, grad_gain, grad_shift = norm_pull(mid_ref[...], vector_ref[3:4], term)
    grad_mid = grad + grad_norm
    grad_mid_ref[...] = grad_mid
    grad_low_ref[...] = grad_mid.astype(BF)
    rows = [jnp.sum(grad_mid, axis=0, keepdims=True), grad_gain, grad_shift, jnp.sum(grad, axis=0, keepdims=True)]
    sums_ref[...] = jnp.concatenate(rows + [jnp.zeros((4, grad.shape[1]), F32)], axis=0)


def mlp_open(near, got, mid, grad, vectors):
    outs = [
        jax.ShapeDtypeStruct(mid.shape, F32),
        jax.ShapeDtypeStruct(mid.shape, BF),
        jax.ShapeDtypeStruct((8, mid.shape[1]), F32),
    ]
    return call_once(mlp_open_kernel, "mlp_open", outs, [near, got, mid, grad, vectors], 5)


def unit_grads_kernel(second, left_ref, other_ref, right_ref, own_ref, pair_ref, single_ref, left_t_ref):
    @pl.when(pl.program_id(0) == 0)
    def _():
        left_t_ref[...] = jnp.concatenate([left_ref[...].astype(BF), other_ref[...]], axis=0).T

    grad = dot_nn(left_t_ref[...], right_ref[...]).astype(BF)
    single, direct = (1, 2) if second == "x" else (2, 1)
    for core in range(2):
        own_ref[0, core] = grad[core * 128:(core + 1) * 128]
        single_ref[0, core] = grad[(2 * single + core) * 128:(2 * single + core + 1) * 128]
        pair_ref[0, 0, core] = grad[(2 * direct + core) * 128:(2 * direct + core + 1) * 128]
        pair_ref[0, 1, core] = grad[(6 + core) * 128:(7 + core) * 128]


def unit_grads(second, left, other, right):
    rows, features = left.shape
    units = right.shape[1]
    tile = 512
    whole = pl.BlockSpec((rows, features), lambda f: (0, 0))
    out = pl.BlockSpec((1, 2, 128, tile), lambda f: (f // 2, 0, 0, f % 2))
    one = jax.ShapeDtypeStruct((2, 2, 128, 1024), BF)
    return pl.pallas_call(
        functools.partial(unit_grads_kernel, second),
        grid=(units // tile,),
        in_specs=[whole, whole, pl.BlockSpec((2 * rows, tile), lambda f: (0, f))],
        out_specs=[out, pl.BlockSpec((1, 2, 2, 128, tile), lambda f: (f // 2, 0, 0, 0, f % 2)), out],
        out_shape=[one, jax.ShapeDtypeStruct((2, 2, 2, 128, 1024), BF), one],
        scratch_shapes=[pltpu.VMEM((features, 2 * rows), BF)],
        compiler_params=pltpu.CompilerParams(vmem_limit_bytes=VMEM_LIMIT),
        cost_estimate=took(10),
        name="unit_grads",
    )(left, other, right)


def unit_grads_whole_kernel(turn_ref, left_ref, other_ref, right_ref, out_ref, left_t_ref):
    @pl.when(pl.program_id(0) == 0)
    def _():
        left_t_ref[...] = jnp.concatenate([left_ref[...].astype(BF), other_ref[...]], axis=0).T

    grad = dot_nn(left_t_ref[...], right_ref[...]).astype(BF)
    for chip in range(4):
        for core in range(2):
            first = (2 * chip + core) * 128
            out_ref[chip ^ turn_ref[0], 0, core] = grad[first:first + 128]


def unit_grads_whole(turn, left, other, right):
    rows, features = left.shape
    units = right.shape[1]
    tile = 512
    whole = pl.BlockSpec((rows, features), lambda f: (0, 0))
    return pl.pallas_call(
        unit_grads_whole_kernel,
        grid=(units // tile,),
        in_specs=[
            pl.BlockSpec(memory_space=pltpu.SMEM),
            whole,
            whole,
            pl.BlockSpec((2 * rows, tile), lambda f: (0, f)),
        ],
        out_specs=pl.BlockSpec((4, 1, 2, 128, tile), lambda f: (0, f // 2, 0, 0, f % 2)),
        out_shape=jax.ShapeDtypeStruct((4, 2, 2, 128, 1024), BF),
        scratch_shapes=[pltpu.VMEM((features, 2 * rows), BF)],
        compiler_params=pltpu.CompilerParams(vmem_limit_bytes=VMEM_LIMIT),
        cost_estimate=took(10),
        name="unit_grads_whole",
    )(turn, left, other, right)


MESH = pl.DeviceIdType.MESH


def flip(index, bit):
    return index + bit - 2 * bit * ((index // bit) % 2)


def peer(mask):
    dp, tensor = lax.axis_index("dp"), lax.axis_index("tensor")
    for bit in (1, 2):
        tensor = flip(tensor, bit) if mask & bit else tensor
        dp = flip(dp, bit) if mask & (CORE * bit) else dp
    dp = flip(dp, 4) if mask & YBIT else dp
    return {"dp": dp, "tensor": tensor}


def xor_block(block, own):
    return sum(bit * ((block // bit + own // bit) % 2) for bit in (1, 2, 4))


def greet(masks):
    barrier = pltpu.get_barrier_semaphore()
    for mask in masks:
        pl.semaphore_signal(barrier, inc=1, device_id=peer(mask), device_id_type=MESH)
    pl.semaphore_wait(barrier, len(masks))


def project_rows(rows, weight_refs, bias_ref, layer, out_refs):
    for quarter in (1, 0):
        weight = jnp.concatenate(
            [weight_refs[odd][chip, 1 - quarter if odd else quarter, :, 0:768] for chip in range(4) for odd in range(2)],
            axis=0,
        )
        out_refs[quarter][...] = (dot_nn(rows, weight) + bias_ref[layer, quarter:quarter + 1]).astype(BF)


SMALL_ROWS = 11


def start_kernel(layers, x_ref, *rest):
    sources, rest = rest[:13], rest[13:]
    targets, (vector_ref, head_bias_ref, unit_bias_ref, starts_ref), rest = rest[:12], rest[12:16], rest[16:]
    loaded, made, rest = rest[:13], rest[13:25], rest[25:]
    project_ref, output_ref, expand_ref, reduce_ref, *six_refs, bias_ref, unit_row_ref, places_ref = loaded
    (
        resid_ref, normed_ref, far_ref, even_ref, odd_ref, first_ref, heads_ref, pairs_ref,
        near_mine_ref, far_mine_ref, got_near_ref, got_far_ref,
    ) = made
    (
        came_ref, piece_ref, every_ref, near_other_ref, far_other_ref, local_sem, load_sem, store_sem, send_sem, recv_sem,
    ) = rest
    loads = [pltpu.make_async_copy(s, t, load_sem.at[i]) for i, (s, t) in enumerate(zip(sources, loaded))]
    for one in loads:
        one.start()
    stores = {id(s): pltpu.make_async_copy(s, t, store_sem.at[i]) for i, (s, t) in enumerate(zip(made, targets))}

    def store(*refs):
        for ref in refs:
            stores[id(ref)].start()

    own, place = lax.axis_index("dp"), lax.axis_index("tensor")
    core = own % 2
    keep = core == place // 2
    count = [0]

    def copy(source, target, device):
        index = count[0]
        count[0] += 1
        return pltpu.make_async_remote_copy(
            src_ref=source, dst_ref=target, send_sem=send_sem.at[index], recv_sem=recv_sem.at[index],
            device_id=device, device_id_type=MESH,
        )

    greet((1, 2, 4, 6, 8, 16))
    tokens = copy(x_ref, came_ref, peer(CORE | Z1))
    stay = pltpu.make_async_copy(x_ref, came_ref, local_sem)

    @pl.when(keep)
    def _():
        stay.start()

    @pl.when(jnp.logical_not(keep))
    def _():
        tokens.start()

    for one in loads:
        one.wait()

    def pack_heads_into(target, layer):
        for part in range(3):
            target[:, part * 256:(part + 1) * 256] = project_ref[layer, part]
        target[:, 768:1024] = output_ref[layer].T

    def pack_units_into(target, layer):
        for half in range(2):
            here = slice(half * 512, (half + 1) * 512)
            target[:, half * 1024:half * 1024 + 512] = expand_ref[layer, :, here]
            target[:, half * 1024 + 512:half * 1024 + 1024] = reduce_ref[layer, here, :].T

    pack_heads_into(even_ref.at[0, core], 0)
    along = copy(even_ref.at[0, core], even_ref.at[0, 1 - core], peer(Z1))
    along.start()
    every_ref[0, 0] = jnp.zeros(every_ref.shape[2:], F32)
    lane = lax.broadcasted_iota(jnp.int32, (1, 128), 1)
    for layer in range(layers):
        base = layer * SMALL_ROWS
        for row, ref in enumerate(six_refs):
            every_ref[0, 0, base + row:base + row + 1, :] = ref[layer:layer + 1, :].astype(F32)
        for part in range(2):
            ours = jnp.where(lane // 32 == own % 4, bias_ref[layer, part:part + 1, :].astype(F32), 0.0)
            every_ref[0, 0, pl.ds(base + 6 + 2 * part + own // 4, 1), :] = ours
        every_ref[0, 0, base + 10:base + 11, :] = unit_row_ref[layer:layer + 1, :].astype(F32)
    every_ref[0, 0, layers * SMALL_ROWS:layers * SMALL_ROWS + 1, :] = places_ref[...]
    smalls = [
        (copy(every_ref.at[0, pl.ds(0, width)], every_ref.at[0, pl.ds(width, width)], peer(mask)))
        for width, mask in ((1, CORE), (2, XBIT), (4, YBIT))
    ]
    smalls += [
        copy(every_ref.at[pl.ds(0, width)], every_ref.at[pl.ds(width, width)], peer(mask)) for width, mask in ((1, Z0), (2, Z1))
    ]
    smalls[0].start()
    pack_units_into(piece_ref, 0)
    cross = copy(piece_ref, first_ref.at[1], {
        "dp": flip(own, 1), "tensor": place + (1 - core) * (flip(place, 2) - place)
    })
    same = copy(piece_ref, first_ref.at[0], peer(Z1))

    @pl.when(core == 0)
    def _():
        first_ref[0] = piece_ref[...]

    for step in range(1, 5):
        smalls[step - 1].wait()
        smalls[step].start()
    along.wait()
    over_x = copy(even_ref.at[0], even_ref.at[1], peer(XBIT))
    over_y = copy(even_ref.at[0], even_ref.at[2], peer(YBIT))
    over_x.start()
    over_y.start()
    cores = [copy(even_ref.at[chip], odd_ref.at[chip], peer(CORE)) for chip in range(4)]
    cores[0].start()
    smalls[4].wait()
    half = place // 2
    starts_ref[...] = every_ref[0, core + half - 2 * core * half, layers * SMALL_ROWS:layers * SMALL_ROWS + 1, :]
    for layer in range(layers):
        base = layer * SMALL_ROWS
        later = min(layer + 1, layers - 1) * SMALL_ROWS
        rows = [base + row for row in range(6)] + [later, later + 1]
        for row, source in enumerate(rows):
            vector_ref[layer, row:row + 1, :] = jnp.concatenate(
                [every_ref[0, block, source:source + 1, :] for block in range(8)], axis=1
            )
        for quarter in range(2):
            which = 2 * (core + quarter - 2 * core * quarter)
            total = every_ref[which, 0, base + 6:base + 10, :]
            for block in range(1, 8):
                total = total + every_ref[which, block, base + 6:base + 10, :]
            head_bias_ref[layer, quarter:quarter + 1, :] = jnp.concatenate(
                [total[0:1], total[1:2], jnp.zeros((1, 256), F32), total[2:3], total[3:4]], axis=1
            )
            for block in range(8):
                unit_bias_ref[layer, :, quarter * 1024 + block * 128:quarter * 1024 + (block + 1) * 128] = every_ref[
                    2 * core + quarter, xor_block(block, own), base + 10:base + 11, :
                ]
    @pl.when(keep)
    def _():
        stay.wait()

    @pl.when(jnp.logical_not(keep))
    def _():
        tokens.wait()

    for block in range(8):
        here = pl.ds(pl.multiple_of(xor_block(block, own) * 128, 128), 128)
        resid_ref[:, block * 128:(block + 1) * 128] = came_ref[:, here].astype(F32)
    normed = (normalize(resid_ref[...])[0] * vector_ref[0, 0:1] + vector_ref[0, 1:2]).astype(BF)
    normed_ref[...] = normed
    store(resid_ref, normed_ref)
    beside = copy(normed_ref, far_ref, peer(Z0))
    beside.start()
    cross.start()

    @pl.when(core == 1)
    def _():
        same.start()

    ahead = []
    for layer in range(1, layers):
        pack_heads_into(heads_ref.at[layer - 1], layer)
        pack_units_into(pairs_ref.at[layer - 1, 0], layer)
        ahead.append(copy(pairs_ref.at[layer - 1, 0], pairs_ref.at[layer - 1, 1], peer(CORE)))
    for one in ahead:
        one.start()
    over_y.wait()
    over_x.wait()
    across = copy(even_ref.at[2], even_ref.at[3], peer(XBIT))
    across.start()
    cores[1].start()
    cores[2].start()
    across.wait()
    cores[3].start()
    for one in cores:
        one.wait()
    store(even_ref, odd_ref)
    weights = (even_ref, odd_ref)
    project_rows(normed_ref[...], weights, head_bias_ref, 0, (near_mine_ref, near_other_ref))
    back_near = copy(near_other_ref, got_near_ref, peer(CORE))
    back_near.start()
    store(near_mine_ref)
    beside.wait()
    project_rows(far_ref[...], weights, head_bias_ref, 0, (far_mine_ref, far_other_ref))
    back_far = copy(far_other_ref, got_far_ref, peer(CORE))
    back_far.start()
    store(far_ref, far_mine_ref)
    for one in ahead:
        one.wait()
    store(heads_ref, pairs_ref)
    back_near.wait()
    store(got_near_ref)
    cross.wait()

    @pl.when(core == 1)
    def _():
        same.wait()

    store(first_ref)
    back_far.wait()
    store(got_far_ref)
    for one in stores.values():
        one.wait()


def start(x, project_weight, output_weight, expand_weight, reduce_weight, six, project_bias, expand_bias, places):
    rows, features = x.shape
    layers = expand_bias.shape[0]
    small = 8 * (-(-(SMALL_ROWS * layers + 1) // 8))
    project_bias = jnp.tile(project_bias, (1, 1, 4))
    places = jnp.pad(places.astype(F32), ((0, 0), (0, 128 - places.shape[1])))
    args = [project_weight, output_weight, expand_weight, reduce_weight, *six, project_bias, expand_bias, places]
    vmem, hbm = pl.BlockSpec(memory_space=pltpu.VMEM), pl.BlockSpec(memory_space=pltpu.HBM)
    triple = jax.ShapeDtypeStruct((rows, 768), BF)
    heads = jax.ShapeDtypeStruct((4, 2, 128, 1024), BF)
    made = [
        jax.ShapeDtypeStruct((rows, features), F32),
        jax.ShapeDtypeStruct((rows, features), BF),
        jax.ShapeDtypeStruct((rows, features), BF),
        heads,
        heads,
        jax.ShapeDtypeStruct((2, 128, 2048), BF),
        jax.ShapeDtypeStruct((layers - 1, 128, 1024), BF),
        jax.ShapeDtypeStruct((layers - 1, 2, 128, 2048), BF),
        triple,
        triple,
        triple,
        triple,
    ]
    spread = [
        jax.ShapeDtypeStruct((layers, 8, features), F32),
        jax.ShapeDtypeStruct((layers, 2, 768), F32),
        jax.ShapeDtypeStruct((layers, 1, 2048), F32),
        jax.ShapeDtypeStruct((1, 128), F32),
    ]
    copies = 19 + layers - 1
    return pl.pallas_call(
        functools.partial(start_kernel, layers),
        in_specs=[hbm] * (1 + len(args)),
        out_specs=[hbm] * len(made) + [vmem] * len(spread),
        out_shape=made + spread,
        scratch_shapes=[
            *[pltpu.VMEM(a.shape, a.dtype) for a in args + made],
            pltpu.VMEM((rows, features), BF),
            pltpu.VMEM((128, 2048), BF),
            pltpu.VMEM((4, 8, small, 128), F32),
            pltpu.VMEM((rows, 768), BF),
            pltpu.VMEM((rows, 768), BF),
            pltpu.SemaphoreType.DMA,
            pltpu.SemaphoreType.DMA((len(args),)),
            pltpu.SemaphoreType.DMA((len(made),)),
            pltpu.SemaphoreType.DMA((copies,)),
            pltpu.SemaphoreType.DMA((copies,)),
        ],
        compiler_params=pltpu.CompilerParams(vmem_limit_bytes=60 * 1024 * 1024, collective_id=0, has_side_effects=True),
        cost_estimate=took(60),
        name="start",
    )(x, *args)


def finish_kernel(
    layers, grad_ref, even_ref, odd_ref, here_ref, away_ref, *rest,
):
    sums, rest = rest[:4 * layers], rest[4 * layers:]
    grad_out_ref, project_ref, output_ref, reduce_ref, expand_ref, small_ref, rest = *rest[:6], rest[6:]
    odd_got, y_send, y_got, x_send, x_got, relay_send, relay_got, z_send, z_got, away_got, part_ref, part_got, rest = *rest[:12], rest[12:]
    rows_ref, core_got, x_rows, y_rows, near_send, near_got, far_send, far_got, local_sem, send_sem, recv_sem = rest
    own, place = lax.axis_index("dp"), lax.axis_index("tensor")
    core = own % 2
    keep = core == place // 2
    count = [0]

    def copy(source, target, device):
        index = count[0]
        count[0] += 1
        return pltpu.make_async_remote_copy(
            src_ref=source, dst_ref=target, send_sem=send_sem.at[index], recv_sem=recv_sem.at[index],
            device_id=device, device_id_type=MESH,
        )

    greet((1, 2, 4, 6, 8, 16))
    across = copy(odd_ref, odd_got, peer(CORE))
    across.start()
    beside = copy(away_ref, away_got, peer(Z0))
    beside.start()
    tokens = copy(grad_ref, grad_out_ref, peer(CORE | Z1))
    stay = pltpu.make_async_copy(grad_ref, grad_out_ref, local_sem)

    @pl.when(keep)
    def _():
        stay.start()

    @pl.when(jnp.logical_not(keep))
    def _():
        tokens.start()

    vectors = 6 * layers
    rows_ref[...] = jnp.zeros_like(rows_ref)
    for layer in range(layers):
        first_ref, second_ref, unit_ref, head_ref = sums[4 * layer:4 * layer + 4]
        base = vectors + 12 * layer
        for block in range(8):
            slot = (block % 2) * 4 + (block // 2 % 2) * 2 + block // 4
            lanes = slice(block * 128, (block + 1) * 128)
            rows_ref[slot, 6 * layer:6 * layer + 2, :] = first_ref[0:2, lanes]
            rows_ref[slot, 6 * layer + 2:6 * layer + 6, :] = second_ref[0:4, lanes]
            for quarter in range(2):
                lane = pl.multiple_of(quarter * 1024 + xor_block(block, own) * 128, 128)
                rows_ref[slot, pl.ds(base + 2 * core + quarter, 1), :] = unit_ref[0:1, pl.ds(lane, 128)]
                row = base + 4 + 4 * (quarter + core - 2 * quarter * core)
                for half in range(2):
                    rows_ref[slot, pl.ds(row + 2 * half, 2), :] = head_ref[
                        2 * quarter:2 * quarter + 2, half * 128:(half + 1) * 128
                    ]
    hop = copy(rows_ref.at[pl.ds(4, 4)], core_got, peer(CORE))
    hop.start()
    hop.wait()
    rows_ref[0:4] = rows_ref[0:4] + core_got[...]
    hop = copy(rows_ref.at[pl.ds(2, 2)], x_rows, peer(XBIT))
    hop.start()
    across.wait()
    for chip in range(4):
        for quarter in range(2):
            odd_got[chip, quarter] = odd_got[chip, quarter] + even_ref[chip, quarter]
    y_send[0], y_send[1] = odd_got[2, 0], odd_got[3, 0]
    x_send[0], x_send[1] = odd_got[1, 1], odd_got[3, 1]
    over_y = copy(y_send, y_got, peer(YBIT))
    over_x = copy(x_send, x_got, peer(XBIT))
    over_y.start()
    over_x.start()
    hop.wait()
    rows_ref[0:2] = rows_ref[0:2] + x_rows[...]
    hop = copy(rows_ref.at[pl.ds(1, 1)], y_rows, peer(YBIT))
    hop.start()
    hop.wait()
    rows_ref[0] = rows_ref[0] + y_rows[0]
    near_send[...] = jnp.zeros_like(near_send)
    far_send[...] = jnp.zeros_like(far_send)
    near_send[0:vectors, :] = rows_ref[0, 0:vectors, :]
    for layer in range(layers):
        base = vectors + 12 * layer
        near_send[vectors + 2 * layer:vectors + 2 * layer + 1, :] = rows_ref[0, base + 1:base + 2, :]
        near_send[vectors + 2 * layer + 1:vectors + 2 * layer + 2, :] = rows_ref[0, base + 3:base + 4, :]
    hop = copy(near_send, near_got, peer(Z0))
    hop.start()
    over_y.wait()
    over_x.wait()
    relay_send[0] = odd_got[1, 0] + y_got[1]
    relay_send[1] = odd_got[2, 1] + x_got[1]
    relays = [copy(relay_send.at[i], relay_got.at[i], peer(mask)) for i, mask in ((0, XBIT), (1, YBIT))]
    for one in relays:
        one.start()
    beside.wait()
    for kind in range(2):
        for side in range(2):
            part_ref[side, kind] = here_ref[kind, side] + away_got[kind, side]
    crossing = copy(part_ref.at[1], part_got.at[1], {
        "dp": flip(own, 1), "tensor": place + core * (flip(place, 2) - place)
    })
    crossing.start()
    along = copy(part_ref.at[0], part_got.at[0], peer(Z1))

    @pl.when(core == 1)
    def _():
        along.start()

    @pl.when(core == 0)
    def _():
        part_got[0] = part_ref[0]

    for one in relays:
        one.wait()
    total = [odd_got[0, 0] + y_got[0] + relay_got[0], odd_got[0, 1] + x_got[0] + relay_got[1]]
    z_send[core] = total[0]
    z_send[1 - core] = total[1]
    heads = copy(z_send.at[1], z_got, peer(Z1))
    heads.start()
    hop.wait()
    far_send[0:vectors, :] = rows_ref[0, 0:vectors, :] + near_got[0:vectors, :]
    for layer in range(layers):
        base = vectors + 12 * layer
        far_send[vectors + layer:vectors + layer + 1, :] = (
            rows_ref[0, base + 2:base + 3, :] + near_got[vectors + 2 * layer + 1:vectors + 2 * layer + 2, :]
        )
        far_send[vectors + layers + 4 * layer:vectors + layers + 4 * layer + 4, :] = rows_ref[0, base + 8:base + 12, :]
    hop = copy(far_send, far_got, peer(Z1))
    hop.start()
    crossing.wait()

    @pl.when(core == 1)
    def _():
        along.wait()

    reduce_ref[...] = (part_got[0, 0].astype(F32) + part_got[1, 0].astype(F32)).T
    expand_ref[...] = part_got[0, 1].astype(F32) + part_got[1, 1].astype(F32)
    hop.wait()
    small_ref[0:vectors, :] = far_send[0:vectors, :] + far_got[0:vectors, :]
    for layer in range(layers):
        base = vectors + 12 * layer
        row = vectors + layer
        small_ref[row:row + 1, :] = (
            rows_ref[0, base:base + 1, :] + near_got[vectors + 2 * layer:vectors + 2 * layer + 1, :] + far_got[row:row + 1, :]
        )
        row = vectors + layers + 4 * layer
        small_ref[row:row + 4, :] = rows_ref[0, base + 4:base + 8, :] + far_got[row:row + 4, :]
    heads.wait()
    for part in range(3):
        here = slice(part * 256, (part + 1) * 256)
        project_ref[part] = z_send[0, :, here].astype(F32) + z_got[:, here].astype(F32)
    output_ref[...] = (z_send[0, :, 768:].astype(F32) + z_got[:, 768:].astype(F32)).T

    @pl.when(keep)
    def _():
        stay.wait()

    @pl.when(jnp.logical_not(keep))
    def _():
        tokens.wait()


def finish(grad, even, odd, here, away, sums):
    layers = len(sums)
    vmem = pl.BlockSpec(memory_space=pltpu.VMEM)
    rows = 18 * layers
    args = [grad, even, odd, here, away, *[array for layer in sums for array in layer]]
    small = 8 * (-(-11 * layers // 8))
    outs = [
        jax.ShapeDtypeStruct(grad.shape, BF),
        jax.ShapeDtypeStruct((3, 128, 256), F32),
        jax.ShapeDtypeStruct((256, 128), F32),
        jax.ShapeDtypeStruct((1024, 128), F32),
        jax.ShapeDtypeStruct((128, 1024), F32),
        jax.ShapeDtypeStruct((small, 128), F32),
    ]
    one = (128, 1024)
    copies = 15
    return pl.pallas_call(
        functools.partial(finish_kernel, layers),
        in_specs=[vmem] * len(args),
        out_specs=[vmem] * len(outs),
        out_shape=outs,
        scratch_shapes=[
            pltpu.VMEM((4, 2, *one), BF),
            *[pltpu.VMEM((2, *one), BF)] * 7,
            pltpu.VMEM(one, BF),
            *[pltpu.VMEM((2, 2, *one), BF)] * 3,
            pltpu.VMEM((8, rows, 128), F32),
            pltpu.VMEM((4, rows, 128), F32),
            pltpu.VMEM((2, rows, 128), F32),
            pltpu.VMEM((1, rows, 128), F32),
            *[pltpu.VMEM((small, 128), F32)] * 4,
            pltpu.SemaphoreType.DMA,
            pltpu.SemaphoreType.DMA((copies,)),
            pltpu.SemaphoreType.DMA((copies,)),
        ],
        compiler_params=pltpu.CompilerParams(vmem_limit_bytes=VMEM_LIMIT, collective_id=1, has_side_effects=True),
        cost_estimate=took(50),
        name="finish",
    )(*args)


def fetch_heads(piece, core, turn, out):
    token = yield
    far = swap(after(piece, token), Z1)
    token = yield []
    far = after(far, token)
    own = jnp.stack([jnp.where(core == 0, piece, far), jnp.where(core == 0, far, piece)])
    from_x = swap(own, XBIT)
    from_y = swap(own, YBIT)
    token = yield [own]
    from_x, from_y = after_all((from_x, from_y), token)
    across = swap(from_y, XBIT)
    token = yield [from_x, from_y]
    quads = jnp.stack([own, from_x, from_y, after(across, token)])
    other = swap(quads, CORE)
    token = yield [quads]
    out += [quads, other, turn]


def join_units(first, first_x, first_y, second, first_out, second_out):
    second_x, second_y = swap(second, XBIT), swap(second, YBIT)
    token = yield [first_x, first_y, second]
    first_x, second_x, second_y = after_all((first_x, second_x, second_y), token)
    first_across, second_across = swap(first_x, YBIT), swap(second_y, XBIT)
    token = yield [second_x, second_y]
    first_across, second_across = after_all((first_across, second_across), token)
    first_out += [first, first_x, first_y, first_across]
    second_out += [second, second_x, second_y, second_across]
    yield [first_across, second_across]


def fetch_units_near(first, first_out, second_out):
    token = yield
    first = after(first, token)
    first_x, first_y, second = swap(first, XBIT), swap(first, YBIT), swap(first, Z0)
    token = yield []
    first_x, first_y, second = after_all((first_x, first_y, second), token)
    yield from join_units(first, first_x, first_y, second, first_out, second_out)


def fetch_units(pair, core, first_out, second_out):
    token = yield
    far = swap_some(after(pair, token), (0, Z1))
    token = yield []
    first = jnp.where(core == 0, pair, after(far, token))
    second = swap(first, Z0)
    token = yield [first]
    second = after(second, token)
    token = yield [second]
    first = after(first, token)
    first_x, first_y = swap(first, XBIT), swap(first, YBIT)
    token = yield []
    first_x, first_y = after_all((first_x, first_y), token)
    yield from join_units(first, first_x, first_y, second, first_out, second_out)


def unpack_heads(values):
    return values[:, :768].reshape(128, 3, 256).transpose(1, 0, 2), values[:, 768:].T


def reduce_heads(even, odd, core, out):
    token = yield
    got = swap(odd, CORE)
    token = yield []
    got = after(got, token)
    low, high = even[:2] + got[:2], even[2:] + got[2:]
    from_y = swap(high, YBIT)
    token = yield [low, high]
    from_y = after(from_y, token)
    relayed = low[1] + from_y[1]
    relay = swap(relayed, XBIT)
    token = yield [relayed]
    total = low[0] + from_y[0] + after(relay, token)
    yield from close_heads(total, core, out)


def close_heads(total, core, out):
    near = jnp.where(core == 0, total[0], total[1])
    away = jnp.where(core == 0, total[1], total[0])
    far = swap(away, Z1)
    token = yield [near, away]
    out.append(unpack_heads(near.astype(F32) + after(far, token).astype(F32)))
    yield list(out[-1])


def reduce_units(reduce_parts, expand_parts, core, out):
    yield
    own_r, pair_r, single_r = reduce_parts
    from_y = swap(pair_r, YBIT)
    yield []
    own_e, pair_e, single_e = expand_parts
    from_x = swap(pair_e, XBIT)
    token = yield []
    from_y = after(from_y, token)
    relayed_r = single_r + from_y[:, 1]
    relay_r = swap(relayed_r, XBIT)
    token = yield [relayed_r]
    from_x = after(from_x, token)
    relayed_e = single_e + from_x[:, 1]
    relay_e = swap(relayed_e, YBIT)
    token = yield [relayed_e]
    relay_r, relay_e = after_all((relay_r, relay_e), token)
    totals = [
        jnp.stack([own_r[i] + from_y[i, 0] + relay_r[i], own_e[i] + from_x[i, 0] + relay_e[i]]) for i in range(2)
    ]
    if core is None:
        out += totals
        yield totals
        return
    yield from close_units(*totals, core, out)


def close_units(here, away, core, out):
    got = swap(away, Z0)
    token = yield [here, away]
    here = here + after(got, token)
    token = yield [here]
    here = after(here, token)
    same, cross = here[:, 0], here[:, 1]
    same_got, cross_got = swap_some(same, (0, Z1)), swap_some(cross, (CORE, CORE | Z1))
    token = yield [same, cross]
    same_got, cross_got = after_all((same_got, cross_got), token)
    out.append(jnp.where(core == 0, same, same_got).astype(F32) + cross_got.astype(F32))
    yield [out[-1]]


def fast_device(
    layer_input,
    first_gain,
    first_shift,
    project_weight,
    project_bias,
    output_weight,
    output_bias,
    second_gain,
    second_shift,
    expand_weight,
    expand_bias,
    reduce_weight,
    reduce_bias,
    picture_start,
    cotangent,
):
    own = lax.axis_index("dp")
    place = lax.axis_index("tensor")
    core = own & 1
    keep = core == (place >> 1)
    own_keep = jnp.stack([own, keep.astype(jnp.int32)]).astype(jnp.int32)
    me = (2 * core + (place & 1)).astype(jnp.int32).reshape(1)
    slopes = head_slopes((place ^ (2 * core)) * 4, 4)

    turn = jnp.zeros((1,), jnp.int32)
    (
        resid, normed, far, even, odd, first_pieces, own_heads, own_units, near_mine, far_mine, got_near, got_far,
        vectors_of, head_bias_of, unit_bias_of, places,
    ) = start(
        layer_input, project_weight, output_weight, expand_weight, reduce_weight,
        (first_gain, first_shift, output_bias, second_gain, second_shift, reduce_bias), project_bias, expand_bias,
        picture_start,
    )
    small = [(vectors_of[i], head_bias_of[i], unit_bias_of[i]) for i in range(LAYERS)]
    starts = places[0, :picture_start.shape[1]].astype(jnp.int32)
    heads, units = [[] for i in range(LAYERS)], [([], []) for i in range(LAYERS)]
    heads[0] += [even, odd, turn]
    head_tasks, unit_tasks = [None], [task(fetch_units_near(first_pieces, *units[0]))]
    for layer in range(1, LAYERS):
        head_tasks.append(task(fetch_heads(own_heads[layer - 1], core, turn, heads[layer])))
        unit_tasks.append(task(fetch_units(own_units[layer - 1], core, *units[layer])))
    saved = []
    for layer in range(LAYERS):
        vectors, head_bias, unit_bias = small[layer]
        first, last = layer == 0, layer + 1 == LAYERS
        if not first:
            far = swap(normed, Z0)
            while not heads[layer]:
                advance(normed, head_tasks[layer])
            near_mine, near_other = project(normed, head_bias, heads[layer])
            got_near = swap(near_other, CORE)
            far_mine, far_other = project(after(far, near_mine), head_bias, heads[layer])
            got_far = swap(far_other, CORE)
        pieces = heads[layer]
        made = advance(far_mine, unit_tasks[layer])
        blocks = after_all((near_mine, far_mine, got_near, got_far), *made)
        if last:
            cotangent_far = redeal(after(cotangent, far_mine))
        far_mixed, far_send, far_exact, far_log = attend(blocks, 1, slopes, starts, me)
        far_got = swap(far_send, CORE)
        far_part = mix_far(far_mixed, far_got, pieces)
        far_term = swap(far_part, Z0)
        made = advance(far_part, unit_tasks[layer])
        if last:
            grad, unused, flip_grad = enter(own_keep, cotangent, after(cotangent_far, far_part), vectors)
            grad_other = swap(flip_grad, CORE)
            made.append(grad)
        near_blocks = after_all(blocks, far_part, *made)
        near_mixed, near_send, near_exact, near_log = attend(near_blocks, 0, slopes, starts, me)
        near_got = swap(near_send, CORE)
        made = advance(near_mixed, unit_tasks[layer])
        if first:
            advance(near_mixed, unit_tasks[1], head_tasks[1])
        mid, normed_two, flip_two = mix_near(near_mixed, near_got, after(far_term, near_mixed, *made), resid, vectors, pieces)
        normed_other = swap(flip_two, CORE)
        if first:
            made = advance(mid, unit_tasks[0])
            made += advance(mid, unit_tasks[1], head_tasks[1])
            normed_two = after(normed_two, *made)
        hidden, active, near_out, away_out = mlp_forward(turn, normed_two, normed_other, unit_bias, units[layer])
        got_out = swap(away_out, CORE)
        if not last:
            got_out = after(got_out, *advance(near_out, head_tasks[layer + 1], unit_tasks[layer + 1]))
        out, following = mlp_close(last, own_keep, near_out, got_out, mid, vectors)
        if not last:
            advance(out, head_tasks[layer + 1])
            advance(out, unit_tasks[layer + 1])
        saved.append((
            resid, normed, far, blocks, (near_exact, far_exact), (near_log, far_log), (near_mixed, far_mixed),
            (near_got, far_got), mid, normed_two, normed_other, hidden, active,
        ))
        resid, normed = out, following
    layer_output = jnp.where(keep, normed, redeal(normed))
    grad = after(grad, normed)
    sums = [None] * LAYERS
    head_grad, unit_grad = ([[] for i in range(LAYERS)] for j in range(2))
    pending = []
    for layer in reversed(range(LAYERS)):
        vectors, pieces = small[layer][0], heads[layer]
        (
            resid, normed, far, blocks, exacts, logs, mixed, mixed_got, mid, normed_two, normed_other, hidden, active,
        ) = saved[layer]
        grad_hidden, unit_sums, near_term, away_term = mlp_backward(turn, grad, grad_other, hidden, units[layer])
        got_term = after(swap(away_term, CORE), *advance(near_term, *pending))
        grad_mid, grad_low, second_sums = mlp_open(near_term, got_term, mid, grad, vectors)
        grad_far = swap(grad_low, Z0)
        first = layer == 0
        reduce_parts = unit_grads("x", grad, grad_other, after(active, grad_low))
        near_mine, near_other = unmix(after(grad_low, reduce_parts[0]), pieces)
        got_near = swap(near_other, CORE)
        expand_parts = unit_grads("y", normed_two, normed_other, after(grad_hidden, near_mine))
        unit_task = task(reduce_units(reduce_parts, expand_parts, None if first else core, unit_grad[layer]))
        advance(None, unit_task)
        advance(None, unit_task)
        far_mine, far_other = unmix(after(grad_far, expand_parts[0]), pieces)
        got_far = swap(far_other, CORE)
        made = advance(far_mine, *pending)
        grads_mixed = after_all((near_mine, far_mine, got_near, got_far), *made)
        mine_0, away_0 = attend_pull(0, blocks, grads_mixed, exacts, logs, slopes, starts, me)
        other_0 = swap(away_0, CORE)
        made = advance(mine_0, unit_task)
        grads_mixed = after_all(grads_mixed, mine_0, *made)
        mine_1, away_1 = attend_pull(1, blocks, grads_mixed, exacts, logs, slopes, starts, me)
        other_1 = swap(away_1, CORE)
        made = advance(mine_1, unit_task, *pending)
        other_1 = after(other_1, *made, *([layer_output] if layer == LAYERS - 1 else []))
        mine, other = (mine_0, mine_1), (other_0, other_1)
        far_part = unproject_far(mine, other, pieces)
        far_term = swap(far_part, Z0)
        even, odd, head_sums = head_grads(
            turn, normed, far, grad_low, after(grad_far, far_part), mine, other, mixed, mixed_got
        )
        if not first:
            head_task = task(reduce_heads(even, odd, core, head_grad[layer]))
            advance(None, head_task)
        made = advance(head_sums, unit_task)
        grad, grad_low, first_sums = unproject_near(
            first, own_keep, mine, other, after(far_term, *made), resid, grad_mid, vectors, pieces
        )
        sums[layer] = (first_sums, second_sums, unit_sums, head_sums)
        if not first:
            grad_other = swap(grad_low, CORE)
            grad = after(grad, *advance(grad, head_task))
        pending = [unit_task, head_task]
    input_grad, *grads, small_sums = finish(grad_low, even, odd, *unit_grad[0], sums)
    head_grad[0], unit_grad[0] = [grads[:2]], [grads[2:]]
    unit_grad[1:] = [[(g[0][0].T, g[0][1])] for g in unit_grad[1:]]
    six = small_sums[:6 * LAYERS].reshape(LAYERS, 6, 128)
    unit_sum = small_sums[6 * LAYERS:7 * LAYERS]
    head_sum = small_sums[7 * LAYERS:11 * LAYERS].reshape(LAYERS, 2, 2, 128).transpose(0, 2, 1, 3).reshape(LAYERS, 2, 256)
    head_sum = lax.dynamic_slice_in_dim(head_sum, own * 32, 32, 2)
    return (
        layer_output,
        input_grad,
        six[:, 0],
        six[:, 1],
        jnp.stack([g[0][0] for g in head_grad]),
        head_sum,
        jnp.stack([g[0][1] for g in head_grad]),
        six[:, 2],
        six[:, 3],
        six[:, 4],
        jnp.stack([g[0][1] for g in unit_grad]),
        unit_sum,
        jnp.stack([g[0][0] for g in unit_grad]),
        six[:, 5],
    )


def solution(mesh):
    placed = (
        P(("dp", "tensor"), None),
        P(None, "dp"),
        P(None, "dp"),
        P(None, None, "dp", "tensor"),
        P(None, None, ("tensor", "dp")),
        P(None, "tensor", "dp"),
        P(None, "dp"),
        P(None, "dp"),
        P(None, "dp"),
        P(None, "dp", "tensor"),
        P(None, ("tensor", "dp")),
        P(None, "tensor", "dp"),
        P(None, "dp"),
        P("dp", None),
        P(("dp", "tensor"), None),
    )
    return jax.shard_map(
        fast_device if mesh_is_paired(mesh) else on_device,
        mesh=mesh,
        in_specs=placed,
        out_specs=(
            P(("dp", "tensor"), None),
            P(("dp", "tensor"), None),
            P(None, "dp"),
            P(None, "dp"),
            P(None, None, "dp", "tensor"),
            P(None, None, ("tensor", "dp")),
            P(None, "tensor", "dp"),
            P(None, "dp"),
            P(None, "dp"),
            P(None, "dp"),
            P(None, "dp", "tensor"),
            P(None, ("tensor", "dp")),
            P(None, "tensor", "dp"),
            P(None, "dp"),
        ),
        check_vma=False,
    )
```

```python
import functools

import jax
import jax.numpy as jnp
from jax import lax
from jax.experimental import pallas as pl
from jax.experimental.pallas import tpu as pltpu
from jax.sharding import PartitionSpec as P

HEADS = 16
HD = 64
LAYERS = 2
SEQ_LEN = 2048
PIECE = 256


NORM_EPS = 1e-05


def layer_norm(values, gain, shift):
    centred = values - jnp.mean(values, axis=-1, keepdims=True)
    spread = jnp.mean(centred * centred, axis=-1, keepdims=True)
    return centred * lax.rsqrt(spread + NORM_EPS) * gain + shift


def gelu_tanh(values):
    return jax.nn.gelu(values, approximate=True)


def piece_numbers(starts):
    places = jnp.arange(SEQ_LEN, dtype=jnp.int32)
    inside = (places[:, None] >= starts[None, :]) & (places[:, None] < starts[None, :] + PIECE)
    numbers = jnp.arange(1, starts.shape[0] + 1, dtype=jnp.int32)
    return jnp.sum(jnp.where(inside, numbers[None, :], 0), axis=1)


def head_slopes(first_head, count_heads):
    heads_at = (first_head + jnp.arange(count_heads, dtype=jnp.int32)).astype(jnp.float32)
    return jnp.exp2(-8.0 * (heads_at + 1.0) / HEADS)


def gather_rows(values):
    return lax.all_gather(values, "tensor", axis=0, tiled=True)


def gather_grads(values):
    return lax.all_gather(values, "tensor", axis=0, tiled=True)


def scatter_rows(values, weight):
    rows_here = values.shape[0] // lax.axis_size("tensor")

    def partial_term(offset, count_rows):
        return jnp.dot(values, weight, preferred_element_type=jnp.float32)

    return lax.psum_scatter(
        partial_term(jnp.int32(0), rows_here * lax.axis_size("tensor")).astype(jnp.bfloat16),
        "tensor",
        scatter_dimension=0,
        tiled=True,
    ).astype(jnp.float32)


def scatter_back(partial_term, rows_here):
    return lax.psum_scatter(
        partial_term(jnp.int32(0), rows_here * lax.axis_size("tensor")).astype(jnp.bfloat16),
        "tensor",
        scatter_dimension=0,
        tiled=True,
    ).astype(jnp.float32)


def block_scores(query_block, key_rows, offset, piece_ids, slopes):
    length = key_rows.shape[0]
    count_rows = query_block.shape[0]
    query_places = offset + jnp.arange(count_rows, dtype=jnp.int32)
    key_places = jnp.arange(length, dtype=jnp.int32)
    product = jnp.einsum("qhe,khe->hqk", query_block, key_rows, preferred_element_type=jnp.float32)
    distance = jnp.abs(query_places[:, None] - key_places[None, :]).astype(jnp.float32)
    scores = product * HD ** (-0.5) - slopes[:, None, None] * distance[None]
    query_pieces = lax.dynamic_slice_in_dim(piece_ids, offset, count_rows, 0)
    allowed = (key_places[None, :] <= query_places[:, None]) | (
        query_pieces[:, None] == piece_ids[None, :]
    ) & (query_pieces[:, None] > 0)
    return jnp.where(allowed[None], scores, -jnp.inf)


def sequence_forward(operands, slopes):
    queries, key_rows, value_rows, piece_ids = operands
    length = queries.shape[0]
    block_rows = min(512, length)

    def one_block(block_index):
        offset = block_index * block_rows
        query_block = lax.dynamic_slice_in_dim(queries, offset, block_rows, 0)
        scores = block_scores(query_block, key_rows, offset, piece_ids, slopes)
        row_max = jnp.max(scores, axis=-1, keepdims=True)
        raw_weights = jnp.exp(scores - row_max)
        totals = jnp.sum(raw_weights, axis=-1, keepdims=True)
        soft_weights = (raw_weights / totals).astype(jnp.bfloat16)
        attended = jnp.einsum(
            "hqk,khe->qhe", soft_weights, value_rows, preferred_element_type=jnp.float32
        )
        return (attended.astype(jnp.bfloat16), (row_max + jnp.log(totals))[..., 0])

    attended, log_total = lax.map(one_block, jnp.arange(length // block_rows, dtype=jnp.int32))
    return (attended.reshape(length, queries.shape[1], queries.shape[2]), log_total)


def sequence_backward(operands, slopes):
    queries, key_rows, value_rows, piece_ids, grad_mixed, log_total = operands
    length = queries.shape[0]
    block_rows = min(512, length)

    def one_block(carry, block_index):
        key_grad, value_grad = carry
        offset = block_index * block_rows
        query_block = lax.dynamic_slice_in_dim(queries, offset, block_rows, 0)
        grad_block = lax.dynamic_slice_in_dim(grad_mixed, offset, block_rows, 0)
        scores = block_scores(query_block, key_rows, offset, piece_ids, slopes)
        probs = jnp.exp(scores - log_total[block_index][..., None])
        soft_weights = probs.astype(jnp.bfloat16)
        value_grad = value_grad + jnp.einsum(
            "hqk,qhe->khe", soft_weights, grad_block, preferred_element_type=jnp.float32
        )
        prob_grad = jnp.einsum(
            "qhe,khe->hqk", grad_block, value_rows, preferred_element_type=jnp.float32
        )
        centred = jnp.sum(probs * prob_grad, axis=-1, keepdims=True)
        score_grad = (probs * (prob_grad - centred) * HD ** (-0.5)).astype(jnp.bfloat16)
        query_grad = jnp.einsum(
            "hqk,khe->qhe", score_grad, key_rows, preferred_element_type=jnp.float32
        )
        key_grad = key_grad + jnp.einsum(
            "hqk,qhe->khe", score_grad, query_block, preferred_element_type=jnp.float32
        )
        return ((key_grad, value_grad), query_grad)

    empty = jnp.zeros(queries.shape, jnp.float32)
    (key_grad, value_grad), query_grad = lax.scan(
        one_block, (empty, empty), jnp.arange(length // block_rows, dtype=jnp.int32)
    )
    return (query_grad.reshape(queries.shape), key_grad, value_grad)


def attend_forward(triple, piece_ids, slopes):
    width = triple.shape[2]
    count_seq = piece_ids.shape[0]
    length = piece_ids.shape[1]
    shaped = triple.reshape(3, count_seq, length, width // HD, HD)
    attended, log_total = lax.map(
        lambda operands: sequence_forward(operands, slopes),
        (shaped[0], shaped[1], shaped[2], piece_ids),
    )
    return (attended.reshape(count_seq * length, width), log_total)


def attend_backward(triple, grad_attended, log_total, piece_ids, slopes):
    width = triple.shape[2]
    count_seq = piece_ids.shape[0]
    length = piece_ids.shape[1]
    shaped = triple.reshape(3, count_seq, length, width // HD, HD)
    grad_shaped = grad_attended.reshape(count_seq, length, width // HD, HD)
    query_grad, key_grad, value_grad = lax.map(
        lambda operands: sequence_backward(operands, slopes),
        (shaped[0], shaped[1], shaped[2], piece_ids, grad_shaped, log_total),
    )
    return (
        query_grad.reshape(-1, width),
        key_grad.reshape(-1, width),
        value_grad.reshape(-1, width),
    )


def fetch_layer(
    project_weight,
    project_bias,
    output_weight,
    expand_weight,
    expand_bias,
    reduce_weight,
    small_stack,
    layer_index,
):
    return (
        lax.all_gather(project_weight[layer_index], "dp", axis=1, tiled=True),
        lax.all_gather(project_bias[layer_index], "dp", axis=1, tiled=True),
        lax.all_gather(output_weight[layer_index], "dp", axis=1, tiled=True),
        lax.all_gather(expand_weight[layer_index], "dp", axis=0, tiled=True),
        lax.all_gather(expand_bias[layer_index], "dp", axis=0, tiled=True),
        lax.all_gather(reduce_weight[layer_index], "dp", axis=1, tiled=True),
        lax.all_gather(small_stack[layer_index], "dp", axis=1, tiled=True),
    )


def forward_layer(resid, weights, piece_ids, slopes):
    w_project, bias_project, w_output, w_expand, bias_expand, w_reduce, small = weights
    vectors = small.astype(jnp.float32)
    normed = layer_norm(resid, vectors[0], vectors[1])
    gathered = gather_rows(normed.astype(jnp.bfloat16))
    product = jnp.einsum("gd,cde->cge", gathered, w_project, preferred_element_type=jnp.float32)
    biases = jnp.stack([bias_project[0], jnp.zeros_like(bias_project[0]), bias_project[1]]).astype(
        jnp.float32
    )
    triple = (product + biases[:, None, :]).astype(jnp.bfloat16)
    attended, log_total = attend_forward(triple, piece_ids, slopes)
    resid_mid = resid + (scatter_rows(attended, w_output) + vectors[2])
    normed_two = layer_norm(resid_mid, vectors[3], vectors[4])
    gathered_two = gather_rows(normed_two.astype(jnp.bfloat16))
    hidden = jnp.dot(
        gathered_two, w_expand, preferred_element_type=jnp.float32
    ) + bias_expand.astype(jnp.float32)
    active = gelu_tanh(hidden).astype(jnp.bfloat16)
    mlp_sum = scatter_rows(active, w_reduce)
    mlp_keep = (gathered_two, hidden, None)
    resid_out = resid_mid + (mlp_sum + vectors[5])
    return (resid_out, (gathered, triple, attended, log_total, resid_mid, mlp_keep))


def backward_layer(grad_out, resid, weights, kept, piece_ids, slopes):
    w_project, bias_project, w_output, w_expand, bias_expand, w_reduce, small = weights
    vectors = small.astype(jnp.float32)
    gathered, triple, attended, log_total, resid_mid, mlp_keep = kept
    rows_here = grad_out.shape[0]
    rows_in, hidden, full_weights = mlp_keep
    grad_bias_reduce = jnp.sum(grad_out, axis=0)
    active, gelu_pull = jax.vjp(gelu_tanh, hidden)
    active_low = active.astype(jnp.bfloat16)
    grad_mlp = gather_grads(grad_out.astype(jnp.bfloat16))
    grad_reduce = jnp.einsum("gf,gd->fd", active_low, grad_mlp, preferred_element_type=jnp.float32)
    grad_active = jnp.einsum("gd,fd->gf", grad_mlp, w_reduce, preferred_element_type=jnp.float32)
    (grad_hidden,) = gelu_pull(grad_active)
    grad_bias_expand = jnp.sum(grad_hidden, axis=0)
    grad_hidden_low = grad_hidden.astype(jnp.bfloat16)
    grad_expand = jnp.einsum(
        "gd,gf->df", rows_in, grad_hidden_low, preferred_element_type=jnp.float32
    )

    def expand_term(offset, count_rows):
        return jnp.einsum(
            "gf,df->gd", grad_hidden_low, w_expand, preferred_element_type=jnp.float32
        )

    grad_normed_two = scatter_back(expand_term, rows_here)
    unused_two, second_pull = jax.vjp(layer_norm, resid_mid, vectors[3], vectors[4])
    grad_from_norm, grad_gain_two, grad_shift_two = second_pull(grad_normed_two)
    grad_mid = grad_out + grad_from_norm
    grad_bias_output = jnp.sum(grad_mid, axis=0)
    grad_attn = gather_grads(grad_mid.astype(jnp.bfloat16))
    grad_output = jnp.einsum("gt,gd->td", attended, grad_attn, preferred_element_type=jnp.float32)
    grad_attended = jnp.einsum(
        "gd,td->gt", grad_attn, w_output, preferred_element_type=jnp.float32
    ).astype(jnp.bfloat16)
    query_grad, key_grad, value_grad = attend_backward(
        triple, grad_attended, log_total, piece_ids, slopes
    )
    grad_bias_project = jnp.stack([jnp.sum(query_grad, axis=0), jnp.sum(value_grad, axis=0)])
    grad_triple = jnp.stack([query_grad, key_grad, value_grad]).astype(jnp.bfloat16)
    grad_project = jnp.einsum(
        "gd,cge->cde", gathered, grad_triple, preferred_element_type=jnp.float32
    )

    def project_term(offset, count_rows):
        return jnp.einsum("cge,cde->gd", grad_triple, w_project, preferred_element_type=jnp.float32)

    grad_normed = scatter_back(project_term, rows_here)
    unused_one, first_pull = jax.vjp(layer_norm, resid, vectors[0], vectors[1])
    grad_from_first, grad_gain_one, grad_shift_one = first_pull(grad_normed)
    grad_stream = grad_mid + grad_from_first
    small_grads = jnp.stack(
        [
            grad_gain_one,
            grad_shift_one,
            grad_bias_output,
            grad_gain_two,
            grad_shift_two,
            grad_bias_reduce,
        ]
    )
    return (
        grad_stream,
        (
            grad_project,
            grad_bias_project,
            grad_output,
            grad_expand,
            grad_bias_expand,
            grad_reduce,
            small_grads,
        ),
    )


def reduce_layer(layer_grads):
    (
        grad_project,
        grad_bias_project,
        grad_output,
        grad_expand,
        grad_bias_expand,
        grad_reduce,
        small_grads,
    ) = layer_grads
    return (
        lax.psum_scatter(
            grad_project.astype(jnp.bfloat16), "dp", scatter_dimension=1, tiled=True
        ).astype(jnp.float32),
        lax.psum_scatter(
            grad_bias_project.astype(jnp.bfloat16), "dp", scatter_dimension=1, tiled=True
        ).astype(jnp.float32),
        lax.psum_scatter(
            grad_output.astype(jnp.bfloat16), "dp", scatter_dimension=1, tiled=True
        ).astype(jnp.float32),
        lax.psum_scatter(
            grad_expand.astype(jnp.bfloat16), "dp", scatter_dimension=0, tiled=True
        ).astype(jnp.float32),
        lax.psum_scatter(
            grad_bias_expand.astype(jnp.bfloat16), "dp", scatter_dimension=0, tiled=True
        ).astype(jnp.float32),
        lax.psum_scatter(
            grad_reduce.astype(jnp.bfloat16), "dp", scatter_dimension=1, tiled=True
        ).astype(jnp.float32),
        lax.psum_scatter(
            small_grads.astype(jnp.bfloat16), "dp", scatter_dimension=1, tiled=True
        ).astype(jnp.float32),
    )


def on_device(
    layer_input,
    first_gain,
    first_shift,
    project_weight,
    project_bias,
    output_weight,
    output_bias,
    second_gain,
    second_shift,
    expand_weight,
    expand_bias,
    reduce_weight,
    reduce_bias,
    picture_start,
    cotangent,
):
    small_stack = jnp.stack(
        [first_gain, first_shift, output_bias, second_gain, second_shift, reduce_bias], axis=1
    )
    piece_ids = jax.vmap(piece_numbers)(picture_start)
    heads_here = project_weight.shape[3] // HD
    slopes = head_slopes(lax.axis_index("tensor") * heads_here, heads_here)
    resid = layer_input.astype(jnp.float32)
    saved = []
    for layer_index in range(LAYERS):
        weights = fetch_layer(
            project_weight,
            project_bias,
            output_weight,
            expand_weight,
            expand_bias,
            reduce_weight,
            small_stack,
            layer_index,
        )
        resid_next, kept = forward_layer(resid, weights, piece_ids, slopes)
        saved.append((resid, weights, kept))
        resid = resid_next
    layer_output = resid.astype(jnp.bfloat16)
    grad_stream = cotangent.astype(jnp.float32)
    collected = []
    for layer_index in reversed(range(LAYERS)):
        resid_in, weights, kept = saved[layer_index]
        grad_stream, layer_grads = backward_layer(
            grad_stream, resid_in, weights, kept, piece_ids, slopes
        )
        layer_grads = reduce_layer(layer_grads)
        collected.insert(0, layer_grads)
    stacked = tuple(
        (jnp.stack([grad_entry[member] for grad_entry in collected]) for member in range(7))
    )
    (
        grad_project,
        grad_bias_project,
        grad_output,
        grad_expand,
        grad_bias_expand,
        grad_reduce,
        small_grads,
    ) = stacked
    small_grads = lax.psum(small_grads, "tensor")
    return (
        layer_output,
        grad_stream.astype(jnp.bfloat16),
        small_grads[:, 0],
        small_grads[:, 1],
        grad_project,
        grad_bias_project,
        grad_output,
        small_grads[:, 2],
        small_grads[:, 3],
        small_grads[:, 4],
        grad_expand,
        grad_bias_expand,
        grad_reduce,
        small_grads[:, 5],
    )


Z0, Z1, CORE, XBIT, YBIT = 1, 2, 4, 8, 16
AXES = ("dp", "tensor")
NEG = -1e30
BF = jnp.bfloat16
F32 = jnp.float32
VMEM_LIMIT = 24 * 1024 * 1024


def took(us):
    return pl.CostEstimate(flops=int(us * 5e8), bytes_accessed=1, transcendentals=0)


def mesh_is_paired(mesh):
    return dict(mesh.shape) == {"dp": 8, "tensor": 4}


def swap(values, mask):
    return lax.ppermute(values, AXES, [(i, i ^ mask) for i in range(32)])


def swap_some(values, masks):
    pairs = [(i, i ^ masks[(i >> 2) & 1]) for i in range(32)]
    return lax.ppermute(values, AXES, [pair for pair in pairs if pair[0] != pair[1]])


def redeal(values):
    def target(i):
        core, z1 = (i >> 2) & 1, (i >> 1) & 1
        return (i & ~6) | (z1 << 2) | (core << 1)

    return lax.ppermute(values, AXES, [(i, target(i)) for i in range(32) if target(i) != i])


CHIPS = [[0, 2, 4, 6], [1, 3, 5, 7]]


def plane_gather(values):
    return lax.all_gather(values, "dp", axis_index_groups=CHIPS, axis=0, tiled=False)


def plane_scatter(values):
    return lax.psum_scatter(values, "dp", axis_index_groups=CHIPS, scatter_dimension=0, tiled=False)


def turn_index(values, own):
    shape = values.shape
    for bit in range(3):
        values = values.reshape(8 >> (bit + 1), 2, (1 << bit), *shape[1:])
        values = jnp.where((own >> bit) & 1, jnp.concatenate([values[:, 1:], values[:, :1]], axis=1), values)
    return values.reshape(shape)


def after(values, *others):
    return lax.optimization_barrier((values, *others))[0]


def after_all(values, *others):
    if not others:
        return tuple(values)
    return lax.optimization_barrier((*values, *others))[:len(values)]


def task(steps):
    next(steps)
    return steps


def advance(token, *tasks):
    made = []
    for steps in tasks:
        try:
            made += steps.send(token)
        except StopIteration:
            pass
    return made


def dot_nt(a, b):
    return lax.dot_general(a, b, (((1,), (1,)), ((), ())), preferred_element_type=F32)


def dot_nn(a, b):
    return lax.dot_general(a, b, (((1,), (0,)), ((), ())), preferred_element_type=F32)


def head_mask(shape, head):
    lane = lax.broadcasted_iota(jnp.int32, shape, 1)
    return (lane < HD) if head == 0 else (lane >= HD)


def diagonal_bias(rows, columns, first_row, first_column, start):
    key = first_row + lax.broadcasted_iota(jnp.int32, (rows, 1), 0)
    query = first_column + lax.broadcasted_iota(jnp.int32, (1, columns), 1)
    key_in = (key >= start) & (key < start + PIECE)
    query_in = (query >= start) & (query < start + PIECE)
    allowed = (key <= query) | (key_in & query_in)
    reach = (jnp.minimum(key, 2 * query - key) - first_column).astype(F32)
    return jnp.where(allowed, reach, NEG)


def ramp(rows, first_row, first_column):
    return (first_row - first_column + lax.broadcasted_iota(jnp.int32, (rows, 1), 0)).astype(F32)


def attend_kernel(block, rest_bit, slope_ref, start_ref, me_ref, *rest):
    triple_refs, rest = rest[:12], rest[12:]
    near_ref, away_ref, exact_ref, lse_ref, q_ref, k_ref, v_ref, vt_ref, acc_ref, max_ref, bias_ref, tail_ref = rest
    pair = pl.program_id(0)
    turn = pl.program_id(1)
    me = me_ref[0]
    step = (2 * turn + rest_bit) ^ me
    length = k_ref.shape[0]
    first = step * block

    def at(index):
        return pl.multiple_of((index ^ me) * block, block)

    start = start_ref[first // (length // start_ref.shape[0])]

    @pl.when(turn == 0)
    def _():
        for index in range(4):
            here = slice(index * block, (index + 1) * block)
            q_ref[here, :] = triple_refs[3 * index][...] * jnp.asarray(HD ** -0.5, BF)
            k_ref[here, :] = triple_refs[3 * index + 1][...]
            v_ref[here, :] = triple_refs[3 * index + 2][...]
        for head in range(2):
            mixed = jnp.where(head_mask((length, 2 * HD), head), v_ref[...], jnp.ones((), BF))
            vt_ref[head] = mixed.T

    bias_ref[...] = diagonal_bias(block, block, first, first, start)
    q_block = q_ref[pl.ds(at(step), block), :]
    heads = [jnp.where(head_mask(q_block.shape, head), q_block, jnp.zeros((), BF)) for head in range(2)]
    slopes = [slope_ref[2 * pair + head] for head in range(2)]
    acc_ref[...] = jnp.zeros_like(acc_ref)
    max_ref[...] = jnp.full_like(max_ref, NEG)

    def absorb(head, scores, vt):
        old = max_ref[head]
        new = jnp.maximum(old, jnp.max(scores, axis=0, keepdims=True))
        weights = jnp.exp(scores - new).astype(BF)
        acc_ref[head] = acc_ref[head] * jnp.exp(old - new) + dot_nn(vt, weights)
        max_ref[head] = new

    def absorb_both(both, place, rows):
        olds = [max_ref[head] for head in range(2)]
        news = [jnp.maximum(olds[head], jnp.max(both[head], axis=0, keepdims=True)) for head in range(2)]
        weights = [jnp.exp(both[head] - news[head]).astype(BF) for head in range(2)]
        terms = [dot_nn(vt_ref[head, :, pl.ds(place, rows)], weights[head]) for head in range(2)]
        for head in range(2):
            acc_ref[head] = acc_ref[head] * jnp.exp(olds[head] - news[head]) + terms[head]
            max_ref[head] = news[head]

    def full(index, carry):
        place = at(index)
        keys = k_ref[pl.ds(place, block), :]
        slant = ramp(block, index * block, first)
        both = [dot_nt(keys, heads[head]) + slopes[head] * slant for head in range(2)]
        absorb_both(both, place, block)
        return carry

    place = at(step)
    keys = k_ref[pl.ds(place, block), :]
    absorb_both([dot_nt(keys, heads[head]) + slopes[head] * bias_ref[...] for head in range(2)], place, block)
    lax.fori_loop(0, step, full, 0)
    edge = first + block

    @pl.when((start < edge) & (start + PIECE > edge))
    def _():
        after = at(step + 1)
        tail_ref[...] = diagonal_bias(PIECE, block, edge, first, start)
        for head in range(2):
            absorb(
                head,
                dot_nt(k_ref[pl.ds(after, PIECE), :], heads[head]) + slopes[head] * tail_ref[...],
                vt_ref[head, :, pl.ds(after, PIECE)],
            )

    outs = []
    for head in range(2):
        acc = acc_ref[head]
        total = acc[HD:HD + 1] if head == 0 else acc[0:1]
        outs.append((acc * (1.0 / total))[head * HD:(head + 1) * HD])
        lse_ref[0, head:head + 1, :] = max_ref[head] + jnp.log(total)
    mixed = jnp.concatenate(outs, axis=0)
    exact_ref[...] = mixed
    final = mixed.T.astype(BF)

    @pl.when(turn == 0)
    def _():
        near_ref[...] = final

    @pl.when(turn == 1)
    def _():
        away_ref[...] = final


def triple_specs(block, pairs):
    specs = []
    for index in range(4):
        for part in range(3):
            specs.append(pl.BlockSpec((block, 2 * HD), functools.partial(lambda part, p, i: (0, part * pairs + p), part)))
    return specs


def attend(blocks, rest_bit, slopes, starts, me):
    block, width = blocks[0].shape[0], blocks[0].shape[1] // 3
    pairs = width // (2 * HD)
    length = 4 * block
    smem = pl.BlockSpec(memory_space=pltpu.SMEM)
    return pl.pallas_call(
        functools.partial(attend_kernel, block, rest_bit),
        grid=(pairs, 2),
        in_specs=[smem, smem, smem] + triple_specs(block, pairs),
        out_specs=[
            pl.BlockSpec((block, 2 * HD), lambda p, i: (0, p)),
            pl.BlockSpec((block, 2 * HD), lambda p, i: (0, p)),
            pl.BlockSpec((2 * HD, block), lambda p, i: (p, i)),
            pl.BlockSpec((1, 8, block), lambda p, i: (p, 0, i)),
        ],
        out_shape=[
            jax.ShapeDtypeStruct((block, width), BF),
            jax.ShapeDtypeStruct((block, width), BF),
            jax.ShapeDtypeStruct((width, 2 * block), F32),
            jax.ShapeDtypeStruct((pairs, 8, 2 * block), F32),
        ],
        scratch_shapes=[
            pltpu.VMEM((length, 2 * HD), BF),
            pltpu.VMEM((length, 2 * HD), BF),
            pltpu.VMEM((length, 2 * HD), BF),
            pltpu.VMEM((2, 2 * HD, length), BF),
            pltpu.VMEM((2, 2 * HD, block), F32),
            pltpu.VMEM((2, 1, block), F32),
            pltpu.VMEM((block, block), F32),
            pltpu.VMEM((PIECE, block), F32),
        ],
        compiler_params=pltpu.CompilerParams(vmem_limit_bytes=VMEM_LIMIT),
        cost_estimate=took(17),
        name="attend",
    )(slopes, starts, me, *[b for b in blocks for _ in range(3)])


def pull_kernel(block, pair, slope_ref, start_ref, me_ref, *rest):
    triple_refs, grad_refs, rest = rest[:12], rest[12:16], rest[16:]
    exact_refs, lse_refs, rest = rest[0:2], rest[2:4], rest[4:]
    mine_ref, away_ref, q_ref, k_ref, v_ref, g_ref, kt_ref, dk_acc, dv_acc, dqt_ref, bias_ref, tail_ref = rest
    turn = pl.program_id(0)
    me = me_ref[0]
    step = turn ^ me
    length = k_ref.shape[0]
    first = step * block
    half, bit = turn // 2, turn % 2

    def at(index):
        return pl.multiple_of((index ^ me) * block, block)

    start = start_ref[first // (length // start_ref.shape[0])]

    @pl.when(turn == 0)
    def _():
        for index in range(4):
            here = slice(index * block, (index + 1) * block)
            q_ref[here, :] = triple_refs[3 * index][...] * jnp.asarray(HD ** -0.5, BF)
            k_ref[here, :] = triple_refs[3 * index + 1][...]
            v_ref[here, :] = triple_refs[3 * index + 2][...]
            g_ref[here, :] = grad_refs[index][...]
        kt_ref[...] = k_ref[...].T
        dk_acc[...] = jnp.zeros_like(dk_acc)
        dv_acc[...] = jnp.zeros_like(dv_acc)

    bias_ref[...] = diagonal_bias(block, block, first, first, start)
    dqt_ref[...] = jnp.zeros_like(dqt_ref)
    zero = jnp.zeros((), BF)
    q_block = q_ref[pl.ds(at(step), block), :]
    g_block = g_ref[pl.ds(at(step), block), :]
    masks = [head_mask(q_block.shape, head) for head in range(2)]
    q_heads = [jnp.where(mask, q_block, zero) for mask in masks]
    g_heads = [jnp.where(mask, g_block, zero) for mask in masks]
    slopes = [slope_ref[2 * pair + head] for head in range(2)]
    lanes = pl.ds(pl.multiple_of(half * block, block), block)
    exact = jnp.where(bit == 0, exact_refs[0][:, lanes], exact_refs[1][:, lanes])
    log_total = jnp.where(bit == 0, lse_refs[0][0, :, lanes], lse_refs[1][0, :, lanes])
    product = g_block.astype(F32).T * exact
    deltas = [jnp.sum(product[head * HD:(head + 1) * HD], axis=0, keepdims=True) for head in range(2)]

    def absorb(place, rows, bias_of):
        keys = k_ref[pl.ds(place, rows), :]
        values = v_ref[pl.ds(place, rows), :]
        dk = dk_acc[pl.ds(place, rows), :]
        dv = dv_acc[pl.ds(place, rows), :]
        scores = [dot_nt(keys, q_heads[head]) + slopes[head] * bias_of for head in range(2)]
        grad_p = [dot_nt(values, g_heads[head]) for head in range(2)]
        weights = [jnp.exp(scores[head] - log_total[head:head + 1, :]) for head in range(2)]
        grad_s = [(weights[head] * (grad_p[head] - deltas[head])).astype(BF) for head in range(2)]
        dv = dv + dot_nn(
            jnp.concatenate([weights[head].astype(BF) for head in range(2)], axis=1), jnp.concatenate(g_heads, axis=0)
        )
        dk = dk + dot_nn(jnp.concatenate(grad_s, axis=1), jnp.concatenate(q_heads, axis=0))
        for head in range(2):
            dqt_ref[head * HD:(head + 1) * HD, :] += dot_nn(
                kt_ref[head * HD:(head + 1) * HD, pl.ds(place, rows)], grad_s[head]
            )
        dk_acc[pl.ds(place, rows), :] = dk
        dv_acc[pl.ds(place, rows), :] = dv

    absorb(at(step), block, bias_ref[...])

    def full(index, carry):
        absorb(at(index), block, ramp(block, index * block, first))
        return carry

    lax.fori_loop(0, step, full, 0)
    edge = first + block

    @pl.when((start < edge) & (start + PIECE > edge))
    def _():
        tail_ref[...] = diagonal_bias(PIECE, block, edge, first, start)
        absorb(at(step + 1), PIECE, tail_ref[...])

    grad_q = (dqt_ref[...].T * (HD ** -0.5)).astype(BF)
    here = pl.ds(pl.multiple_of(bit * block, block), block)

    @pl.when(half == 0)
    def _():
        mine_ref[0, here, :] = grad_q

    @pl.when(half == 1)
    def _():
        away_ref[0, here, :] = grad_q

    @pl.when(turn == 3)
    def _():
        for part, ref in ((1, dk_acc), (2, dv_acc)):
            mine_ref[part] = ref[:2 * block].astype(BF)
            away_ref[part] = ref[2 * block:].astype(BF)


def attend_pull(pair, blocks, grads, exacts, log_totals, slopes, starts, me):
    block, width = blocks[0].shape[0], blocks[0].shape[1] // 3
    pairs = width // (2 * HD)
    length = 4 * block
    smem = pl.BlockSpec(memory_space=pltpu.SMEM)
    triples = [pl.BlockSpec((block, 2 * HD), functools.partial(lambda part, i: (0, part * pairs + pair), part)) for part in range(3)]
    rows = pl.BlockSpec((block, 2 * HD), lambda i: (0, pair))
    wide = pl.BlockSpec((2 * HD, 2 * block), lambda i: (pair, 0))
    sums = pl.BlockSpec((1, 8, 2 * block), lambda i: (pair, 0, 0))
    out = pl.BlockSpec((3, 2 * block, 2 * HD), lambda i: (0, 0, 0))
    return pl.pallas_call(
        functools.partial(pull_kernel, block, pair),
        grid=(4,),
        in_specs=[smem, smem, smem] + triples * 4 + [rows] * 4 + [wide] * 2 + [sums] * 2,
        out_specs=[out, out],
        out_shape=[jax.ShapeDtypeStruct((3, 2 * block, 2 * HD), BF)] * 2,
        scratch_shapes=[
            pltpu.VMEM((length, 2 * HD), BF),
            pltpu.VMEM((length, 2 * HD), BF),
            pltpu.VMEM((length, 2 * HD), BF),
            pltpu.VMEM((length, 2 * HD), BF),
            pltpu.VMEM((2 * HD, length), BF),
            pltpu.VMEM((length, 2 * HD), F32),
            pltpu.VMEM((length, 2 * HD), F32),
            pltpu.VMEM((2 * HD, block), F32),
            pltpu.VMEM((block, block), F32),
            pltpu.VMEM((PIECE, block), F32),
        ],
        compiler_params=pltpu.CompilerParams(vmem_limit_bytes=VMEM_LIMIT),
        cost_estimate=took(22),
        name="attend_pull",
    )(slopes, starts, me, *[b for b in blocks for _ in range(3)], *grads, *exacts, *log_totals)


def head_columns(refs, quarter, first, last):
    return jnp.concatenate(
        [refs[odd][chip ^ refs[2][0], 1 - quarter if odd else quarter, :, first:last] for chip in range(4) for odd in range(2)],
        axis=0,
    )


def placed(arrays):
    return [
        pl.BlockSpec(memory_space=pltpu.SMEM if a.dtype == jnp.int32 else pltpu.VMEM) for a in arrays
    ]


def call_once(kernel, name, outs, args, us):
    return pl.pallas_call(
        kernel,
        in_specs=placed(args),
        out_specs=placed(outs),
        out_shape=outs,
        compiler_params=pltpu.CompilerParams(vmem_limit_bytes=VMEM_LIMIT),
        cost_estimate=took(us),
        name=name,
    )(*args)


def project_kernel(rows_ref, bias_ref, *rest):
    weight_refs, out_refs = rest[:3], rest[3:]
    rows = rows_ref[...]
    for quarter in (1, 0):
        out = dot_nn(rows, head_columns(weight_refs, quarter, 0, 768)) + bias_ref[quarter:quarter + 1]
        out_refs[quarter][...] = out.astype(BF)


def project(rows, bias, pieces):
    out = jax.ShapeDtypeStruct((rows.shape[0], 768), BF)
    return call_once(project_kernel, "project", [out, out], [rows, bias, *pieces], 5)


def mix_term(mixed_refs, weight_refs):
    rows = jnp.concatenate([ref[...] for ref in mixed_refs], axis=1)
    weight = jnp.concatenate([head_columns(weight_refs, quarter, 768, 1024) for quarter in range(2)], axis=1)
    return dot_nt(rows, weight)


def mix_far_kernel(mine_ref, other_ref, *rest):
    rest[3][...] = mix_term((mine_ref, other_ref), rest[:3]).astype(BF)


def mix_far(mine, other, pieces):
    out = jax.ShapeDtypeStruct((mine.shape[0], 1024), BF)
    return call_once(mix_far_kernel, "mix_far", [out], [mine, other, *pieces], 4)[0]


def mix_near_kernel(mine_ref, other_ref, far_ref, resid_ref, vector_ref, *rest):
    weight_refs, (mid_ref, normed_ref, flip_ref) = rest[:3], rest[3:]
    term = mix_term((mine_ref, other_ref), weight_refs)
    mid = resid_ref[...] + (term + far_ref[...].astype(F32) + vector_ref[2:3])
    mid_ref[...] = mid
    normed = (normalize(mid)[0] * vector_ref[3:4] + vector_ref[4:5]).astype(BF)
    normed_ref[...] = normed
    flip_ref[...] = flipped(normed)


def mix_near(mine, other, far, resid, vectors, pieces):
    outs = [
        jax.ShapeDtypeStruct(resid.shape, F32),
        jax.ShapeDtypeStruct(resid.shape, BF),
        jax.ShapeDtypeStruct(resid.shape, BF),
    ]
    return call_once(mix_near_kernel, "mix_near", outs, [mine, other, far, resid, vectors, *pieces], 6)


def unmix_kernel(grad_ref, *rest):
    weight_refs, out_refs = rest[:3], rest[3:]
    grad = grad_ref[...]
    for quarter in (1, 0):
        out_refs[quarter][...] = dot_nn(grad, head_columns(weight_refs, quarter, 768, 1024)).astype(BF)


def unmix(grad, pieces):
    out = jax.ShapeDtypeStruct((grad.shape[0], 256), BF)
    return call_once(unmix_kernel, "unmix", [out, out], [grad, *pieces], 4)


def unproject_term(grad_refs, weight_refs, first):
    rows = jnp.concatenate(
        [ref[part, first:first + 512] for pair in grad_refs for part in range(3) for ref in pair], axis=1
    )
    weight = jnp.concatenate([head_columns(weight_refs, quarter, 0, 768) for quarter in range(2)], axis=1)
    return dot_nt(rows, weight)


def unproject_far_kernel(*rest):
    rest[7][...] = unproject_term((rest[0:2], rest[2:4]), rest[4:7], 512).astype(BF)


def unproject_far(mine, other, pieces):
    out = jax.ShapeDtypeStruct((512, 1024), BF)
    return call_once(unproject_far_kernel, "unproject_far", [out], [*mine, *other, *pieces], 6)[0]


def unproject_near_kernel(last, own_ref, *rest):
    mine, other, rest = rest[0:2], rest[2:4], rest[4:]
    far_ref, resid_ref, grad_mid_ref, vector_ref, rest = *rest[:4], rest[4:]
    weight_refs, (grad_ref, low_ref, sums_ref) = rest[:3], rest[3:]
    term = unproject_term((mine, other), weight_refs, 0) + far_ref[...].astype(F32)
    grad_norm, grad_gain, grad_shift = norm_pull(resid_ref[...], vector_ref[0:1], term)
    grad = grad_mid_ref[...] + grad_norm
    grad_ref[...] = grad
    if last:
        put_turned(low_ref, own_ref[0], grad.astype(BF))
    else:
        low_ref[...] = flipped(grad).astype(BF)
    sums_ref[...] = jnp.concatenate([grad_gain, grad_shift, jnp.zeros((6, grad.shape[1]), F32)], axis=0)


def unproject_near(last, own_keep, mine, other, far, resid, grad_mid, vectors, pieces):
    outs = [
        jax.ShapeDtypeStruct(resid.shape, F32),
        jax.ShapeDtypeStruct(resid.shape, BF),
        jax.ShapeDtypeStruct((8, resid.shape[1]), F32),
    ]
    args = [own_keep, *mine, *other, far, resid, grad_mid, vectors, *pieces]
    kernel = functools.partial(unproject_near_kernel, last)
    return call_once(kernel, "unproject_near", outs, args, 9)


def head_grads_kernel(turn_ref, near_ref, far_ref, grad_near_ref, grad_far_ref, *rest):
    pairs, rest = (rest[0:2], rest[2:4]), rest[4:]
    mixed_refs, out_refs, bias_ref = (rest[0:2], rest[2:4]), rest[4:6], rest[6]
    rows_t = jnp.concatenate([near_ref[...], far_ref[...]], axis=0).T
    grad_t = jnp.concatenate([grad_near_ref[...], grad_far_ref[...]], axis=0).T
    for quarter, refs in enumerate(pairs):
        grads = [jnp.concatenate([ref[part] for ref in refs], axis=1) for part in range(3)]
        for part in range(4):
            if part < 3:
                term = dot_nn(rows_t, grads[part])
            else:
                term = dot_nn(grad_t, jnp.concatenate([m[...] for m in mixed_refs[quarter]], axis=0))
            term = term.astype(BF)
            for index in range(8):
                chip, odd = index // 2, index % 2
                place = 1 - quarter if odd else quarter
                out_refs[odd][chip ^ turn_ref[0], place, :, part * 256:(part + 1) * 256] = term[index * 128:(index + 1) * 128]
        for row, part in ((0, 0), (1, 2)):
            total = jnp.sum(grads[part].astype(F32), axis=0, keepdims=True)
            bias_ref[2 * quarter + row:2 * quarter + row + 1, :] = total
    bias_ref[4:8, :] = jnp.zeros((4, 256), F32)


def head_grads(turn, near, far, grad_near, grad_far, mine, other, mixed_mine, mixed_other):
    outs = [jax.ShapeDtypeStruct((4, 2, 128, 1024), BF)] * 2 + [jax.ShapeDtypeStruct((8, 256), F32)]
    args = [turn, near, far, grad_near, grad_far, *mine, *other, *mixed_mine, *mixed_other]
    return call_once(head_grads_kernel, "head_grads", outs, args, 10)


GELU_A = 0.7978845608028654
GELU_B = 0.044715


def normalize(values):
    centred = values - jnp.mean(values, axis=-1, keepdims=True)
    spread = lax.rsqrt(jnp.mean(centred * centred, axis=-1, keepdims=True) + NORM_EPS)
    return centred * spread, spread


def norm_pull(values, gain, grad):
    unit, spread = normalize(values)
    grad_unit = grad * gain
    inner = grad_unit - jnp.mean(grad_unit, axis=-1, keepdims=True)
    inner = inner - unit * jnp.mean(grad_unit * unit, axis=-1, keepdims=True)
    return spread * inner, jnp.sum(grad * unit, axis=0, keepdims=True), jnp.sum(grad, axis=0, keepdims=True)


def flipped(values):
    return jnp.concatenate([values[:, (block ^ 1) * 128:(block ^ 1) * 128 + 128] for block in range(8)], axis=1)


def put_turned(out_ref, own, values):
    for block in range(8):
        here = pl.ds(pl.multiple_of((block ^ own) * 128, 128), 128)
        out_ref[:, here] = values[:, block * 128:(block + 1) * 128]


def enter_kernel(own_ref, direct_ref, moved_ref, vector_ref, resid_ref, normed_ref, flip_ref):
    own, keep = own_ref[0], own_ref[1]
    for block in range(8):
        here = pl.ds(pl.multiple_of((block ^ own) * 128, 128), 128)
        rows = jnp.where(keep > 0, direct_ref[:, here].astype(F32), moved_ref[:, here].astype(F32))
        resid_ref[:, block * 128:(block + 1) * 128] = rows
    values = resid_ref[...]
    normed_ref[...] = (normalize(values)[0] * vector_ref[0:1] + vector_ref[1:2]).astype(BF)
    flip_ref[...] = flipped(values).astype(BF)


def enter(own_keep, direct, moved, vectors):
    rows, features = direct.shape
    smem = pl.BlockSpec(memory_space=pltpu.SMEM)
    vmem = pl.BlockSpec(memory_space=pltpu.VMEM)
    return pl.pallas_call(
        enter_kernel,
        in_specs=[smem, vmem, vmem, vmem],
        out_specs=[vmem, vmem, vmem],
        out_shape=[
            jax.ShapeDtypeStruct((rows, features), F32),
            jax.ShapeDtypeStruct((rows, features), BF),
            jax.ShapeDtypeStruct((rows, features), BF),
        ],
        compiler_params=pltpu.CompilerParams(vmem_limit_bytes=VMEM_LIMIT),
        cost_estimate=took(4),
        name="enter",
    )(own_keep, direct, moved, vectors)


def half_specs(tile, weights):
    def spec(half, chip, whole):
        def index(f, turn):
            column = jnp.clip(f - 2 * half, 0, 1)
            return (chip ^ turn[0], 0, 0, column) if whole else (0, 0, column)

        return pl.BlockSpec((None, 2, 128, 2 * tile) if whole else (2, 128, 2 * tile), index)

    return [spec(half, chip, len(weights[half]) == 1) for half in range(2) for chip in range(4)]


def half_arrays(weights):
    return [array for half in weights for array in (half if len(half) == 4 else half * 4)]


def by_half(step, weight_refs, body):
    @pl.when(step < 2)
    def _():
        body(weight_refs[:4])

    @pl.when(step >= 2)
    def _():
        body(weight_refs[4:])


def joined(refs, first, last):
    return jnp.concatenate([ref[core, :, first:last] for ref in refs for core in range(2)], axis=0)


def mlp_kernel(turn_ref, normed_ref, other_ref, bias_ref, *rest):
    weight_refs, (hidden_ref, active_ref, near_ref, away_ref, acc_ref) = rest[:8], rest[8:]
    rows, tile = normed_ref.shape[0], hidden_ref.shape[1]
    step = pl.program_id(0)

    @pl.when(step == 0)
    def _():
        acc_ref[...] = jnp.zeros_like(acc_ref)

    def body(refs):
        expand, reduce = joined(refs, 0, tile), joined(refs, tile, 2 * tile)
        for first, ref in ((0, normed_ref), (rows, other_ref)):
            hidden = dot_nn(ref[...], expand) + bias_ref[...]
            inner = jnp.tanh(GELU_A * (hidden + GELU_B * hidden * hidden * hidden))
            active = (0.5 * hidden * (1.0 + inner)).astype(BF)
            hidden_ref[first:first + rows] = hidden.astype(BF)
            active_ref[first:first + rows] = active
            acc_ref[first:first + rows] += dot_nt(active, reduce)

    by_half(step, weight_refs, body)

    @pl.when(step == pl.num_programs(0) - 1)
    def _():
        near_ref[...] = acc_ref[:rows]
        away_ref[...] = flipped(acc_ref[rows:]).astype(BF)


def mlp_forward(turn, normed, other, bias, weights):
    rows, features = normed.shape
    units = bias.shape[1]
    tile = 512
    whole = pl.BlockSpec((rows, features), lambda f, turn: (0, 0))
    tiles = pl.BlockSpec((2 * rows, tile), lambda f, turn: (0, f))
    return pl.pallas_call(
        mlp_kernel,
        grid_spec=pltpu.PrefetchScalarGridSpec(
            num_scalar_prefetch=1,
            grid=(units // tile,),
            in_specs=[whole, whole, pl.BlockSpec((1, tile), lambda f, turn: (0, f))] + half_specs(tile, weights),
            out_specs=[tiles, tiles, whole, whole],
            scratch_shapes=[pltpu.VMEM((2 * rows, features), F32)],
        ),
        out_shape=[
            jax.ShapeDtypeStruct((2 * rows, units), BF),
            jax.ShapeDtypeStruct((2 * rows, units), BF),
            jax.ShapeDtypeStruct((rows, features), F32),
            jax.ShapeDtypeStruct((rows, features), BF),
        ],
        compiler_params=pltpu.CompilerParams(vmem_limit_bytes=VMEM_LIMIT),
        cost_estimate=took(18),
        name="mlp_forward",
    )(turn, normed, other, bias, *half_arrays(weights))


def mlp_close_kernel(last, own_ref, near_ref, got_ref, mid_ref, vector_ref, out_ref, next_ref):
    out = mid_ref[...] + (near_ref[...] + got_ref[...].astype(F32) + vector_ref[5:6])
    out_ref[...] = out
    if last:
        put_turned(next_ref, own_ref[0], out.astype(BF))
    else:
        next_ref[...] = (normalize(out)[0] * vector_ref[6:7] + vector_ref[7:8]).astype(BF)


def mlp_close(last, own_keep, near, got, mid, vectors):
    outs = [jax.ShapeDtypeStruct(mid.shape, F32), jax.ShapeDtypeStruct(mid.shape, BF)]
    args = [own_keep, near, got, mid, vectors]
    return call_once(functools.partial(mlp_close_kernel, last), "mlp_close", outs, args, 3)


def mlp_pull_kernel(turn_ref, grad_ref, other_ref, hidden_ref, *rest):
    weight_refs = rest[:8]
    grad_hidden_ref, grad_bias_ref, near_ref, away_ref, acc_ref, low_ref = rest[8:]
    rows, tile = grad_ref.shape[0], hidden_ref.shape[1]
    step = pl.program_id(0)

    @pl.when(step == 0)
    def _():
        low_ref[:rows] = grad_ref[...].astype(BF)
        low_ref[rows:] = other_ref[...]
        acc_ref[...] = jnp.zeros_like(acc_ref)

    def body(refs):
        expand, reduce = joined(refs, 0, tile), joined(refs, tile, 2 * tile)
        total = jnp.zeros((1, tile), F32)
        for first in (0, rows):
            here = slice(first, first + rows)
            hidden = hidden_ref[here].astype(F32)
            squared = hidden * hidden
            inner = jnp.tanh(GELU_A * hidden * (1.0 + GELU_B * squared))
            slope = 0.5 * (1.0 + inner) + 0.5 * hidden * (1.0 - inner * inner) * (GELU_A * (1.0 + 3.0 * GELU_B * squared))
            grad_hidden = dot_nn(low_ref[here], reduce) * slope
            total = total + jnp.sum(grad_hidden, axis=0, keepdims=True)
            grad_hidden = grad_hidden.astype(BF)
            grad_hidden_ref[here] = grad_hidden
            acc_ref[here] += dot_nt(grad_hidden, expand)
        grad_bias_ref[...] = total

    by_half(step, weight_refs, body)

    @pl.when(step == pl.num_programs(0) - 1)
    def _():
        near_ref[...] = acc_ref[:rows]
        away_ref[...] = flipped(acc_ref[rows:]).astype(BF)


def mlp_backward(turn, grad, other, hidden, weights):
    rows, features = grad.shape
    units = hidden.shape[1]
    tile = 512
    whole = pl.BlockSpec((rows, features), lambda f, turn: (0, 0))
    tiles = pl.BlockSpec((2 * rows, tile), lambda f, turn: (0, f))
    return pl.pallas_call(
        mlp_pull_kernel,
        grid_spec=pltpu.PrefetchScalarGridSpec(
            num_scalar_prefetch=1,
            grid=(units // tile,),
            in_specs=[whole, whole, tiles] + half_specs(tile, weights),
            out_specs=[tiles, pl.BlockSpec((1, tile), lambda f, turn: (0, f)), whole, whole],
            scratch_shapes=[pltpu.VMEM((2 * rows, features), F32), pltpu.VMEM((2 * rows, features), BF)],
        ),
        out_shape=[
            jax.ShapeDtypeStruct((2 * rows, units), BF),
            jax.ShapeDtypeStruct((1, units), F32),
            jax.ShapeDtypeStruct((rows, features), F32),
            jax.ShapeDtypeStruct((rows, features), BF),
        ],
        compiler_params=pltpu.CompilerParams(vmem_limit_bytes=VMEM_LIMIT),
        cost_estimate=took(22),
        name="mlp_backward",
    )(turn, grad, other, hidden, *half_arrays(weights))


def mlp_open_kernel(near_ref, got_ref, mid_ref, grad_ref, vector_ref, grad_mid_ref, grad_low_ref, sums_ref):
    grad = grad_ref[...]
    term = near_ref[...] + got_ref[...].astype(F32)
    grad_norm, grad_gain, grad_shift = norm_pull(mid_ref[...], vector_ref[3:4], term)
    grad_mid = grad + grad_norm
    grad_mid_ref[...] = grad_mid
    grad_low_ref[...] = grad_mid.astype(BF)
    rows = [jnp.sum(grad_mid, axis=0, keepdims=True), grad_gain, grad_shift, jnp.sum(grad, axis=0, keepdims=True)]
    sums_ref[...] = jnp.concatenate(rows + [jnp.zeros((4, grad.shape[1]), F32)], axis=0)


def mlp_open(near, got, mid, grad, vectors):
    outs = [
        jax.ShapeDtypeStruct(mid.shape, F32),
        jax.ShapeDtypeStruct(mid.shape, BF),
        jax.ShapeDtypeStruct((8, mid.shape[1]), F32),
    ]
    return call_once(mlp_open_kernel, "mlp_open", outs, [near, got, mid, grad, vectors], 5)


def unit_grads_kernel(second, left_ref, other_ref, right_ref, own_ref, pair_ref, single_ref, left_t_ref):
    @pl.when(pl.program_id(0) == 0)
    def _():
        left_t_ref[...] = jnp.concatenate([left_ref[...].astype(BF), other_ref[...]], axis=0).T

    grad = dot_nn(left_t_ref[...], right_ref[...]).astype(BF)
    single, direct = (1, 2) if second == "x" else (2, 1)
    for core in range(2):
        own_ref[0, core] = grad[core * 128:(core + 1) * 128]
        single_ref[0, core] = grad[(2 * single + core) * 128:(2 * single + core + 1) * 128]
        pair_ref[0, 0, core] = grad[(2 * direct + core) * 128:(2 * direct + core + 1) * 128]
        pair_ref[0, 1, core] = grad[(6 + core) * 128:(7 + core) * 128]


def unit_grads(second, left, other, right):
    rows, features = left.shape
    units = right.shape[1]
    tile = 512
    whole = pl.BlockSpec((rows, features), lambda f: (0, 0))
    out = pl.BlockSpec((1, 2, 128, tile), lambda f: (f // 2, 0, 0, f % 2))
    one = jax.ShapeDtypeStruct((2, 2, 128, 1024), BF)
    return pl.pallas_call(
        functools.partial(unit_grads_kernel, second),
        grid=(units // tile,),
        in_specs=[whole, whole, pl.BlockSpec((2 * rows, tile), lambda f: (0, f))],
        out_specs=[out, pl.BlockSpec((1, 2, 2, 128, tile), lambda f: (f // 2, 0, 0, 0, f % 2)), out],
        out_shape=[one, jax.ShapeDtypeStruct((2, 2, 2, 128, 1024), BF), one],
        scratch_shapes=[pltpu.VMEM((features, 2 * rows), BF)],
        compiler_params=pltpu.CompilerParams(vmem_limit_bytes=VMEM_LIMIT),
        cost_estimate=took(10),
        name="unit_grads",
    )(left, other, right)


def unit_grads_whole_kernel(turn_ref, left_ref, other_ref, right_ref, out_ref, left_t_ref):
    @pl.when(pl.program_id(0) == 0)
    def _():
        left_t_ref[...] = jnp.concatenate([left_ref[...].astype(BF), other_ref[...]], axis=0).T

    grad = dot_nn(left_t_ref[...], right_ref[...]).astype(BF)
    for chip in range(4):
        for core in range(2):
            first = (2 * chip + core) * 128
            out_ref[chip ^ turn_ref[0], 0, core] = grad[first:first + 128]


def unit_grads_whole(turn, left, other, right):
    rows, features = left.shape
    units = right.shape[1]
    tile = 512
    whole = pl.BlockSpec((rows, features), lambda f: (0, 0))
    return pl.pallas_call(
        unit_grads_whole_kernel,
        grid=(units // tile,),
        in_specs=[
            pl.BlockSpec(memory_space=pltpu.SMEM),
            whole,
            whole,
            pl.BlockSpec((2 * rows, tile), lambda f: (0, f)),
        ],
        out_specs=pl.BlockSpec((4, 1, 2, 128, tile), lambda f: (0, f // 2, 0, 0, f % 2)),
        out_shape=jax.ShapeDtypeStruct((4, 2, 2, 128, 1024), BF),
        scratch_shapes=[pltpu.VMEM((features, 2 * rows), BF)],
        compiler_params=pltpu.CompilerParams(vmem_limit_bytes=VMEM_LIMIT),
        cost_estimate=took(10),
        name="unit_grads_whole",
    )(turn, left, other, right)


MESH = pl.DeviceIdType.MESH


def flip(index, bit):
    return index + bit - 2 * bit * ((index // bit) % 2)


def peer(mask):
    dp, tensor = lax.axis_index("dp"), lax.axis_index("tensor")
    for bit in (1, 2):
        tensor = flip(tensor, bit) if mask & bit else tensor
        dp = flip(dp, bit) if mask & (CORE * bit) else dp
    dp = flip(dp, 4) if mask & YBIT else dp
    return {"dp": dp, "tensor": tensor}


def xor_block(block, own):
    return sum(bit * ((block // bit + own // bit) % 2) for bit in (1, 2, 4))


def greet(masks):
    barrier = pltpu.get_barrier_semaphore()
    for mask in masks:
        pl.semaphore_signal(barrier, inc=1, device_id=peer(mask), device_id_type=MESH)
    pl.semaphore_wait(barrier, len(masks))


def project_rows(rows, weight_refs, bias_ref, layer, out_refs):
    for quarter in (1, 0):
        weight = jnp.concatenate(
            [weight_refs[odd][chip, 1 - quarter if odd else quarter, :, 0:768] for chip in range(4) for odd in range(2)],
            axis=0,
        )
        out_refs[quarter][...] = (dot_nn(rows, weight) + bias_ref[layer, quarter:quarter + 1]).astype(BF)


SMALL_ROWS = 11


def start_kernel(layers, x_ref, *rest):
    sources, rest = rest[:13], rest[13:]
    targets, (vector_ref, head_bias_ref, unit_bias_ref, starts_ref), rest = rest[:12], rest[12:16], rest[16:]
    loaded, made, rest = rest[:13], rest[13:25], rest[25:]
    project_ref, output_ref, expand_ref, reduce_ref, *six_refs, bias_ref, unit_row_ref, places_ref = loaded
    (
        resid_ref, normed_ref, far_ref, even_ref, odd_ref, first_ref, heads_ref, pairs_ref,
        near_mine_ref, far_mine_ref, got_near_ref, got_far_ref,
    ) = made
    (
        came_ref, piece_ref, every_ref, near_other_ref, far_other_ref, local_sem, load_sem, store_sem, send_sem, recv_sem,
    ) = rest
    loads = [pltpu.make_async_copy(s, t, load_sem.at[i]) for i, (s, t) in enumerate(zip(sources, loaded))]
    for one in loads:
        one.start()
    stores = {id(s): pltpu.make_async_copy(s, t, store_sem.at[i]) for i, (s, t) in enumerate(zip(made, targets))}

    def store(*refs):
        for ref in refs:
            stores[id(ref)].start()

    own, place = lax.axis_index("dp"), lax.axis_index("tensor")
    core = own % 2
    keep = core == place // 2
    count = [0]

    def copy(source, target, device):
        index = count[0]
        count[0] += 1
        return pltpu.make_async_remote_copy(
            src_ref=source, dst_ref=target, send_sem=send_sem.at[index], recv_sem=recv_sem.at[index],
            device_id=device, device_id_type=MESH,
        )

    greet((1, 2, 4, 6, 8, 16))
    tokens = copy(x_ref, came_ref, peer(CORE | Z1))
    stay = pltpu.make_async_copy(x_ref, came_ref, local_sem)

    @pl.when(keep)
    def _():
        stay.start()

    @pl.when(jnp.logical_not(keep))
    def _():
        tokens.start()

    for one in loads:
        one.wait()

    def pack_heads_into(target, layer):
        for part in range(3):
            target[:, part * 256:(part + 1) * 256] = project_ref[layer, part]
        target[:, 768:1024] = output_ref[layer].T

    def pack_units_into(target, layer):
        for half in range(2):
            here = slice(half * 512, (half + 1) * 512)
            target[:, half * 1024:half * 1024 + 512] = expand_ref[layer, :, here]
            target[:, half * 1024 + 512:half * 1024 + 1024] = reduce_ref[layer, here, :].T

    pack_heads_into(even_ref.at[0, core], 0)
    along = copy(even_ref.at[0, core], even_ref.at[0, 1 - core], peer(Z1))
    along.start()
    every_ref[0, 0] = jnp.zeros(every_ref.shape[2:], F32)
    lane = lax.broadcasted_iota(jnp.int32, (1, 128), 1)
    for layer in range(layers):
        base = layer * SMALL_ROWS
        for row, ref in enumerate(six_refs):
            every_ref[0, 0, base + row:base + row + 1, :] = ref[layer:layer + 1, :].astype(F32)
        for part in range(2):
            ours = jnp.where(lane // 32 == own % 4, bias_ref[layer, part:part + 1, :].astype(F32), 0.0)
            every_ref[0, 0, pl.ds(base + 6 + 2 * part + own // 4, 1), :] = ours
        every_ref[0, 0, base + 10:base + 11, :] = unit_row_ref[layer:layer + 1, :].astype(F32)
    every_ref[0, 0, layers * SMALL_ROWS:layers * SMALL_ROWS + 1, :] = places_ref[...]
    smalls = [
        (copy(every_ref.at[0, pl.ds(0, width)], every_ref.at[0, pl.ds(width, width)], peer(mask)))
        for width, mask in ((1, CORE), (2, XBIT), (4, YBIT))
    ]
    smalls += [
        copy(every_ref.at[pl.ds(0, width)], every_ref.at[pl.ds(width, width)], peer(mask)) for width, mask in ((1, Z0), (2, Z1))
    ]
    smalls[0].start()
    pack_units_into(piece_ref, 0)
    cross = copy(piece_ref, first_ref.at[1], {
        "dp": flip(own, 1), "tensor": place + (1 - core) * (flip(place, 2) - place)
    })
    same = copy(piece_ref, first_ref.at[0], peer(Z1))

    @pl.when(core == 0)
    def _():
        first_ref[0] = piece_ref[...]

    for step in range(1, 5):
        smalls[step - 1].wait()
        smalls[step].start()
    along.wait()
    over_x = copy(even_ref.at[0], even_ref.at[1], peer(XBIT))
    over_y = copy(even_ref.at[0], even_ref.at[2], peer(YBIT))
    over_x.start()
    over_y.start()
    cores = [copy(even_ref.at[chip], odd_ref.at[chip], peer(CORE)) for chip in range(4)]
    cores[0].start()
    smalls[4].wait()
    half = place // 2
    starts_ref[...] = every_ref[0, core + half - 2 * core * half, layers * SMALL_ROWS:layers * SMALL_ROWS + 1, :]
    for layer in range(layers):
        base = layer * SMALL_ROWS
        later = min(layer + 1, layers - 1) * SMALL_ROWS
        rows = [base + row for row in range(6)] + [later, later + 1]
        for row, source in enumerate(rows):
            vector_ref[layer, row:row + 1, :] = jnp.concatenate(
                [every_ref[0, block, source:source + 1, :] for block in range(8)], axis=1
            )
        for quarter in range(2):
            which = 2 * (core + quarter - 2 * core * quarter)
            total = every_ref[which, 0, base + 6:base + 10, :]
            for block in range(1, 8):
                total = total + every_ref[which, block, base + 6:base + 10, :]
            head_bias_ref[layer, quarter:quarter + 1, :] = jnp.concatenate(
                [total[0:1], total[1:2], jnp.zeros((1, 256), F32), total[2:3], total[3:4]], axis=1
            )
            for block in range(8):
                unit_bias_ref[layer, :, quarter * 1024 + block * 128:quarter * 1024 + (block + 1) * 128] = every_ref[
                    2 * core + quarter, xor_block(block, own), base + 10:base + 11, :
                ]
    @pl.when(keep)
    def _():
        stay.wait()

    @pl.when(jnp.logical_not(keep))
    def _():
        tokens.wait()

    for block in range(8):
        here = pl.ds(pl.multiple_of(xor_block(block, own) * 128, 128), 128)
        resid_ref[:, block * 128:(block + 1) * 128] = came_ref[:, here].astype(F32)
    normed = (normalize(resid_ref[...])[0] * vector_ref[0, 0:1] + vector_ref[0, 1:2]).astype(BF)
    normed_ref[...] = normed
    store(resid_ref, normed_ref)
    beside = copy(normed_ref, far_ref, peer(Z0))
    beside.start()
    cross.start()

    @pl.when(core == 1)
    def _():
        same.start()

    ahead = []
    for layer in range(1, layers):
        pack_heads_into(heads_ref.at[layer - 1], layer)
        pack_units_into(pairs_ref.at[layer - 1, 0], layer)
        ahead.append(copy(pairs_ref.at[layer - 1, 0], pairs_ref.at[layer - 1, 1], peer(CORE)))
    for one in ahead:
        one.start()
    over_y.wait()
    over_x.wait()
    across = copy(even_ref.at[2], even_ref.at[3], peer(XBIT))
    across.start()
    cores[1].start()
    cores[2].start()
    across.wait()
    cores[3].start()
    for one in cores:
        one.wait()
    store(even_ref, odd_ref)
    weights = (even_ref, odd_ref)
    project_rows(normed_ref[...], weights, head_bias_ref, 0, (near_mine_ref, near_other_ref))
    back_near = copy(near_other_ref, got_near_ref, peer(CORE))
    back_near.start()
    store(near_mine_ref)
    beside.wait()
    project_rows(far_ref[...], weights, head_bias_ref, 0, (far_mine_ref, far_other_ref))
    back_far = copy(far_other_ref, got_far_ref, peer(CORE))
    back_far.start()
    store(far_ref, far_mine_ref)
    for one in ahead:
        one.wait()
    store(heads_ref, pairs_ref)
    back_near.wait()
    store(got_near_ref)
    cross.wait()

    @pl.when(core == 1)
    def _():
        same.wait()

    store(first_ref)
    back_far.wait()
    store(got_far_ref)
    for one in stores.values():
        one.wait()


def start(x, project_weight, output_weight, expand_weight, reduce_weight, six, project_bias, expand_bias, places):
    rows, features = x.shape
    layers = expand_bias.shape[0]
    small = 8 * (-(-(SMALL_ROWS * layers + 1) // 8))
    project_bias = jnp.tile(project_bias, (1, 1, 4))
    places = jnp.pad(places.astype(F32), ((0, 0), (0, 128 - places.shape[1])))
    args = [project_weight, output_weight, expand_weight, reduce_weight, *six, project_bias, expand_bias, places]
    vmem, hbm = pl.BlockSpec(memory_space=pltpu.VMEM), pl.BlockSpec(memory_space=pltpu.HBM)
    triple = jax.ShapeDtypeStruct((rows, 768), BF)
    heads = jax.ShapeDtypeStruct((4, 2, 128, 1024), BF)
    made = [
        jax.ShapeDtypeStruct((rows, features), F32),
        jax.ShapeDtypeStruct((rows, features), BF),
        jax.ShapeDtypeStruct((rows, features), BF),
        heads,
        heads,
        jax.ShapeDtypeStruct((2, 128, 2048), BF),
        jax.ShapeDtypeStruct((layers - 1, 128, 1024), BF),
        jax.ShapeDtypeStruct((layers - 1, 2, 128, 2048), BF),
        triple,
        triple,
        triple,
        triple,
    ]
    spread = [
        jax.ShapeDtypeStruct((layers, 8, features), F32),
        jax.ShapeDtypeStruct((layers, 2, 768), F32),
        jax.ShapeDtypeStruct((layers, 1, 2048), F32),
        jax.ShapeDtypeStruct((1, 128), F32),
    ]
    copies = 19 + layers - 1
    return pl.pallas_call(
        functools.partial(start_kernel, layers),
        in_specs=[hbm] * (1 + len(args)),
        out_specs=[hbm] * len(made) + [vmem] * len(spread),
        out_shape=made + spread,
        scratch_shapes=[
            *[pltpu.VMEM(a.shape, a.dtype) for a in args + made],
            pltpu.VMEM((rows, features), BF),
            pltpu.VMEM((128, 2048), BF),
            pltpu.VMEM((4, 8, small, 128), F32),
            pltpu.VMEM((rows, 768), BF),
            pltpu.VMEM((rows, 768), BF),
            pltpu.SemaphoreType.DMA,
            pltpu.SemaphoreType.DMA((len(args),)),
            pltpu.SemaphoreType.DMA((len(made),)),
            pltpu.SemaphoreType.DMA((copies,)),
            pltpu.SemaphoreType.DMA((copies,)),
        ],
        compiler_params=pltpu.CompilerParams(vmem_limit_bytes=60 * 1024 * 1024, collective_id=0, has_side_effects=True),
        cost_estimate=took(60),
        name="start",
    )(x, *args)


def finish_kernel(
    layers, grad_ref, even_ref, odd_ref, here_ref, away_ref, *rest,
):
    sums, rest = rest[:4 * layers], rest[4 * layers:]
    grad_out_ref, project_ref, output_ref, reduce_ref, expand_ref, small_ref, rest = *rest[:6], rest[6:]
    odd_got, y_send, y_got, x_send, x_got, relay_send, relay_got, z_send, z_got, away_got, part_ref, part_got, rest = *rest[:12], rest[12:]
    rows_ref, core_got, x_rows, y_rows, near_send, near_got, far_send, far_got, local_sem, send_sem, recv_sem = rest
    own, place = lax.axis_index("dp"), lax.axis_index("tensor")
    core = own % 2
    keep = core == place // 2
    count = [0]

    def copy(source, target, device):
        index = count[0]
        count[0] += 1
        return pltpu.make_async_remote_copy(
            src_ref=source, dst_ref=target, send_sem=send_sem.at[index], recv_sem=recv_sem.at[index],
            device_id=device, device_id_type=MESH,
        )

    greet((1, 2, 4, 6, 8, 16))
    across = copy(odd_ref, odd_got, peer(CORE))
    across.start()
    beside = copy(away_ref, away_got, peer(Z0))
    beside.start()
    tokens = copy(grad_ref, grad_out_ref, peer(CORE | Z1))
    stay = pltpu.make_async_copy(grad_ref, grad_out_ref, local_sem)

    @pl.when(keep)
    def _():
        stay.start()

    @pl.when(jnp.logical_not(keep))
    def _():
        tokens.start()

    vectors = 6 * layers
    rows_ref[...] = jnp.zeros_like(rows_ref)
    for layer in range(layers):
        first_ref, second_ref, unit_ref, head_ref = sums[4 * layer:4 * layer + 4]
        base = vectors + 12 * layer
        for block in range(8):
            slot = (block % 2) * 4 + (block // 2 % 2) * 2 + block // 4
            lanes = slice(block * 128, (block + 1) * 128)
            rows_ref[slot, 6 * layer:6 * layer + 2, :] = first_ref[0:2, lanes]
            rows_ref[slot, 6 * layer + 2:6 * layer + 6, :] = second_ref[0:4, lanes]
            for quarter in range(2):
                lane = pl.multiple_of(quarter * 1024 + xor_block(block, own) * 128, 128)
                rows_ref[slot, pl.ds(base + 2 * core + quarter, 1), :] = unit_ref[0:1, pl.ds(lane, 128)]
                row = base + 4 + 4 * (quarter + core - 2 * quarter * core)
                for half in range(2):
                    rows_ref[slot, pl.ds(row + 2 * half, 2), :] = head_ref[
                        2 * quarter:2 * quarter + 2, half * 128:(half + 1) * 128
                    ]
    hop = copy(rows_ref.at[pl.ds(4, 4)], core_got, peer(CORE))
    hop.start()
    hop.wait()
    rows_ref[0:4] = rows_ref[0:4] + core_got[...]
    hop = copy(rows_ref.at[pl.ds(2, 2)], x_rows, peer(XBIT))
    hop.start()
    across.wait()
    for chip in range(4):
        for quarter in range(2):
            odd_got[chip, quarter] = odd_got[chip, quarter] + even_ref[chip, quarter]
    y_send[0], y_send[1] = odd_got[2, 0], odd_got[3, 0]
    x_send[0], x_send[1] = odd_got[1, 1], odd_got[3, 1]
    over_y = copy(y_send, y_got, peer(YBIT))
    over_x = copy(x_send, x_got, peer(XBIT))
    over_y.start()
    over_x.start()
    hop.wait()
    rows_ref[0:2] = rows_ref[0:2] + x_rows[...]
    hop = copy(rows_ref.at[pl.ds(1, 1)], y_rows, peer(YBIT))
    hop.start()
    hop.wait()
    rows_ref[0] = rows_ref[0] + y_rows[0]
    near_send[...] = jnp.zeros_like(near_send)
    far_send[...] = jnp.zeros_like(far_send)
    near_send[0:vectors, :] = rows_ref[0, 0:vectors, :]
    for layer in range(layers):
        base = vectors + 12 * layer
        near_send[vectors + 2 * layer:vectors + 2 * layer + 1, :] = rows_ref[0, base + 1:base + 2, :]
        near_send[vectors + 2 * layer + 1:vectors + 2 * layer + 2, :] = rows_ref[0, base + 3:base + 4, :]
    hop = copy(near_send, near_got, peer(Z0))
    hop.start()
    over_y.wait()
    over_x.wait()
    relay_send[0] = odd_got[1, 0] + y_got[1]
    relay_send[1] = odd_got[2, 1] + x_got[1]
    relays = [copy(relay_send.at[i], relay_got.at[i], peer(mask)) for i, mask in ((0, XBIT), (1, YBIT))]
    for one in relays:
        one.start()
    beside.wait()
    for kind in range(2):
        for side in range(2):
            part_ref[side, kind] = here_ref[kind, side] + away_got[kind, side]
    crossing = copy(part_ref.at[1], part_got.at[1], {
        "dp": flip(own, 1), "tensor": place + core * (flip(place, 2) - place)
    })
    crossing.start()
    along = copy(part_ref.at[0], part_got.at[0], peer(Z1))

    @pl.when(core == 1)
    def _():
        along.start()

    @pl.when(core == 0)
    def _():
        part_got[0] = part_ref[0]

    for one in relays:
        one.wait()
    total = [odd_got[0, 0] + y_got[0] + relay_got[0], odd_got[0, 1] + x_got[0] + relay_got[1]]
    z_send[core] = total[0]
    z_send[1 - core] = total[1]
    heads = copy(z_send.at[1], z_got, peer(Z1))
    heads.start()
    hop.wait()
    far_send[0:vectors, :] = rows_ref[0, 0:vectors, :] + near_got[0:vectors, :]
    for layer in range(layers):
        base = vectors + 12 * layer
        far_send[vectors + layer:vectors + layer + 1, :] = (
            rows_ref[0, base + 2:base + 3, :] + near_got[vectors + 2 * layer + 1:vectors + 2 * layer + 2, :]
        )
        far_send[vectors + layers + 4 * layer:vectors + layers + 4 * layer + 4, :] = rows_ref[0, base + 8:base + 12, :]
    hop = copy(far_send, far_got, peer(Z1))
    hop.start()
    crossing.wait()

    @pl.when(core == 1)
    def _():
        along.wait()

    reduce_ref[...] = (part_got[0, 0].astype(F32) + part_got[1, 0].astype(F32)).T
    expand_ref[...] = part_got[0, 1].astype(F32) + part_got[1, 1].astype(F32)
    hop.wait()
    small_ref[0:vectors, :] = far_send[0:vectors, :] + far_got[0:vectors, :]
    for layer in range(layers):
        base = vectors + 12 * layer
        row = vectors + layer
        small_ref[row:row + 1, :] = (
            rows_ref[0, base:base + 1, :] + near_got[vectors + 2 * layer:vectors + 2 * layer + 1, :] + far_got[row:row + 1, :]
        )
        row = vectors + layers + 4 * layer
        small_ref[row:row + 4, :] = rows_ref[0, base + 4:base + 8, :] + far_got[row:row + 4, :]
    heads.wait()
    for part in range(3):
        here = slice(part * 256, (part + 1) * 256)
        project_ref[part] = z_send[0, :, here].astype(F32) + z_got[:, here].astype(F32)
    output_ref[...] = (z_send[0, :, 768:].astype(F32) + z_got[:, 768:].astype(F32)).T

    @pl.when(keep)
    def _():
        stay.wait()

    @pl.when(jnp.logical_not(keep))
    def _():
        tokens.wait()


def finish(grad, even, odd, here, away, sums):
    layers = len(sums)
    vmem = pl.BlockSpec(memory_space=pltpu.VMEM)
    rows = 18 * layers
    args = [grad, even, odd, here, away, *[array for layer in sums for array in layer]]
    small = 8 * (-(-11 * layers // 8))
    outs = [
        jax.ShapeDtypeStruct(grad.shape, BF),
        jax.ShapeDtypeStruct((3, 128, 256), F32),
        jax.ShapeDtypeStruct((256, 128), F32),
        jax.ShapeDtypeStruct((1024, 128), F32),
        jax.ShapeDtypeStruct((128, 1024), F32),
        jax.ShapeDtypeStruct((small, 128), F32),
    ]
    one = (128, 1024)
    copies = 15
    return pl.pallas_call(
        functools.partial(finish_kernel, layers),
        in_specs=[vmem] * len(args),
        out_specs=[vmem] * len(outs),
        out_shape=outs,
        scratch_shapes=[
            pltpu.VMEM((4, 2, *one), BF),
            *[pltpu.VMEM((2, *one), BF)] * 7,
            pltpu.VMEM(one, BF),
            *[pltpu.VMEM((2, 2, *one), BF)] * 3,
            pltpu.VMEM((8, rows, 128), F32),
            pltpu.VMEM((4, rows, 128), F32),
            pltpu.VMEM((2, rows, 128), F32),
            pltpu.VMEM((1, rows, 128), F32),
            *[pltpu.VMEM((small, 128), F32)] * 4,
            pltpu.SemaphoreType.DMA,
            pltpu.SemaphoreType.DMA((copies,)),
            pltpu.SemaphoreType.DMA((copies,)),
        ],
        compiler_params=pltpu.CompilerParams(vmem_limit_bytes=VMEM_LIMIT, collective_id=1, has_side_effects=True),
        cost_estimate=took(50),
        name="finish",
    )(*args)


def fetch_heads(piece, core, turn, out):
    token = yield
    far = swap(after(piece, token), Z1)
    token = yield []
    far = after(far, token)
    own = jnp.stack([jnp.where(core == 0, piece, far), jnp.where(core == 0, far, piece)])
    from_x = swap(own, XBIT)
    from_y = swap(own, YBIT)
    token = yield [own]
    from_x, from_y = after_all((from_x, from_y), token)
    across = swap(from_y, XBIT)
    token = yield [from_x, from_y]
    quads = jnp.stack([own, from_x, from_y, after(across, token)])
    other = swap(quads, CORE)
    token = yield [quads]
    out += [quads, other, turn]


def join_units(first, first_x, first_y, second, first_out, second_out):
    second_x, second_y = swap(second, XBIT), swap(second, YBIT)
    token = yield [first_x, first_y, second]
    first_x, second_x, second_y = after_all((first_x, second_x, second_y), token)
    first_across, second_across = swap(first_x, YBIT), swap(second_y, XBIT)
    token = yield [second_x, second_y]
    first_across, second_across = after_all((first_across, second_across), token)
    first_out += [first, first_x, first_y, first_across]
    second_out += [second, second_x, second_y, second_across]
    yield [first_across, second_across]


def fetch_units_near(first, first_out, second_out):
    token = yield
    first = after(first, token)
    first_x, first_y, second = swap(first, XBIT), swap(first, YBIT), swap(first, Z0)
    token = yield []
    first_x, first_y, second = after_all((first_x, first_y, second), token)
    yield from join_units(first, first_x, first_y, second, first_out, second_out)


def fetch_units(pair, core, first_out, second_out):
    token = yield
    far = swap_some(after(pair, token), (0, Z1))
    token = yield []
    first = jnp.where(core == 0, pair, after(far, token))
    second = swap(first, Z0)
    token = yield [first]
    second = after(second, token)
    token = yield [second]
    first = after(first, token)
    first_x, first_y = swap(first, XBIT), swap(first, YBIT)
    token = yield []
    first_x, first_y = after_all((first_x, first_y), token)
    yield from join_units(first, first_x, first_y, second, first_out, second_out)


def unpack_heads(values):
    return values[:, :768].reshape(128, 3, 256).transpose(1, 0, 2), values[:, 768:].T


def reduce_heads(even, odd, core, out):
    token = yield
    got = swap(odd, CORE)
    token = yield []
    got = after(got, token)
    low, high = even[:2] + got[:2], even[2:] + got[2:]
    from_y = swap(high, YBIT)
    token = yield [low, high]
    from_y = after(from_y, token)
    relayed = low[1] + from_y[1]
    relay = swap(relayed, XBIT)
    token = yield [relayed]
    total = low[0] + from_y[0] + after(relay, token)
    yield from close_heads(total, core, out)


def close_heads(total, core, out):
    near = jnp.where(core == 0, total[0], total[1])
    away = jnp.where(core == 0, total[1], total[0])
    far = swap(away, Z1)
    token = yield [near, away]
    out.append(unpack_heads(near.astype(F32) + after(far, token).astype(F32)))
    yield list(out[-1])


def reduce_units(reduce_parts, expand_parts, core, out):
    yield
    own_r, pair_r, single_r = reduce_parts
    from_y = swap(pair_r, YBIT)
    yield []
    own_e, pair_e, single_e = expand_parts
    from_x = swap(pair_e, XBIT)
    token = yield []
    from_y = after(from_y, token)
    relayed_r = single_r + from_y[:, 1]
    relay_r = swap(relayed_r, XBIT)
    token = yield [relayed_r]
    from_x = after(from_x, token)
    relayed_e = single_e + from_x[:, 1]
    relay_e = swap(relayed_e, YBIT)
    token = yield [relayed_e]
    relay_r, relay_e = after_all((relay_r, relay_e), token)
    totals = [
        jnp.stack([own_r[i] + from_y[i, 0] + relay_r[i], own_e[i] + from_x[i, 0] + relay_e[i]]) for i in range(2)
    ]
    if core is None:
        out += totals
        yield totals
        return
    yield from close_units(*totals, core, out)


def close_units(here, away, core, out):
    got = swap(away, Z0)
    token = yield [here, away]
    here = here + after(got, token)
    token = yield [here]
    here = after(here, token)
    same, cross = here[:, 0], here[:, 1]
    same_got, cross_got = swap_some(same, (0, Z1)), swap_some(cross, (CORE, CORE | Z1))
    token = yield [same, cross]
    same_got, cross_got = after_all((same_got, cross_got), token)
    out.append(jnp.where(core == 0, same, same_got).astype(F32) + cross_got.astype(F32))
    yield [out[-1]]


def fast_device(
    layer_input,
    first_gain,
    first_shift,
    project_weight,
    project_bias,
    output_weight,
    output_bias,
    second_gain,
    second_shift,
    expand_weight,
    expand_bias,
    reduce_weight,
    reduce_bias,
    picture_start,
    cotangent,
):
    own = lax.axis_index("dp")
    place = lax.axis_index("tensor")
    core = own & 1
    keep = core == (place >> 1)
    own_keep = jnp.stack([own, keep.astype(jnp.int32)]).astype(jnp.int32)
    me = (2 * core + (place & 1)).astype(jnp.int32).reshape(1)
    slopes = head_slopes((place ^ (2 * core)) * 4, 4)

    turn = jnp.zeros((1,), jnp.int32)
    (
        resid, normed, far, even, odd, first_pieces, own_heads, own_units, near_mine, far_mine, got_near, got_far,
        vectors_of, head_bias_of, unit_bias_of, places,
    ) = start(
        layer_input, project_weight, output_weight, expand_weight, reduce_weight,
        (first_gain, first_shift, output_bias, second_gain, second_shift, reduce_bias), project_bias, expand_bias,
        picture_start,
    )
    small = [(vectors_of[i], head_bias_of[i], unit_bias_of[i]) for i in range(LAYERS)]
    starts = places[0, :picture_start.shape[1]].astype(jnp.int32)
    heads, units = [[] for i in range(LAYERS)], [([], []) for i in range(LAYERS)]
    heads[0] += [even, odd, turn]
    head_tasks, unit_tasks = [None], [task(fetch_units_near(first_pieces, *units[0]))]
    for layer in range(1, LAYERS):
        head_tasks.append(task(fetch_heads(own_heads[layer - 1], core, turn, heads[layer])))
        unit_tasks.append(task(fetch_units(own_units[layer - 1], core, *units[layer])))
    saved = []
    for layer in range(LAYERS):
        vectors, head_bias, unit_bias = small[layer]
        first, last = layer == 0, layer + 1 == LAYERS
        if not first:
            far = swap(normed, Z0)
            while not heads[layer]:
                advance(normed, head_tasks[layer])
            near_mine, near_other = project(normed, head_bias, heads[layer])
            got_near = swap(near_other, CORE)
            far_mine, far_other = project(after(far, near_mine), head_bias, heads[layer])
            got_far = swap(far_other, CORE)
        pieces = heads[layer]
        made = advance(far_mine, unit_tasks[layer])
        blocks = after_all((near_mine, far_mine, got_near, got_far), *made)
        if last:
            cotangent_far = redeal(after(cotangent, far_mine))
        far_mixed, far_send, far_exact, far_log = attend(blocks, 1, slopes, starts, me)
        far_got = swap(far_send, CORE)
        far_part = mix_far(far_mixed, far_got, pieces)
        far_term = swap(far_part, Z0)
        made = advance(far_part, unit_tasks[layer])
        if last:
            grad, unused, flip_grad = enter(own_keep, cotangent, after(cotangent_far, far_part), vectors)
            grad_other = swap(flip_grad, CORE)
            made.append(grad)
        near_blocks = after_all(blocks, far_part, *made)
        near_mixed, near_send, near_exact, near_log = attend(near_blocks, 0, slopes, starts, me)
        near_got = swap(near_send, CORE)
        made = advance(near_mixed, unit_tasks[layer])
        if first:
            advance(near_mixed, unit_tasks[1], head_tasks[1])
        mid, normed_two, flip_two = mix_near(near_mixed, near_got, after(far_term, near_mixed, *made), resid, vectors, pieces)
        normed_other = swap(flip_two, CORE)
        if first:
            made = advance(mid, unit_tasks[0])
            made += advance(mid, unit_tasks[1], head_tasks[1])
            normed_two = after(normed_two, *made)
        hidden, active, near_out, away_out = mlp_forward(turn, normed_two, normed_other, unit_bias, units[layer])
        got_out = swap(away_out, CORE)
        if not last:
            got_out = after(got_out, *advance(near_out, head_tasks[layer + 1], unit_tasks[layer + 1]))
        out, following = mlp_close(last, own_keep, near_out, got_out, mid, vectors)
        if not last:
            advance(out, head_tasks[layer + 1])
            advance(out, unit_tasks[layer + 1])
        saved.append((
            resid, normed, far, blocks, (near_exact, far_exact), (near_log, far_log), (near_mixed, far_mixed),
            (near_got, far_got), mid, normed_two, normed_other, hidden, active,
        ))
        resid, normed = out, following
    layer_output = jnp.where(keep, normed, redeal(normed))
    grad = after(grad, normed)
    sums = [None] * LAYERS
    head_grad, unit_grad = ([[] for i in range(LAYERS)] for j in range(2))
    pending = []
    for layer in reversed(range(LAYERS)):
        vectors, pieces = small[layer][0], heads[layer]
        (
            resid, normed, far, blocks, exacts, logs, mixed, mixed_got, mid, normed_two, normed_other, hidden, active,
        ) = saved[layer]
        grad_hidden, unit_sums, near_term, away_term = mlp_backward(turn, grad, grad_other, hidden, units[layer])
        got_term = after(swap(away_term, CORE), *advance(near_term, *pending))
        grad_mid, grad_low, second_sums = mlp_open(near_term, got_term, mid, grad, vectors)
        grad_far = swap(grad_low, Z0)
        first = layer == 0
        reduce_parts = unit_grads("x", grad, grad_other, after(active, grad_low))
        near_mine, near_other = unmix(after(grad_low, reduce_parts[0]), pieces)
        got_near = swap(near_other, CORE)
        expand_parts = unit_grads("y", normed_two, normed_other, after(grad_hidden, near_mine))
        unit_task = task(reduce_units(reduce_parts, expand_parts, None if first else core, unit_grad[layer]))
        advance(None, unit_task)
        advance(None, unit_task)
        far_mine, far_other = unmix(after(grad_far, expand_parts[0]), pieces)
        got_far = swap(far_other, CORE)
        made = advance(far_mine, *pending)
        grads_mixed = after_all((near_mine, far_mine, got_near, got_far), *made)
        mine_0, away_0 = attend_pull(0, blocks, grads_mixed, exacts, logs, slopes, starts, me)
        other_0 = swap(away_0, CORE)
        made = advance(mine_0, unit_task)
        grads_mixed = after_all(grads_mixed, mine_0, *made)
        mine_1, away_1 = attend_pull(1, blocks, grads_mixed, exacts, logs, slopes, starts, me)
        other_1 = swap(away_1, CORE)
        made = advance(mine_1, unit_task, *pending)
        other_1 = after(other_1, *made, *([layer_output] if layer == LAYERS - 1 else []))
        mine, other = (mine_0, mine_1), (other_0, other_1)
        far_part = unproject_far(mine, other, pieces)
        far_term = swap(far_part, Z0)
        even, odd, head_sums = head_grads(
            turn, normed, far, grad_low, after(grad_far, far_part), mine, other, mixed, mixed_got
        )
        if not first:
            head_task = task(reduce_heads(even, odd, core, head_grad[layer]))
            advance(None, head_task)
        made = advance(head_sums, unit_task)
        grad, grad_low, first_sums = unproject_near(
            first, own_keep, mine, other, after(far_term, *made), resid, grad_mid, vectors, pieces
        )
        sums[layer] = (first_sums, second_sums, unit_sums, head_sums)
        if not first:
            grad_other = swap(grad_low, CORE)
            grad = after(grad, *advance(grad, head_task))
        pending = [unit_task, head_task]
    input_grad, *grads, small_sums = finish(grad_low, even, odd, *unit_grad[0], sums)
    head_grad[0], unit_grad[0] = [grads[:2]], [grads[2:]]
    unit_grad[1:] = [[(g[0][0].T, g[0][1])] for g in unit_grad[1:]]
    six = small_sums[:6 * LAYERS].reshape(LAYERS, 6, 128)
    unit_sum = small_sums[6 * LAYERS:7 * LAYERS]
    head_sum = small_sums[7 * LAYERS:11 * LAYERS].reshape(LAYERS, 2, 2, 128).transpose(0, 2, 1, 3).reshape(LAYERS, 2, 256)
    head_sum = lax.dynamic_slice_in_dim(head_sum, own * 32, 32, 2)
    return (
        layer_output,
        input_grad,
        six[:, 0],
        six[:, 1],
        jnp.stack([g[0][0] for g in head_grad]),
        head_sum,
        jnp.stack([g[0][1] for g in head_grad]),
        six[:, 2],
        six[:, 3],
        six[:, 4],
        jnp.stack([g[0][1] for g in unit_grad]),
        unit_sum,
        jnp.stack([g[0][0] for g in unit_grad]),
        six[:, 5],
    )


def solution(mesh):
    placed = (
        P(("dp", "tensor"), None),
        P(None, "dp"),
        P(None, "dp"),
        P(None, None, "dp", "tensor"),
        P(None, None, ("tensor", "dp")),
        P(None, "tensor", "dp"),
        P(None, "dp"),
        P(None, "dp"),
        P(None, "dp"),
        P(None, "dp", "tensor"),
        P(None, ("tensor", "dp")),
        P(None, "tensor", "dp"),
        P(None, "dp"),
        P("dp", None),
        P(("dp", "tensor"), None),
    )
    return jax.shard_map(
        fast_device if mesh_is_paired(mesh) else on_device,
        mesh=mesh,
        in_specs=placed,
        out_specs=(
            P(("dp", "tensor"), None),
            P(("dp", "tensor"), None),
            P(None, "dp"),
            P(None, "dp"),
            P(None, None, "dp", "tensor"),
            P(None, None, ("tensor", "dp")),
            P(None, "tensor", "dp"),
            P(None, "dp"),
            P(None, "dp"),
            P(None, "dp"),
            P(None, "dp", "tensor"),
            P(None, ("tensor", "dp")),
            P(None, "tensor", "dp"),
            P(None, "dp"),
        ),
        check_vma=False,
    )
```
